32 devices in a mesh: dp: 8 (over y, x, core), fsdp: 4 (over z).
Axes of the slice: x: 2, y: 2, z: 4, core: 2. Of those that a mesh axis runs over, the one named last changes fastest.
Arguments:
- tokens: bfloat16 [2, 8192, 1024], P(None, ('dp', 'fsdp')), may hold values from -6 to 6
- cotangent: bfloat16 [2, 8192, 1024], P(None, ('dp', 'fsdp')), may hold values from -6 to 6
- doc_lengths: int32 [2, 8], replicated, may hold values from 0 to 8192, as said below
- partner: int32 [2, 8], replicated, may hold values from 0 to 7, as said below
- memory_picks: int32 [2, 8, 8, 128], P(None, 'dp'), may hold values from 0 to 1023, as said below
- attention_in: bfloat16 [2, 1024, 3072], P(None, ('dp', 'fsdp')), may hold values from -0.1875 to 0.1875
- attention_out: bfloat16 [2, 1024, 1024], P(None, ('dp', 'fsdp')), may hold values from -1.5 to 1.5
- feed_in: bfloat16 [2, 1024, 5632], P(None, ('dp', 'fsdp')), may hold values from -0.1875 to 0.1875
- feed_out: bfloat16 [2, 2816, 1024], P(None, ('dp', 'fsdp')), may hold values from -0.109375 to 0.109375
- norm_gains: bfloat16 [2, 2, 1024], P(None, None, ('dp', 'fsdp')), may hold values from 0.5 to 1.5
Outputs:
- layer_output: bfloat16 [2, 8192, 1024], P(None, ('dp', 'fsdp'))
- input_grad: float32 [2, 8192, 1024], P(None, ('dp', 'fsdp'))
- grad_attention_in: float32 [2, 1024, 3072], P(None, ('dp', 'fsdp'))
- grad_attention_out: float32 [2, 1024, 1024], P(None, ('dp', 'fsdp'))
- grad_feed_in: float32 [2, 1024, 5632], P(None, ('dp', 'fsdp'))
- grad_feed_out: float32 [2, 2816, 1024], P(None, ('dp', 'fsdp'))
- grad_norm_gains: float32 [2, 2, 1024], P(None, None, ('dp', 'fsdp'))
The draws below stay inside these ranges and needn't reach their ends.
Inputs may be any that keep to these rules, and one draw needn't show every extreme that they name: `doc_lengths`: the documents of a row fill its slots exactly, each one's last slot at least half full. A slot's partner is another slot of the same micro-batch. `memory_picks`: for each micro-batch, slot and head, 128 distinct places, all among the slot's non-padding tokens.
All inputs are finite; a program needn't handle non-finite values.
Results may differ from the reference program's by a relative error of at most 0.02.
Values may be sent and summed in bfloat16 or wider, within the bound.
A program may use at most 576 MiB of HBM per device.

```python
import math
from functools import reduce
import jax
import jax.numpy as jnp
from jax import lax

D = 1024
HEADS = 8
HEAD_DIM = 128
FF = 2816
SEG = 1024
TOPK = 128
LAYERS = 2
MICRO = 2
ROWS = 8192
N_DP = 8


def document_plan(key):
    keys = jax.random.split(key, 3)
    whole_row = jax.random.randint(keys[0], (), 0, MICRO)
    cut_marks = jax.random.randint(keys[1], (MICRO, N_DP), 0, 3) == 0
    slot_ids = jnp.arange(N_DP, dtype=jnp.int32)
    row_ids = jnp.arange(MICRO, dtype=jnp.int32)
    start_marks = cut_marks & (row_ids[:, None] != whole_row) | (slot_ids[None, :] == 0)
    owner_doc = jnp.cumsum(start_marks.astype(jnp.int32), axis=1) - 1
    doc_counts = jnp.sum((owner_doc[:, :, None] == slot_ids[None, None, :]).astype(jnp.int32), axis=1)
    last_fill = jax.random.randint(keys[2], (MICRO, N_DP), SEG // 2, SEG + 1)
    last_fill = jnp.where(row_ids[:, None] == whole_row, SEG, last_fill)
    return jnp.where(doc_counts > 0, (doc_counts - 1) * SEG + last_fill, 0).astype(jnp.int32)


def slot_valid(lengths):
    slot_counts = ((lengths + SEG - 1) // SEG).astype(jnp.int32)
    slot_starts = (jnp.cumsum(slot_counts) - slot_counts).astype(jnp.int32)
    slot_index = jnp.arange(lengths.shape[0], dtype=jnp.int32)
    started = (slot_starts[None, :] <= slot_index[:, None]) & (slot_counts[None, :] > 0)
    owner_doc = (jnp.sum(started.astype(jnp.int32), axis=1) - 1).astype(jnp.int32)
    owner_pick = slot_index[None, :] == owner_doc[:, None]
    first_slot = jnp.sum(jnp.where(owner_pick, slot_starts[None, :], 0), axis=1)
    doc_total = jnp.sum(jnp.where(owner_pick, lengths[None, :], 0), axis=1)
    return jnp.clip(doc_total - (slot_index - first_slot) * SEG, 0, SEG).astype(jnp.int32)


def draw_doc_lengths(key, part):
    return document_plan(key)


def draw_memory_picks(key, part):
    lengths = document_plan(key)
    key = jax.random.fold_in(key, 7)
    valid_rows = jax.vmap(slot_valid)(lengths)
    noise_ints = jax.random.randint(key, (MICRO, N_DP, HEADS, SEG), 0, 1 << 20)
    positions = jnp.arange(SEG, dtype=jnp.int32)
    rank_score = noise_ints * SEG + positions
    ends = (positions == 0) | (positions == valid_rows[:, :, None, None] - 1)
    rank_score = jnp.where(ends, (1 << 20) * SEG + positions, rank_score)
    rank_score = jnp.where(positions < valid_rows[:, :, None, None], rank_score, -1)
    return lax.top_k(rank_score, TOPK)[1].astype(jnp.int32)


def draw_partner(key, part):
    key = jax.random.fold_in(key, 5)
    offsets = jax.random.randint(key, (MICRO, N_DP), 1, N_DP)
    offsets = offsets.at[0, 0].set(N_DP - 1).at[0, 1].set(N_DP - 1)
    return ((jnp.arange(N_DP, dtype=jnp.int32)[None, :] + offsets) % N_DP).astype(jnp.int32)


def level_of(own_key, extent, cuts, least, high):
    gain, own = 1.0, jax.random.fold_in(own_key, 6)
    for position, shards_of in cuts:
        steps = jnp.exp(jax.random.uniform(jax.random.fold_in(own, position), (shards_of,), jnp.float32, least / len(cuts), high / len(cuts)))
        gain = gain * jnp.repeat(steps, extent[position] // shards_of).reshape([-1 if axis == position else 1 for axis in range(len(extent))])
    return gain


def normal_values(stream_key, extent, width, most, shards=(), held_as=jnp.bfloat16):
    values = jax.random.normal(stream_key, extent, jnp.float32) * width
    if len(shards) > 0:
        values = level_of(stream_key, extent, shards, -0.22, 0.18) * values
    return jnp.clip(values, min=-most, max=most).astype(held_as)


def setup_inputs(seed: int = 0) -> dict:
    key_list = jax.random.split(jax.random.key(seed), 11)
    return {
        "tokens": normal_values(key_list[0], (MICRO, ROWS, D), 1.0, 6.0, ((1, 32),)),
        "cotangent": normal_values(key_list[1], (MICRO, ROWS, D), 1.0, 6.0, ((1, 32),)),
        "doc_lengths": draw_doc_lengths(jax.random.fold_in(key_list[10], 71), 0),
        "partner": draw_partner(jax.random.fold_in(key_list[10], 71), 0),
        "memory_picks": draw_memory_picks(jax.random.fold_in(key_list[10], 71), 0),
        "attention_in": normal_values(key_list[5], (LAYERS, D, 3 * D), D ** -0.5, 0.1875, ((1, 32),)),
        "attention_out": normal_values(key_list[6], (LAYERS, D, D), (D // 64) ** -0.5, 1.5, ((1, 32),)),
        "feed_in": normal_values(key_list[7], (LAYERS, D, 2 * FF), D ** -0.5, 0.1875, ((1, 32),)),
        "feed_out": normal_values(key_list[8], (LAYERS, FF, D), FF ** -0.5, 0.109375, ((1, 32),)),
        "norm_gains": jnp.clip(1.0 + 0.1 * jax.random.normal(key_list[9], (LAYERS, 2, D), jnp.float32), 0.5, 1.5).astype(jnp.bfloat16),
    }


@jax.custom_vjp
def low(v):
    return lax.optimization_barrier(v.astype(jnp.bfloat16)).astype(jnp.float32)

@jax.custom_vjp
def low_back(v):
    return v

def low_keep(v):
    return (low(v), None)

def low_pass(kept, grad):
    return (grad,)

def back_keep(v):
    return (v, None)

def back_low(kept, grad):
    return (low(grad),)
low.defvjp(low_keep, low_pass)
low_back.defvjp(back_keep, back_low)
epsilon = 1e-06
masked_score = -1e+30
highest = lax.Precision.HIGHEST

def rms_gain(hidden, gain_row):
    return hidden * lax.rsqrt(lax.optimization_barrier(jnp.mean(hidden * hidden, axis=-1, keepdims=True)) + epsilon) * gain_row

def rotate(values):
    half_dim = values.shape[-1] // 2
    return jnp.concatenate([-values[..., half_dim:], values[..., :half_dim]], axis=-1)

def rope_tables(positions):
    half_dim = HEAD_DIM // 2
    frequency = jnp.exp(jnp.arange(half_dim, dtype=jnp.float32) * (-2.0 * math.log(10000.0) / HEAD_DIM))
    angles = positions.astype(jnp.float32)[:, None] * frequency[None, :]
    cos_table = jnp.concatenate([jnp.cos(angles), jnp.cos(angles)], axis=-1)[:, None, :]
    sin_table = jnp.concatenate([jnp.sin(angles), jnp.sin(angles)], axis=-1)[:, None, :]
    return (cos_table, sin_table)

def rotary(values, cos_table, sin_table):
    return values * cos_table + rotate(values) * sin_table

def slot_layout(lengths):
    slot_total = lengths.shape[0]
    slot_counts = ((lengths + SEG - 1) // SEG).astype(jnp.int32)
    slot_starts = (jnp.cumsum(slot_counts) - slot_counts).astype(jnp.int32)
    slot_index = jnp.arange(slot_total, dtype=jnp.int32)
    started = (slot_starts[None, :] <= slot_index[:, None]) & (slot_counts[None, :] > 0)
    owner_doc = (lax.optimization_barrier(jnp.sum(started.astype(jnp.int32), axis=1)) - 1).astype(jnp.int32)
    owner_pick = slot_index[None, :] == owner_doc[:, None]
    first_slot = lax.optimization_barrier(jnp.sum(jnp.where(owner_pick, slot_starts[None, :], 0), axis=1)).astype(jnp.int32)
    doc_total = lax.optimization_barrier(jnp.sum(jnp.where(owner_pick, lengths[None, :], 0), axis=1)).astype(jnp.int32)
    valid_rows = jnp.clip(doc_total - (slot_index - first_slot) * SEG, 0, SEG).astype(jnp.int32)
    return (valid_rows, owner_doc)

def memory_plan(lengths, partner_row):
    valid_rows, owner_doc = slot_layout(lengths)
    block_ids = jnp.arange(lengths.shape[0], dtype=jnp.int32)
    earlier = (block_ids[None, :] < block_ids[:, None]) & (owner_doc[None, :] == owner_doc[:, None])
    visible = earlier | (block_ids[None, :] == partner_row[:, None])
    return (valid_rows, visible)

def local_scores(query_rot, key_rot, valid_rows):
    score_scale = HEAD_DIM ** (-0.5)
    raw_scores = low_back(jnp.einsum('ihd,jhd->hij', query_rot, key_rot, precision=highest) * score_scale)
    places = jnp.arange(SEG, dtype=jnp.int32)
    allowed = (places[None, :] <= places[:, None]) & (places[None, :] < valid_rows)
    return jnp.where(allowed[None], raw_scores, masked_score)

def softmax_mix(score_list, value_list):
    row_max = reduce(jnp.maximum, [lax.optimization_barrier(jnp.max(score_block, axis=-1, keepdims=True)) for score_block in score_list])
    exp_list = [jnp.exp(score_block - row_max) for score_block in score_list]
    row_total = sum((lax.optimization_barrier(jnp.sum(exp_block, axis=-1, keepdims=True)) for exp_block in exp_list))
    return sum((jnp.einsum('hij,jhd->ihd', low(exp_block / row_total), values, precision=highest) for exp_block, values in zip(exp_list, value_list)))

def causal_slot(query_rot, key_rot, values_slot, valid_rows):
    return softmax_mix([local_scores(query_rot, key_rot, valid_rows)], [values_slot])

def memory_slot(query_rot, key_rot, values_slot, valid_rows, query_raw, allowed_row, memory_keys, memory_values):
    score_scale = HEAD_DIM ** (-0.5)
    memory_scores = low_back(jnp.einsum('ihd,jhd->hij', query_raw, memory_keys, precision=highest) * score_scale)
    memory_scores = jnp.where(allowed_row[None, None, :], memory_scores, masked_score)
    return softmax_mix([local_scores(query_rot, key_rot, valid_rows), memory_scores], [values_slot, memory_values])

def pick_memory(values, pick_rows):
    heads_first = jnp.swapaxes(values, 1, 2)
    chosen = jnp.take_along_axis(heads_first, pick_rows[..., None], axis=2)
    return jnp.swapaxes(chosen, 1, 2).reshape(N_DP * TOPK, HEADS, HEAD_DIM)

def layer_forward(hidden, weights, valid_row, visible_row, pick_rows, memory):
    weight_qkv, weight_out, weight_gate_up, weight_down, gain_pair = weights
    normed = low(rms_gain(hidden, gain_pair[0]))
    projected = low_back(jnp.einsum('sid,dk->sik', normed, weight_qkv, precision=highest))
    query_part, key_part, value_part = [block.reshape(N_DP, SEG, HEADS, HEAD_DIM) for block in jnp.split(projected, 3, axis=-1)]
    cos_table, sin_table = rope_tables(jnp.arange(SEG, dtype=jnp.int32))
    query_rot = low(rotary(query_part, cos_table, sin_table))
    key_rot = low(rotary(key_part, cos_table, sin_table))
    value_low = low(value_part)
    if memory:
        query_raw = low(query_part)
        key_raw = low(key_part)
        chosen_keys = pick_memory(key_raw, pick_rows)
        chosen_values = pick_memory(value_low, pick_rows)
        allowed = jnp.repeat(visible_row, TOPK, axis=1)
        slot_fn = jax.checkpoint(memory_slot)
        attended = lax.map(lambda entries: slot_fn(*entries, chosen_keys, chosen_values), (query_rot, key_rot, value_low, valid_row, query_raw, allowed))
    else:
        slot_fn = jax.checkpoint(causal_slot)
        attended = lax.map(lambda entries: slot_fn(*entries), (query_rot, key_rot, value_low, valid_row))
    attended_low = low(low_back(attended.reshape(N_DP, SEG, D)))
    mid_stream = hidden + low_back(jnp.einsum('sik,kd->sid', attended_low, weight_out, precision=highest))
    normed_ffn = low(rms_gain(mid_stream, gain_pair[1]))
    gate_up = low_back(jnp.einsum('sid,dk->sik', normed_ffn, weight_gate_up, precision=highest))
    gate_half, up_half = jnp.split(gate_up, 2, axis=-1)
    ffn_hidden = low(jax.nn.silu(gate_half) * up_half)
    return mid_stream + low_back(jnp.einsum('sik,kd->sid', ffn_hidden, weight_down, precision=highest))

def forward(plan_parts, tokens, attention_in, attention_out, feed_in, feed_out, norm_gains):

    def one_batch(entries):
        hidden, valid_row, visible_row, pick_rows = entries
        hidden = hidden.reshape(N_DP, SEG, D)
        for layer_index in range(LAYERS):
            weights = (attention_in[layer_index], attention_out[layer_index], feed_in[layer_index], feed_out[layer_index], norm_gains[layer_index])
            hidden = layer_forward(hidden, weights, valid_row, visible_row, pick_rows, layer_index == LAYERS - 1)
        return hidden.reshape(N_DP * SEG, D)
    return lax.map(one_batch, (tokens,) + plan_parts)

def reference(tokens, cotangent, doc_lengths, partner, memory_picks, attention_in, attention_out, feed_in, feed_out, norm_gains):
    valid_all, visible_all = jax.vmap(memory_plan)(doc_lengths, partner)
    plan_parts = (valid_all, visible_all, memory_picks)

    def wrapped(*floats):
        return forward(plan_parts, *floats)
    floats = tuple((entry.astype(jnp.float32) for entry in (tokens, attention_in, attention_out, feed_in, feed_out, norm_gains)))
    result, pullback = jax.vjp(wrapped, *floats)
    gradients = pullback(cotangent.astype(jnp.float32))
    return (result.astype(jnp.bfloat16), gradients[0], gradients[1], gradients[2], gradients[3], gradients[4], gradients[5])
```

```python
import functools
import math

import jax
import jax.numpy as jnp
from jax import lax
from jax.experimental import pallas as pl
from jax.experimental.pallas import tpu as pltpu
from jax.sharding import PartitionSpec as P

HEAD_DIM = 128
SEG = 1024
MICRO = 2
EPSILON = 1e-06
MASKED = -1e30
SCALE = HEAD_DIM ** (-0.5)
LOG2E = 1.0 / math.log(2.0)
BF = jnp.bfloat16
F32 = jnp.float32
VMEM_LIMIT = 48 * 1024 * 1024


def slot_layout(lengths):
    slot_total = lengths.shape[0]
    slot_counts = ((lengths + SEG - 1) // SEG).astype(jnp.int32)
    slot_starts = (jnp.cumsum(slot_counts) - slot_counts).astype(jnp.int32)
    slot_index = jnp.arange(slot_total, dtype=jnp.int32)
    started = (slot_starts[None, :] <= slot_index[:, None]) & (slot_counts[None, :] > 0)
    owner_doc = (jnp.sum(started.astype(jnp.int32), axis=1) - 1).astype(jnp.int32)
    owner_pick = slot_index[None, :] == owner_doc[:, None]
    first_slot = jnp.sum(jnp.where(owner_pick, slot_starts[None, :], 0), axis=1).astype(jnp.int32)
    doc_total = jnp.sum(jnp.where(owner_pick, lengths[None, :], 0), axis=1).astype(jnp.int32)
    valid_rows = jnp.clip(doc_total - (slot_index - first_slot) * SEG, 0, SEG).astype(jnp.int32)
    return (valid_rows, owner_doc)


def memory_plan(lengths, partner_row):
    valid_rows, owner_doc = slot_layout(lengths)
    block_ids = jnp.arange(lengths.shape[0], dtype=jnp.int32)
    earlier = (block_ids[None, :] < block_ids[:, None]) & (owner_doc[None, :] == owner_doc[:, None])
    visible = earlier | (block_ids[None, :] == partner_row[:, None])
    return (valid_rows, visible)


class Grid:
    def __init__(self, n_dp, pieces):
        self.n_dp, self.F = n_dp, pieces
        self.J = n_dp // 2
        self.bits = self.J.bit_length() - 1
        self.Q = pieces // 4
        self.U = 2 * self.Q
        self.R = SEG // pieces
        self.T = 2 * self.R

    def trace(self):
        dp = lax.axis_index("dp")
        self.c, self.j, self.f = dp % 2, dp // 2, lax.axis_index("fsdp")
        self.q, self.g = self.f // self.Q, self.f % self.Q
        self.m, self.r = self.q // 2, self.q % 2
        self.k = self.c * self.Q + self.g
        self.slot = 2 * self.j + self.r

    def permute(self, value, target):
        pairs = []
        for j in range(self.J):
            for c in range(2):
                for f in range(self.F):
                    j2, c2, f2 = target(j, c, f)
                    pairs.append(((j * 2 + c) * self.F + f, (j2 * 2 + c2) * self.F + f2))
        return lax.ppermute(value, ("dp", "fsdp"), pairs)

    def swap(self, value):
        return self.permute(value, lambda j, c, f: (j, 1 - c, f))

    def ring(self, value, t):
        return self.permute(value, lambda j, c, f: (j, c, (f + t) % self.F))

    def bit(self, phase, c):
        return phase if c == 0 else self.bits - 1 - phase

    def flip(self, value, phase):
        return self.permute(value, lambda j, c, f: (j ^ (1 << self.bit(phase, c)), c, f))

    def mask(self, key, c):
        return sum(1 << self.bit(p, c) for p in range(self.bits) if key >> p & 1)

    def place(self, key, c):
        return jnp.where(c == 0, self.j ^ self.mask(key, 0), self.j ^ self.mask(key, 1))

    def member(self, value, t):
        def target(j, c, f):
            q, g = f // self.Q, f % self.Q
            k = (c * self.Q + g + t) % self.U
            return (j, k // self.Q, q * self.Q + k % self.Q)

        return self.permute(value, target)

    def within(self, value, t):
        return self.permute(
            value, lambda j, c, f: (j, c, f // self.Q * self.Q + (f % self.Q + t) % self.Q)
        )

    def slots(self, value, t):
        def target(j, c, f):
            q, g = f // self.Q, f % self.Q
            slot = (2 * j + q % 2 + t) % self.n_dp
            return (slot // 2, c, (2 * (q // 2) + slot % 2) * self.Q + g)

        return self.permute(value, target)

    def _spread(self, second):
        def target(j, c, f):
            m = f // (self.F // 2)
            m = 1 - m if second else m
            k = min(f, self.F - 1 - f)
            return (j, k // self.Q, (2 * m + c) * self.Q + k % self.Q)

        return target

    def _collect(self, second):
        there = self._spread(second)
        back = {
            there(0, c, f): (c, f) for c in range(2) for f in range(self.F)
        }
        return lambda j, c, f: (j,) + back[(0, c, f)]

    def to_units(self, value):
        here = self.f // (self.F // 2)
        first = self.permute(jnp.where(here == 0, value[0], value[1]), self._spread(False))
        second = self.permute(jnp.where(here == 0, value[1], value[0]), self._spread(True))
        return jnp.concatenate(
            [jnp.where(self.m == 0, first, second), jnp.where(self.m == 0, second, first)]
        )

    def from_units(self, value):
        low, high = value[: self.R], value[self.R :]
        first = self.permute(jnp.where(self.m == 0, low, high), self._collect(False))
        second = self.permute(jnp.where(self.m == 0, high, low), self._collect(True))
        here = self.f // (self.F // 2)
        return jnp.stack([jnp.where(here == 0, first, second), jnp.where(here == 0, second, first)])


def any_spec():
    return pl.BlockSpec(memory_space=pl.ANY)


def assemble_body(count, place_ref, *refs):
    blocks, out, sem = refs[: 2 * count], refs[2 * count], refs[2 * count + 1]
    step = pl.program_id(0)
    for i in range(2 * count):

        @pl.when(step == i)
        def _():
            copy = pltpu.make_async_copy(blocks[i], out, sem)
            copy.start()
            copy.wait()


def assemble(grid, own, other):
    count, (rows, half) = len(own), own[0].shape
    places = [grid.place(key, grid.c) for key in range(count)]
    places += [grid.place(key, 1 - grid.c) for key in range(count)]
    places = jnp.stack(places + [grid.c, 1 - grid.c]).astype(jnp.int32)
    size = count * rows * 2 * half
    return pl.pallas_call(
        functools.partial(assemble_body, count),
        grid_spec=pltpu.PrefetchScalarGridSpec(
            num_scalar_prefetch=1,
            grid=(2 * count,),
            in_specs=[any_spec()] * (2 * count),
            out_specs=pl.BlockSpec(
                (rows, half), lambda i, place: (place[i], place[2 * count + i // count])
            ),
            scratch_shapes=[pltpu.SemaphoreType.DMA],
        ),
        out_shape=jax.ShapeDtypeStruct((count * rows, 2 * half), own[0].dtype),
        compiler_params=params(),
        cost_estimate=pl.CostEstimate(flops=0, bytes_accessed=4 * size, transcendentals=0),
    )(places, *own, *other)


def roll_blocks(grid, arrived):
    ordered = [arrived[(grid.F - i) % grid.F] for i in range(grid.F)]
    both = jnp.stack(ordered + ordered[:-1])
    return lax.dynamic_slice_in_dim(both, (grid.F - grid.f) % grid.F, grid.F, axis=0)


def gather_weight(grid, shard):
    rows, width = shard.shape
    half = width // 2
    mine = lax.dynamic_slice_in_dim(shard, grid.c * half, half, axis=1)
    got = grid.swap(lax.dynamic_slice_in_dim(shard, (1 - grid.c) * half, half, axis=1))
    pair = jnp.stack([jnp.where(grid.c == 0, mine, got), jnp.where(grid.c == 0, got, mine)])
    arrived = [pair] + [grid.ring(pair, t) for t in range(1, grid.F)]
    line = jnp.swapaxes(roll_blocks(grid, arrived), 0, 1).reshape(2 * grid.F * rows, half)
    blocks = [line]
    for phase in range(grid.bits):
        blocks = blocks + [grid.flip(block, phase) for block in blocks]
    return assemble(grid, blocks, [grid.swap(block) for block in blocks])


def scatter_gradient(grid, total):
    height, half = total.shape
    rows = height // (grid.J * 2 * grid.F)
    parts = total.reshape(grid.J, height // grid.J, half)
    pieces = {
        key: lax.dynamic_index_in_dim(parts, grid.place(key, grid.c), 0, keepdims=False)
        for key in range(grid.J)
    }
    for phase in range(grid.bits):
        for key in sorted(pieces, reverse=True):
            if key >> phase & 1:
                got = grid.flip(pieces.pop(key), phase)
                here = key ^ (1 << phase)
                pieces[here] = (pieces[here].astype(F32) + got.astype(F32)).astype(BF)
    line = pieces[0].reshape(2, grid.F, rows, half)

    def block(t):
        return lax.dynamic_index_in_dim(line, (grid.f + t) % grid.F, 1, keepdims=False)

    summed = block(0).astype(F32)
    for got in [grid.ring(block(t), t) for t in range(1, grid.F)]:
        summed = summed + got.astype(F32)
    mine = lax.dynamic_index_in_dim(summed, grid.c, 0, keepdims=False)
    give = lax.dynamic_index_in_dim(summed, 1 - grid.c, 0, keepdims=False)
    got = grid.swap(give.astype(BF)).astype(F32)
    return jnp.concatenate(
        [jnp.where(grid.c == 0, mine, got), jnp.where(grid.c == 0, got, mine)], axis=1
    )


def gather_gains(grid, shard):
    value = shard.astype(BF)
    arrived = [value] + [grid.ring(value, t) for t in range(1, grid.F)]
    line = roll_blocks(grid, arrived)
    other = grid.swap(line)
    line = jnp.stack([jnp.where(grid.c == 0, line, other), jnp.where(grid.c == 0, other, line)])
    blocks = [line]
    for phase in range(grid.bits):
        blocks = blocks + [grid.flip(block, phase) for block in blocks]
    whole = jnp.stack(blocks)
    order = jnp.arange(grid.J) ^ grid.j
    if grid.bits > 1:
        turned = sum(((order >> p) & 1) << grid.bit(p, 1) for p in range(grid.bits))
        order = jnp.where(grid.c == 0, order, turned)
    whole = jnp.take(whole, order, axis=0)
    whole = jnp.transpose(whole, (3, 4, 0, 1, 2, 5))
    return whole.reshape(shard.shape[0], shard.shape[1], -1)


def scatter_gains(grid, total):
    layers, kinds, width = total.shape
    rows = width // (grid.n_dp * grid.F)
    total = total + grid.swap(total)
    for phase in range(grid.bits):
        total = total + grid.flip(total, phase)
    parts = total.reshape(layers, kinds, grid.J, 2, grid.F, rows)
    mine = lax.dynamic_index_in_dim(parts, grid.j, 2, keepdims=False)
    mine = lax.dynamic_index_in_dim(mine, grid.c, 2, keepdims=False)

    def block(t):
        return lax.dynamic_index_in_dim(mine, (grid.f + t) % grid.F, 2, keepdims=False)

    return block(0) + sum(grid.ring(block(t), t) for t in range(1, grid.F))


def rope_tables():
    half_dim = HEAD_DIM // 2
    frequency = jnp.exp(
        jnp.arange(half_dim, dtype=F32) * (-2.0 * math.log(10000.0) / HEAD_DIM)
    )
    angles = jnp.arange(SEG, dtype=jnp.int32).astype(F32)[:, None] * frequency[None, :]
    cos, sin = jnp.cos(angles), jnp.sin(angles)
    return (jnp.concatenate([cos, cos], axis=-1), jnp.concatenate([-sin, sin], axis=-1))


def turn(values, cos, sin):
    return values * cos + pltpu.roll(values, HEAD_DIM // 2, 1) * sin


def params():
    return pltpu.CompilerParams(vmem_limit_bytes=VMEM_LIMIT)


def smem():
    return pl.BlockSpec(memory_space=pltpu.SMEM)


def whole_spec(shape):
    return pl.BlockSpec(shape, lambda *_: (0,) * len(shape))


def piece_start(grid, member, part):
    return (member if part == 0 else grid.F - 1 - member) * grid.R


def table_rows(grid, table_ref, member, part):
    start = pl.multiple_of(piece_start(grid, member, part), grid.R)
    return table_ref[pl.ds(start, grid.R), :]


def split_body(grid, memory, info_ref, cos_ref, sin_ref, q_ref, k_ref, v_ref, *outs):
    me = info_ref[0]
    for part in range(2):
        rows = pl.ds(part * grid.R, grid.R)
        cos = table_rows(grid, cos_ref, me, part)
        sin = table_rows(grid, sin_ref, me, part)
        query, key = q_ref[rows, :], k_ref[rows, :]
        outs[0][rows, :] = turn(query, cos, sin).astype(BF)
        outs[1][rows, :] = turn(key, cos, sin).astype(BF)
        outs[2][rows, :] = v_ref[rows, :].astype(BF)
        if memory:
            outs[3][rows, :] = query.astype(BF)
            outs[4][rows, :] = key.astype(BF)


def split_heads(grid, memory, info, tables, projected):
    rows, width = projected.shape
    heads = width // (3 * HEAD_DIM)
    count = 5 if memory else 3
    piece = lambda at: pl.BlockSpec((rows, HEAD_DIM), lambda h: (0, at * heads + h))
    return pl.pallas_call(
        functools.partial(split_body, grid, memory),
        grid=(heads,),
        out_shape=[jax.ShapeDtypeStruct((rows, heads * HEAD_DIM), BF)] * count,
        in_specs=[smem(), whole_spec((SEG, HEAD_DIM)), whole_spec((SEG, HEAD_DIM))]
        + [piece(0), piece(1), piece(2)],
        out_specs=[piece(0)] * count,
        compiler_params=params(),
        cost_estimate=pl.CostEstimate(
            flops=10 * rows * width, bytes_accessed=8 * rows * width, transcendentals=0
        ),
    )(info, *tables, projected, projected, projected)


def dot(left, right, contract):
    return lax.dot_general(
        left, right, (((contract[0],), (contract[1],)), ((), ())), preferred_element_type=F32
    )


def part_scores(grid, info_ref, part, query, keys):
    me, valid = info_ref[0], info_ref[1]
    shape = (grid.R, grid.R)
    apart = lax.broadcasted_iota(jnp.int32, shape, 0) - lax.broadcasted_iota(jnp.int32, shape, 1)
    found = []
    for t in range(grid.U):
        member = lax.rem(me - t + grid.U, grid.U)
        for side in range(part + 1):
            score = dot(keys[t][side * grid.R : (side + 1) * grid.R], query, (1, 1))
            if side == part:
                start = piece_start(grid, member, side)
                allowed = apart <= piece_start(grid, me, part) - start
                if side == 1:
                    down = lax.broadcasted_iota(jnp.int32, shape, 0)
                    allowed = allowed & (down < valid - start)
                score = jnp.where(allowed, score, MASKED)
            found.append((t, side, score))
    return found


def head_halves(own_ref, other_ref, step, per_half):
    return jnp.where(step < per_half, own_ref[...], other_ref[...])


def softmax_parts(scores):
    top = functools.reduce(jnp.maximum, [jnp.max(s, axis=0, keepdims=True) for s in scores])
    powers = [jnp.exp2((s - top) * (SCALE * LOG2E)) for s in scores]
    inverse = 1.0 / sum(jnp.sum(p, axis=0, keepdims=True) for p in powers)
    return [p * inverse for p in powers]


def attend_body(grid, memory, heads, info_ref, *refs):
    U, R = grid.U, grid.R
    q_ref, k_refs, v_refs = refs[0], refs[1 : 1 + U], refs[1 + U : 1 + 2 * U]
    refs = refs[1 + 2 * U :]
    keys, values = [r[...] for r in k_refs], [r[...] for r in v_refs]
    if memory:
        step = pl.program_id(0)
        memory_keys = head_halves(refs[1], refs[2], step, heads // 2)
        memory_values = head_halves(refs[3], refs[4], step, heads // 2)
        bias = refs[5][...]
    out_ref = refs[-1]
    for part in range(2):
        rows = pl.ds(part * R, R)
        found = part_scores(grid, info_ref, part, q_ref[rows, :], keys)
        scores = [s for _, _, s in found]
        mixed = [values[t][side * R : (side + 1) * R] for t, side, _ in found]
        if memory:
            scores.append(dot(memory_keys, refs[0][rows, :], (1, 1)) + bias)
            mixed.append(memory_values)
        total = sum(
            dot(value, p.astype(BF), (0, 0)) for value, p in zip(mixed, softmax_parts(scores))
        )
        out_ref[rows, :] = total.T.astype(BF)


def head_specs(grid, heads, memory_rows):
    per = heads // 2

    def head(h, info):
        return lax.rem(info[2] + h // per, 2) * per + h % per

    piece = pl.BlockSpec((grid.T, HEAD_DIM), lambda h, info: (0, head(h, info)))
    own = pl.BlockSpec((memory_rows, HEAD_DIM), lambda h, info: (0, jnp.minimum(h, per - 1)))
    other = pl.BlockSpec((memory_rows, HEAD_DIM), lambda h, info: (0, jnp.maximum(h - per, 0)))
    return piece, own, other


def attention_cost(grid, heads, memory_rows, products):
    pairs = grid.T * (SEG * 3 // 4 + memory_rows) * heads
    return pl.CostEstimate(
        flops=2 * products * HEAD_DIM * pairs,
        bytes_accessed=2 * HEAD_DIM * heads * 4 * (SEG + memory_rows),
        transcendentals=pairs,
    )


def attend(grid, info, query, keys, values, extra):
    heads = query.shape[1] // HEAD_DIM
    memory = extra is not None
    memory_rows = grid.n_dp * extra["topk"] if memory else 8
    piece, own, other = head_specs(grid, heads, memory_rows)
    operands, specs = [query, *keys, *values], [piece] * (1 + 2 * grid.U)
    if memory:
        operands += [extra["query"], *extra["keys"], *extra["values"], extra["bias"]]
        specs += [piece, own, other, own, other, pl.BlockSpec((memory_rows, 1), lambda h, info: (0, 0))]
    return pl.pallas_call(
        functools.partial(attend_body, grid, memory, heads),
        grid_spec=pltpu.PrefetchScalarGridSpec(
            num_scalar_prefetch=1, grid=(heads,), in_specs=specs, out_specs=piece
        ),
        out_shape=jax.ShapeDtypeStruct(query.shape, BF),
        compiler_params=params(),
        cost_estimate=attention_cost(grid, heads, memory_rows if memory else 0, 2),
    )(info, *operands)


def attend_back_body(grid, memory, heads, info_ref, *refs):
    U, R = grid.U, grid.R
    cos_ref, sin_ref, q_ref, g_ref = refs[:4]
    k_refs, v_refs = refs[4 : 4 + U], refs[4 + U : 4 + 2 * U]
    refs = refs[4 + 2 * U :]
    keys, values = [r[...] for r in k_refs], [r[...] for r in v_refs]
    step = pl.program_id(0)
    if memory:
        query_raw_ref = refs[0]
        memory_keys = head_halves(refs[1], refs[2], step, heads // 2)
        memory_values = head_halves(refs[3], refs[4], step, heads // 2)
        bias = refs[5][...]
        refs = refs[6:]
    dq_ref, dk_refs, dv_refs, refs = refs[0], refs[1 : 1 + U], refs[1 + U : 1 + 2 * U], refs[1 + 2 * U :]
    me = info_ref[0]
    grad_keys, grad_values = {}, {}

    def add(store, at, value):
        store[at] = store[at] + value if at in store else value

    for part in range(2):
        rows = pl.ds(part * R, R)
        query, grad = q_ref[rows, :], g_ref[rows, :]
        found = part_scores(grid, info_ref, part, query, keys)
        places = [(t, side) for t, side, _ in found]
        scores = [s for _, _, s in found]
        part_keys = [keys[t][side * R : (side + 1) * R] for t, side in places]
        part_values = [values[t][side * R : (side + 1) * R] for t, side in places]
        queries = [query] * len(places)
        if memory:
            places.append("memory")
            queries.append(query_raw_ref[rows, :])
            scores.append(dot(memory_keys, queries[-1], (1, 1)) + bias)
            part_keys.append(memory_keys)
            part_values.append(memory_values)
        probs = softmax_parts(scores)
        grads = [dot(value, grad, (1, 1)) for value in part_values]
        inner = sum(jnp.sum(p * d, axis=0, keepdims=True) for p, d in zip(probs, grads))
        local_query, raw_query = None, None
        for at, p, d, key, asked in zip(places, probs, grads, part_keys, queries):
            moved = (p * (d - inner)).astype(BF)
            add(grad_keys, at, dot(moved, asked, (1, 0)))
            add(grad_values, at, dot(p.astype(BF), grad, (1, 0)))
            back = dot(key, moved, (0, 0))
            if at == "memory":
                raw_query = back
            else:
                local_query = back if local_query is None else local_query + back
        cos = table_rows(grid, cos_ref, me, part)
        sin = table_rows(grid, sin_ref, me, part)
        result = turn(local_query.T, cos, -sin)
        if memory:
            result = result + raw_query.T
        dq_ref[rows, :] = (result * SCALE).astype(BF)
    for t in range(U):
        member = lax.rem(me - t + U, U)
        for side in range(2):
            rows = pl.ds(side * R, R)
            cos = table_rows(grid, cos_ref, member, side)
            sin = table_rows(grid, sin_ref, member, side)
            key = turn(grad_keys[(t, side)], cos, -sin) * SCALE
            dk_refs[t][rows, :] = key.astype(dk_refs[t].dtype)
            dv_refs[t][rows, :] = grad_values[(t, side)].astype(dv_refs[t].dtype)
    if memory:
        key = (grad_keys["memory"] * SCALE).astype(BF)
        value = grad_values["memory"].astype(BF)

        @pl.when(step < heads // 2)
        def _():
            refs[0][...] = key
            refs[1][...] = value

        @pl.when(step >= heads // 2)
        def _():
            refs[2][...] = key
            refs[3][...] = value


def attend_back(grid, info, tables, query, grad, keys, values, extra):
    rows, width = query.shape
    heads = width // HEAD_DIM
    memory = extra is not None
    memory_rows = grid.n_dp * extra["topk"] if memory else 8
    piece, own, other = head_specs(grid, heads, memory_rows)
    table = pl.BlockSpec((SEG, HEAD_DIM), lambda h, info: (0, 0))
    operands = [*tables, query, grad, *keys, *values]
    specs = [table, table] + [piece] * (2 + 2 * grid.U)
    own_kind = jax.ShapeDtypeStruct((rows, width), F32)
    sent_kind = jax.ShapeDtypeStruct((rows, width), BF)
    kinds = [own_kind] + [sent_kind] * (grid.U - 1)
    out_shape = [sent_kind] + kinds + kinds
    out_specs = [piece] * len(out_shape)
    if memory:
        operands += [extra["query"], *extra["keys"], *extra["values"], extra["bias"]]
        specs += [piece, own, other, own, other, pl.BlockSpec((memory_rows, 1), lambda h, info: (0, 0))]
        out_shape += [jax.ShapeDtypeStruct((memory_rows, width // 2), BF)] * 4
        out_specs += [own, own, other, other]
    outs = pl.pallas_call(
        functools.partial(attend_back_body, grid, memory, heads),
        grid_spec=pltpu.PrefetchScalarGridSpec(
            num_scalar_prefetch=1, grid=(heads,), in_specs=specs, out_specs=out_specs
        ),
        out_shape=out_shape,
        compiler_params=params(),
        cost_estimate=attention_cost(grid, heads, memory_rows if memory else 0, 5),
    )(info, *operands)
    U = grid.U
    return outs[0], outs[1 : 1 + U], outs[1 + U : 1 + 2 * U], outs[1 + 2 * U :]


def pick_body(grid, info_ref, picks_ref, *refs):
    U, R = grid.U, grid.R
    out_ref = refs[-1]
    picks = picks_ref[0]
    key, value = 0.0, 0.0
    for t in range(U):
        member = lax.rem(info_ref[0] - t + U, U)
        for side in range(2):
            across = lax.broadcasted_iota(jnp.int32, (picks.shape[0], R), 1)
            chosen = (picks == across + piece_start(grid, member, side)).astype(BF)
            rows = pl.ds(side * R, R)
            key = key + dot(chosen, refs[t][rows, :], (1, 0))
            value = value + dot(chosen, refs[U + t][rows, :], (1, 0))
    out_ref[0] = key.astype(BF)
    out_ref[1] = value.astype(BF)


def pick_memory(grid, info, picks, keys, values):
    heads, topk = picks.shape
    per = heads // 2
    at = lambda h, info: info[2] * per + h
    piece = pl.BlockSpec((grid.T, HEAD_DIM), lambda h, info: (0, at(h, info)))
    return pl.pallas_call(
        functools.partial(pick_body, grid),
        grid_spec=pltpu.PrefetchScalarGridSpec(
            num_scalar_prefetch=1,
            grid=(per,),
            in_specs=[pl.BlockSpec((1, topk, 1), lambda h, info: (at(h, info), 0, 0))]
            + [piece] * (2 * grid.U),
            out_specs=pl.BlockSpec((2, topk, HEAD_DIM), lambda h, info: (0, 0, h)),
        ),
        out_shape=jax.ShapeDtypeStruct((2, topk, per * HEAD_DIM), BF),
        compiler_params=params(),
        cost_estimate=pl.CostEstimate(
            flops=4 * topk * SEG * HEAD_DIM * per, bytes_accessed=4 * SEG * HEAD_DIM * per, transcendentals=0
        ),
    )(info, picks[:, :, None], *keys, *values)


def finish_body(grid, memory, heads, info_ref, *refs):
    U, R = grid.U, grid.R
    dk_refs, dv_refs = refs[:U], refs[U : 2 * U]
    refs = refs[2 * U :]
    key = sum(r[...].astype(F32) for r in dk_refs)
    value = sum(r[...].astype(F32) for r in dv_refs)
    key_ref, value_ref = refs[-2:]
    if not memory:
        key_ref[...] = key.astype(BF)
        value_ref[...] = value.astype(BF)
        return
    picks = refs[0][0]
    step = pl.program_id(0)
    back = head_halves(refs[1], refs[2], step, heads // 2)
    for side in range(2):
        down = lax.broadcasted_iota(jnp.int32, (R, picks.shape[1]), 0)
        chosen = (down + piece_start(grid, info_ref[0], side) == picks).astype(BF)
        rows = slice(side * R, (side + 1) * R)
        key_ref[rows, :] = (key[rows] + dot(chosen, back[0], (1, 0))).astype(BF)
        value_ref[rows, :] = (value[rows] + dot(chosen, back[1], (1, 0))).astype(BF)


def finish_keys(grid, info, grad_keys, grad_values, picks, halves):
    rows, width = grad_keys[0].shape
    heads = width // HEAD_DIM
    memory = halves is not None
    per = heads // 2
    piece, _, _ = head_specs(grid, heads, 8)
    operands, specs = [*grad_keys, *grad_values], [piece] * (2 * grid.U)
    if memory:
        topk = picks.shape[1]
        operands += [picks[:, None, :], *halves]
        specs += [
            pl.BlockSpec((1, 1, topk), lambda h, info: (lax.rem(info[2] + h // per, 2) * per + h % per, 0, 0)),
            pl.BlockSpec((2, topk, HEAD_DIM), lambda h, info: (0, 0, jnp.minimum(h, per - 1))),
            pl.BlockSpec((2, topk, HEAD_DIM), lambda h, info: (0, 0, jnp.maximum(h - per, 0))),
        ]
    return pl.pallas_call(
        functools.partial(finish_body, grid, memory, heads),
        grid_spec=pltpu.PrefetchScalarGridSpec(
            num_scalar_prefetch=1, grid=(heads,), in_specs=specs, out_specs=[piece, piece]
        ),
        out_shape=[jax.ShapeDtypeStruct((rows, width), BF)] * 2,
        compiler_params=params(),
        cost_estimate=pl.CostEstimate(
            flops=2 * rows * width, bytes_accessed=16 * rows * width, transcendentals=0
        ),
    )(info, *operands)


def norm(value, gain):
    return value * lax.rsqrt(jnp.mean(value * value, axis=-1, keepdims=True) + EPSILON) * gain


def norm_back(value, gain, grad):
    inverse = lax.rsqrt(jnp.mean(value * value, axis=-1, keepdims=True) + EPSILON)
    unit = value * inverse
    grad_gain = jnp.sum(grad * unit, axis=0)
    scaled = grad * gain
    pulled = inverse * (scaled - unit * jnp.mean(scaled * unit, axis=-1, keepdims=True))
    return pulled, grad_gain


def mm(left, right, contract=(1, 0)):
    return dot(left, right, contract)


def local(
    n_dp,
    pieces,
    tokens,
    cotangent,
    doc_lengths,
    partner,
    memory_picks,
    attention_in,
    attention_out,
    feed_in,
    feed_out,
    norm_gains,
):
    grid = Grid(n_dp, pieces)
    grid.trace()
    layers = attention_in.shape[0]
    width = tokens.shape[2]
    heads = width // HEAD_DIM
    topk = memory_picks.shape[3]
    valid_all, visible_all = jax.vmap(memory_plan)(doc_lengths, partner)
    valid = valid_all[grid.m, grid.slot]
    visible = visible_all[grid.m, grid.slot]
    relative = (grid.slot - jnp.arange(n_dp)) % n_dp
    bias = jnp.repeat(jnp.where(visible[relative], 0.0, MASKED), topk)[:, None].astype(F32)
    info = jnp.stack([grid.k, valid, grid.c]).astype(jnp.int32)
    tables = rope_tables()

    hidden = grid.to_units(tokens).astype(F32)
    gains = gather_gains(grid, norm_gains).astype(F32)
    picks_there = grid.swap(memory_picks)
    picks = jnp.where(
        grid.r == grid.c, memory_picks[grid.m, 0], picks_there[grid.m, 0]
    )

    weights = []
    for l in range(layers):
        weights.append(
            [gather_weight(grid, w[l]) for w in (attention_in, attention_out, feed_in, feed_out)]
        )
    grad_stream = grid.to_units(cotangent).astype(F32)

    def exchange(value):
        return [value] + [grid.member(value, t) for t in range(1, grid.U)]

    saved = []
    for l in range(layers):
        w_qkv, w_out, w_up, w_down = weights[l]
        memory = l == layers - 1
        normed = norm(hidden, gains[l, 0]).astype(BF)
        projected = mm(normed, w_qkv)
        split = split_heads(grid, memory, info, tables, projected)
        query = split[0]
        keys, values = exchange(split[1]), exchange(split[2])
        extra = None
        if memory:
            raw_keys = exchange(split[4])
            chosen = pick_memory(grid, info, picks, raw_keys, values)
            slots = [chosen] + [grid.slots(chosen, t) for t in range(1, n_dp)]
            half = [jnp.concatenate([s[i] for s in slots]) for i in range(2)]
            there = [grid.swap(h) for h in half]
            extra = {
                "topk": topk,
                "query": split[3],
                "keys": (half[0], there[0]),
                "values": (half[1], there[1]),
                "bias": bias,
            }
        attended = attend(grid, info, query, keys, values, extra)
        middle = hidden + mm(attended, w_out)
        normed_feed = norm(middle, gains[l, 1]).astype(BF)
        gate_up = mm(normed_feed, w_up)
        gate, up = jnp.split(gate_up, 2, axis=1)
        inner = (jax.nn.silu(gate) * up).astype(BF)
        saved.append((hidden, middle, normed, normed_feed, gate_up, inner, query, keys, values, extra, attended))
        hidden = middle + mm(inner, w_down)
    layer_output = grid.from_units(hidden.astype(BF))

    def gradient(left, right):
        half = right.shape[1] // 2
        mine = lax.dynamic_slice_in_dim(right, grid.c * half, half, axis=1)
        give = lax.dynamic_slice_in_dim(right, (1 - grid.c) * half, half, axis=1)
        left = jnp.concatenate([left, grid.swap(left)])
        right = jnp.concatenate([mine, grid.swap(give)])
        return scatter_gradient(grid, mm(left, right, (0, 0)).astype(BF))

    grads = [None] * layers
    grad_gains = [None] * layers
    for l in reversed(range(layers)):
        w_qkv, w_out, w_up, w_down = weights[l]
        hidden, middle, normed, normed_feed, gate_up, inner, query, keys, values, extra, attended = saved[l]
        grad_low = grad_stream.astype(BF)
        grad_inner = mm(grad_low, w_down, (1, 1))
        grad_w_down = gradient(inner, grad_low)
        gate, up = jnp.split(gate_up, 2, axis=1)
        sigmoid = jax.nn.sigmoid(gate)
        grad_gate = grad_inner * up * sigmoid * (1.0 + gate * (1.0 - sigmoid))
        grad_up = grad_inner * gate * sigmoid
        grad_gate_up = jnp.concatenate([grad_gate, grad_up], axis=1).astype(BF)
        grad_w_up = gradient(normed_feed, grad_gate_up)
        pulled, gain_feed = norm_back(middle, gains[l, 1], mm(grad_gate_up, w_up, (1, 1)))
        grad_middle = grad_stream + pulled
        grad_attended = grad_middle.astype(BF)
        grad_w_out = gradient(attended, grad_attended)
        grad_heads = mm(grad_attended, w_out, (1, 1)).astype(BF)
        grad_query, grad_keys, grad_values, memory_grads = attend_back(
            grid, info, tables, query, grad_heads, keys, values, extra
        )
        grad_keys = [grad_keys[0]] + [
            grid.member(grad_keys[t], grid.U - t) for t in range(1, grid.U)
        ]
        grad_values = [grad_values[0]] + [
            grid.member(grad_values[t], grid.U - t) for t in range(1, grid.U)
        ]
        halves = None
        if extra is not None:
            own = [memory_grads[0], memory_grads[1]]
            there = [grid.swap(memory_grads[2]), grid.swap(memory_grads[3])]
            joined = jnp.stack([a.astype(F32) + b.astype(F32) for a, b in zip(own, there)])
            joined = joined.astype(BF).reshape(2, n_dp, topk, -1)
            total = joined[:, 0].astype(F32)
            for t in range(1, n_dp):
                total = total + grid.slots(joined[:, t], n_dp - t).astype(F32)
            low = total.astype(BF)
            for t in range(1, grid.Q):
                total = total + grid.within(low, t).astype(F32)
            total = total.astype(BF)
            halves = (total, grid.swap(total))
        grad_key, grad_value = finish_keys(grid, info, grad_keys, grad_values, picks, halves)
        grad_projected = jnp.concatenate([grad_query, grad_key, grad_value], axis=1)
        grad_w_qkv = gradient(normed, grad_projected)
        pulled, gain_attention = norm_back(hidden, gains[l, 0], mm(grad_projected, w_qkv, (1, 1)))
        grad_stream = grad_middle + pulled
        grads[l] = (grad_w_qkv, grad_w_out, grad_w_up, grad_w_down)
        grad_gains[l] = jnp.stack([gain_attention, gain_feed])
    input_grad = grid.from_units(grad_stream.astype(BF)).astype(F32)
    return (
        layer_output,
        input_grad,
        *(jnp.stack([grads[l][i] for l in range(layers)]) for i in range(4)),
        scatter_gains(grid, jnp.stack(grad_gains)),
    )


def solution(mesh):
    rows = P(None, ("dp", "fsdp"), None)
    in_specs = (rows, rows, P(), P(), P(None, "dp", None, None), rows, rows, rows, rows, P(None, None, ("dp", "fsdp")))
    out_specs = (rows, rows, rows, rows, rows, rows, P(None, None, ("dp", "fsdp")))
    body = functools.partial(local, mesh.shape["dp"], mesh.shape["fsdp"])
    return jax.shard_map(body, mesh=mesh, in_specs=in_specs, out_specs=out_specs, check_vma=False)
```

```python
import functools
import math

import jax
import jax.numpy as jnp
from jax import lax
from jax.experimental import pallas as pl
from jax.experimental.pallas import tpu as pltpu
from jax.sharding import PartitionSpec as P

HEAD_DIM = 128
SEG = 1024
MICRO = 2
EPSILON = 1e-06
MASKED = -1e30
SCALE = HEAD_DIM ** (-0.5)
LOG2E = 1.0 / math.log(2.0)
BF = jnp.bfloat16
F32 = jnp.float32
VMEM_LIMIT = 48 * 1024 * 1024


def slot_layout(lengths):
    slot_total = lengths.shape[0]
    slot_counts = ((lengths + SEG - 1) // SEG).astype(jnp.int32)
    slot_starts = (jnp.cumsum(slot_counts) - slot_counts).astype(jnp.int32)
    slot_index = jnp.arange(slot_total, dtype=jnp.int32)
    started = (slot_starts[None, :] <= slot_index[:, None]) & (slot_counts[None, :] > 0)
    owner_doc = (jnp.sum(started.astype(jnp.int32), axis=1) - 1).astype(jnp.int32)
    owner_pick = slot_index[None, :] == owner_doc[:, None]
    first_slot = jnp.sum(jnp.where(owner_pick, slot_starts[None, :], 0), axis=1).astype(jnp.int32)
    doc_total = jnp.sum(jnp.where(owner_pick, lengths[None, :], 0), axis=1).astype(jnp.int32)
    valid_rows = jnp.clip(doc_total - (slot_index - first_slot) * SEG, 0, SEG).astype(jnp.int32)
    return (valid_rows, owner_doc)


def memory_plan(lengths, partner_row):
    valid_rows, owner_doc = slot_layout(lengths)
    block_ids = jnp.arange(lengths.shape[0], dtype=jnp.int32)
    earlier = (block_ids[None, :] < block_ids[:, None]) & (owner_doc[None, :] == owner_doc[:, None])
    visible = earlier | (block_ids[None, :] == partner_row[:, None])
    return (valid_rows, visible)


class Grid:
    def __init__(self, n_dp, pieces):
        self.n_dp, self.F = n_dp, pieces
        self.J = n_dp // 2
        self.bits = self.J.bit_length() - 1
        self.Q = pieces // 4
        self.U = 2 * self.Q
        self.R = SEG // pieces
        self.T = 2 * self.R

    def trace(self):
        dp = lax.axis_index("dp")
        self.c, self.j, self.f = dp % 2, dp // 2, lax.axis_index("fsdp")
        self.q, self.g = self.f // self.Q, self.f % self.Q
        self.m, self.r = self.q // 2, self.q % 2
        self.k = self.c * self.Q + self.g
        self.slot = 2 * self.j + self.r

    def permute(self, value, target):
        pairs = []
        for j in range(self.J):
            for c in range(2):
                for f in range(self.F):
                    j2, c2, f2 = target(j, c, f)
                    pairs.append(((j * 2 + c) * self.F + f, (j2 * 2 + c2) * self.F + f2))
        return lax.ppermute(value, ("dp", "fsdp"), pairs)

    def swap(self, value):
        return self.permute(value, lambda j, c, f: (j, 1 - c, f))

    def ring(self, value, t):
        return self.permute(value, lambda j, c, f: (j, c, (f + t) % self.F))

    def bit(self, phase, c):
        return phase if c == 0 else self.bits - 1 - phase

    def flip(self, value, phase):
        return self.permute(value, lambda j, c, f: (j ^ (1 << self.bit(phase, c)), c, f))

    def mask(self, key, c):
        return sum(1 << self.bit(p, c) for p in range(self.bits) if key >> p & 1)

    def place(self, key, c):
        return jnp.where(c == 0, self.j ^ self.mask(key, 0), self.j ^ self.mask(key, 1))

    def member(self, value, t):
        def target(j, c, f):
            q, g = f // self.Q, f % self.Q
            k = (c * self.Q + g + t) % self.U
            return (j, k // self.Q, q * self.Q + k % self.Q)

        return self.permute(value, target)

    def within(self, value, t):
        return self.permute(
            value, lambda j, c, f: (j, c, f // self.Q * self.Q + (f % self.Q + t) % self.Q)
        )

    def slots(self, value, t):
        def target(j, c, f):
            q, g = f // self.Q, f % self.Q
            slot = (2 * j + q % 2 + t) % self.n_dp
            return (slot // 2, c, (2 * (q // 2) + slot % 2) * self.Q + g)

        return self.permute(value, target)

    def _spread(self, second):
        def target(j, c, f):
            m = f // (self.F // 2)
            m = 1 - m if second else m
            k = min(f, self.F - 1 - f)
            return (j, k // self.Q, (2 * m + c) * self.Q + k % self.Q)

        return target

    def _collect(self, second):
        there = self._spread(second)
        back = {
            there(0, c, f): (c, f) for c in range(2) for f in range(self.F)
        }
        return lambda j, c, f: (j,) + back[(0, c, f)]

    def to_units(self, value):
        here = self.f // (self.F // 2)
        first = self.permute(jnp.where(here == 0, value[0], value[1]), self._spread(False))
        second = self.permute(jnp.where(here == 0, value[1], value[0]), self._spread(True))
        return jnp.concatenate(
            [jnp.where(self.m == 0, first, second), jnp.where(self.m == 0, second, first)]
        )

    def from_units(self, value):
        low, high = value[: self.R], value[self.R :]
        first = self.permute(jnp.where(self.m == 0, low, high), self._collect(False))
        second = self.permute(jnp.where(self.m == 0, high, low), self._collect(True))
        here = self.f // (self.F // 2)
        return jnp.stack([jnp.where(here == 0, first, second), jnp.where(here == 0, second, first)])


def any_spec():
    return pl.BlockSpec(memory_space=pl.ANY)


MESH = pl.DeviceIdType.MESH


class Here:
    def __init__(self, grid):
        self.grid = grid
        dp = lax.axis_index("dp")
        self.j, self.c, self.f = dp // 2, dp % 2, lax.axis_index("fsdp")
        self.q, self.g = self.f // grid.Q, self.f % grid.Q
        self.m, self.r = self.q // 2, self.q % 2
        self.k = self.c * grid.Q + self.g
        self.swap = self.device(self.j, 1 - self.c, self.f)

    def device(self, j, c, f):
        return {"dp": 2 * j + c, "fsdp": f}

    def ring(self, t):
        return self.device(self.j, self.c, (self.f + t) % self.grid.F)

    def step(self, phase):
        first, second = (1 << self.grid.bit(phase, c) for c in (0, 1))
        return first + self.c * (second - first)

    def moved(self, j, phase):
        step = self.step(phase)
        return j + step * (1 - 2 * ((j // step) % 2))

    def flip(self, phase):
        return self.device(self.moved(self.j, phase), self.c, self.f)

    def place(self, key):
        j = self.j
        for phase in range(self.grid.bits):
            if key >> phase & 1:
                j = self.moved(j, phase)
        return j

    def greet(self):
        grid = self.grid
        barrier = pltpu.get_barrier_semaphore()
        peers = [self.ring(t) for t in range(1, grid.F)]
        peers += [self.device(self.j, 1 - self.c, (self.f + t) % grid.F) for t in range(grid.F)]
        for bit in range(grid.bits):
            step = 1 << bit
            peers.append(self.device(self.j + step * (1 - 2 * ((self.j // step) % 2)), self.c, self.f))
        for peer in peers:
            pl.semaphore_signal(barrier, inc=1, device_id=peer, device_id_type=MESH)
        pl.semaphore_wait(barrier, len(peers))


def remote(source, target, sems, index, device):
    return pltpu.make_async_remote_copy(
        src_ref=source,
        dst_ref=target,
        send_sem=sems.at[0, index],
        recv_sem=sems.at[1, index],
        device_id=device,
        device_id_type=MESH,
    )


class Spread:
    def __init__(self, here, shard, whole, sems, own_sem, split):
        grid = here.grid
        self.here, self.split = here, split
        rows, width = shard.shape
        half = width // 2 if split else width

        def part(ref, c):
            if not split:
                return ref
            return ref.at[(slice(None),) * (len(ref.shape) - 1) + (pl.ds(pl.multiple_of(c * half, 128), half),)]

        j, c, f = here.j, here.c, here.f
        mine = part(whole, c)
        self.own = pltpu.make_async_copy(part(shard, c), part(whole.at[j, c, f], c), own_sem)
        other = 1 - c if split else c
        self.pre = remote(part(shard, other), part(whole.at[j, c, f], other), sems, 0, here.swap)
        at = 1
        self.line = []
        for t in range(1, grid.F):
            block = mine.at[j, :, f]
            self.line.append(remote(block, block, sems, at, here.ring(t)))
            at += 1
        self.flips = []
        for phase in range(grid.bits):
            sent = []
            for key in range(1 << phase):
                block = mine.at[here.place(key)]
                sent.append(remote(block, block, sems, at, here.flip(phase)))
                at += 1
            self.flips.append(sent)
        self.swaps = []
        for key in range(grid.J if split else 0):
            block = mine.at[here.place(key)]
            self.swaps.append(remote(block, block, sems, at, here.swap))
            at += 1

    @staticmethod
    def count(grid):
        return 1 + (grid.F - 1) + (grid.J - 1) + grid.J

    def begin(self):
        self.own.start()
        self.pre.start()

    def to_line(self):
        self.own.wait()
        self.pre.wait()
        for copy in self.line:
            copy.start()

    def _send(self, keys):
        for key in keys:
            if self.swaps:
                self.swaps[key].start()
        for phase, sent in enumerate(self.flips):
            for key in keys:
                if key < 1 << phase:
                    sent[key].start()

    def steps(self):
        def first():
            for copy in self.line:
                copy.wait()
            self._send([0])

        def later(phase):
            for copy in self.flips[phase]:
                copy.wait()
            self._send([key + (1 << phase) for key in range(1 << phase)])

        def last():
            for copy in self.swaps:
                copy.wait()

        return [first] + [functools.partial(later, p) for p in range(len(self.flips))] + [last]


class Regroup:
    def __init__(self, here, source, target, sems, own_sem):
        grid = here.grid
        half = grid.F // 2
        k = jnp.minimum(here.f, grid.F - 1 - here.f)
        side = here.f // half
        self.sends = []
        for m in range(2):
            c2, f2 = k // grid.Q, (2 * m + here.c) * grid.Q + k % grid.Q
            same = (c2 == here.c) & (f2 == here.f)
            own = pltpu.make_async_copy(source.at[m], target.at[side], own_sem)
            away = pltpu.make_async_remote_copy(
                src_ref=source.at[m],
                dst_ref=target.at[side],
                send_sem=sems.at[0, m],
                recv_sem=sems.at[1, side],
                device_id=here.device(here.j, c2, f2),
                device_id_type=MESH,
            )
            self.sends.append((same, own, away))
        self.arrivals = []
        for side in range(2):
            from_f = here.k if side == 0 else grid.F - 1 - here.k
            same = (here.r == here.c) & (from_f == here.f)
            came = pltpu.make_async_remote_copy(
                src_ref=source.at[0],
                dst_ref=target.at[side],
                send_sem=sems.at[0, 0],
                recv_sem=sems.at[1, side],
                device_id=here.swap,
                device_id_type=MESH,
            )
            self.arrivals.append((same, came))

    def start(self):
        for same, own, away in self.sends:
            pl.when(same)(own.start)
            pl.when(jnp.logical_not(same))(away.start)

    def wait(self):
        for same, own, away in self.sends:
            pl.when(same)(own.wait)
            pl.when(jnp.logical_not(same))(away.wait_send)
        for same, came in self.arrivals:
            pl.when(jnp.logical_not(same))(came.wait_recv)


def gather_body(grid, layers, kinds, *refs):
    tokens, cotangent, gains = refs[:3]
    shards = refs[3 : 3 + kinds]
    outs = refs[3 + kinds :]
    tokens_out, cotangent_out, gains_out = outs[:3]
    wholes = outs[3 : 3 + layers * kinds]
    sems, own_sems, regroup_sems = outs[3 + layers * kinds :]
    here = Here(grid)
    here.greet()
    rows = Regroup(here, tokens, tokens_out, regroup_sems.at[0], own_sems.at[0])
    rows_back = Regroup(here, cotangent, cotangent_out, regroup_sems.at[1], own_sems.at[1])
    moves = [Spread(here, gains, gains_out, sems.at[0], own_sems.at[2], False)]
    for l in range(layers):
        for i in range(kinds):
            n = l * kinds + i
            moves.append(
                Spread(here, shards[i].at[l], wholes[n], sems.at[n + 1], own_sems.at[n + 3], True)
            )
    for move in moves:
        move.begin()
    rows.start()
    steps = [move.steps() for move in moves]
    count = len(steps[0])
    moves[0].to_line()
    moves[1].to_line()
    for at in range(len(moves) + count - 1):
        if at + 2 < len(moves):
            moves[at + 2].to_line()
        if at == len(moves) - 3:
            rows_back.start()
        for back in range(count):
            if 0 <= at - back < len(moves):
                steps[at - back][back]()
    rows.wait()
    rows_back.wait()


def gather_all(grid, tokens, cotangent, gains, shards):
    layers, kinds = shards[0].shape[0], len(shards)
    packed = jnp.zeros((8, 128), F32).at[: layers * 2, : gains.shape[2]].set(
        gains.astype(F32).reshape(layers * 2, -1)
    )
    whole = lambda shard: jax.ShapeDtypeStruct((grid.J, 2, grid.F) + shard.shape[-2:], shard.dtype)
    out_shape = [jax.ShapeDtypeStruct(tokens.shape, BF), jax.ShapeDtypeStruct(tokens.shape, BF), whole(packed)]
    out_shape += [whole(shard) for _ in range(layers) for shard in shards]
    moves = 1 + layers * kinds
    outs = pl.pallas_call(
        functools.partial(gather_body, grid, layers, kinds),
        in_specs=[any_spec()] * (3 + kinds),
        out_specs=[any_spec()] * len(out_shape),
        out_shape=out_shape,
        scratch_shapes=[
            pltpu.SemaphoreType.DMA((moves, 2, Spread.count(grid))),
            pltpu.SemaphoreType.DMA((moves + 2,)),
            pltpu.SemaphoreType.DMA((2, 2, 2)),
        ],
        compiler_params=pltpu.CompilerParams(
            collective_id=0, has_side_effects=True, vmem_limit_bytes=VMEM_LIMIT
        ),
    )(tokens, cotangent, packed, *shards)
    width = tokens.shape[2]
    gains_all = outs[2][..., : layers * 2, : gains.shape[2]]
    gains_all = jnp.moveaxis(gains_all, 3, 0).reshape(layers, 2, -1)
    weights = [
        [outs[3 + l * kinds + i].reshape(-1, shards[i].shape[2]) for i in range(kinds)]
        for l in range(layers)
    ]
    return outs[0].reshape(-1, width), outs[1].reshape(-1, width), gains_all, weights


def tie(*values):
    return lax.optimization_barrier(values)


def in_key_order(grid, value, keys, axis):
    size = value.shape[axis] // grid.J
    return jnp.concatenate(
        [
            lax.dynamic_slice_in_dim(value, grid.place(key, grid.c) * size, size, axis=axis)
            for key in keys
        ],
        axis=axis,
    )


class Scatter:
    def __init__(self, grid, pairs):
        self.grid = grid
        self.halves = [right.shape[1] // 2 for _, right in pairs]
        joined = []
        for (left, right), half in zip(pairs, self.halves):
            mine = lax.dynamic_slice_in_dim(right, grid.c * half, half, axis=1)
            give = lax.dynamic_slice_in_dim(right, (1 - grid.c) * half, half, axis=1)
            joined.append(
                (jnp.concatenate([left, grid.swap(left)]), jnp.concatenate([mine, grid.swap(give)]))
            )
        self.height = joined[0][0].shape[1]
        if self.height // grid.J % 128:
            whole = [mm(left, right, (0, 0)).astype(BF) for left, right in joined]
            whole = jnp.concatenate(whole, axis=1)
            part = lambda keys: in_key_order(grid, whole, keys, 0)
        else:
            part = lambda keys: jnp.concatenate(
                [mm(in_key_order(grid, left, keys, 1), right, (0, 0)).astype(BF) for left, right in joined],
                axis=1,
            )
        self.parts = [
            part([key for key in range(grid.J) if key & 1 == side]) for side in (1, 0)
        ]

    def across(self):
        grid, (give, held) = self.grid, self.parts
        for phase in range(grid.bits):
            if phase > 0:
                held = held.reshape(-1, 2, self.height // grid.J, held.shape[1])
                give, held = (held[:, side].reshape(-1, held.shape[3]) for side in (1, 0))
            got = grid.flip(give, phase)
            held = (held.astype(F32) + got.astype(F32)).astype(BF)
        self.line = held

    def along_line(self):
        grid = self.grid
        line = self.line.reshape(2, grid.F, -1, self.line.shape[1])

        def block(t):
            return lax.dynamic_index_in_dim(line, (grid.f + t) % grid.F, 1, keepdims=False)

        summed = block(0).astype(F32)
        for got in [grid.ring(block(t), t) for t in range(1, grid.F)]:
            summed = summed + got.astype(F32)
        mine = lax.dynamic_index_in_dim(summed, grid.c, 0, keepdims=False)
        give = lax.dynamic_index_in_dim(summed, 1 - grid.c, 0, keepdims=False)
        got = grid.swap(give.astype(BF)).astype(F32)
        self.found, start = [], 0
        for half in self.halves:
            a, b = mine[:, start : start + half], got[:, start : start + half]
            start += half
            self.found.append(
                jnp.concatenate([jnp.where(grid.c == 0, a, b), jnp.where(grid.c == 0, b, a)], axis=1)
            )


def scatter_gains(grid, total):
    layers, kinds, width = total.shape
    devices = grid.n_dp * grid.F
    total = total + grid.swap(total)
    for p in range(grid.bits):
        total = total + grid.permute(total, lambda j, c, f: (j ^ (1 << p), c, f))
    for step in [1 << p for p in range(grid.F.bit_length() - 1)]:
        total = total + grid.permute(total, lambda j, c, f: (j, c, f ^ step))
    here = (grid.j * 2 + grid.c) * grid.F + grid.f
    return lax.dynamic_slice_in_dim(total, here * (width // devices), width // devices, axis=2)


def rope_tables():
    half_dim = HEAD_DIM // 2
    frequency = jnp.exp(
        jnp.arange(half_dim, dtype=F32) * (-2.0 * math.log(10000.0) / HEAD_DIM)
    )
    angles = jnp.arange(SEG, dtype=jnp.int32).astype(F32)[:, None] * frequency[None, :]
    cos, sin = jnp.cos(angles), jnp.sin(angles)
    return (jnp.concatenate([cos, cos], axis=-1), jnp.concatenate([-sin, sin], axis=-1))


def turn(values, cos, sin):
    return values * cos + pltpu.roll(values, HEAD_DIM // 2, 1) * sin


def params():
    return pltpu.CompilerParams(vmem_limit_bytes=VMEM_LIMIT)


def smem():
    return pl.BlockSpec(memory_space=pltpu.SMEM)


def whole_spec(shape):
    return pl.BlockSpec(shape, lambda *_: (0,) * len(shape))


def piece_start(grid, member, part):
    return (member if part == 0 else grid.F - 1 - member) * grid.R


def table_rows(grid, table_ref, member, part):
    start = pl.multiple_of(piece_start(grid, member, part), grid.R)
    return table_ref[pl.ds(start, grid.R), :]


def split_body(grid, memory, info_ref, cos_ref, sin_ref, q_ref, k_ref, v_ref, *outs):
    me = info_ref[0]
    for part in range(2):
        rows = pl.ds(part * grid.R, grid.R)
        cos = table_rows(grid, cos_ref, me, part)
        sin = table_rows(grid, sin_ref, me, part)
        query, key = q_ref[rows, :], k_ref[rows, :]
        outs[0][rows, :] = turn(query, cos, sin).astype(BF)
        outs[1][0, rows, :] = turn(key, cos, sin).astype(BF)
        outs[1][1, rows, :] = v_ref[rows, :].astype(BF)
        if memory:
            outs[1][2, rows, :] = key.astype(BF)
            outs[2][rows, :] = query.astype(BF)


def split_heads(grid, memory, info, tables, projected):
    rows, width = projected.shape
    heads = width // (3 * HEAD_DIM)
    count = 3 if memory else 2
    piece = lambda at: pl.BlockSpec((rows, HEAD_DIM), lambda h: (0, at * heads + h))
    flat = jax.ShapeDtypeStruct((rows, heads * HEAD_DIM), BF)
    stacked = jax.ShapeDtypeStruct((count, rows, heads * HEAD_DIM), BF)
    return pl.pallas_call(
        functools.partial(split_body, grid, memory),
        grid=(heads,),
        out_shape=[flat, stacked] + [flat] * memory,
        in_specs=[smem(), whole_spec((SEG, HEAD_DIM)), whole_spec((SEG, HEAD_DIM))]
        + [piece(0), piece(1), piece(2)],
        out_specs=[piece(0), pl.BlockSpec((count, rows, HEAD_DIM), lambda h: (0, 0, h))]
        + [piece(0)] * memory,
        compiler_params=params(),
        cost_estimate=pl.CostEstimate(
            flops=10 * rows * width, bytes_accessed=8 * rows * width, transcendentals=0
        ),
    )(info, *tables, projected, projected, projected)


def dot(left, right, contract):
    return lax.dot_general(
        left, right, (((contract[0],), (contract[1],)), ((), ())), preferred_element_type=F32
    )


def part_scores(grid, info_ref, part, query, keys):
    me, valid = info_ref[0], info_ref[1]
    shape = (grid.R, grid.R)
    apart = lax.broadcasted_iota(jnp.int32, shape, 0) - lax.broadcasted_iota(jnp.int32, shape, 1)
    found = []
    for t in range(grid.U):
        member = lax.rem(me - t + grid.U, grid.U)
        for side in range(part + 1):
            score = dot(keys[t][side * grid.R : (side + 1) * grid.R], query, (1, 1))
            if side == part:
                start = piece_start(grid, member, side)
                allowed = apart <= piece_start(grid, me, part) - start
                if side == 1:
                    down = lax.broadcasted_iota(jnp.int32, shape, 0)
                    allowed = allowed & (down < valid - start)
                score = jnp.where(allowed, score, MASKED)
            found.append((t, side, score))
    return found


def head_halves(own_ref, other_ref, step, per_half):
    return jnp.where(step < per_half, own_ref[...], other_ref[...])


def softmax_parts(scores):
    top = functools.reduce(jnp.maximum, [jnp.max(s, axis=0, keepdims=True) for s in scores])
    powers = [jnp.exp2((s - top) * (SCALE * LOG2E)) for s in scores]
    inverse = 1.0 / sum(jnp.sum(p, axis=0, keepdims=True) for p in powers)
    return [p * inverse for p in powers]


def attend_body(grid, memory, heads, info_ref, *refs):
    U, R = grid.U, grid.R
    q_ref, kv_refs = refs[0], refs[1 : 1 + U]
    refs = refs[1 + U :]
    keys, values = [r[0] for r in kv_refs], [r[1] for r in kv_refs]
    if memory:
        step = pl.program_id(0)
        memory_keys = head_halves(refs[1], refs[2], step, heads // 2)
        memory_values = head_halves(refs[3], refs[4], step, heads // 2)
        bias = refs[5][...]
    out_ref = refs[-1]
    for part in range(2):
        rows = pl.ds(part * R, R)
        found = part_scores(grid, info_ref, part, q_ref[rows, :], keys)
        scores = [s for _, _, s in found]
        mixed = [values[t][side * R : (side + 1) * R] for t, side, _ in found]
        if memory:
            scores.append(dot(memory_keys, refs[0][rows, :], (1, 1)) + bias)
            mixed.append(memory_values)
        total = sum(
            dot(value, p.astype(BF), (0, 0)) for value, p in zip(mixed, softmax_parts(scores))
        )
        out_ref[rows, :] = total.T.astype(BF)


def head_specs(grid, heads, memory_rows):
    per = heads // 2

    def head(h, info):
        return lax.rem(info[2] + h // per, 2) * per + h % per

    piece = pl.BlockSpec((grid.T, HEAD_DIM), lambda h, info: (0, head(h, info)))
    own = pl.BlockSpec((memory_rows, HEAD_DIM), lambda h, info: (0, jnp.minimum(h, per - 1)))
    other = pl.BlockSpec((memory_rows, HEAD_DIM), lambda h, info: (0, jnp.maximum(h - per, 0)))
    pair = pl.BlockSpec((2, grid.T, HEAD_DIM), lambda h, info: (0, 0, head(h, info)))
    return piece, pair, own, other


def attention_cost(grid, heads, memory_rows, products):
    pairs = grid.T * (SEG * 3 // 4 + memory_rows) * heads
    return pl.CostEstimate(
        flops=2 * products * HEAD_DIM * pairs,
        bytes_accessed=2 * HEAD_DIM * heads * 4 * (SEG + memory_rows),
        transcendentals=pairs,
    )


def attend(grid, info, query, pairs, extra):
    heads = query.shape[1] // HEAD_DIM
    memory = extra is not None
    memory_rows = grid.n_dp * extra["topk"] if memory else 8
    piece, pair, own, other = head_specs(grid, heads, memory_rows)
    operands, specs = [query, *pairs], [piece] + [pair] * grid.U
    if memory:
        operands += [extra["query"], *extra["keys"], *extra["values"], extra["bias"]]
        specs += [piece, own, other, own, other, pl.BlockSpec((memory_rows, 1), lambda h, info: (0, 0))]
    return pl.pallas_call(
        functools.partial(attend_body, grid, memory, heads),
        grid_spec=pltpu.PrefetchScalarGridSpec(
            num_scalar_prefetch=1, grid=(heads,), in_specs=specs, out_specs=piece
        ),
        out_shape=jax.ShapeDtypeStruct(query.shape, BF),
        compiler_params=params(),
        cost_estimate=attention_cost(grid, heads, memory_rows if memory else 0, 2),
    )(info, *operands)


def attend_back_body(grid, memory, heads, info_ref, *refs):
    U, R = grid.U, grid.R
    cos_ref, sin_ref, q_ref, g_ref = refs[:4]
    kv_refs = refs[4 : 4 + U]
    refs = refs[4 + U :]
    keys, values = [r[0] for r in kv_refs], [r[1] for r in kv_refs]
    step = pl.program_id(0)
    if memory:
        query_raw_ref = refs[0]
        memory_keys = head_halves(refs[1], refs[2], step, heads // 2)
        memory_values = head_halves(refs[3], refs[4], step, heads // 2)
        bias = refs[5][...]
        refs = refs[6:]
    dq_ref, dkv_refs, refs = refs[0], refs[1 : 1 + U], refs[1 + U :]
    me = info_ref[0]
    grad_keys, grad_values = {}, {}

    def add(store, at, value):
        store[at] = store[at] + value if at in store else value

    for part in range(2):
        rows = pl.ds(part * R, R)
        query, grad = q_ref[rows, :], g_ref[rows, :]
        found = part_scores(grid, info_ref, part, query, keys)
        places = [(t, side) for t, side, _ in found]
        scores = [s for _, _, s in found]
        part_keys = [keys[t][side * R : (side + 1) * R] for t, side in places]
        part_values = [values[t][side * R : (side + 1) * R] for t, side in places]
        queries = [query] * len(places)
        if memory:
            places.append("memory")
            queries.append(query_raw_ref[rows, :])
            scores.append(dot(memory_keys, queries[-1], (1, 1)) + bias)
            part_keys.append(memory_keys)
            part_values.append(memory_values)
        probs = softmax_parts(scores)
        grads = [dot(value, grad, (1, 1)) for value in part_values]
        inner = sum(jnp.sum(p * d, axis=0, keepdims=True) for p, d in zip(probs, grads))
        local_query, raw_query = None, None
        for at, p, d, key, asked in zip(places, probs, grads, part_keys, queries):
            moved = (p * (d - inner)).astype(BF)
            add(grad_keys, at, dot(moved, asked, (1, 0)))
            add(grad_values, at, dot(p.astype(BF), grad, (1, 0)))
            back = dot(key, moved, (0, 0))
            if at == "memory":
                raw_query = back
            else:
                local_query = back if local_query is None else local_query + back
        cos = table_rows(grid, cos_ref, me, part)
        sin = table_rows(grid, sin_ref, me, part)
        result = turn(local_query.T, cos, -sin)
        if memory:
            result = result + raw_query.T
        dq_ref[rows, :] = (result * SCALE).astype(BF)
    for t in range(U):
        member = lax.rem(me - t + U, U)
        for side in range(2):
            rows = pl.ds(side * R, R)
            cos = table_rows(grid, cos_ref, member, side)
            sin = table_rows(grid, sin_ref, member, side)
            key = turn(grad_keys[(t, side)], cos, -sin) * SCALE
            dkv_refs[t][0, rows, :] = key.astype(dkv_refs[t].dtype)
            dkv_refs[t][1, rows, :] = grad_values[(t, side)].astype(dkv_refs[t].dtype)
    if memory:
        key = (grad_keys["memory"] * SCALE).astype(BF)
        value = grad_values["memory"].astype(BF)

        @pl.when(step < heads // 2)
        def _():
            refs[0][...] = key
            refs[1][...] = value

        @pl.when(step >= heads // 2)
        def _():
            refs[2][...] = key
            refs[3][...] = value


def attend_back(grid, info, tables, query, grad, pairs, extra):
    rows, width = query.shape
    heads = width // HEAD_DIM
    memory = extra is not None
    memory_rows = grid.n_dp * extra["topk"] if memory else 8
    piece, pair, own, other = head_specs(grid, heads, memory_rows)
    table = pl.BlockSpec((SEG, HEAD_DIM), lambda h, info: (0, 0))
    operands = [*tables, query, grad, *pairs]
    specs = [table, table, piece, piece] + [pair] * grid.U
    out_shape = [jax.ShapeDtypeStruct((rows, width), BF), jax.ShapeDtypeStruct((2, rows, width), F32)]
    out_shape += [jax.ShapeDtypeStruct((2, rows, width), BF)] * (grid.U - 1)
    out_specs = [piece] + [pair] * grid.U
    if memory:
        operands += [extra["query"], *extra["keys"], *extra["values"], extra["bias"]]
        specs += [piece, own, other, own, other, pl.BlockSpec((memory_rows, 1), lambda h, info: (0, 0))]
        out_shape += [jax.ShapeDtypeStruct((memory_rows, width // 2), BF)] * 4
        out_specs += [own, own, other, other]
    outs = pl.pallas_call(
        functools.partial(attend_back_body, grid, memory, heads),
        grid_spec=pltpu.PrefetchScalarGridSpec(
            num_scalar_prefetch=1, grid=(heads,), in_specs=specs, out_specs=out_specs
        ),
        out_shape=out_shape,
        compiler_params=params(),
        cost_estimate=attention_cost(grid, heads, memory_rows if memory else 0, 5),
    )(info, *operands)
    return outs[0], outs[1 : 1 + grid.U], outs[1 + grid.U :]


def pick_body(grid, info_ref, picks_ref, *refs):
    U, R = grid.U, grid.R
    out_ref = refs[-1]
    picks = picks_ref[0]
    key, value = 0.0, 0.0
    for t in range(U):
        member = lax.rem(info_ref[0] - t + U, U)
        for side in range(2):
            across = lax.broadcasted_iota(jnp.int32, (picks.shape[0], R), 1)
            chosen = (picks == across + piece_start(grid, member, side)).astype(BF)
            rows = pl.ds(side * R, R)
            key = key + dot(chosen, refs[t][2, rows, :], (1, 0))
            value = value + dot(chosen, refs[t][1, rows, :], (1, 0))
    out_ref[0] = key.astype(BF)
    out_ref[1] = value.astype(BF)


def pick_memory(grid, info, picks, stacked):
    heads, topk = picks.shape
    per = heads // 2
    at = lambda h, info: info[2] * per + h
    piece = pl.BlockSpec((3, grid.T, HEAD_DIM), lambda h, info: (0, 0, at(h, info)))
    return pl.pallas_call(
        functools.partial(pick_body, grid),
        grid_spec=pltpu.PrefetchScalarGridSpec(
            num_scalar_prefetch=1,
            grid=(per,),
            in_specs=[pl.BlockSpec((1, topk, 1), lambda h, info: (at(h, info), 0, 0))]
            + [piece] * grid.U,
            out_specs=pl.BlockSpec((2, topk, HEAD_DIM), lambda h, info: (0, 0, h)),
        ),
        out_shape=jax.ShapeDtypeStruct((2, topk, per * HEAD_DIM), BF),
        compiler_params=params(),
        cost_estimate=pl.CostEstimate(
            flops=4 * topk * SEG * HEAD_DIM * per, bytes_accessed=4 * SEG * HEAD_DIM * per, transcendentals=0
        ),
    )(info, picks[:, :, None], *stacked)


def finish_body(grid, memory, heads, info_ref, *refs):
    U, R = grid.U, grid.R
    dq_ref, dkv_refs, out_ref = refs[0], refs[1 : 1 + U], refs[-1]
    refs = refs[1 + U :]
    kind, head = pl.program_id(0) // heads, pl.program_id(0) % heads

    @pl.when(kind == 0)
    def _():
        out_ref[...] = dq_ref[...]

    @pl.when(kind > 0)
    def _():
        total = sum(r[0].astype(F32) for r in dkv_refs)
        if memory:
            picks = refs[0][0]
            own = head // (heads // 2) == info_ref[2]
            back = jnp.where(own, refs[1][0], refs[2][0])
        for side in range(2):
            rows = slice(side * R, (side + 1) * R)
            value = total[rows]
            if memory:
                down = lax.broadcasted_iota(jnp.int32, (R, picks.shape[1]), 0)
                chosen = (down + piece_start(grid, info_ref[0], side) == picks).astype(BF)
                value = value + dot(chosen, back, (1, 0))
            out_ref[rows, :] = value.astype(BF)


def finish_gradient(grid, info, grad_query, grad_pairs, picks, halves):
    rows, width = grad_query.shape
    heads = width // HEAD_DIM
    memory = halves is not None
    per = heads // 2
    which = lambda b: jnp.maximum(b // heads - 1, 0)
    pair = pl.BlockSpec((1, rows, HEAD_DIM), lambda b, info: (which(b), 0, jnp.where(b < heads, 0, b % heads)))
    operands = [grad_query, *grad_pairs]
    specs = [pl.BlockSpec((rows, HEAD_DIM), lambda b, info: (0, jnp.minimum(b, heads - 1)))] + [pair] * grid.U
    if memory:
        topk = picks.shape[1]
        own = lambda b, info: jnp.clip(b % heads - info[2] * per, 0, per - 1)
        other = lambda b, info: jnp.clip(b % heads - (1 - info[2]) * per, 0, per - 1)
        operands += [picks[:, None, :], *halves]
        specs += [
            pl.BlockSpec((1, 1, topk), lambda b, info: (b % heads, 0, 0)),
            pl.BlockSpec((1, topk, HEAD_DIM), lambda b, info: (which(b), 0, own(b, info))),
            pl.BlockSpec((1, topk, HEAD_DIM), lambda b, info: (which(b), 0, other(b, info))),
        ]
    return pl.pallas_call(
        functools.partial(finish_body, grid, memory, heads),
        grid_spec=pltpu.PrefetchScalarGridSpec(
            num_scalar_prefetch=1,
            grid=(3 * heads,),
            in_specs=specs,
            out_specs=pl.BlockSpec((rows, HEAD_DIM), lambda b, info: (0, b)),
        ),
        out_shape=jax.ShapeDtypeStruct((rows, 3 * width), BF),
        compiler_params=params(),
        cost_estimate=pl.CostEstimate(
            flops=2 * rows * width, bytes_accessed=16 * rows * width, transcendentals=0
        ),
    )(info, *operands)


def norm(value, gain):
    return value * lax.rsqrt(jnp.mean(value * value, axis=-1, keepdims=True) + EPSILON) * gain


def norm_back(value, gain, grad):
    inverse = lax.rsqrt(jnp.mean(value * value, axis=-1, keepdims=True) + EPSILON)
    unit = value * inverse
    grad_gain = jnp.sum(grad * unit, axis=0)
    scaled = grad * gain
    pulled = inverse * (scaled - unit * jnp.mean(scaled * unit, axis=-1, keepdims=True))
    return pulled, grad_gain


def mm(left, right, contract=(1, 0)):
    return dot(left, right, contract)


def local(
    n_dp,
    pieces,
    tokens,
    cotangent,
    doc_lengths,
    partner,
    memory_picks,
    attention_in,
    attention_out,
    feed_in,
    feed_out,
    norm_gains,
):
    grid = Grid(n_dp, pieces)
    grid.trace()
    layers = attention_in.shape[0]
    width = tokens.shape[2]
    heads = width // HEAD_DIM
    topk = memory_picks.shape[3]
    valid_all, visible_all = jax.vmap(memory_plan)(doc_lengths, partner)
    valid = valid_all[grid.m, grid.slot]
    visible = visible_all[grid.m, grid.slot]
    relative = (grid.slot - jnp.arange(n_dp)) % n_dp
    bias = jnp.repeat(jnp.where(visible[relative], 0.0, MASKED), topk)[:, None].astype(F32)
    info = jnp.stack([grid.k, valid, grid.c]).astype(jnp.int32)
    tables = rope_tables()

    picks_there = grid.swap(memory_picks)
    picks = jnp.where(
        grid.r == grid.c, memory_picks[grid.m, 0], picks_there[grid.m, 0]
    )

    def exchange(value):
        return [value] + [grid.member(value, t) for t in range(1, grid.U)]

    def attention(l, hidden, w_qkv, w_out):
        memory = l == layers - 1
        normed = norm(hidden, gains[l, 0]).astype(BF)
        split = split_heads(grid, memory, info, tables, mm(normed, w_qkv))
        query, pairs = split[0], exchange(split[1])
        extra = None
        if memory:
            chosen = pick_memory(grid, info, picks, pairs)
            slots = [chosen] + [grid.slots(chosen, t) for t in range(1, n_dp)]
            half = jnp.stack(slots, axis=1).reshape(2, n_dp * topk, -1)
            there = grid.swap(half)
            extra = {
                "topk": topk,
                "query": split[2],
                "keys": (half[0], there[0]),
                "values": (half[1], there[1]),
                "bias": bias,
            }
        attended = attend(grid, info, query, pairs, extra)
        middle = hidden + mm(attended, w_out)
        return middle, (hidden, normed, query, pairs, extra, attended)

    def feed(l, middle, w_up, w_down):
        normed = norm(middle, gains[l, 1]).astype(BF)
        gate_up = mm(normed, w_up)
        gate, up = jnp.split(gate_up, 2, axis=1)
        inner = (jax.nn.silu(gate) * up).astype(BF)
        return middle + mm(inner, w_down), (middle, normed, gate_up, inner)

    def feed_back(l, grad, kept, w_up, w_down):
        middle, normed, gate_up, inner = kept
        grad_low = grad.astype(BF)
        grad_inner = mm(grad_low, w_down, (1, 1))
        down = Scatter(grid, [(inner, grad_low)])
        gate, up = jnp.split(gate_up, 2, axis=1)
        sigmoid = jax.nn.sigmoid(gate)
        grad_gate = grad_inner * up * sigmoid * (1.0 + gate * (1.0 - sigmoid))
        grad_up = grad_inner * gate * sigmoid
        grad_gate_up = jnp.concatenate([grad_gate, grad_up], axis=1).astype(BF)
        up = Scatter(grid, [(normed, grad_gate_up)])
        pulled, grad_gain = norm_back(middle, gains[l, 1], mm(grad_gate_up, w_up, (1, 1)))
        return grad + pulled, grad_gain, down, up

    def attention_back(l, grad, kept, w_qkv, w_out):
        hidden, normed, query, pairs, extra, attended = kept
        grad_attended = grad.astype(BF)
        grad_heads = mm(grad_attended, w_out, (1, 1)).astype(BF)
        grad_query, grad_pairs, memory_grads = attend_back(
            grid, info, tables, query, grad_heads, pairs, extra
        )
        grad_pairs = [grad_pairs[0]] + [
            grid.member(grad_pairs[t], grid.U - t) for t in range(1, grid.U)
        ]
        halves = None
        if extra is not None:
            own = jnp.stack(memory_grads[:2])
            there = grid.swap(jnp.stack(memory_grads[2:]))
            joined = own.astype(F32) + there.astype(F32)
            joined = joined.astype(BF).reshape(2, n_dp, topk, -1)
            total = joined[:, 0].astype(F32)
            for t in range(1, n_dp):
                total = total + grid.slots(joined[:, t], n_dp - t).astype(F32)
            low = total.astype(BF)
            for t in range(1, grid.Q):
                total = total + grid.within(low, t).astype(F32)
            total = total.astype(BF)
            halves = (total, grid.swap(total))
        grad_projected = finish_gradient(grid, info, grad_query, grad_pairs, picks, halves)
        both = Scatter(grid, [(attended, grad_attended), (normed, grad_projected)])
        pulled, grad_gain = norm_back(hidden, gains[l, 0], mm(grad_projected, w_qkv, (1, 1)))
        return grad + pulled, grad_gain, both

    hidden, cotangent_rows, gains, weights = gather_all(
        grid, tokens, cotangent, norm_gains, [attention_in, attention_out, feed_in, feed_out]
    )
    hidden = hidden.astype(F32)
    first = [w[:2] for w in weights]
    second = [w[2:3] for w in weights]
    third = [w[3:] for w in weights]
    kept_attention, kept_feed = [None] * layers, [None] * layers
    for l in range(layers):
        middle, kept_attention[l] = attention(l, hidden, *first[l])
        hidden, kept_feed[l] = feed(l, middle, *second[l], *third[l])
    layer_output = grid.from_units(hidden.astype(BF))

    grad = cotangent_rows.astype(F32)
    downs, ups, boths = [None] * layers, [None] * layers, [None] * layers
    grad_gains = [[None, None] for _ in range(layers)]
    for l in reversed(range(layers)):
        grad, grad_gains[l][1], downs[l], ups[l] = feed_back(
            l, grad, kept_feed[l], *second[l], *third[l]
        )
        if l < layers - 1:
            boths[l + 1].across()
            downs[l + 1].along_line()
            ups[l + 1].along_line()
            boths[l + 1].line, downs[l + 1].found, ups[l + 1].found, grad, downs[l].parts, ups[l].parts = tie(
                boths[l + 1].line, downs[l + 1].found, ups[l + 1].found, grad, downs[l].parts, ups[l].parts
            )
            boths[l + 1].along_line()
        else:
            grad, downs[l].parts, ups[l].parts = tie(grad, downs[l].parts, ups[l].parts)
        downs[l].across()
        ups[l].across()
        grad, grad_gains[l][0], boths[l] = attention_back(l, grad, kept_attention[l], *first[l])
        grad, boths[l].parts, downs[l].line, ups[l].line = tie(
            grad, boths[l].parts, downs[l].line, ups[l].line
        )
    boths[0].across()
    boths[0].along_line()
    downs[0].along_line()
    ups[0].along_line()
    input_grad = grid.from_units(grad.astype(BF)).astype(F32)
    return (
        layer_output,
        input_grad,
        jnp.stack([both.found[1] for both in boths]),
        jnp.stack([both.found[0] for both in boths]),
        jnp.stack([up.found[0] for up in ups]),
        jnp.stack([down.found[0] for down in downs]),
        scatter_gains(grid, jnp.stack([jnp.stack(pair) for pair in grad_gains])),
    )


def solution(mesh):
    rows = P(None, ("dp", "fsdp"), None)
    in_specs = (rows, rows, P(), P(), P(None, "dp", None, None), rows, rows, rows, rows, P(None, None, ("dp", "fsdp")))
    out_specs = (rows, rows, rows, rows, rows, rows, P(None, None, ("dp", "fsdp")))
    body = functools.partial(local, mesh.shape["dp"], mesh.shape["fsdp"])
    return jax.shard_map(body, mesh=mesh, in_specs=in_specs, out_specs=out_specs, check_vma=False)
```

```python
import functools
import math

import jax
import jax.numpy as jnp
from jax import lax
from jax.experimental import pallas as pl
from jax.experimental.pallas import tpu as pltpu
from jax.sharding import PartitionSpec as P

HEAD_DIM = 128
SEG = 1024
MICRO = 2
EPSILON = 1e-06
MASKED = -1e30
SCALE = HEAD_DIM ** (-0.5)
LOG2E = 1.0 / math.log(2.0)
BF = jnp.bfloat16
F32 = jnp.float32
VMEM_LIMIT = 48 * 1024 * 1024


def slot_layout(lengths):
    slot_total = lengths.shape[0]
    slot_counts = ((lengths + SEG - 1) // SEG).astype(jnp.int32)
    slot_starts = (jnp.cumsum(slot_counts) - slot_counts).astype(jnp.int32)
    slot_index = jnp.arange(slot_total, dtype=jnp.int32)
    started = (slot_starts[None, :] <= slot_index[:, None]) & (slot_counts[None, :] > 0)
    owner_doc = (jnp.sum(started.astype(jnp.int32), axis=1) - 1).astype(jnp.int32)
    owner_pick = slot_index[None, :] == owner_doc[:, None]
    first_slot = jnp.sum(jnp.where(owner_pick, slot_starts[None, :], 0), axis=1).astype(jnp.int32)
    doc_total = jnp.sum(jnp.where(owner_pick, lengths[None, :], 0), axis=1).astype(jnp.int32)
    valid_rows = jnp.clip(doc_total - (slot_index - first_slot) * SEG, 0, SEG).astype(jnp.int32)
    return (valid_rows, owner_doc)


def memory_plan(lengths, partner_row):
    valid_rows, owner_doc = slot_layout(lengths)
    block_ids = jnp.arange(lengths.shape[0], dtype=jnp.int32)
    earlier = (block_ids[None, :] < block_ids[:, None]) & (owner_doc[None, :] == owner_doc[:, None])
    visible = earlier | (block_ids[None, :] == partner_row[:, None])
    return (valid_rows, visible)


class Grid:
    def __init__(self, n_dp, pieces):
        self.n_dp, self.F = n_dp, pieces
        self.J = n_dp // 2
        self.bits = self.J.bit_length() - 1
        self.Q = pieces // 4
        self.U = 2 * self.Q
        self.R = SEG // pieces
        self.T = 2 * self.R

    def trace(self):
        dp = lax.axis_index("dp")
        self.c, self.j, self.f = dp % 2, dp // 2, lax.axis_index("fsdp")
        self.q, self.g = self.f // self.Q, self.f % self.Q
        self.m, self.r = self.q // 2, self.q % 2
        self.k = self.c * self.Q + self.g
        self.slot = 2 * self.j + self.r

    def permute(self, value, target):
        pairs = []
        for j in range(self.J):
            for c in range(2):
                for f in range(self.F):
                    j2, c2, f2 = target(j, c, f)
                    pairs.append(((j * 2 + c) * self.F + f, (j2 * 2 + c2) * self.F + f2))
        return lax.ppermute(value, ("dp", "fsdp"), pairs)

    def swap(self, value):
        return self.permute(value, lambda j, c, f: (j, 1 - c, f))

    def ring(self, value, t):
        return self.permute(value, lambda j, c, f: (j, c, (f + t) % self.F))

    def bit(self, phase, c):
        return phase if c == 0 else self.bits - 1 - phase

    def flip(self, value, phase):
        return self.permute(value, lambda j, c, f: (j ^ (1 << self.bit(phase, c)), c, f))

    def mask(self, key, c):
        return sum(1 << self.bit(p, c) for p in range(self.bits) if key >> p & 1)

    def place(self, key, c):
        return jnp.where(c == 0, self.j ^ self.mask(key, 0), self.j ^ self.mask(key, 1))

    def member(self, value, t):
        def target(j, c, f):
            q, g = f // self.Q, f % self.Q
            k = (c * self.Q + g + t) % self.U
            return (j, k // self.Q, q * self.Q + k % self.Q)

        return self.permute(value, target)

    def within(self, value, t):
        return self.permute(
            value, lambda j, c, f: (j, c, f // self.Q * self.Q + (f % self.Q + t) % self.Q)
        )

    def slots(self, value, t):
        def target(j, c, f):
            q, g = f // self.Q, f % self.Q
            slot = (2 * j + q % 2 + t) % self.n_dp
            return (slot // 2, c, (2 * (q // 2) + slot % 2) * self.Q + g)

        return self.permute(value, target)

    def _spread(self, second):
        def target(j, c, f):
            m = f // (self.F // 2)
            m = 1 - m if second else m
            k = min(f, self.F - 1 - f)
            return (j, k // self.Q, (2 * m + c) * self.Q + k % self.Q)

        return target

    def _collect(self, second):
        there = self._spread(second)
        back = {
            there(0, c, f): (c, f) for c in range(2) for f in range(self.F)
        }
        return lambda j, c, f: (j,) + back[(0, c, f)]

    def to_units(self, value):
        here = self.f // (self.F // 2)
        first = self.permute(jnp.where(here == 0, value[0], value[1]), self._spread(False))
        second = self.permute(jnp.where(here == 0, value[1], value[0]), self._spread(True))
        return jnp.concatenate(
            [jnp.where(self.m == 0, first, second), jnp.where(self.m == 0, second, first)]
        )

    def from_units(self, value):
        low, high = value[: self.R], value[self.R :]
        first = self.permute(jnp.where(self.m == 0, low, high), self._collect(False))
        second = self.permute(jnp.where(self.m == 0, high, low), self._collect(True))
        here = self.f // (self.F // 2)
        return jnp.stack([jnp.where(here == 0, first, second), jnp.where(here == 0, second, first)])


def any_spec():
    return pl.BlockSpec(memory_space=pl.ANY)


MESH = pl.DeviceIdType.MESH


class Here:
    def __init__(self, grid):
        self.grid = grid
        dp = lax.axis_index("dp")
        self.j, self.c, self.f = dp // 2, dp % 2, lax.axis_index("fsdp")
        self.q, self.g = self.f // grid.Q, self.f % grid.Q
        self.m, self.r = self.q // 2, self.q % 2
        self.k = self.c * grid.Q + self.g
        self.swap = self.device(self.j, 1 - self.c, self.f)

    def device(self, j, c, f):
        return {"dp": 2 * j + c, "fsdp": f}

    def ring(self, t):
        return self.device(self.j, self.c, (self.f + t) % self.grid.F)

    def step(self, phase):
        first, second = (1 << self.grid.bit(phase, c) for c in (0, 1))
        return first + self.c * (second - first)

    def moved(self, j, phase):
        step = self.step(phase)
        return j + step * (1 - 2 * ((j // step) % 2))

    def flip(self, phase):
        return self.device(self.moved(self.j, phase), self.c, self.f)

    def slots(self, t):
        grid = self.grid
        slot = (2 * self.j + self.r + t) % grid.n_dp
        return self.device(slot // 2, self.c, (2 * self.m + slot % 2) * grid.Q + self.g)

    def member(self, t):
        grid = self.grid
        k = (self.k + t) % grid.U
        return self.device(self.j, k // grid.Q, self.q * grid.Q + k % grid.Q)

    def place(self, key):
        j = self.j
        for phase in range(self.grid.bits):
            if key >> phase & 1:
                j = self.moved(j, phase)
        return j

    def greet(self):
        grid = self.grid
        barrier = pltpu.get_barrier_semaphore()
        peers = [self.ring(t) for t in range(1, grid.F)]
        peers += [self.device(self.j, 1 - self.c, (self.f + t) % grid.F) for t in range(grid.F)]
        for bit in range(grid.bits):
            step = 1 << bit
            peers.append(self.device(self.j + step * (1 - 2 * ((self.j // step) % 2)), self.c, self.f))
        for peer in peers:
            pl.semaphore_signal(barrier, inc=1, device_id=peer, device_id_type=MESH)
        pl.semaphore_wait(barrier, len(peers))


def remote(source, target, sems, index, device):
    return pltpu.make_async_remote_copy(
        src_ref=source,
        dst_ref=target,
        send_sem=sems.at[0, index],
        recv_sem=sems.at[1, index],
        device_id=device,
        device_id_type=MESH,
    )


class Spread:
    def __init__(self, here, shard, whole, sems, own_sem, split):
        grid = here.grid
        self.here, self.split = here, split
        rows, width = shard.shape
        half = width // 2 if split else width

        def part(ref, c):
            if not split:
                return ref
            return ref.at[(slice(None),) * (len(ref.shape) - 1) + (pl.ds(pl.multiple_of(c * half, 128), half),)]

        j, c, f = here.j, here.c, here.f
        mine = part(whole, c)
        self.own = pltpu.make_async_copy(part(shard, c), part(whole.at[j, c, f], c), own_sem)
        other = 1 - c if split else c
        self.pre = remote(part(shard, other), part(whole.at[j, c, f], other), sems, 0, here.swap)
        at = 1
        self.line = []
        for t in range(1, grid.F):
            block = mine.at[j, :, f]
            self.line.append(remote(block, block, sems, at, here.ring(t)))
            at += 1
        self.flips = []
        for phase in range(grid.bits):
            sent = []
            for key in range(1 << phase):
                block = mine.at[here.place(key)]
                sent.append(remote(block, block, sems, at, here.flip(phase)))
                at += 1
            self.flips.append(sent)
        self.swaps = []
        for key in range(grid.J if split else 0):
            block = mine.at[here.place(key)]
            self.swaps.append(remote(block, block, sems, at, here.swap))
            at += 1

    @staticmethod
    def count(grid):
        return 1 + (grid.F - 1) + (grid.J - 1) + grid.J

    def begin(self):
        self.own.start()
        self.pre.start()

    def to_line(self):
        self.own.wait()
        self.pre.wait()
        for copy in self.line:
            copy.start()

    def _send(self, keys):
        for key in keys:
            if self.swaps:
                self.swaps[key].start()
        for phase, sent in enumerate(self.flips):
            for key in keys:
                if key < 1 << phase:
                    sent[key].start()

    def steps(self):
        def first():
            for copy in self.line:
                copy.wait()
            self._send([0])

        def later(phase):
            for copy in self.flips[phase]:
                copy.wait()
            self._send([key + (1 << phase) for key in range(1 << phase)])

        def last():
            for copy in self.swaps:
                copy.wait()

        return [first] + [functools.partial(later, p) for p in range(len(self.flips))] + [last]


class Regroup:
    def __init__(self, here, source, target, sems, own_sem):
        grid = here.grid
        half = grid.F // 2
        k = jnp.minimum(here.f, grid.F - 1 - here.f)
        side = here.f // half
        self.sends = []
        for m in range(2):
            c2, f2 = k // grid.Q, (2 * m + here.c) * grid.Q + k % grid.Q
            same = (c2 == here.c) & (f2 == here.f)
            own = pltpu.make_async_copy(source.at[m], target.at[side], own_sem)
            away = pltpu.make_async_remote_copy(
                src_ref=source.at[m],
                dst_ref=target.at[side],
                send_sem=sems.at[0, m],
                recv_sem=sems.at[1, side],
                device_id=here.device(here.j, c2, f2),
                device_id_type=MESH,
            )
            self.sends.append((same, own, away))
        self.arrivals = []
        for side in range(2):
            from_f = here.k if side == 0 else grid.F - 1 - here.k
            same = (here.r == here.c) & (from_f == here.f)
            came = pltpu.make_async_remote_copy(
                src_ref=source.at[0],
                dst_ref=target.at[side],
                send_sem=sems.at[0, 0],
                recv_sem=sems.at[1, side],
                device_id=here.swap,
                device_id_type=MESH,
            )
            self.arrivals.append((same, came))

    def start(self):
        for same, own, away in self.sends:
            pl.when(same)(own.start)
            pl.when(jnp.logical_not(same))(away.start)

    def wait(self):
        for same, own, away in self.sends:
            pl.when(same)(own.wait)
            pl.when(jnp.logical_not(same))(away.wait_send)
        for same, came in self.arrivals:
            pl.when(jnp.logical_not(same))(came.wait_recv)


def gather_body(grid, layers, kinds, *refs):
    tokens, cotangent, gains = refs[:3]
    shards = refs[3 : 3 + kinds]
    outs = refs[3 + kinds :]
    tokens_out, cotangent_out, gains_out = outs[:3]
    wholes = outs[3 : 3 + layers * kinds]
    sems, own_sems, regroup_sems = outs[3 + layers * kinds :]
    here = Here(grid)
    here.greet()
    rows = Regroup(here, tokens, tokens_out, regroup_sems.at[0], own_sems.at[0])
    rows_back = Regroup(here, cotangent, cotangent_out, regroup_sems.at[1], own_sems.at[1])
    moves = [Spread(here, gains, gains_out, sems.at[0], own_sems.at[2], False)]
    for l in range(layers):
        for i in range(kinds):
            n = l * kinds + i
            moves.append(
                Spread(here, shards[i].at[l], wholes[n], sems.at[n + 1], own_sems.at[n + 3], True)
            )
    for move in moves:
        move.begin()
    rows.start()
    steps = [move.steps() for move in moves]
    count = len(steps[0])
    moves[0].to_line()
    moves[1].to_line()
    for at in range(len(moves) + count - 1):
        if at + 2 < len(moves):
            moves[at + 2].to_line()
        if at == len(moves) - 3:
            rows_back.start()
        for back in range(count):
            if 0 <= at - back < len(moves):
                steps[at - back][back]()
    rows.wait()
    rows_back.wait()


def gather_all(grid, tokens, cotangent, gains, shards):
    layers, kinds = shards[0].shape[0], len(shards)
    packed = jnp.zeros((8, 128), F32).at[: layers * 2, : gains.shape[2]].set(
        gains.astype(F32).reshape(layers * 2, -1)
    )
    whole = lambda shard: jax.ShapeDtypeStruct((grid.J, 2, grid.F) + shard.shape[-2:], shard.dtype)
    out_shape = [jax.ShapeDtypeStruct(tokens.shape, BF), jax.ShapeDtypeStruct(tokens.shape, BF), whole(packed)]
    out_shape += [whole(shard) for _ in range(layers) for shard in shards]
    moves = 1 + layers * kinds
    outs = pl.pallas_call(
        functools.partial(gather_body, grid, layers, kinds),
        in_specs=[any_spec()] * (3 + kinds),
        out_specs=[any_spec()] * len(out_shape),
        out_shape=out_shape,
        scratch_shapes=[
            pltpu.SemaphoreType.DMA((moves, 2, Spread.count(grid))),
            pltpu.SemaphoreType.DMA((moves + 2,)),
            pltpu.SemaphoreType.DMA((2, 2, 2)),
        ],
        compiler_params=pltpu.CompilerParams(
            collective_id=0, has_side_effects=True, vmem_limit_bytes=VMEM_LIMIT
        ),
    )(tokens, cotangent, packed, *shards)
    width = tokens.shape[2]
    gains_all = outs[2][..., : layers * 2, : gains.shape[2]]
    gains_all = jnp.moveaxis(gains_all, 3, 0).reshape(layers, 2, -1)
    weights = [
        [outs[3 + l * kinds + i].reshape(-1, shards[i].shape[2]) for i in range(kinds)]
        for l in range(layers)
    ]
    return outs[0].reshape(-1, width), outs[1].reshape(-1, width), gains_all, weights


class Move:
    def __init__(self, array, shape, count, copies):
        self.array, self.shape, self.count, self.copies = array, shape, count, copies


def flip_move(grid, parts, phase):
    count = parts.shape[0] // 2

    def copies(here, source, target):
        found = []
        for i in range(count):
            at = here.place(2 * i + 1) if phase == 0 else 2 * i + 1
            peer = here.flip(phase)
            found.append((source.at[at], target.at[i], peer, peer))
        return found

    return Move(parts, (count,) + parts.shape[1:], count, copies)


def ring_move(grid, line):
    def copies(here, source, target):
        return [
            (source.at[:, (here.f + t) % grid.F], target.at[t - 1], here.ring(t), here.ring(grid.F - t))
            for t in range(1, grid.F)
        ]

    return Move(line, (grid.F - 1, 2) + line.shape[2:], grid.F - 1, copies)


def swap_move(array, give=None):
    def copies(here, source, target):
        return [(source if give is None else source.at[give(here)], target, here.swap, here.swap)]

    return Move(array, array.shape if give is None else array.shape[1:], 1, copies)


def slots_move(grid, array, back):
    def copies(here, source, target):
        found = []
        for t in range(1, grid.n_dp):
            ahead, behind = here.slots(t), here.slots(grid.n_dp - t)
            if back:
                found.append((source.at[:, t], target.at[t - 1], behind, ahead))
            else:
                found.append((source, target.at[t - 1], ahead, behind))
        return found

    shape = array.shape if not back else array.shape[:1] + array.shape[2:]
    return Move(array, (grid.n_dp - 1,) + shape, grid.n_dp - 1, copies)


def member_move(grid, array, back):
    def copies(here, source, target):
        found = []
        for t in range(1, grid.U):
            ahead, behind = here.member(t), here.member(grid.U - t)
            if back:
                found.append((source.at[t - 1], target.at[t - 1], behind, ahead))
            else:
                found.append((source, target.at[t - 1], ahead, behind))
        return found

    shape = array.shape[1:] if back else array.shape
    return Move(array, (grid.U - 1,) + shape, grid.U - 1, copies)


IDS = [1]


def host(grid, body, steps, in_specs, operands, out_specs, out_shape, moves=(), scratch=(), cost=None, first=None):
    counts = [len(operands), len(moves), len(out_shape), len(moves), len(scratch)]

    def kernel(*refs):
        parts, at = [], 0
        for count in counts:
            parts.append(refs[at : at + count])
            at += count
        ins, sources, outs, targets, held = parts
        here = Here(grid)
        step = pl.program_id(0)
        copies = []
        if moves:
            send_sems, recv_sems = refs[at:]
            listed = [c for m, s, t in zip(moves, sources, targets) for c in m.copies(here, s, t)]
            for i, (source, target, peer, _) in enumerate(listed):
                copies.append(
                    pltpu.make_async_remote_copy(
                        src_ref=source,
                        dst_ref=target,
                        send_sem=send_sems.at[i],
                        recv_sem=recv_sems.at[i],
                        device_id=peer,
                        device_id_type=MESH,
                    )
                )

            @pl.when(step == 0)
            def _():
                barrier = pltpu.get_barrier_semaphore()
                for _, _, _, peer in listed:
                    pl.semaphore_signal(barrier, inc=1, device_id=peer, device_id_type=MESH)
                pl.semaphore_wait(barrier, len(listed))
                for copy in copies:
                    copy.start()

        if body is not None:
            body(here, step, ins, outs, held)
        if moves:

            @pl.when(step == steps - 1)
            def _():
                for copy in copies:
                    copy.wait()

    total = sum(move.count for move in moves)
    extra = {}
    sems = []
    if moves:
        extra = {"collective_id": IDS[0], "has_side_effects": True}
        IDS[0] += 1
        sems = [pltpu.SemaphoreType.DMA((total,)), pltpu.SemaphoreType.DMA((total,))]
    outs = pl.pallas_call(
        kernel,
        grid=(steps,),
        in_specs=list(in_specs) + [any_spec()] * len(moves),
        out_specs=list(out_specs) + [any_spec()] * len(moves),
        out_shape=list(out_shape) + [jax.ShapeDtypeStruct(m.shape, m.array.dtype) for m in moves],
        scratch_shapes=list(scratch) + sems,
        compiler_params=pltpu.CompilerParams(vmem_limit_bytes=VMEM_LIMIT, **extra),
        cost_estimate=cost,
    )(*operands, *[move.array for move in moves])
    return outs[: len(out_shape)], outs[len(out_shape) :]


def send(grid, moves):
    return host(grid, None, 1, [], [], [], [], moves)[1]


def scatter_gains(grid, total):
    layers, kinds, width = total.shape
    devices = grid.n_dp * grid.F
    total = total + grid.swap(total)
    for p in range(grid.bits):
        total = total + grid.permute(total, lambda j, c, f: (j ^ (1 << p), c, f))
    for step in [1 << p for p in range(grid.F.bit_length() - 1)]:
        total = total + grid.permute(total, lambda j, c, f: (j, c, f ^ step))
    here = (grid.j * 2 + grid.c) * grid.F + grid.f
    return lax.dynamic_slice_in_dim(total, here * (width // devices), width // devices, axis=2)


def rope_tables():
    half_dim = HEAD_DIM // 2
    frequency = jnp.exp(
        jnp.arange(half_dim, dtype=F32) * (-2.0 * math.log(10000.0) / HEAD_DIM)
    )
    angles = jnp.arange(SEG, dtype=jnp.int32).astype(F32)[:, None] * frequency[None, :]
    cos, sin = jnp.cos(angles), jnp.sin(angles)
    return (jnp.concatenate([cos, cos], axis=-1), jnp.concatenate([-sin, sin], axis=-1))


def turn(values, cos, sin):
    return values * cos + pltpu.roll(values, HEAD_DIM // 2, 1) * sin


def smem():
    return pl.BlockSpec(memory_space=pltpu.SMEM)


def whole_spec(*shape):
    return pl.BlockSpec(shape, lambda i: (0,) * len(shape))


def columns_spec(*shape, first=0):
    return pl.BlockSpec(shape, lambda i: (0,) * (len(shape) - 1) + (i + first,))


def rows_spec(*shape):
    return pl.BlockSpec(shape, lambda i: (i,) + (0,) * (len(shape) - 1))


def kind(*shape, dtype=BF):
    return jax.ShapeDtypeStruct(shape, dtype)


def piece_start(grid, member, part):
    return (member if part == 0 else grid.F - 1 - member) * grid.R


def table_rows(grid, table_ref, member, part):
    start = pl.multiple_of(piece_start(grid, member, part), grid.R)
    return table_ref[pl.ds(start, grid.R), :]


def dot(left, right, contract):
    return lax.dot_general(
        left, right, (((contract[0],), (contract[1],)), ((), ())), preferred_element_type=F32
    )


def mm(left, right, contract=(1, 0)):
    return dot(left, right, contract)


def split_heads(grid, memory, tables, projected, moves=()):
    rows, width = projected.shape
    heads = width // (3 * HEAD_DIM)
    count = 3 if memory else 2

    def body(here, step, ins, outs, held):
        cos_ref, sin_ref, q_ref, k_ref, v_ref = ins
        for part in range(2):
            at = pl.ds(part * grid.R, grid.R)
            cos = table_rows(grid, cos_ref, here.k, part)
            sin = table_rows(grid, sin_ref, here.k, part)
            query, key = q_ref[at, :], k_ref[at, :]
            outs[0][at, :] = turn(query, cos, sin).astype(BF)
            outs[1][0, at, :] = turn(key, cos, sin).astype(BF)
            outs[1][1, at, :] = v_ref[at, :].astype(BF)
            if memory:
                outs[1][2, at, :] = key.astype(BF)
                outs[2][at, :] = query.astype(BF)

    piece = lambda at: columns_spec(rows, HEAD_DIM, first=at * heads)
    flat = kind(rows, heads * HEAD_DIM)
    table = whole_spec(SEG, HEAD_DIM)
    return host(
        grid,
        body,
        heads,
        [table, table, piece(0), piece(1), piece(2)],
        [*tables, projected, projected, projected],
        [piece(0), columns_spec(count, rows, HEAD_DIM)] + [piece(0)] * memory,
        [flat, kind(count, rows, heads * HEAD_DIM)] + [flat] * memory,
        moves,
        cost=pl.CostEstimate(flops=10 * rows * width, bytes_accessed=8 * rows * width, transcendentals=0),
    )


def part_scores(grid, here, valid, part, query, keys):
    shape = (grid.R, grid.R)
    apart = lax.broadcasted_iota(jnp.int32, shape, 0) - lax.broadcasted_iota(jnp.int32, shape, 1)
    found = []
    for t in range(grid.U):
        member = (here.k - t + grid.U) % grid.U
        for side in range(part + 1):
            score = dot(keys[t][side * grid.R : (side + 1) * grid.R], query, (1, 1))
            if side == part:
                start = piece_start(grid, member, side)
                allowed = apart <= piece_start(grid, here.k, part) - start
                if side == 1:
                    down = lax.broadcasted_iota(jnp.int32, shape, 0)
                    allowed = allowed & (down < valid - start)
                score = jnp.where(allowed, score, MASKED)
            found.append((t, side, score))
    return found


def softmax_parts(scores):
    top = functools.reduce(jnp.maximum, [jnp.max(s, axis=0, keepdims=True) for s in scores])
    powers = [jnp.exp2((s - top) * (SCALE * LOG2E)) for s in scores]
    inverse = 1.0 / sum(jnp.sum(p, axis=0, keepdims=True) for p in powers)
    return [p * inverse for p in powers]


def attention_cost(grid, heads, memory_rows, products):
    pairs = grid.T * (SEG * 3 // 4 + memory_rows) * heads
    return pl.CostEstimate(
        flops=2 * products * HEAD_DIM * pairs,
        bytes_accessed=2 * HEAD_DIM * heads * 4 * (SEG + memory_rows),
        transcendentals=pairs,
    )


def memory_operands(grid, extra):
    rows = extra["keys"].shape[0]
    piece = columns_spec(grid.T, HEAD_DIM)
    column = columns_spec(rows, HEAD_DIM)
    return [extra["query"], extra["keys"], extra["values"], extra["bias"]], [
        piece, column, column, whole_spec(rows, 1)
    ], rows


def attend(grid, valid, query, pairs, extra, moves=()):
    rows, width = query.shape
    heads = width // HEAD_DIM
    R, U = grid.R, grid.U

    def body(here, step, ins, outs, held):
        valid_ref, q_ref, kv_refs, refs = ins[0], ins[1], ins[2 : 2 + U], ins[2 + U :]
        keys, values = [r[0] for r in kv_refs], [r[1] for r in kv_refs]
        for part in range(2):
            at = pl.ds(part * R, R)
            found = part_scores(grid, here, valid_ref[0], part, q_ref[at, :], keys)
            scores = [s for _, _, s in found]
            mixed = [values[t][side * R : (side + 1) * R] for t, side, _ in found]
            if extra is not None:
                scores.append(dot(refs[1][...], refs[0][at, :], (1, 1)) + refs[3][...])
                mixed.append(refs[2][...])
            total = sum(
                dot(value, p.astype(BF), (0, 0)) for value, p in zip(mixed, softmax_parts(scores))
            )
            outs[0][at, :] = total.T.astype(BF)

    piece = columns_spec(rows, HEAD_DIM)
    operands = [valid, query, *pairs]
    specs = [smem(), piece] + [columns_spec(2, rows, HEAD_DIM)] * U
    memory_rows = 0
    if extra is not None:
        more, more_specs, memory_rows = memory_operands(grid, extra)
        operands, specs = operands + more, specs + more_specs
    outs, got = host(
        grid, body, heads, specs, operands, [piece], [kind(rows, width)], moves,
        cost=attention_cost(grid, heads, memory_rows, 2),
    )
    return outs[0], got


def attend_back(grid, valid, tables, query, grad, pairs, extra, moves=()):
    rows, width = query.shape
    heads = width // HEAD_DIM
    R, U = grid.R, grid.U

    def body(here, step, ins, outs, held):
        valid_ref, cos_ref, sin_ref, q_ref, g_ref = ins[:5]
        kv_refs, refs = ins[5 : 5 + U], ins[5 + U :]
        keys, values = [r[0] for r in kv_refs], [r[1] for r in kv_refs]
        grad_keys, grad_values = {}, {}

        def add(store, at, value):
            store[at] = store[at] + value if at in store else value

        for part in range(2):
            at_rows = pl.ds(part * R, R)
            asked, grads_in = q_ref[at_rows, :], g_ref[at_rows, :]
            found = part_scores(grid, here, valid_ref[0], part, asked, keys)
            places = [(t, side) for t, side, _ in found]
            scores = [s for _, _, s in found]
            part_keys = [keys[t][side * R : (side + 1) * R] for t, side in places]
            part_values = [values[t][side * R : (side + 1) * R] for t, side in places]
            queries = [asked] * len(places)
            if extra is not None:
                places.append("memory")
                queries.append(refs[0][at_rows, :])
                scores.append(dot(refs[1][...], queries[-1], (1, 1)) + refs[3][...])
                part_keys.append(refs[1][...])
                part_values.append(refs[2][...])
            probs = softmax_parts(scores)
            grads = [dot(value, grads_in, (1, 1)) for value in part_values]
            inner = sum(jnp.sum(p * d, axis=0, keepdims=True) for p, d in zip(probs, grads))
            local_query, raw_query = None, None
            for at, p, d, key, by in zip(places, probs, grads, part_keys, queries):
                moved = (p * (d - inner)).astype(BF)
                add(grad_keys, at, dot(moved, by, (1, 0)))
                add(grad_values, at, dot(p.astype(BF), grads_in, (1, 0)))
                back = dot(key, moved, (0, 0))
                if at == "memory":
                    raw_query = back
                else:
                    local_query = back if local_query is None else local_query + back
            cos = table_rows(grid, cos_ref, here.k, part)
            sin = table_rows(grid, sin_ref, here.k, part)
            result = turn(local_query.T, cos, -sin)
            if extra is not None:
                result = result + raw_query.T
            outs[0][at_rows, :] = (result * SCALE).astype(BF)
        for t in range(U):
            member = (here.k - t + U) % U
            for side in range(2):
                at_rows = pl.ds(side * R, R)
                cos = table_rows(grid, cos_ref, member, side)
                sin = table_rows(grid, sin_ref, member, side)
                key = turn(grad_keys[(t, side)], cos, -sin) * SCALE
                if t == 0:
                    outs[1][0, at_rows, :] = key
                    outs[1][1, at_rows, :] = grad_values[(t, side)]
                else:
                    outs[2][t - 1, 0, at_rows, :] = key.astype(BF)
                    outs[2][t - 1, 1, at_rows, :] = grad_values[(t, side)].astype(BF)
        if extra is not None:
            outs[3][0] = (grad_keys["memory"] * SCALE).astype(BF)
            outs[3][1] = grad_values["memory"].astype(BF)

    piece = columns_spec(rows, HEAD_DIM)
    pair = columns_spec(2, rows, HEAD_DIM)
    table = whole_spec(SEG, HEAD_DIM)
    operands = [valid, *tables, query, grad, *pairs]
    specs = [smem(), table, table, piece, piece] + [pair] * U
    out_shape = [kind(rows, width), kind(2, rows, width, dtype=F32), kind(U - 1, 2, rows, width)]
    out_specs = [piece, pair, columns_spec(U - 1, 2, rows, HEAD_DIM)]
    memory_rows = 0
    if extra is not None:
        more, more_specs, memory_rows = memory_operands(grid, extra)
        operands, specs = operands + more, specs + more_specs
        out_shape.append(kind(2, memory_rows, width))
        out_specs.append(columns_spec(2, memory_rows, HEAD_DIM))
    return host(
        grid, body, heads, specs, operands, out_specs, out_shape, moves,
        cost=attention_cost(grid, heads, memory_rows, 5),
    )


def pick_memory(grid, picks, stacked, c):
    heads, topk = picks.shape
    per = heads // 2
    R, U = grid.R, grid.U

    def body(info_ref, picks_ref, *refs):
        chosen_from, out_ref = refs[:U], refs[U]
        here = Here(grid)
        picked = picks_ref[0]
        key, value = 0.0, 0.0
        for t in range(U):
            member = (here.k - t + U) % U
            for side in range(2):
                across = lax.broadcasted_iota(jnp.int32, (picked.shape[0], R), 1)
                chosen = (picked == across + piece_start(grid, member, side)).astype(BF)
                at = pl.ds(side * R, R)
                key = key + dot(chosen, chosen_from[t][2, at, :], (1, 0))
                value = value + dot(chosen, chosen_from[t][1, at, :], (1, 0))
        out_ref[0] = key.astype(BF)
        out_ref[1] = value.astype(BF)

    at = lambda h, info: info[0] * per + h
    piece = pl.BlockSpec((3, grid.T, HEAD_DIM), lambda h, info: (0, 0, at(h, info)))
    return pl.pallas_call(
        body,
        grid_spec=pltpu.PrefetchScalarGridSpec(
            num_scalar_prefetch=1,
            grid=(per,),
            in_specs=[pl.BlockSpec((1, topk, 1), lambda h, info: (at(h, info), 0, 0))] + [piece] * U,
            out_specs=pl.BlockSpec((2, topk, HEAD_DIM), lambda h, info: (0, 0, h)),
        ),
        out_shape=kind(2, topk, per * HEAD_DIM),
        compiler_params=pltpu.CompilerParams(vmem_limit_bytes=VMEM_LIMIT),
        cost_estimate=pl.CostEstimate(
            flops=4 * topk * SEG * HEAD_DIM * per, bytes_accessed=4 * SEG * HEAD_DIM * per, transcendentals=0
        ),
    )(c.reshape(1).astype(jnp.int32), picks[:, :, None], *stacked)


def finish_gradient(grid, grad_query, own, others, picks, memory, moves=()):
    rows, width = grad_query.shape
    heads = width // HEAD_DIM
    R, U = grid.R, grid.U

    def body(here, step, ins, outs, held):
        dq_ref, own_ref, others_ref = ins[:3]
        out_ref = outs[0]

        @pl.when(step < heads)
        def _():
            out_ref[...] = dq_ref[...]

        @pl.when(step >= heads)
        def _():
            total = own_ref[0] + sum(others_ref[t, 0].astype(F32) for t in range(U - 1))
            for side in range(2):
                at = slice(side * R, (side + 1) * R)
                value = total[at]
                if memory is not None:
                    picked = ins[3][0]
                    down = lax.broadcasted_iota(jnp.int32, (R, picked.shape[1]), 0)
                    chosen = (down + piece_start(grid, here.k, side) == picked).astype(BF)
                    value = value + dot(chosen, ins[4][0], (1, 0))
                out_ref[at, :] = value.astype(BF)

    which = lambda b: jnp.maximum(b // heads - 1, 0)
    head = lambda b: jnp.where(b < heads, 0, b % heads)
    operands = [grad_query, own, others]
    specs = [
        pl.BlockSpec((rows, HEAD_DIM), lambda b: (0, jnp.minimum(b, heads - 1))),
        pl.BlockSpec((1, rows, HEAD_DIM), lambda b: (which(b), 0, head(b))),
        pl.BlockSpec((U - 1, 1, rows, HEAD_DIM), lambda b: (0, which(b), 0, head(b))),
    ]
    if memory is not None:
        topk = picks.shape[1]
        operands += [picks[:, None, :], memory]
        specs += [
            pl.BlockSpec((1, 1, topk), lambda b: (b % heads, 0, 0)),
            pl.BlockSpec((1, topk, HEAD_DIM), lambda b: (which(b), 0, head(b))),
        ]
    outs, got = host(
        grid, body, 3 * heads, specs, operands, [columns_spec(rows, HEAD_DIM)], [kind(rows, 3 * width)], moves,
        cost=pl.CostEstimate(flops=2 * rows * width, bytes_accessed=16 * rows * width, transcendentals=0),
    )
    return outs[0], got


FEED_TILE = 256


def feed(grid, middle, gain, w_up, w_down, moves=()):
    rows, width = middle.shape
    hidden = w_down.shape[0]
    steps = hidden // FEED_TILE

    def body(here, step, ins, outs, held):
        middle_ref, gain_ref, gate_w, up_w, down_w = ins
        out_ref, normed_ref, both_ref, inner_ref = outs

        @pl.when(step == 0)
        def _():
            value = middle_ref[...]
            normed_ref[...] = norm(value, gain_ref[...]).astype(BF)
            held[0][...] = value

        normed = normed_ref[...]
        gate, up = dot(normed, gate_w[...], (1, 0)), dot(normed, up_w[...], (1, 0))
        both_ref[0] = gate.astype(BF)
        both_ref[1] = up.astype(BF)
        inner = (gate / (1.0 + jnp.exp(-gate)) * up).astype(BF)
        inner_ref[...] = inner
        held[0][...] += dot(inner, down_w[...], (1, 0))

        @pl.when(step == steps - 1)
        def _():
            out_ref[...] = held[0][...]

    tile = columns_spec(width, FEED_TILE)
    return host(
        grid, body, steps,
        [whole_spec(rows, width), whole_spec(1, width), tile, columns_spec(width, FEED_TILE, first=steps), rows_spec(FEED_TILE, width)],
        [middle, gain, w_up, w_up, w_down],
        [whole_spec(rows, width), whole_spec(rows, width), columns_spec(2, rows, FEED_TILE), columns_spec(rows, FEED_TILE)],
        [kind(rows, width, dtype=F32), kind(rows, width), kind(2, rows, hidden), kind(rows, hidden)],
        moves,
        scratch=[pltpu.VMEM((rows, width), F32)],
        cost=pl.CostEstimate(flops=6 * rows * width * hidden, bytes_accessed=6 * width * hidden, transcendentals=rows * hidden),
    )


def feed_back(grid, grad, middle, gain, both, w_up, w_down, moves=()):
    rows, width = grad.shape
    hidden = w_down.shape[0]
    steps = hidden // FEED_TILE

    def body(here, step, ins, outs, held):
        grad_ref, middle_ref, gain_ref, both_ref, gate_w, up_w, down_w = ins
        out_ref, low_ref, grads_ref, gain_out = outs
        total = held[0]

        @pl.when(step == 0)
        def _():
            held[1][...] = grad_ref[...].astype(BF)
            total[...] = jnp.zeros_like(total)

        grad_inner = dot(held[1][...], down_w[...], (1, 1))
        gate, up = both_ref[0].astype(F32), both_ref[1].astype(F32)
        sigmoid = 1.0 / (1.0 + jnp.exp(-gate))
        scaled = grad_inner * sigmoid
        grad_gate = (scaled * up * (1.0 + gate * (1.0 - sigmoid))).astype(BF)
        grad_up = (scaled * gate).astype(BF)
        grads_ref[0] = grad_gate
        grads_ref[1] = grad_up
        total[...] += dot(grad_gate, gate_w[...], (1, 1)) + dot(grad_up, up_w[...], (1, 1))

        @pl.when(step == steps - 1)
        def _():
            pulled, grad_gain = norm_back(middle_ref[...], gain_ref[...], total[...])
            result = grad_ref[...] + pulled
            out_ref[...] = result
            low_ref[...] = result.astype(BF)
            gain_out[...] = grad_gain

    tile = columns_spec(width, FEED_TILE)
    whole = whole_spec(rows, width)
    return host(
        grid, body, steps,
        [whole, whole, whole_spec(1, width), columns_spec(2, rows, FEED_TILE), tile,
         columns_spec(width, FEED_TILE, first=steps), rows_spec(FEED_TILE, width)],
        [grad, middle, gain, both, w_up, w_up, w_down],
        [whole, whole, columns_spec(2, rows, FEED_TILE), whole_spec(1, width)],
        [kind(rows, width, dtype=F32), kind(rows, width), kind(2, rows, hidden), kind(1, width, dtype=F32)],
        moves,
        scratch=[pltpu.VMEM((rows, width), F32), pltpu.VMEM((rows, width), BF)],
        cost=pl.CostEstimate(flops=6 * rows * width * hidden, bytes_accessed=6 * width * hidden, transcendentals=rows * hidden),
    )


def norm(value, gain):
    return value * lax.rsqrt(jnp.mean(value * value, axis=-1, keepdims=True) + EPSILON) * gain


def norm_back(value, gain, grad):
    inverse = lax.rsqrt(jnp.mean(value * value, axis=-1, keepdims=True) + EPSILON)
    unit = value * inverse
    grad_gain = jnp.sum(grad * unit, axis=0, keepdims=True)
    scaled = grad * gain
    pulled = inverse * (scaled - unit * jnp.mean(scaled * unit, axis=-1, keepdims=True))
    return pulled, grad_gain


class Reduce:
    def __init__(self, grid, total):
        self.grid = grid
        self.parts = total.reshape(grid.J, total.shape[0] // grid.J, total.shape[1])
        self.phase = 0

    def flip(self):
        return flip_move(self.grid, self.parts, self.phase)

    def flipped(self, got):
        grid = self.grid
        if self.phase == 0:
            kept = jnp.stack(
                [
                    lax.dynamic_index_in_dim(self.parts, grid.place(2 * i, grid.c), 0, keepdims=False)
                    for i in range(grid.J // 2)
                ]
            )
        else:
            kept = self.parts[0::2]
        self.parts = (kept.astype(F32) + got.astype(F32)).astype(BF)
        self.phase += 1
        if self.phase == grid.bits:
            self.line = self.parts.reshape(2, grid.F, -1, self.parts.shape[2])

    def ring(self):
        while self.phase < self.grid.bits:
            self.flipped(send(self.grid, [self.flip()])[0])
        return ring_move(self.grid, self.line)

    def arrived(self, got):
        grid = self.grid
        here = lax.dynamic_index_in_dim(self.line, grid.f, 1, keepdims=False)
        self.summed = here.astype(F32) + sum(got[t].astype(F32) for t in range(grid.F - 1))
        give = lax.dynamic_index_in_dim(self.summed, 1 - grid.c, 0, keepdims=False)
        self.give = give.astype(BF)

    def done(self, got):
        grid = self.grid
        mine = lax.dynamic_index_in_dim(self.summed, grid.c, 0, keepdims=False)
        got = got.astype(F32)
        return jnp.concatenate(
            [jnp.where(grid.c == 0, mine, got), jnp.where(grid.c == 0, got, mine)], axis=1
        )


def local(
    n_dp,
    pieces,
    tokens,
    cotangent,
    doc_lengths,
    partner,
    memory_picks,
    attention_in,
    attention_out,
    feed_in,
    feed_out,
    norm_gains,
):
    IDS[0] = 1
    grid = Grid(n_dp, pieces)
    grid.trace()
    layers = attention_in.shape[0]
    width = tokens.shape[2]
    heads = width // HEAD_DIM
    topk = memory_picks.shape[3]
    valid_all, visible_all = jax.vmap(memory_plan)(doc_lengths, partner)
    valid = valid_all[grid.m, grid.slot].reshape(1)
    visible = visible_all[grid.m, grid.slot]
    relative = (grid.slot - jnp.arange(n_dp)) % n_dp
    bias = jnp.repeat(jnp.where(visible[relative], 0.0, MASKED), topk)[:, None].astype(F32)
    tables = rope_tables()
    picks_there = grid.swap(memory_picks)
    picks = jnp.where(grid.r == grid.c, memory_picks[grid.m, 0], picks_there[grid.m, 0])
    zero = grid.c == 0

    def both_halves(mine, other):
        return jnp.where(
            zero, jnp.concatenate([mine, other], axis=-1), jnp.concatenate([other, mine], axis=-1)
        )

    def half(value, c):
        size = value.shape[-1] // 2
        return lax.dynamic_slice_in_dim(value, c * size, size, axis=value.ndim - 1)

    def chip(value):
        return jnp.concatenate([value, grid.swap(value)])

    hidden, cotangent_rows, gains, weights = gather_all(
        grid, tokens, cotangent, norm_gains, [attention_in, attention_out, feed_in, feed_out]
    )
    hidden = hidden.astype(F32)
    gain = lambda l, i: gains[l, i][None]
    saved = []
    for l in range(layers):
        w_qkv, w_out, w_up, w_down = weights[l]
        memory = l == layers - 1
        normed = norm(hidden, gain(l, 0)).astype(BF)
        split, _ = split_heads(grid, memory, tables, mm(normed, w_qkv))
        (others,) = send(grid, [member_move(grid, split[1], False)])
        pairs = [split[1]] + [others[t] for t in range(grid.U - 1)]
        extra = None
        if memory:
            chosen = pick_memory(grid, picks, pairs, grid.c)
            (came,) = send(grid, [slots_move(grid, chosen, False)])
            slots = jnp.concatenate([chosen[None], came])
            slots = jnp.swapaxes(slots, 0, 1).reshape(2, n_dp * topk, -1)
            slots = both_halves(slots, grid.swap(slots))
            extra = {"query": split[2], "keys": slots[0], "values": slots[1], "bias": bias}
        attended, _ = attend(grid, valid, split[0], pairs, extra)
        middle = hidden + mm(attended, w_out)
        (out, normed_feed, both, inner), _ = feed(grid, middle, gain(l, 1), w_up, w_down)
        saved.append((hidden, normed, split[0], pairs, extra, attended, middle, normed_feed, both, inner))
        hidden = out
    layer_output = grid.from_units(hidden.astype(BF))

    grad = cotangent_rows.astype(F32)
    found = [[None] * 4 for _ in range(layers)]
    grad_gains = [[None, None] for _ in range(layers)]
    before = None
    for l in reversed(range(layers)):
        w_qkv, w_out, w_up, w_down = weights[l]
        hidden, normed, query, pairs, extra, attended, middle, normed_feed, both, inner = saved[l]
        low = grad.astype(BF)
        right = jnp.concatenate([half(low, grid.c), grid.swap(half(low, 1 - grid.c))])
        down = Reduce(grid, mm(chip(inner), right, (0, 0)).astype(BF))

        moves = [down.flip()] + ([up_before.ring(), last_before.flip()] if before else [])
        (grad, grad_low, grads, gain_feed), got = feed_back(
            grid, grad, middle, gain(l, 1), both, w_up, w_down, moves
        )
        down.flipped(got[0])
        if before:
            up_before.arrived(got[1])
            last_before.flipped(got[2])
        grads_mine = lax.dynamic_index_in_dim(grads, grid.c, 0, keepdims=False)
        grads_give = lax.dynamic_index_in_dim(grads, 1 - grid.c, 0, keepdims=False)
        right = jnp.concatenate([grads_mine, grid.swap(grads_give)])
        up = Reduce(grid, mm(chip(normed_feed), right, (0, 0)).astype(BF))
        grad_heads = mm(grad_low, w_out, (1, 1)).astype(BF)

        moves = [up.flip(), down.flip()] + ([last_before.ring()] if before else [])
        outs, got = attend_back(grid, valid, tables, query, grad_heads, pairs, extra, moves)
        up.flipped(got[0])
        down.flipped(got[1])
        if before:
            last_before.arrived(got[2])
        grad_query, own, others = outs[:3]
        memory_grad = None
        moves = [member_move(grid, others, True)]
        if extra is not None:
            moves.append(swap_move(half(outs[3], 1 - grid.c)))
        got = send(grid, moves)
        others = got[0]
        if extra is not None:
            joined = half(outs[3], grid.c).astype(F32) + got[1].astype(F32)
            joined = joined.astype(BF).reshape(2, n_dp, topk, -1)
            (came,) = send(grid, [slots_move(grid, joined, True)])
            total = joined[:, 0].astype(F32) + sum(came[t].astype(F32) for t in range(n_dp - 1))
            for t in range(1, grid.Q):
                total = total + grid.within(total.astype(BF), t).astype(F32)
            total = total.astype(BF)
            memory_grad = both_halves(total, grid.swap(total))
        grad_projected, got = finish_gradient(
            grid, grad_query, own, others, picks, memory_grad, [up.flip(), down.ring()]
        )
        up.flipped(got[0])
        down.arrived(got[1])
        grads_mine, grads_give = half(grad_projected, grid.c), half(grad_projected, 1 - grid.c)
        right = jnp.concatenate([grads_mine, grid.swap(grads_give)])
        w_qkv_sum = mm(chip(normed), right, (0, 0)).astype(BF)
        right = jnp.concatenate([half(grad_low, grid.c), grid.swap(half(grad_low, 1 - grid.c))])
        w_out_sum = mm(chip(attended), right, (0, 0)).astype(BF)
        last = Reduce(grid, jnp.concatenate([w_out_sum, w_qkv_sum], axis=1))
        pulled, gain_attention = norm_back(hidden, gain(l, 0), mm(grad_projected, w_qkv, (1, 1)))
        grad = grad + pulled
        grad_gains[l] = [gain_attention[0], gain_feed[0]]
        found[l][3] = down.done(grid.swap(down.give))
        if before:
            found[l + 1][2] = up_before.done(grid.swap(up_before.give))
            both_last = last_before.done(grid.swap(last_before.give))
            found[l + 1][0], found[l + 1][1] = last_parts(both_last, width)
        if l > 0:
            (came,) = send(grid, [last.flip()])
            last.flipped(came)
        before, up_before, last_before = True, up, last
    came = send(grid, [last.flip(), up.ring()])
    last.flipped(came[0])
    up.arrived(came[1])
    last.arrived(send(grid, [last.ring()])[0])
    found[0][2] = up.done(grid.swap(up.give))
    found[0][0], found[0][1] = last_parts(last.done(grid.swap(last.give)), width)
    input_grad = grid.from_units(grad.astype(BF)).astype(F32)
    return (
        layer_output,
        input_grad,
        *(jnp.stack([found[l][i] for l in range(layers)]) for i in range(4)),
        scatter_gains(grid, jnp.stack([jnp.stack(pair) for pair in grad_gains])),
    )


def last_parts(value, width):
    size = value.shape[1] // 2
    halves = [value[:, :size], value[:, size:]]
    return (
        jnp.concatenate([h[:, width // 2 :] for h in halves], axis=1),
        jnp.concatenate([h[:, : width // 2] for h in halves], axis=1),
    )


def solution(mesh):
    rows = P(None, ("dp", "fsdp"), None)
    in_specs = (rows, rows, P(), P(), P(None, "dp", None, None), rows, rows, rows, rows, P(None, None, ("dp", "fsdp")))
    out_specs = (rows, rows, rows, rows, rows, rows, P(None, None, ("dp", "fsdp")))
    body = functools.partial(local, mesh.shape["dp"], mesh.shape["fsdp"])
    return jax.shard_map(body, mesh=mesh, in_specs=in_specs, out_specs=out_specs, check_vma=False)
```

```python
import functools
import math

import jax
import jax.numpy as jnp
from jax import lax
from jax.experimental import pallas as pl
from jax.experimental.pallas import tpu as pltpu
from jax.sharding import PartitionSpec as P

HEAD_DIM = 128
SEG = 1024
MICRO = 2
EPSILON = 1e-06
MASKED = -1e30
SCALE = HEAD_DIM ** (-0.5)
LOG2E = 1.0 / math.log(2.0)
BF = jnp.bfloat16
F32 = jnp.float32
VMEM_LIMIT = 48 * 1024 * 1024


def slot_layout(lengths):
    slot_total = lengths.shape[0]
    slot_counts = ((lengths + SEG - 1) // SEG).astype(jnp.int32)
    slot_starts = (jnp.cumsum(slot_counts) - slot_counts).astype(jnp.int32)
    slot_index = jnp.arange(slot_total, dtype=jnp.int32)
    started = (slot_starts[None, :] <= slot_index[:, None]) & (slot_counts[None, :] > 0)
    owner_doc = (jnp.sum(started.astype(jnp.int32), axis=1) - 1).astype(jnp.int32)
    owner_pick = slot_index[None, :] == owner_doc[:, None]
    first_slot = jnp.sum(jnp.where(owner_pick, slot_starts[None, :], 0), axis=1).astype(jnp.int32)
    doc_total = jnp.sum(jnp.where(owner_pick, lengths[None, :], 0), axis=1).astype(jnp.int32)
    valid_rows = jnp.clip(doc_total - (slot_index - first_slot) * SEG, 0, SEG).astype(jnp.int32)
    return (valid_rows, owner_doc)


def memory_plan(lengths, partner_row):
    valid_rows, owner_doc = slot_layout(lengths)
    block_ids = jnp.arange(lengths.shape[0], dtype=jnp.int32)
    earlier = (block_ids[None, :] < block_ids[:, None]) & (owner_doc[None, :] == owner_doc[:, None])
    visible = earlier | (block_ids[None, :] == partner_row[:, None])
    return (valid_rows, visible)


class Grid:
    def __init__(self, n_dp, pieces):
        self.n_dp, self.F = n_dp, pieces
        self.J = n_dp // 2
        self.bits = self.J.bit_length() - 1
        self.Q = pieces // 4
        self.U = 2 * self.Q
        self.R = SEG // pieces
        self.T = 2 * self.R

    def trace(self):
        dp = lax.axis_index("dp")
        self.c, self.j, self.f = dp % 2, dp // 2, lax.axis_index("fsdp")
        self.q, self.g = self.f // self.Q, self.f % self.Q
        self.m, self.r = self.q // 2, self.q % 2
        self.k = self.c * self.Q + self.g
        self.slot = 2 * self.j + self.r

    def permute(self, value, target):
        pairs = []
        for j in range(self.J):
            for c in range(2):
                for f in range(self.F):
                    j2, c2, f2 = target(j, c, f)
                    pairs.append(((j * 2 + c) * self.F + f, (j2 * 2 + c2) * self.F + f2))
        return lax.ppermute(value, ("dp", "fsdp"), pairs)

    def swap(self, value):
        return self.permute(value, lambda j, c, f: (j, 1 - c, f))

    def ring(self, value, t):
        return self.permute(value, lambda j, c, f: (j, c, (f + t) % self.F))

    def bit(self, phase, c):
        return phase if c == 0 else self.bits - 1 - phase

    def flip(self, value, phase):
        return self.permute(value, lambda j, c, f: (j ^ (1 << self.bit(phase, c)), c, f))

    def mask(self, key, c):
        return sum(1 << self.bit(p, c) for p in range(self.bits) if key >> p & 1)

    def place(self, key, c):
        return jnp.where(c == 0, self.j ^ self.mask(key, 0), self.j ^ self.mask(key, 1))

    def member(self, value, t):
        def target(j, c, f):
            q, g = f // self.Q, f % self.Q
            k = (c * self.Q + g + t) % self.U
            return (j, k // self.Q, q * self.Q + k % self.Q)

        return self.permute(value, target)

    def within(self, value, t):
        return self.permute(
            value, lambda j, c, f: (j, c, f // self.Q * self.Q + (f % self.Q + t) % self.Q)
        )

    def slots(self, value, t):
        def target(j, c, f):
            q, g = f // self.Q, f % self.Q
            slot = (2 * j + q % 2 + t) % self.n_dp
            return (slot // 2, c, (2 * (q // 2) + slot % 2) * self.Q + g)

        return self.permute(value, target)

    def _spread(self, second):
        def target(j, c, f):
            m = f // (self.F // 2)
            m = 1 - m if second else m
            k = min(f, self.F - 1 - f)
            return (j, k // self.Q, (2 * m + c) * self.Q + k % self.Q)

        return target

    def _collect(self, second):
        there = self._spread(second)
        back = {
            there(0, c, f): (c, f) for c in range(2) for f in range(self.F)
        }
        return lambda j, c, f: (j,) + back[(0, c, f)]

    def to_units(self, value):
        here = self.f // (self.F // 2)
        first = self.permute(jnp.where(here == 0, value[0], value[1]), self._spread(False))
        second = self.permute(jnp.where(here == 0, value[1], value[0]), self._spread(True))
        return jnp.concatenate(
            [jnp.where(self.m == 0, first, second), jnp.where(self.m == 0, second, first)]
        )

    def from_units(self, value):
        low, high = value[: self.R], value[self.R :]
        first = self.permute(jnp.where(self.m == 0, low, high), self._collect(False))
        second = self.permute(jnp.where(self.m == 0, high, low), self._collect(True))
        here = self.f // (self.F // 2)
        return jnp.stack([jnp.where(here == 0, first, second), jnp.where(here == 0, second, first)])


def any_spec():
    return pl.BlockSpec(memory_space=pl.ANY)


MESH = pl.DeviceIdType.MESH


class Here:
    def __init__(self, grid):
        self.grid = grid
        dp = lax.axis_index("dp")
        self.j, self.c, self.f = dp // 2, dp % 2, lax.axis_index("fsdp")
        self.q, self.g = self.f // grid.Q, self.f % grid.Q
        self.m, self.r = self.q // 2, self.q % 2
        self.k = self.c * grid.Q + self.g
        self.swap = self.device(self.j, 1 - self.c, self.f)

    def device(self, j, c, f):
        return {"dp": 2 * j + c, "fsdp": f}

    def ring(self, t):
        return self.device(self.j, self.c, (self.f + t) % self.grid.F)

    def step(self, phase):
        first, second = (1 << self.grid.bit(phase, c) for c in (0, 1))
        return first + self.c * (second - first)

    def moved(self, j, phase):
        step = self.step(phase)
        return j + step * (1 - 2 * ((j // step) % 2))

    def flip(self, phase):
        return self.device(self.moved(self.j, phase), self.c, self.f)

    def slots(self, t):
        grid = self.grid
        slot = (2 * self.j + self.r + t) % grid.n_dp
        return self.device(slot // 2, self.c, (2 * self.m + slot % 2) * grid.Q + self.g)

    def member(self, t):
        grid = self.grid
        k = (self.k + t) % grid.U
        return self.device(self.j, k // grid.Q, self.q * grid.Q + k % grid.Q)

    def place(self, key):
        j = self.j
        for phase in range(self.grid.bits):
            if key >> phase & 1:
                j = self.moved(j, phase)
        return j

    def greet(self):
        grid = self.grid
        barrier = pltpu.get_barrier_semaphore()
        peers = [self.ring(t) for t in range(1, grid.F)]
        peers += [self.device(self.j, 1 - self.c, (self.f + t) % grid.F) for t in range(grid.F)]
        for bit in range(grid.bits):
            step = 1 << bit
            peers.append(self.device(self.j + step * (1 - 2 * ((self.j // step) % 2)), self.c, self.f))
        for peer in peers:
            pl.semaphore_signal(barrier, inc=1, device_id=peer, device_id_type=MESH)
        pl.semaphore_wait(barrier, len(peers))


def remote(source, target, sems, index, device):
    return pltpu.make_async_remote_copy(
        src_ref=source,
        dst_ref=target,
        send_sem=sems.at[0, index],
        recv_sem=sems.at[1, index],
        device_id=device,
        device_id_type=MESH,
    )


class Spread:
    def __init__(self, here, shard, whole, sems, own_sem, split):
        grid = here.grid
        self.here, self.split = here, split
        rows, width = shard.shape
        half = width // 2 if split else width

        def part(ref, c):
            if not split:
                return ref
            return ref.at[(slice(None),) * (len(ref.shape) - 1) + (pl.ds(pl.multiple_of(c * half, 128), half),)]

        j, c, f = here.j, here.c, here.f
        mine = part(whole, c)
        self.own = pltpu.make_async_copy(part(shard, c), part(whole.at[j, c, f], c), own_sem)
        other = 1 - c if split else c
        self.pre = remote(part(shard, other), part(whole.at[j, c, f], other), sems, 0, here.swap)
        at = 1
        self.hops = []
        for h in range(1, grid.F):
            hop = []
            for way in (1, -1):
                origin = f - way * (h - 1)
                inside = lambda place: (place >= 0) & (place < grid.F)
                block = mine.at[j, :, jnp.clip(origin, 0, grid.F - 1)]
                copy = remote(block, block, sems, at, here.device(j, c, (f + way + grid.F) % grid.F))
                hop.append((copy, inside(origin) & inside(f + way), inside(f - way * h)))
                at += 1
            self.hops.append(hop)
        self.flips = []
        for phase in range(grid.bits):
            sent = []
            for key in range(1 << phase):
                block = mine.at[here.place(key)]
                sent.append(remote(block, block, sems, at, here.flip(phase)))
                at += 1
            self.flips.append(sent)
        self.swaps = []
        for key in range(grid.J if split else 0):
            block = mine.at[here.place(key)]
            self.swaps.append(remote(block, block, sems, at, here.swap))
            at += 1

    @staticmethod
    def count(grid):
        return 1 + 2 * (grid.F - 1) + (grid.J - 1) + grid.J

    def begin(self):
        self.own.start()
        self.pre.start()

    def to_line(self):
        self.own.wait()
        self.pre.wait()
        self._hop(0)

    def _hop(self, h):
        for copy, sends, _ in self.hops[h]:
            pl.when(sends)(copy.start)

    def _send(self, keys):
        for key in keys:
            if self.swaps:
                self.swaps[key].start()
        for phase, sent in enumerate(self.flips):
            for key in keys:
                if key < 1 << phase:
                    sent[key].start()

    def steps(self, whole):
        def along(h):
            for copy, _, comes in self.hops[h]:
                pl.when(comes)(copy.wait_recv)
            if h + 1 < len(self.hops):
                self._hop(h + 1)
                return
            for hop in self.hops:
                for copy, sends, _ in hop:
                    pl.when(sends)(copy.wait_send)
            if whole:
                self._send([0])

        def later(phase):
            for copy in self.flips[phase]:
                copy.wait()
            self._send([key + (1 << phase) for key in range(1 << phase)])

        def last():
            for copy in self.swaps:
                copy.wait()

        line = [functools.partial(along, h) for h in range(len(self.hops))]
        if not whole:
            return line
        return line + [functools.partial(later, p) for p in range(len(self.flips))] + [last]


class Regroup:
    def __init__(self, here, source, target, sems, own_sem):
        grid = here.grid
        half = grid.F // 2
        k = jnp.minimum(here.f, grid.F - 1 - here.f)
        side = here.f // half
        self.sends = []
        for m in range(2):
            c2, f2 = k // grid.Q, (2 * m + here.c) * grid.Q + k % grid.Q
            same = (c2 == here.c) & (f2 == here.f)
            own = pltpu.make_async_copy(source.at[m], target.at[side], own_sem)
            away = pltpu.make_async_remote_copy(
                src_ref=source.at[m],
                dst_ref=target.at[side],
                send_sem=sems.at[0, m],
                recv_sem=sems.at[1, side],
                device_id=here.device(here.j, c2, f2),
                device_id_type=MESH,
            )
            self.sends.append((same, own, away))
        self.arrivals = []
        for side in range(2):
            from_f = here.k if side == 0 else grid.F - 1 - here.k
            same = (here.r == here.c) & (from_f == here.f)
            came = pltpu.make_async_remote_copy(
                src_ref=source.at[0],
                dst_ref=target.at[side],
                send_sem=sems.at[0, 0],
                recv_sem=sems.at[1, side],
                device_id=here.swap,
                device_id_type=MESH,
            )
            self.arrivals.append((same, came))

    def start(self):
        for same, own, away in self.sends:
            pl.when(same)(own.start)
            pl.when(jnp.logical_not(same))(away.start)

    def wait(self):
        for same, own, away in self.sends:
            pl.when(same)(own.wait)
            pl.when(jnp.logical_not(same))(away.wait_send)
        for same, came in self.arrivals:
            pl.when(jnp.logical_not(same))(came.wait_recv)


def gather_body(grid, layers, kinds, *refs):
    tokens, gains = refs[:2]
    shards = refs[2 : 2 + kinds]
    outs = refs[2 + kinds :]
    tokens_out, gains_out = outs[:2]
    wholes = outs[2 : 2 + layers * kinds]
    sems, own_sems, regroup_sems = outs[2 + layers * kinds :]
    here = Here(grid)
    here.greet()
    rows = Regroup(here, tokens, tokens_out, regroup_sems, own_sems.at[0])
    moves = [(Spread(here, gains, gains_out, sems.at[0], own_sems.at[1], False), True)]
    for l in range(layers):
        for i in range(kinds):
            n = l * kinds + i
            move = Spread(here, shards[i].at[l], wholes[n], sems.at[n + 1], own_sems.at[n + 2], True)
            moves.append((move, not later_here(l, i)))
    for move, _ in moves:
        move.begin()
    rows.start()
    steps = [move.steps(whole) for move, whole in moves]
    count = len(steps[0])
    moves[0][0].to_line()
    moves[1][0].to_line()
    for at in range(len(moves) + count - 1):
        if at + 2 < len(moves):
            moves[at + 2][0].to_line()
        for back in reversed(range(count)):
            if 0 <= at - back < len(moves) and back < len(steps[at - back]):
                steps[at - back][back]()
    rows.wait()


def later_here(l, i):
    return l > 0 and i >= 2


def gather_all(grid, tokens, gains, shards):
    layers, kinds = shards[0].shape[0], len(shards)
    packed = jnp.zeros((8, 128), F32).at[: layers * 2, : gains.shape[2]].set(
        gains.astype(F32).reshape(layers * 2, -1)
    )
    whole = lambda shard: jax.ShapeDtypeStruct((grid.J, 2, grid.F) + shard.shape[-2:], shard.dtype)
    out_shape = [jax.ShapeDtypeStruct(tokens.shape, BF), whole(packed)]
    out_shape += [whole(shard) for _ in range(layers) for shard in shards]
    moves = 1 + layers * kinds
    outs = pl.pallas_call(
        functools.partial(gather_body, grid, layers, kinds),
        in_specs=[any_spec()] * (2 + kinds),
        out_specs=[any_spec()] * len(out_shape),
        out_shape=out_shape,
        scratch_shapes=[
            pltpu.SemaphoreType.DMA((moves, 2, Spread.count(grid))),
            pltpu.SemaphoreType.DMA((moves + 1,)),
            pltpu.SemaphoreType.DMA((2, 2)),
        ],
        compiler_params=pltpu.CompilerParams(
            collective_id=0, has_side_effects=True, vmem_limit_bytes=VMEM_LIMIT
        ),
    )(tokens, packed, *shards)
    gains_all = outs[1][..., : layers * 2, : gains.shape[2]]
    gains_all = jnp.moveaxis(gains_all, 3, 0).reshape(layers, 2, -1)
    weights = [list(outs[2 + l * kinds : 2 + (l + 1) * kinds]) for l in range(layers)]
    return outs[0].reshape(-1, tokens.shape[2]), gains_all, weights


def unless(condition, act):
    if condition is None:
        act()
    else:
        pl.when(jnp.logical_not(condition))(act)


class Move:
    def __init__(self, array, shape, count, copies, plan=None, in_place=False):
        self.array, self.shape, self.count, self.copies = array, shape, count, copies
        self.plan, self.in_place = plan or self._plain, in_place

    def _plain(self, here, source, target, sends, recvs, base):
        found = []
        for i, (what, where, peer, giver) in enumerate(self.copies(here, source, target)):
            copy = pltpu.make_async_remote_copy(
                src_ref=what,
                dst_ref=where,
                send_sem=sends.at[base + i],
                recv_sem=recvs.at[base + i],
                device_id=peer,
                device_id_type=MESH,
            )
            found.append((copy, None, None, giver, copy, None))
        return found


def flip_move(grid, parts, phase):
    count = parts.shape[0] // 2

    def copies(here, source, target):
        found = []
        for i in range(count):
            at = here.place(2 * i + 1) if phase == 0 else 2 * i + 1
            peer = here.flip(phase)
            found.append((source.at[at], target.at[i], peer, peer))
        return found

    return Move(parts, (count,) + parts.shape[1:], count, copies)


def ring_move(grid, line):
    def copies(here, source, target):
        return [
            (source.at[:, (here.f + t) % grid.F], target.at[t - 1], here.ring(t), here.ring(grid.F - t))
            for t in range(1, grid.F)
        ]

    return Move(line, (grid.F - 1, 2) + line.shape[2:], grid.F - 1, copies)


def swap_move(array, give=None):
    def copies(here, source, target):
        return [(source if give is None else source.at[give(here)], target, here.swap, here.swap)]

    return Move(array, array.shape if give is None else array.shape[1:], 1, copies)


def slots_move(grid, array, back):
    def copies(here, source, target):
        found = []
        for t in range(1, grid.n_dp):
            ahead, behind = here.slots(t), here.slots(grid.n_dp - t)
            if back:
                found.append((source.at[:, t], target.at[t - 1], behind, ahead))
            else:
                found.append((source, target.at[t - 1], ahead, behind))
        return found

    shape = array.shape if not back else array.shape[:1] + array.shape[2:]
    return Move(array, (grid.n_dp - 1,) + shape, grid.n_dp - 1, copies)


def member_move(grid, array, back):
    def copies(here, source, target):
        found = []
        for t in range(1, grid.U):
            ahead, behind = here.member(t), here.member(grid.U - t)
            if back:
                found.append((source.at[t - 1], target.at[t - 1], behind, ahead))
            else:
                found.append((source, target.at[t - 1], ahead, behind))
        return found

    shape = array.shape[1:] if back else array.shape
    return Move(array, (grid.U - 1,) + shape, grid.U - 1, copies)


def spread_move(grid, whole, stage):
    half = whole.shape[-1] // 2
    keys = [0] if stage == 0 else range(1 << (stage - 1), 1 << stage)

    def copies(here, source, target):
        mine = target.at[:, :, :, :, pl.ds(pl.multiple_of(here.c * half, 128), half)]
        found = []
        for key in keys:
            block = mine.at[here.place(key)]
            found.append((block, block, here.swap, here.swap))
            for phase in range(stage, grid.bits):
                found.append((block, block, here.flip(phase), here.flip(phase)))
        return found

    count = len(keys) * (1 + grid.bits - stage)
    return Move(whole, whole.shape, count, copies, in_place=True)


def peer_move(array, peer):
    return Move(array, array.shape, 1, lambda here, source, target: [(source, target, peer(here), peer(here))])


def line_move(grid, array):
    def copies(here, source, target):
        return [(source, target.at[t - 1], here.ring(t), here.ring(grid.F - t)) for t in range(1, grid.F)]

    return Move(array, (grid.F - 1,) + array.shape, grid.F - 1, copies)


def regroup_move(grid, array):
    def plan(here, source, target, sends, recvs, base):
        found = []
        k = jnp.minimum(here.f, grid.F - 1 - here.f)
        side = here.f // (grid.F // 2)
        for m in range(2):
            c2, f2 = k // grid.Q, (2 * m + here.c) * grid.Q + k % grid.Q
            same = (c2 == here.c) & (f2 == here.f)
            away = pltpu.make_async_remote_copy(
                src_ref=source.at[m],
                dst_ref=target.at[side],
                send_sem=sends.at[base + m],
                recv_sem=recvs.at[base + side],
                device_id=here.device(here.j, c2, f2),
                device_id_type=MESH,
            )
            own = pltpu.make_async_copy(source.at[m], target.at[side], sends.at[base + m])
            from_f = here.k if m == 0 else grid.F - 1 - here.k
            same_in = (here.r == here.c) & (from_f == here.f)
            came = pltpu.make_async_remote_copy(
                src_ref=source.at[0],
                dst_ref=target.at[m],
                send_sem=sends.at[base],
                recv_sem=recvs.at[base + m],
                device_id=here.swap,
                device_id_type=MESH,
            )
            found.append((away, same, own, here.device(here.j, here.r, from_f), came, same_in))
        return found

    return Move(array, array.shape, 2, None, plan)


def regroup_back_move(grid, array):
    def plan(here, source, target, sends, recvs, base):
        found = []
        for piece in range(2):
            f = here.k if piece == 0 else grid.F - 1 - here.k
            same = (here.r == here.c) & (f == here.f)
            away = pltpu.make_async_remote_copy(
                src_ref=source.at[piece],
                dst_ref=target.at[here.m],
                send_sem=sends.at[base + piece],
                recv_sem=recvs.at[base + here.m],
                device_id=here.device(here.j, here.r, f),
                device_id_type=MESH,
            )
            own = pltpu.make_async_copy(source.at[piece], target.at[here.m], sends.at[base + piece])
            k = jnp.minimum(here.f, grid.F - 1 - here.f)
            c2, f2 = k // grid.Q, (2 * piece + here.c) * grid.Q + k % grid.Q
            same_in = (c2 == here.c) & (f2 == here.f)
            came = pltpu.make_async_remote_copy(
                src_ref=source.at[0],
                dst_ref=target.at[piece],
                send_sem=sends.at[base],
                recv_sem=recvs.at[base + piece],
                device_id=here.swap,
                device_id_type=MESH,
            )
            found.append((away, same, own, here.device(here.j, c2, f2), came, same_in))
        return found

    return Move(array, array.shape, 2, None, plan)


IDS = [1]


def host(grid, body, steps, in_specs, operands, out_specs, out_shape, moves=(), scratch=(), cost=None, reaches=False):
    counts = [len(operands), len(moves), len(out_shape), len(moves), len(scratch)]

    def kernel(*refs):
        parts, at = [], 0
        for count in counts:
            parts.append(refs[at : at + count])
            at += count
        ins, sources, outs, targets, held = parts
        here = Here(grid)
        step = pl.program_id(0)
        planned = []
        if moves:
            sends, recvs = refs[at:]
            base = 0
            for move, source, target in zip(moves, sources, targets):
                planned += move.plan(here, source, target, sends, recvs, base)
                base += move.count

        if moves or reaches:

            @pl.when(step == 0)
            def _():
                barrier = pltpu.get_barrier_semaphore()
                if reaches:
                    pl.semaphore_signal(barrier, inc=1, device_id=here.swap, device_id_type=MESH)
                for _, _, _, giver, _, same_in in planned:
                    signal = functools.partial(
                        pl.semaphore_signal, barrier, inc=1, device_id=giver, device_id_type=MESH
                    )
                    unless(same_in, signal)
                due = int(reaches) + sum(same is None for _, same, _, _, _, _ in planned)
                for _, same, _, _, _, _ in planned:
                    if same is not None:
                        due = due + 1 - same.astype(jnp.int32)
                pl.semaphore_wait(barrier, due)
                for away, same, own, _, _, _ in planned:
                    unless(same, away.start)
                    if same is not None:
                        pl.when(same)(own.start)

        if body is not None:
            body(here, step, ins, outs, held)
        if moves:

            @pl.when(step == steps - 1)
            def _():
                for away, same, own, _, came, same_in in planned:
                    unless(same, away.wait_send)
                    if same is not None:
                        pl.when(same)(own.wait)
                    unless(same_in, came.wait_recv)

    total = sum(move.count for move in moves)
    extra = {}
    sems = []
    if moves or reaches:
        extra = {"collective_id": IDS[0], "has_side_effects": True}
        IDS[0] += 1
    if moves:
        sems = [pltpu.SemaphoreType.DMA((total,)), pltpu.SemaphoreType.DMA((total,))]
    outs = pl.pallas_call(
        kernel,
        grid=(steps,),
        in_specs=list(in_specs) + [any_spec()] * len(moves),
        out_specs=list(out_specs) + [any_spec()] * len(moves),
        out_shape=list(out_shape) + [jax.ShapeDtypeStruct(m.shape, m.array.dtype) for m in moves],
        scratch_shapes=list(scratch) + sems,
        input_output_aliases={
            len(operands) + i: len(out_shape) + i for i, move in enumerate(moves) if move.in_place
        },
        compiler_params=pltpu.CompilerParams(vmem_limit_bytes=VMEM_LIMIT, **extra),
        cost_estimate=cost,
    )(*operands, *[move.array for move in moves])
    return outs[: len(out_shape)], outs[len(out_shape) :]


def send(grid, moves):
    return host(grid, None, 1, [], [], [], [], moves)[1]


class GainSum:
    def __init__(self, grid, total):
        self.grid, self.total, self.stage = grid, total, 0

    def move(self):
        grid, phase = self.grid, self.stage - 1
        if self.stage == 0:
            return swap_move(self.total)
        if phase < grid.bits:
            return peer_move(self.total, lambda here: here.flip(phase))
        return line_move(grid, self.total)

    def took(self, got):
        if self.stage > self.grid.bits:
            got = sum(got[t] for t in range(self.grid.F - 1))
        self.total = self.total + got
        self.stage += 1

    def finish(self):
        while self.stage <= self.grid.bits + 1:
            self.took(send(self.grid, [self.move()])[0])
        return self.total


def rope_tables():
    half_dim = HEAD_DIM // 2
    frequency = jnp.exp(
        jnp.arange(half_dim, dtype=F32) * (-2.0 * math.log(10000.0) / HEAD_DIM)
    )
    angles = jnp.arange(SEG, dtype=jnp.int32).astype(F32)[:, None] * frequency[None, :]
    cos, sin = jnp.cos(angles), jnp.sin(angles)
    return (jnp.concatenate([cos, cos], axis=-1), jnp.concatenate([-sin, sin], axis=-1))


def turn(values, cos, sin):
    return values * cos + pltpu.roll(values, HEAD_DIM // 2, 1) * sin


def smem():
    return pl.BlockSpec(memory_space=pltpu.SMEM)


def whole_spec(*shape):
    return pl.BlockSpec(shape, lambda i: (0,) * len(shape))


def columns_spec(*shape, first=0):
    return pl.BlockSpec(shape, lambda i: (0,) * (len(shape) - 1) + (i + first,))


def rows_spec(*shape):
    return pl.BlockSpec(shape, lambda i: (i,) + (0,) * (len(shape) - 1))


def kind(*shape, dtype=BF):
    return jax.ShapeDtypeStruct(shape, dtype)


def piece_start(grid, member, part):
    return (member if part == 0 else grid.F - 1 - member) * grid.R


def table_rows(grid, table_ref, member, part):
    start = pl.multiple_of(piece_start(grid, member, part), grid.R)
    return table_ref[pl.ds(start, grid.R), :]


def dot(left, right, contract):
    return lax.dot_general(
        left, right, (((contract[0],), (contract[1],)), ((), ())), preferred_element_type=F32
    )


def mm(left, right, contract=(1, 0)):
    return dot(left, right, contract)


def split_heads(grid, memory, tables, projected, moves=()):
    rows, width = projected.shape
    heads = width // (3 * HEAD_DIM)
    count = 3 if memory else 2

    def body(here, step, ins, outs, held):
        cos_ref, sin_ref, q_ref, k_ref, v_ref = ins
        for part in range(2):
            at = pl.ds(part * grid.R, grid.R)
            cos = table_rows(grid, cos_ref, here.k, part)
            sin = table_rows(grid, sin_ref, here.k, part)
            query, key = q_ref[at, :], k_ref[at, :]
            outs[0][at, :] = turn(query, cos, sin).astype(BF)
            outs[1][0, at, :] = turn(key, cos, sin).astype(BF)
            outs[1][1, at, :] = v_ref[at, :].astype(BF)
            if memory:
                outs[1][2, at, :] = key.astype(BF)
                outs[2][at, :] = query.astype(BF)

    piece = lambda at: columns_spec(rows, HEAD_DIM, first=at * heads)
    flat = kind(rows, heads * HEAD_DIM)
    table = whole_spec(SEG, HEAD_DIM)
    return host(
        grid,
        body,
        heads,
        [table, table, piece(0), piece(1), piece(2)],
        [*tables, projected, projected, projected],
        [piece(0), columns_spec(count, rows, HEAD_DIM)] + [piece(0)] * memory,
        [flat, kind(count, rows, heads * HEAD_DIM)] + [flat] * memory,
        moves,
        cost=pl.CostEstimate(flops=10 * rows * width, bytes_accessed=8 * rows * width, transcendentals=0),
    )


def part_scores(grid, here, valid, part, query, keys):
    shape = (grid.R, grid.R)
    apart = lax.broadcasted_iota(jnp.int32, shape, 0) - lax.broadcasted_iota(jnp.int32, shape, 1)
    found = []
    for t in range(grid.U):
        member = (here.k - t + grid.U) % grid.U
        for side in range(part + 1):
            score = dot(keys[t][side * grid.R : (side + 1) * grid.R], query, (1, 1))
            if side == part:
                start = piece_start(grid, member, side)
                allowed = apart <= piece_start(grid, here.k, part) - start
                if side == 1:
                    down = lax.broadcasted_iota(jnp.int32, shape, 0)
                    allowed = allowed & (down < valid - start)
                score = jnp.where(allowed, score, MASKED)
            found.append((t, side, score))
    return found


def softmax_parts(scores):
    top = functools.reduce(jnp.maximum, [jnp.max(s, axis=0, keepdims=True) for s in scores])
    powers = [jnp.exp2((s - top) * (SCALE * LOG2E)) for s in scores]
    inverse = 1.0 / sum(jnp.sum(p, axis=0, keepdims=True) for p in powers)
    return [p * inverse for p in powers]


def attention_cost(grid, heads, memory_rows, products):
    pairs = grid.T * (SEG * 3 // 4 + memory_rows) * heads
    return pl.CostEstimate(
        flops=2 * products * HEAD_DIM * pairs,
        bytes_accessed=2 * HEAD_DIM * heads * 4 * (SEG + memory_rows),
        transcendentals=pairs,
    )


def memory_operands(grid, extra):
    rows = extra["keys"].shape[0]
    piece = columns_spec(grid.T, HEAD_DIM)
    column = columns_spec(rows, HEAD_DIM)
    return [extra["query"], extra["keys"], extra["values"], extra["bias"]], [
        piece, column, column, whole_spec(rows, 1)
    ], rows


def attend(grid, valid, query, pairs, extra, moves=()):
    rows, width = query.shape
    heads = width // HEAD_DIM
    R, U = grid.R, grid.U

    def body(here, step, ins, outs, held):
        valid_ref, q_ref, kv_refs, refs = ins[0], ins[1], ins[2 : 2 + U], ins[2 + U :]
        keys, values = [r[0] for r in kv_refs], [r[1] for r in kv_refs]
        for part in range(2):
            at = pl.ds(part * R, R)
            found = part_scores(grid, here, valid_ref[0], part, q_ref[at, :], keys)
            scores = [s for _, _, s in found]
            mixed = [values[t][side * R : (side + 1) * R] for t, side, _ in found]
            if extra is not None:
                scores.append(dot(refs[1][...], refs[0][at, :], (1, 1)) + refs[3][...])
                mixed.append(refs[2][...])
            total = sum(
                dot(value, p.astype(BF), (0, 0)) for value, p in zip(mixed, softmax_parts(scores))
            )
            outs[0][at, :] = total.T.astype(BF)

    piece = columns_spec(rows, HEAD_DIM)
    operands = [valid, query, *pairs]
    specs = [smem(), piece] + [columns_spec(2, rows, HEAD_DIM)] * U
    memory_rows = 0
    if extra is not None:
        more, more_specs, memory_rows = memory_operands(grid, extra)
        operands, specs = operands + more, specs + more_specs
    outs, got = host(
        grid, body, heads, specs, operands, [piece], [kind(rows, width)], moves,
        cost=attention_cost(grid, heads, memory_rows, 2),
    )
    return outs[0], got


def attend_back(grid, valid, tables, query, grad, pairs, extra, moves=()):
    rows, width = query.shape
    heads = width // HEAD_DIM
    R, U = grid.R, grid.U

    def body(here, step, ins, outs, held):
        valid_ref, cos_ref, sin_ref, q_ref, g_ref = ins[:5]
        kv_refs, refs = ins[5 : 5 + U], ins[5 + U :]
        keys, values = [r[0] for r in kv_refs], [r[1] for r in kv_refs]
        grad_keys, grad_values = {}, {}

        def add(store, at, value):
            store[at] = store[at] + value if at in store else value

        for part in range(2):
            at_rows = pl.ds(part * R, R)
            asked, grads_in = q_ref[at_rows, :], g_ref[at_rows, :]
            found = part_scores(grid, here, valid_ref[0], part, asked, keys)
            places = [(t, side) for t, side, _ in found]
            scores = [s for _, _, s in found]
            part_keys = [keys[t][side * R : (side + 1) * R] for t, side in places]
            part_values = [values[t][side * R : (side + 1) * R] for t, side in places]
            queries = [asked] * len(places)
            if extra is not None:
                places.append("memory")
                queries.append(refs[0][at_rows, :])
                scores.append(dot(refs[1][...], queries[-1], (1, 1)) + refs[3][...])
                part_keys.append(refs[1][...])
                part_values.append(refs[2][...])
            probs = softmax_parts(scores)
            grads = [dot(value, grads_in, (1, 1)) for value in part_values]
            inner = sum(jnp.sum(p * d, axis=0, keepdims=True) for p, d in zip(probs, grads))
            local_query, raw_query = None, None
            for at, p, d, key, by in zip(places, probs, grads, part_keys, queries):
                moved = (p * (d - inner)).astype(BF)
                add(grad_keys, at, dot(moved, by, (1, 0)))
                add(grad_values, at, dot(p.astype(BF), grads_in, (1, 0)))
                back = dot(key, moved, (0, 0))
                if at == "memory":
                    raw_query = back
                else:
                    local_query = back if local_query is None else local_query + back
            cos = table_rows(grid, cos_ref, here.k, part)
            sin = table_rows(grid, sin_ref, here.k, part)
            result = turn(local_query.T, cos, -sin)
            if extra is not None:
                result = result + raw_query.T
            outs[0][at_rows, :] = (result * SCALE).astype(BF)
        for t in range(U):
            member = (here.k - t + U) % U
            for side in range(2):
                at_rows = pl.ds(side * R, R)
                cos = table_rows(grid, cos_ref, member, side)
                sin = table_rows(grid, sin_ref, member, side)
                key = turn(grad_keys[(t, side)], cos, -sin) * SCALE
                if t == 0:
                    outs[1][0, at_rows, :] = key
                    outs[1][1, at_rows, :] = grad_values[(t, side)]
                else:
                    outs[2][t - 1, 0, at_rows, :] = key.astype(BF)
                    outs[2][t - 1, 1, at_rows, :] = grad_values[(t, side)].astype(BF)
        if extra is not None:
            outs[3][0] = (grad_keys["memory"] * SCALE).astype(BF)
            outs[3][1] = grad_values["memory"].astype(BF)

    piece = columns_spec(rows, HEAD_DIM)
    pair = columns_spec(2, rows, HEAD_DIM)
    table = whole_spec(SEG, HEAD_DIM)
    operands = [valid, *tables, query, grad, *pairs]
    specs = [smem(), table, table, piece, piece] + [pair] * U
    out_shape = [kind(rows, width), kind(2, rows, width, dtype=F32), kind(U - 1, 2, rows, width)]
    out_specs = [piece, pair, columns_spec(U - 1, 2, rows, HEAD_DIM)]
    memory_rows = 0
    if extra is not None:
        more, more_specs, memory_rows = memory_operands(grid, extra)
        operands, specs = operands + more, specs + more_specs
        out_shape.append(kind(2, memory_rows, width))
        out_specs.append(columns_spec(2, memory_rows, HEAD_DIM))
    return host(
        grid, body, heads, specs, operands, out_specs, out_shape, moves,
        cost=attention_cost(grid, heads, memory_rows, 5),
    )


def pick_memory(grid, picks, stacked, c):
    heads, topk = picks.shape
    per = heads // 2
    R, U = grid.R, grid.U

    def body(info_ref, picks_ref, *refs):
        chosen_from, out_ref = refs[:U], refs[U]
        here = Here(grid)
        picked = picks_ref[0]
        key, value = 0.0, 0.0
        for t in range(U):
            member = (here.k - t + U) % U
            for side in range(2):
                across = lax.broadcasted_iota(jnp.int32, (picked.shape[0], R), 1)
                chosen = (picked == across + piece_start(grid, member, side)).astype(BF)
                at = pl.ds(side * R, R)
                key = key + dot(chosen, chosen_from[t][2, at, :], (1, 0))
                value = value + dot(chosen, chosen_from[t][1, at, :], (1, 0))
        out_ref[0] = key.astype(BF)
        out_ref[1] = value.astype(BF)

    at = lambda h, info: info[0] * per + h
    piece = pl.BlockSpec((3, grid.T, HEAD_DIM), lambda h, info: (0, 0, at(h, info)))
    return pl.pallas_call(
        body,
        grid_spec=pltpu.PrefetchScalarGridSpec(
            num_scalar_prefetch=1,
            grid=(per,),
            in_specs=[pl.BlockSpec((1, topk, 1), lambda h, info: (at(h, info), 0, 0))] + [piece] * U,
            out_specs=pl.BlockSpec((2, topk, HEAD_DIM), lambda h, info: (0, 0, h)),
        ),
        out_shape=kind(2, topk, per * HEAD_DIM),
        compiler_params=pltpu.CompilerParams(vmem_limit_bytes=VMEM_LIMIT),
        cost_estimate=pl.CostEstimate(
            flops=4 * topk * SEG * HEAD_DIM * per, bytes_accessed=4 * SEG * HEAD_DIM * per, transcendentals=0
        ),
    )(c.reshape(1).astype(jnp.int32), picks[:, :, None], *stacked)


def finish_gradient(grid, grad_query, own, others, picks, memory, moves=()):
    rows, width = grad_query.shape
    heads = width // HEAD_DIM
    R, U = grid.R, grid.U

    def body(here, step, ins, outs, held):
        dq_ref, own_ref, others_ref = ins[:3]
        out_ref = outs[0]

        @pl.when(step < heads)
        def _():
            out_ref[...] = dq_ref[...]

        @pl.when(step >= heads)
        def _():
            total = own_ref[0] + sum(others_ref[t, 0].astype(F32) for t in range(U - 1))
            for side in range(2):
                at = slice(side * R, (side + 1) * R)
                value = total[at]
                if memory is not None:
                    picked = ins[3][0]
                    down = lax.broadcasted_iota(jnp.int32, (R, picked.shape[1]), 0)
                    chosen = (down + piece_start(grid, here.k, side) == picked).astype(BF)
                    value = value + dot(chosen, ins[4][0], (1, 0))
                out_ref[at, :] = value.astype(BF)

    which = lambda b: jnp.maximum(b // heads - 1, 0)
    head = lambda b: jnp.where(b < heads, 0, b % heads)
    operands = [grad_query, own, others]
    specs = [
        pl.BlockSpec((rows, HEAD_DIM), lambda b: (0, jnp.minimum(b, heads - 1))),
        pl.BlockSpec((1, rows, HEAD_DIM), lambda b: (which(b), 0, head(b))),
        pl.BlockSpec((U - 1, 1, rows, HEAD_DIM), lambda b: (0, which(b), 0, head(b))),
    ]
    if memory is not None:
        topk = picks.shape[1]
        operands += [picks[:, None, :], memory]
        specs += [
            pl.BlockSpec((1, 1, topk), lambda b: (b % heads, 0, 0)),
            pl.BlockSpec((1, topk, HEAD_DIM), lambda b: (which(b), 0, head(b))),
        ]
    outs, got = host(
        grid, body, 3 * heads, specs, operands, [columns_spec(rows, HEAD_DIM)], [kind(rows, 3 * width)], moves,
        cost=pl.CostEstimate(flops=2 * rows * width, bytes_accessed=16 * rows * width, transcendentals=0),
    )
    return outs[0], got


FEED_TILE = 256


def feed(grid, middle, gain, w_up, w_down, moves=()):
    rows, width = middle.shape
    hidden = w_down.shape[0]
    steps = hidden // FEED_TILE

    def body(here, step, ins, outs, held):
        middle_ref, gain_ref, gate_w, up_w, down_w = ins
        out_ref, normed_ref, both_ref, inner_ref = outs

        @pl.when(step == 0)
        def _():
            value = middle_ref[...]
            normed_ref[...] = norm(value, gain_ref[...]).astype(BF)
            held[0][...] = value

        normed = normed_ref[...]
        gate, up = dot(normed, gate_w[...], (1, 0)), dot(normed, up_w[...], (1, 0))
        both_ref[0] = gate.astype(BF)
        both_ref[1] = up.astype(BF)
        inner = (gate / (1.0 + jnp.exp(-gate)) * up).astype(BF)
        inner_ref[...] = inner
        held[0][...] += dot(inner, down_w[...], (1, 0))

        @pl.when(step == steps - 1)
        def _():
            out_ref[...] = held[0][...]

    tile = columns_spec(width, FEED_TILE)
    return host(
        grid, body, steps,
        [whole_spec(rows, width), whole_spec(1, width), tile, columns_spec(width, FEED_TILE, first=steps), rows_spec(FEED_TILE, width)],
        [middle, gain, w_up, w_up, w_down],
        [whole_spec(rows, width), whole_spec(rows, width), columns_spec(2, rows, FEED_TILE), columns_spec(rows, FEED_TILE)],
        [kind(rows, width, dtype=F32), kind(rows, width), kind(2, rows, hidden), kind(rows, hidden)],
        moves,
        scratch=[pltpu.VMEM((rows, width), F32)],
        cost=pl.CostEstimate(flops=6 * rows * width * hidden, bytes_accessed=6 * width * hidden, transcendentals=rows * hidden),
    )


def feed_back(grid, grad, middle, gain, both, w_up, w_down, moves=()):
    rows, width = grad.shape
    hidden = w_down.shape[0]
    steps = hidden // FEED_TILE

    def body(here, step, ins, outs, held):
        grad_ref, middle_ref, gain_ref, both_ref, gate_w, up_w, down_w = ins
        out_ref, low_ref, grads_ref, gain_out = outs
        total = held[0]

        @pl.when(step == 0)
        def _():
            held[1][...] = grad_ref[...].astype(BF)
            total[...] = jnp.zeros_like(total)

        grad_inner = dot(held[1][...], down_w[...], (1, 1))
        gate, up = both_ref[0].astype(F32), both_ref[1].astype(F32)
        sigmoid = 1.0 / (1.0 + jnp.exp(-gate))
        scaled = grad_inner * sigmoid
        grad_gate = (scaled * up * (1.0 + gate * (1.0 - sigmoid))).astype(BF)
        grad_up = (scaled * gate).astype(BF)
        grads_ref[0] = grad_gate
        grads_ref[1] = grad_up
        total[...] += dot(grad_gate, gate_w[...], (1, 1)) + dot(grad_up, up_w[...], (1, 1))

        @pl.when(step == steps - 1)
        def _():
            pulled, grad_gain = norm_back(middle_ref[...], gain_ref[...], total[...])
            result = grad_ref[...] + pulled
            out_ref[...] = result
            low_ref[...] = result.astype(BF)
            gain_out[...] = grad_gain

    tile = columns_spec(width, FEED_TILE)
    whole = whole_spec(rows, width)
    return host(
        grid, body, steps,
        [whole, whole, whole_spec(1, width), columns_spec(2, rows, FEED_TILE), tile,
         columns_spec(width, FEED_TILE, first=steps), rows_spec(FEED_TILE, width)],
        [grad, middle, gain, both, w_up, w_up, w_down],
        [whole, whole, columns_spec(2, rows, FEED_TILE), whole_spec(1, width)],
        [kind(rows, width, dtype=F32), kind(rows, width), kind(2, rows, hidden), kind(1, width, dtype=F32)],
        moves,
        scratch=[pltpu.VMEM((rows, width), F32), pltpu.VMEM((rows, width), BF)],
        cost=pl.CostEstimate(flops=6 * rows * width * hidden, bytes_accessed=6 * width * hidden, transcendentals=rows * hidden),
    )


def norm(value, gain):
    return value * lax.rsqrt(jnp.mean(value * value, axis=-1, keepdims=True) + EPSILON) * gain


def norm_back(value, gain, grad):
    inverse = lax.rsqrt(jnp.mean(value * value, axis=-1, keepdims=True) + EPSILON)
    unit = value * inverse
    grad_gain = jnp.sum(grad * unit, axis=0, keepdims=True)
    scaled = grad * gain
    pulled = inverse * (scaled - unit * jnp.mean(scaled * unit, axis=-1, keepdims=True))
    return pulled, grad_gain


PRODUCT_TILE = 256


def product(grid, left, left_other, right, moves=()):
    rows, height = left.shape
    stacked = right.ndim == 3
    half = right.shape[-1] if stacked else right.shape[-1] // 2
    tiles = height // PRODUCT_TILE

    def part(ref, c):
        return ref.at[c] if stacked else ref.at[:, pl.ds(pl.multiple_of(c * half, 128), half)]

    def body(here, step, ins, outs, held):
        own_ref, other_ref, right_ref = ins
        own_right, other_right, total, own_sem, sems = held
        own = pltpu.make_async_copy(part(right_ref, here.c), own_right, own_sem)
        swap = pltpu.make_async_remote_copy(
            src_ref=part(right_ref, 1 - here.c),
            dst_ref=other_right,
            send_sem=sems.at[0],
            recv_sem=sems.at[1],
            device_id=here.swap,
            device_id_type=MESH,
        )

        @pl.when(step == 0)
        def _():
            own.start()
            swap.start()
            own.wait()

        @pl.when(step < tiles)
        def _():
            total[step] = dot(own_ref[...], own_right[...], (0, 0))

        @pl.when(step == tiles)
        def _():
            swap.wait()

        @pl.when(step >= tiles)
        def _():
            outs[0][...] = (total[step - tiles] + dot(other_ref[...], other_right[...], (0, 0))).astype(BF)

    early = lambda i: jnp.minimum(i, tiles - 1)
    late = lambda i: jnp.maximum(i - tiles, 0)
    outs, got = host(
        grid, body, 2 * tiles,
        [pl.BlockSpec((rows, PRODUCT_TILE), lambda i: (0, early(i))),
         pl.BlockSpec((rows, PRODUCT_TILE), lambda i: (0, late(i))), any_spec()],
        [left, left_other, right],
        [pl.BlockSpec((PRODUCT_TILE, half), lambda i: (late(i), 0))],
        [kind(height, half)],
        moves,
        scratch=[
            pltpu.VMEM((rows, half), BF),
            pltpu.VMEM((rows, half), BF),
            pltpu.VMEM((tiles, PRODUCT_TILE, half), F32),
            pltpu.SemaphoreType.DMA,
            pltpu.SemaphoreType.DMA((2,)),
        ],
        cost=pl.CostEstimate(flops=4 * rows * height * half, bytes_accessed=2 * height * half, transcendentals=0),
        reaches=True,
    )
    return outs[0], got


class Reduce:
    def __init__(self, grid, total):
        self.grid = grid
        self.parts = total.reshape(grid.J, total.shape[0] // grid.J, total.shape[1])
        self.phase = 0

    def flip(self):
        return flip_move(self.grid, self.parts, self.phase)

    def flipped(self, got):
        grid = self.grid
        if self.phase == 0:
            kept = jnp.stack(
                [
                    lax.dynamic_index_in_dim(self.parts, grid.place(2 * i, grid.c), 0, keepdims=False)
                    for i in range(grid.J // 2)
                ]
            )
        else:
            kept = self.parts[0::2]
        self.parts = (kept.astype(F32) + got.astype(F32)).astype(BF)
        self.phase += 1
        if self.phase == grid.bits:
            self.line = self.parts.reshape(2, grid.F, -1, self.parts.shape[2])

    def ring(self):
        while self.phase < self.grid.bits:
            self.flipped(send(self.grid, [self.flip()])[0])
        return ring_move(self.grid, self.line)

    def arrived(self, got):
        grid = self.grid
        here = lax.dynamic_index_in_dim(self.line, grid.f, 1, keepdims=False)
        self.summed = here.astype(F32) + sum(got[t].astype(F32) for t in range(grid.F - 1))
        give = lax.dynamic_index_in_dim(self.summed, 1 - grid.c, 0, keepdims=False)
        self.give = give.astype(BF)

    def done(self, got):
        grid = self.grid
        mine = lax.dynamic_index_in_dim(self.summed, grid.c, 0, keepdims=False)
        got = got.astype(F32)
        return jnp.concatenate(
            [jnp.where(grid.c == 0, mine, got), jnp.where(grid.c == 0, got, mine)], axis=1
        )


def local(
    n_dp,
    pieces,
    tokens,
    cotangent,
    doc_lengths,
    partner,
    memory_picks,
    attention_in,
    attention_out,
    feed_in,
    feed_out,
    norm_gains,
):
    IDS[0] = 1
    grid = Grid(n_dp, pieces)
    grid.trace()
    layers = attention_in.shape[0]
    width = tokens.shape[2]
    heads = width // HEAD_DIM
    topk = memory_picks.shape[3]
    valid_all, visible_all = jax.vmap(memory_plan)(doc_lengths, partner)
    valid = valid_all[grid.m, grid.slot].reshape(1)
    visible = visible_all[grid.m, grid.slot]
    relative = (grid.slot - jnp.arange(n_dp)) % n_dp
    bias = jnp.repeat(jnp.where(visible[relative], 0.0, MASKED), topk)[:, None].astype(F32)
    tables = rope_tables()
    picks_there = grid.swap(memory_picks)
    picks = jnp.where(grid.r == grid.c, memory_picks[grid.m, 0], picks_there[grid.m, 0])
    zero = grid.c == 0

    def both_halves(mine, other):
        return jnp.where(
            zero, jnp.concatenate([mine, other], axis=-1), jnp.concatenate([other, mine], axis=-1)
        )

    def half(value, c):
        size = value.shape[-1] // 2
        return lax.dynamic_slice_in_dim(value, c * size, size, axis=value.ndim - 1)

    hidden, gains, weights = gather_all(
        grid, tokens, norm_gains, [attention_in, attention_out, feed_in, feed_out]
    )
    hidden = hidden.astype(F32)
    gain = lambda l, i: gains[l, i][None]
    flat = lambda w: w.reshape(-1, w.shape[-1])
    saved = []
    cotangent_rows = None
    for l in range(layers):
        w_qkv, w_out = flat(weights[l][0]), flat(weights[l][1])
        memory = l == layers - 1
        normed = norm(hidden, gain(l, 0)).astype(BF)
        coming = weights[l + 1] if l + 1 < layers else None
        moves = [spread_move(grid, weights[l][3], 1)] if later_here(l, 3) else []
        split, got = split_heads(grid, memory, tables, mm(normed, w_qkv), moves)
        if moves:
            weights[l][3] = got[0]
        (others,) = send(grid, [member_move(grid, split[1], False)])
        pairs = [split[1]] + [others[t] for t in range(grid.U - 1)]
        extra = None
        if memory:
            chosen = pick_memory(grid, picks, pairs, grid.c)
            (came,) = send(grid, [slots_move(grid, chosen, False)])
            slots = jnp.concatenate([chosen[None], came])
            slots = jnp.swapaxes(slots, 0, 1).reshape(2, n_dp * topk, -1)
            slots = both_halves(slots, grid.swap(slots))
            extra = {"query": split[2], "keys": slots[0], "values": slots[1], "bias": bias}
        moves = []
        if later_here(l, 2):
            moves += [spread_move(grid, weights[l][2], 1), spread_move(grid, weights[l][3], 2)]
        if coming is not None:
            moves.append(spread_move(grid, coming[3], 0))
        attended, got = attend(grid, valid, split[0], pairs, extra, moves)
        if later_here(l, 2):
            weights[l][2], weights[l][3] = got[:2]
            (weights[l][2],) = send(grid, [spread_move(grid, weights[l][2], 2)])
            for stage in range(3, grid.bits + 1):
                weights[l][2:] = send(grid, [spread_move(grid, w, stage) for w in weights[l][2:]])
        if coming is not None:
            coming[3] = got[-1]
        middle = hidden + mm(attended, w_out)
        moves = []
        if coming is not None:
            moves = [spread_move(grid, coming[2], 0), regroup_move(grid, cotangent)]
        w_up, w_down = flat(weights[l][2]), flat(weights[l][3])
        (out, normed_feed, both, inner), got = feed(grid, middle, gain(l, 1), w_up, w_down, moves)
        if coming is not None:
            coming[2], cotangent_rows = got
        saved.append((hidden, normed, split[0], pairs, extra, attended, middle, normed_feed, both, inner))
        hidden = out
    weights = [[flat(w) for w in kinds] for kinds in weights]
    cotangent_rows = cotangent_rows.reshape(-1, width)
    out_rows = hidden.astype(BF).reshape(2, grid.R, width)
    grad = cotangent_rows.astype(F32)
    found = [[None] * 4 for _ in range(layers)]
    grad_gains = [[None, None] for _ in range(layers)]
    layer_output = None
    above = None
    for l in reversed(range(layers)):
        w_qkv, w_out, w_up, w_down = weights[l]
        hidden, normed, query, pairs, extra, attended, middle, normed_feed, both, inner = saved[l]
        low = grad.astype(BF)

        moves = [swap_move(inner), swap_move(normed_feed), swap_move(normed), swap_move(attended)]
        if above is None:
            moves.append(regroup_back_move(grid, out_rows))
        else:
            moves += [above[1].flip(), above[2].flip(), above[0].ring()]
        (grad, grad_low, grads, gain_feed), got = feed_back(
            grid, grad, middle, gain(l, 1), both, w_up, w_down, moves
        )
        inner_other, normed_feed_other, normed_other, attended_other = got[:4]
        if above is None:
            layer_output = got[4]
            moves = []
        else:
            above[1].flipped(got[4])
            above[2].flipped(got[5])
            above[0].arrived(got[6])
            moves = [above[1].flip(), above[2].flip()]
        total, got = product(grid, inner, inner_other, low, moves)
        down = Reduce(grid, total)
        if above is not None:
            above[1].flipped(got[0])
            above[2].flipped(got[1])
        total, got = product(grid, normed_feed, normed_feed_other, grads, [down.flip()])
        up = Reduce(grid, total)
        down.flipped(got[0])
        grad_heads = mm(grad_low, w_out, (1, 1)).astype(BF)

        moves = [up.flip(), down.flip()]
        if above is not None:
            moves += [above[1].ring(), above[2].ring()]
        outs, got = attend_back(grid, valid, tables, query, grad_heads, pairs, extra, moves)
        up.flipped(got[0])
        down.flipped(got[1])
        if above is not None:
            above[1].arrived(got[2])
            above[2].arrived(got[3])
        grad_query, own, others = outs[:3]
        memory_grad = None
        moves = [member_move(grid, others, True)]
        if extra is not None:
            moves.append(swap_move(half(outs[3], 1 - grid.c)))
        got = send(grid, moves)
        others = got[0]
        moves = []
        if extra is not None:
            joined = half(outs[3], grid.c).astype(F32) + got[1].astype(F32)
            joined = joined.astype(BF).reshape(2, n_dp, topk, -1)
            moves = [slots_move(grid, joined, True)]
        total, got = product(grid, attended, attended_other, grad_low, moves)
        across = Reduce(grid, total)
        if extra is not None:
            total = joined[:, 0].astype(F32) + sum(got[0][t].astype(F32) for t in range(n_dp - 1))
            for t in range(1, grid.Q):
                total = total + grid.within(total.astype(BF), t).astype(F32)
            total = total.astype(BF)
            memory_grad = both_halves(total, grid.swap(total))
        grad_projected, got = finish_gradient(
            grid, grad_query, own, others, picks, memory_grad, [up.flip(), down.ring()]
        )
        up.flipped(got[0])
        down.arrived(got[1])
        pulled, gain_attention = norm_back(hidden, gain(l, 0), mm(grad_projected, w_qkv, (1, 1)))
        grad = grad + pulled
        grad_gains[l] = [gain_attention[0], gain_feed[0]]
        moves = []
        if l == 0:
            small = GainSum(grid, jnp.stack([jnp.stack(pair) for pair in grad_gains]).reshape(-1, HEAD_DIM))
            moves = [up.ring(), across.flip(), small.move()]
        total, got = product(grid, normed, normed_other, grad_projected, moves)
        last = Reduce(grid, total)
        if l == 0:
            up.arrived(got[0])
            across.flipped(got[1])
            small.took(got[2])
        found[l][3] = down.done(grid.swap(down.give))
        if above is not None:
            for i, reduced in zip((2, 1, 0), above):
                found[l + 1][i] = reduced.done(grid.swap(reduced.give))
        above = (up, across, last)
    up, across, last = above
    in_rows = grad.astype(BF).reshape(2, grid.R, width)
    got = send(grid, [last.flip(), across.flip(), regroup_back_move(grid, in_rows), small.move()])
    last.flipped(got[0])
    across.flipped(got[1])
    input_grad = got[2].astype(F32)
    small.took(got[3])
    got = send(grid, [last.flip(), across.ring(), small.move()])
    last.flipped(got[0])
    across.arrived(got[1])
    small.took(got[2])
    got = send(grid, [last.ring(), small.move()])
    last.arrived(got[0])
    small.took(got[1])
    total_gains = small.finish().reshape(layers, 2, n_dp * pieces, -1)
    device = (grid.j * 2 + grid.c) * grid.F + grid.f
    for i, reduced in zip((2, 1, 0), above):
        found[0][i] = reduced.done(grid.swap(reduced.give))
    return (
        layer_output,
        input_grad,
        *(jnp.stack([found[l][i] for l in range(layers)]) for i in range(4)),
        lax.dynamic_index_in_dim(total_gains, device, 2, keepdims=False),
    )


def solution(mesh):
    rows = P(None, ("dp", "fsdp"), None)
    in_specs = (rows, rows, P(), P(), P(None, "dp", None, None), rows, rows, rows, rows, P(None, None, ("dp", "fsdp")))
    out_specs = (rows, rows, rows, rows, rows, rows, P(None, None, ("dp", "fsdp")))
    body = functools.partial(local, mesh.shape["dp"], mesh.shape["fsdp"])
    return jax.shard_map(body, mesh=mesh, in_specs=in_specs, out_specs=out_specs, check_vma=False)
```

```python
import functools
import math

import jax
import jax.numpy as jnp
from jax import lax
from jax.experimental import pallas as pl
from jax.experimental.pallas import tpu as pltpu
from jax.sharding import PartitionSpec as P

HEAD_DIM = 128
SEG = 1024
MICRO = 2
EPSILON = 1e-06
MASKED = -1e30
SCALE = HEAD_DIM ** (-0.5)
LOG2E = 1.0 / math.log(2.0)
BF = jnp.bfloat16
F32 = jnp.float32
VMEM_LIMIT = 48 * 1024 * 1024


def slot_layout(lengths):
    slot_total = lengths.shape[0]
    slot_counts = ((lengths + SEG - 1) // SEG).astype(jnp.int32)
    slot_starts = (jnp.cumsum(slot_counts) - slot_counts).astype(jnp.int32)
    slot_index = jnp.arange(slot_total, dtype=jnp.int32)
    started = (slot_starts[None, :] <= slot_index[:, None]) & (slot_counts[None, :] > 0)
    owner_doc = (jnp.sum(started.astype(jnp.int32), axis=1) - 1).astype(jnp.int32)
    owner_pick = slot_index[None, :] == owner_doc[:, None]
    first_slot = jnp.sum(jnp.where(owner_pick, slot_starts[None, :], 0), axis=1).astype(jnp.int32)
    doc_total = jnp.sum(jnp.where(owner_pick, lengths[None, :], 0), axis=1).astype(jnp.int32)
    valid_rows = jnp.clip(doc_total - (slot_index - first_slot) * SEG, 0, SEG).astype(jnp.int32)
    return (valid_rows, owner_doc)


def memory_plan(lengths, partner_row):
    valid_rows, owner_doc = slot_layout(lengths)
    block_ids = jnp.arange(lengths.shape[0], dtype=jnp.int32)
    earlier = (block_ids[None, :] < block_ids[:, None]) & (owner_doc[None, :] == owner_doc[:, None])
    visible = earlier | (block_ids[None, :] == partner_row[:, None])
    return (valid_rows, visible)


class Grid:
    def __init__(self, n_dp, pieces):
        self.n_dp, self.F = n_dp, pieces
        self.J = n_dp // 2
        self.bits = self.J.bit_length() - 1
        self.Q = pieces // 4
        self.U = 2 * self.Q
        self.R = SEG // pieces
        self.T = 2 * self.R

    def trace(self):
        dp = lax.axis_index("dp")
        self.c, self.j, self.f = dp % 2, dp // 2, lax.axis_index("fsdp")
        self.q, self.g = self.f // self.Q, self.f % self.Q
        self.m, self.r = self.q // 2, self.q % 2
        self.k = self.c * self.Q + self.g
        self.slot = 2 * self.j + self.r

    def permute(self, value, target):
        pairs = []
        for j in range(self.J):
            for c in range(2):
                for f in range(self.F):
                    j2, c2, f2 = target(j, c, f)
                    pairs.append(((j * 2 + c) * self.F + f, (j2 * 2 + c2) * self.F + f2))
        return lax.ppermute(value, ("dp", "fsdp"), pairs)

    def swap(self, value):
        return self.permute(value, lambda j, c, f: (j, 1 - c, f))

    def ring(self, value, t):
        return self.permute(value, lambda j, c, f: (j, c, (f + t) % self.F))

    def bit(self, phase, c):
        return phase if c == 0 else self.bits - 1 - phase

    def flip(self, value, phase):
        return self.permute(value, lambda j, c, f: (j ^ (1 << self.bit(phase, c)), c, f))

    def mask(self, key, c):
        return sum(1 << self.bit(p, c) for p in range(self.bits) if key >> p & 1)

    def place(self, key, c):
        return jnp.where(c == 0, self.j ^ self.mask(key, 0), self.j ^ self.mask(key, 1))

    def member(self, value, t):
        def target(j, c, f):
            q, g = f // self.Q, f % self.Q
            k = (c * self.Q + g + t) % self.U
            return (j, k // self.Q, q * self.Q + k % self.Q)

        return self.permute(value, target)

    def within(self, value, t):
        return self.permute(
            value, lambda j, c, f: (j, c, f // self.Q * self.Q + (f % self.Q + t) % self.Q)
        )

    def slots(self, value, t):
        def target(j, c, f):
            q, g = f // self.Q, f % self.Q
            slot = (2 * j + q % 2 + t) % self.n_dp
            return (slot // 2, c, (2 * (q // 2) + slot % 2) * self.Q + g)

        return self.permute(value, target)

    def _spread(self, second):
        def target(j, c, f):
            m = f // (self.F // 2)
            m = 1 - m if second else m
            k = min(f, self.F - 1 - f)
            return (j, k // self.Q, (2 * m + c) * self.Q + k % self.Q)

        return target

    def _collect(self, second):
        there = self._spread(second)
        back = {
            there(0, c, f): (c, f) for c in range(2) for f in range(self.F)
        }
        return lambda j, c, f: (j,) + back[(0, c, f)]

    def to_units(self, value):
        here = self.f // (self.F // 2)
        first = self.permute(jnp.where(here == 0, value[0], value[1]), self._spread(False))
        second = self.permute(jnp.where(here == 0, value[1], value[0]), self._spread(True))
        return jnp.concatenate(
            [jnp.where(self.m == 0, first, second), jnp.where(self.m == 0, second, first)]
        )

    def from_units(self, value):
        low, high = value[: self.R], value[self.R :]
        first = self.permute(jnp.where(self.m == 0, low, high), self._collect(False))
        second = self.permute(jnp.where(self.m == 0, high, low), self._collect(True))
        here = self.f // (self.F // 2)
        return jnp.stack([jnp.where(here == 0, first, second), jnp.where(here == 0, second, first)])


def any_spec():
    return pl.BlockSpec(memory_space=pl.ANY)


MESH = pl.DeviceIdType.MESH


class Here:
    def __init__(self, grid):
        self.grid = grid
        dp = lax.axis_index("dp")
        self.j, self.c, self.f = dp // 2, dp % 2, lax.axis_index("fsdp")
        self.q, self.g = self.f // grid.Q, self.f % grid.Q
        self.m, self.r = self.q // 2, self.q % 2
        self.k = self.c * grid.Q + self.g
        self.swap = self.device(self.j, 1 - self.c, self.f)

    def device(self, j, c, f):
        return {"dp": 2 * j + c, "fsdp": f}

    def ring(self, t):
        return self.device(self.j, self.c, (self.f + t) % self.grid.F)

    def step(self, phase):
        first, second = (1 << self.grid.bit(phase, c) for c in (0, 1))
        return first + self.c * (second - first)

    def moved(self, j, phase):
        step = self.step(phase)
        return j + step * (1 - 2 * ((j // step) % 2))

    def flip(self, phase):
        return self.device(self.moved(self.j, phase), self.c, self.f)

    def slots(self, t):
        grid = self.grid
        slot = (2 * self.j + self.r + t) % grid.n_dp
        return self.device(slot // 2, self.c, (2 * self.m + slot % 2) * grid.Q + self.g)

    def member(self, t):
        grid = self.grid
        k = (self.k + t) % grid.U
        return self.device(self.j, k // grid.Q, self.q * grid.Q + k % grid.Q)

    def place(self, key):
        j = self.j
        for phase in range(self.grid.bits):
            if key >> phase & 1:
                j = self.moved(j, phase)
        return j

    def greet(self):
        grid = self.grid
        barrier = pltpu.get_barrier_semaphore()
        peers = [self.ring(t) for t in range(1, grid.F)]
        peers += [self.device(self.j, 1 - self.c, (self.f + t) % grid.F) for t in range(grid.F)]
        for bit in range(grid.bits):
            step = 1 << bit
            peers.append(self.device(self.j + step * (1 - 2 * ((self.j // step) % 2)), self.c, self.f))
        for peer in peers:
            pl.semaphore_signal(barrier, inc=1, device_id=peer, device_id_type=MESH)
        pl.semaphore_wait(barrier, len(peers))


def remote(source, target, sems, index, device):
    return pltpu.make_async_remote_copy(
        src_ref=source,
        dst_ref=target,
        send_sem=sems.at[0, index],
        recv_sem=sems.at[1, index],
        device_id=device,
        device_id_type=MESH,
    )


class Spread:
    def __init__(self, here, shard, whole, sems, own_sem, split):
        grid = here.grid
        self.here, self.split = here, split
        rows, width = shard.shape
        half = width // 2 if split else width

        def part(ref, c):
            if not split:
                return ref
            return ref.at[(slice(None),) * (len(ref.shape) - 1) + (pl.ds(pl.multiple_of(c * half, 128), half),)]

        j, c, f = here.j, here.c, here.f
        mine = part(whole, c)
        self.own = pltpu.make_async_copy(part(shard, c), part(whole.at[j, c, f], c), own_sem)
        other = 1 - c if split else c
        self.pre = remote(part(shard, other), part(whole.at[j, c, f], other), sems, 0, here.swap)
        at = 1
        self.hops = []
        for h in range(1, grid.F):
            hop = []
            for way in (1, -1):
                origin = f - way * (h - 1)
                inside = lambda place: (place >= 0) & (place < grid.F)
                block = mine.at[j, :, jnp.clip(origin, 0, grid.F - 1)]
                copy = remote(block, block, sems, at, here.device(j, c, (f + way + grid.F) % grid.F))
                hop.append((copy, inside(origin) & inside(f + way), inside(f - way * h)))
                at += 1
            self.hops.append(hop)
        self.flips = []
        for phase in range(grid.bits):
            sent = []
            for key in range(1 << phase):
                block = mine.at[here.place(key)]
                sent.append(remote(block, block, sems, at, here.flip(phase)))
                at += 1
            self.flips.append(sent)
        self.swaps = []
        for key in range(grid.J if split else 0):
            block = mine.at[here.place(key)]
            self.swaps.append(remote(block, block, sems, at, here.swap))
            at += 1

    @staticmethod
    def count(grid):
        return 1 + 2 * (grid.F - 1) + (grid.J - 1) + grid.J

    def begin(self):
        self.own.start()
        self.pre.start()

    def to_line(self):
        self.own.wait()
        self.pre.wait()
        self._hop(0)

    def _hop(self, h):
        for copy, sends, _ in self.hops[h]:
            pl.when(sends)(copy.start)

    def _send(self, keys):
        for key in keys:
            if self.swaps:
                self.swaps[key].start()
        for phase, sent in enumerate(self.flips):
            for key in keys:
                if key < 1 << phase:
                    sent[key].start()

    def steps(self, whole):
        def along(h):
            for copy, _, comes in self.hops[h]:
                pl.when(comes)(copy.wait_recv)
            if h + 1 < len(self.hops):
                self._hop(h + 1)
                return
            for hop in self.hops:
                for copy, sends, _ in hop:
                    pl.when(sends)(copy.wait_send)
            if whole:
                self._send([0])

        def later(phase):
            for copy in self.flips[phase]:
                copy.wait()
            self._send([key + (1 << phase) for key in range(1 << phase)])

        def last():
            for copy in self.swaps:
                copy.wait()

        line = [functools.partial(along, h) for h in range(len(self.hops))]
        if not whole:
            return line
        return line + [functools.partial(later, p) for p in range(len(self.flips))] + [last]


class Regroup:
    def __init__(self, here, source, target, sems, own_sem):
        grid = here.grid
        half = grid.F // 2
        k = jnp.minimum(here.f, grid.F - 1 - here.f)
        side = here.f // half
        self.sends = []
        for m in range(2):
            c2, f2 = k // grid.Q, (2 * m + here.c) * grid.Q + k % grid.Q
            same = (c2 == here.c) & (f2 == here.f)
            own = pltpu.make_async_copy(source.at[m], target.at[side], own_sem)
            away = pltpu.make_async_remote_copy(
                src_ref=source.at[m],
                dst_ref=target.at[side],
                send_sem=sems.at[0, m],
                recv_sem=sems.at[1, side],
                device_id=here.device(here.j, c2, f2),
                device_id_type=MESH,
            )
            self.sends.append((same, own, away))
        self.arrivals = []
        for side in range(2):
            from_f = here.k if side == 0 else grid.F - 1 - here.k
            same = (here.r == here.c) & (from_f == here.f)
            came = pltpu.make_async_remote_copy(
                src_ref=source.at[0],
                dst_ref=target.at[side],
                send_sem=sems.at[0, 0],
                recv_sem=sems.at[1, side],
                device_id=here.swap,
                device_id_type=MESH,
            )
            self.arrivals.append((same, came))

    def start(self):
        for same, own, away in self.sends:
            pl.when(same)(own.start)
            pl.when(jnp.logical_not(same))(away.start)

    def wait(self):
        for same, own, away in self.sends:
            pl.when(same)(own.wait)
            pl.when(jnp.logical_not(same))(away.wait_send)
        for same, came in self.arrivals:
            pl.when(jnp.logical_not(same))(came.wait_recv)


def gather_body(grid, layers, kinds, *refs):
    tokens, gains = refs[:2]
    shards = refs[2 : 2 + kinds]
    outs = refs[2 + kinds :]
    tokens_out, gains_out = outs[:2]
    wholes = outs[2 : 2 + layers * kinds]
    sems, own_sems, regroup_sems = outs[2 + layers * kinds :]
    here = Here(grid)
    here.greet()
    rows = Regroup(here, tokens, tokens_out, regroup_sems, own_sems.at[0])
    moves = []
    for l, i in ORDER:
        n = l * kinds + i
        move = Spread(here, shards[i].at[l], wholes[n], sems.at[n + 1], own_sems.at[n + 2], True)
        moves.append((move, not later_here(l, i)))
    moves.insert(GAINS_AT, (Spread(here, gains, gains_out, sems.at[0], own_sems.at[1], False), True))
    for move, _ in moves:
        move.begin()
    steps = [move.steps(whole) for move, whole in moves]
    count = len(steps[0])
    for at in range(AHEAD):
        moves[at][0].to_line()
    for at in range(len(moves) + count - 1):
        if at == ROWS_AT:
            rows.start()
        if at + AHEAD < len(moves):
            moves[at + AHEAD][0].to_line()
        for back in reversed(range(count)):
            if 0 <= at - back < len(moves) and back < len(steps[at - back]):
                steps[at - back][back]()
    rows.wait()


ORDER = [(0, 1), (0, 3), (0, 2), (0, 0), (1, 0), (1, 1), (1, 3), (1, 2)]
GAINS_AT, ROWS_AT, AHEAD = 3, 6, 1


def later_here(l, i):
    return l > 0 and i >= 2


def gather_all(grid, tokens, gains, shards):
    layers, kinds = shards[0].shape[0], len(shards)
    packed = jnp.zeros((8, 128), F32).at[: layers * 2, : gains.shape[2]].set(
        gains.astype(F32).reshape(layers * 2, -1)
    )
    whole = lambda shard: jax.ShapeDtypeStruct((grid.J, 2, grid.F) + shard.shape[-2:], shard.dtype)
    out_shape = [jax.ShapeDtypeStruct(tokens.shape, BF), whole(packed)]
    out_shape += [whole(shard) for _ in range(layers) for shard in shards]
    moves = 1 + layers * kinds
    outs = pl.pallas_call(
        functools.partial(gather_body, grid, layers, kinds),
        in_specs=[any_spec()] * (2 + kinds),
        out_specs=[any_spec()] * len(out_shape),
        out_shape=out_shape,
        scratch_shapes=[
            pltpu.SemaphoreType.DMA((moves, 2, Spread.count(grid))),
            pltpu.SemaphoreType.DMA((moves + 1,)),
            pltpu.SemaphoreType.DMA((2, 2)),
        ],
        compiler_params=pltpu.CompilerParams(
            collective_id=0, has_side_effects=True, vmem_limit_bytes=VMEM_LIMIT
        ),
    )(tokens, packed, *shards)
    gains_all = outs[1][..., : layers * 2, : gains.shape[2]]
    gains_all = jnp.moveaxis(gains_all, 3, 0).reshape(layers, 2, -1)
    weights = [list(outs[2 + l * kinds : 2 + (l + 1) * kinds]) for l in range(layers)]
    return outs[0].reshape(-1, tokens.shape[2]), gains_all, weights


def unless(condition, act):
    if condition is None:
        act()
    else:
        pl.when(jnp.logical_not(condition))(act)


class Move:
    def __init__(self, array, shape, count, copies, plan=None, in_place=False):
        self.array, self.shape, self.count, self.copies = array, shape, count, copies
        self.plan, self.in_place = plan or self._plain, in_place

    def _plain(self, here, source, target, sends, recvs, base):
        found = []
        for i, (what, where, peer, giver) in enumerate(self.copies(here, source, target)):
            copy = pltpu.make_async_remote_copy(
                src_ref=what,
                dst_ref=where,
                send_sem=sends.at[base + i],
                recv_sem=recvs.at[base + i],
                device_id=peer,
                device_id_type=MESH,
            )
            found.append((copy, None, None, giver, copy, None))
        return found


def flip_move(grid, parts, phase):
    count = parts.shape[0] // 2

    def copies(here, source, target):
        found = []
        for i in range(count):
            at = here.place(2 * i + 1) if phase == 0 else 2 * i + 1
            peer = here.flip(phase)
            found.append((source.at[at], target.at[i], peer, peer))
        return found

    return Move(parts, (count,) + parts.shape[1:], count, copies)


def ring_move(grid, line):
    def copies(here, source, target):
        return [
            (source.at[:, (here.f + t) % grid.F], target.at[t - 1], here.ring(t), here.ring(grid.F - t))
            for t in range(1, grid.F)
        ]

    return Move(line, (grid.F - 1, 2) + line.shape[2:], grid.F - 1, copies)


def swap_move(array, give=None):
    def copies(here, source, target):
        return [(source if give is None else source.at[give(here)], target, here.swap, here.swap)]

    return Move(array, array.shape if give is None else array.shape[1:], 1, copies)


def swap_half_move(array):
    half = array.shape[-1] // 2

    def copies(here, source, target):
        start = pl.multiple_of((1 - here.c) * half, 128)
        return [(source.at[:, :, pl.ds(start, half)], target, here.swap, here.swap)]

    return Move(array, array.shape[:-1] + (half,), 1, copies)


def slots_move(grid, array, back):
    def copies(here, source, target):
        found = []
        for t in range(1, grid.n_dp):
            ahead, behind = here.slots(t), here.slots(grid.n_dp - t)
            if back:
                found.append((source.at[:, t], target.at[t - 1], behind, ahead))
            else:
                found.append((source, target.at[t - 1], ahead, behind))
        return found

    shape = array.shape if not back else array.shape[:1] + array.shape[2:]
    return Move(array, (grid.n_dp - 1,) + shape, grid.n_dp - 1, copies)


def member_move(grid, array, back):
    def copies(here, source, target):
        found = []
        for t in range(1, grid.U):
            ahead, behind = here.member(t), here.member(grid.U - t)
            if back:
                found.append((source.at[t - 1], target.at[t - 1], behind, ahead))
            else:
                found.append((source, target.at[t - 1], ahead, behind))
        return found

    shape = array.shape[1:] if back else array.shape
    return Move(array, (grid.U - 1,) + shape, grid.U - 1, copies)


def spread_move(grid, whole, stages):
    half = whole.shape[-1] // 2

    def keys_of(stage):
        return [0] if stage == 0 else range(1 << (stage - 1), 1 << stage)

    def copies(here, source, target):
        found = []
        for stage, part, parts in stages:
            size = half // parts
            columns = pl.ds(pl.multiple_of(here.c * half + part * size, 128), size)
            mine = target.at[:, :, :, :, columns]
            for key in keys_of(stage):
                block = mine.at[here.place(key)]
                found.append((block, block, here.swap, here.swap))
                for phase in range(stage, grid.bits):
                    found.append((block, block, here.flip(phase), here.flip(phase)))
        return found

    count = sum(len(keys_of(stage)) * (1 + grid.bits - stage) for stage, _, _ in stages)
    return Move(whole, whole.shape, count, copies, in_place=True)


def peer_move(array, peer):
    return Move(array, array.shape, 1, lambda here, source, target: [(source, target, peer(here), peer(here))])


def line_move(grid, array):
    def copies(here, source, target):
        return [(source, target.at[t - 1], here.ring(t), here.ring(grid.F - t)) for t in range(1, grid.F)]

    return Move(array, (grid.F - 1,) + array.shape, grid.F - 1, copies)


def regroup_move(grid, array):
    def plan(here, source, target, sends, recvs, base):
        found = []
        k = jnp.minimum(here.f, grid.F - 1 - here.f)
        side = here.f // (grid.F // 2)
        for m in range(2):
            c2, f2 = k // grid.Q, (2 * m + here.c) * grid.Q + k % grid.Q
            same = (c2 == here.c) & (f2 == here.f)
            away = pltpu.make_async_remote_copy(
                src_ref=source.at[m],
                dst_ref=target.at[side],
                send_sem=sends.at[base + m],
                recv_sem=recvs.at[base + side],
                device_id=here.device(here.j, c2, f2),
                device_id_type=MESH,
            )
            own = pltpu.make_async_copy(source.at[m], target.at[side], sends.at[base + m])
            from_f = here.k if m == 0 else grid.F - 1 - here.k
            same_in = (here.r == here.c) & (from_f == here.f)
            came = pltpu.make_async_remote_copy(
                src_ref=source.at[0],
                dst_ref=target.at[m],
                send_sem=sends.at[base],
                recv_sem=recvs.at[base + m],
                device_id=here.swap,
                device_id_type=MESH,
            )
            found.append((away, same, own, here.device(here.j, here.r, from_f), came, same_in))
        return found

    return Move(array, array.shape, 2, None, plan)


def regroup_back_move(grid, array):
    def plan(here, source, target, sends, recvs, base):
        found = []
        for piece in range(2):
            f = here.k if piece == 0 else grid.F - 1 - here.k
            same = (here.r == here.c) & (f == here.f)
            away = pltpu.make_async_remote_copy(
                src_ref=source.at[piece],
                dst_ref=target.at[here.m],
                send_sem=sends.at[base + piece],
                recv_sem=recvs.at[base + here.m],
                device_id=here.device(here.j, here.r, f),
                device_id_type=MESH,
            )
            own = pltpu.make_async_copy(source.at[piece], target.at[here.m], sends.at[base + piece])
            k = jnp.minimum(here.f, grid.F - 1 - here.f)
            c2, f2 = k // grid.Q, (2 * piece + here.c) * grid.Q + k % grid.Q
            same_in = (c2 == here.c) & (f2 == here.f)
            came = pltpu.make_async_remote_copy(
                src_ref=source.at[0],
                dst_ref=target.at[piece],
                send_sem=sends.at[base],
                recv_sem=recvs.at[base + piece],
                device_id=here.swap,
                device_id_type=MESH,
            )
            found.append((away, same, own, here.device(here.j, c2, f2), came, same_in))
        return found

    return Move(array, array.shape, 2, None, plan)


IDS = [1]


def host(grid, body, steps, in_specs, operands, out_specs, out_shape, moves=(), scratch=(), cost=None, reaches=False):
    counts = [len(operands), len(moves), len(out_shape), len(moves), len(scratch)]

    def kernel(*refs):
        parts, at = [], 0
        for count in counts:
            parts.append(refs[at : at + count])
            at += count
        ins, sources, outs, targets, held = parts
        here = Here(grid)
        step = pl.program_id(0)
        planned = []
        if moves:
            sends, recvs = refs[at:]
            base = 0
            for move, source, target in zip(moves, sources, targets):
                planned += move.plan(here, source, target, sends, recvs, base)
                base += move.count

        if moves or reaches:

            @pl.when(step == 0)
            def _():
                barrier = pltpu.get_barrier_semaphore()
                if reaches:
                    pl.semaphore_signal(barrier, inc=1, device_id=here.swap, device_id_type=MESH)
                for _, _, _, giver, _, same_in in planned:
                    signal = functools.partial(
                        pl.semaphore_signal, barrier, inc=1, device_id=giver, device_id_type=MESH
                    )
                    unless(same_in, signal)
                due = int(reaches) + sum(same is None for _, same, _, _, _, _ in planned)
                for _, same, _, _, _, _ in planned:
                    if same is not None:
                        due = due + 1 - same.astype(jnp.int32)
                pl.semaphore_wait(barrier, due)
                for away, same, own, _, _, _ in planned:
                    unless(same, away.start)
                    if same is not None:
                        pl.when(same)(own.start)

        if body is not None:
            body(here, step, ins, outs, held)
        if moves:

            @pl.when(step == steps - 1)
            def _():
                for away, same, own, _, came, same_in in planned:
                    unless(same, away.wait_send)
                    if same is not None:
                        pl.when(same)(own.wait)
                    unless(same_in, came.wait_recv)

    total = sum(move.count for move in moves)
    extra = {}
    sems = []
    if moves or reaches:
        extra = {"collective_id": IDS[0], "has_side_effects": True}
        IDS[0] += 1
    if moves:
        sems = [pltpu.SemaphoreType.DMA((total,)), pltpu.SemaphoreType.DMA((total,))]
    outs = pl.pallas_call(
        kernel,
        grid=(steps,),
        in_specs=list(in_specs) + [any_spec()] * len(moves),
        out_specs=list(out_specs) + [any_spec()] * len(moves),
        out_shape=list(out_shape) + [jax.ShapeDtypeStruct(m.shape, m.array.dtype) for m in moves],
        scratch_shapes=list(scratch) + sems,
        input_output_aliases={
            len(operands) + i: len(out_shape) + i for i, move in enumerate(moves) if move.in_place
        },
        compiler_params=pltpu.CompilerParams(vmem_limit_bytes=VMEM_LIMIT, **extra),
        cost_estimate=cost,
    )(*operands, *[move.array for move in moves])
    return outs[: len(out_shape)], outs[len(out_shape) :]


def send(grid, moves):
    return host(grid, None, 1, [], [], [], [], moves)[1]


class GainSum:
    def __init__(self, grid, total):
        self.grid, self.total, self.stage = grid, total, 0

    def move(self):
        grid, phase = self.grid, self.stage - 1
        if self.stage == 0:
            return swap_move(self.total)
        if phase < grid.bits:
            return peer_move(self.total, lambda here: here.flip(phase))
        return line_move(grid, self.total)

    def took(self, got):
        if self.stage > self.grid.bits:
            got = sum(got[t] for t in range(self.grid.F - 1))
        self.total = self.total + got
        self.stage += 1

    def finish(self):
        while self.stage <= self.grid.bits + 1:
            self.took(send(self.grid, [self.move()])[0])
        return self.total


def rope_tables():
    half_dim = HEAD_DIM // 2
    frequency = jnp.exp(
        jnp.arange(half_dim, dtype=F32) * (-2.0 * math.log(10000.0) / HEAD_DIM)
    )
    angles = jnp.arange(SEG, dtype=jnp.int32).astype(F32)[:, None] * frequency[None, :]
    cos, sin = jnp.cos(angles), jnp.sin(angles)
    return (jnp.concatenate([cos, cos], axis=-1), jnp.concatenate([-sin, sin], axis=-1))


def turn(values, cos, sin):
    return values * cos + pltpu.roll(values, HEAD_DIM // 2, 1) * sin


def smem():
    return pl.BlockSpec(memory_space=pltpu.SMEM)


def whole_spec(*shape):
    return pl.BlockSpec(shape, lambda i: (0,) * len(shape))


def columns_spec(*shape, first=0):
    return pl.BlockSpec(shape, lambda i: (0,) * (len(shape) - 1) + (i + first,))


def rows_spec(*shape):
    return pl.BlockSpec(shape, lambda i: (i,) + (0,) * (len(shape) - 1))


def kind(*shape, dtype=BF):
    return jax.ShapeDtypeStruct(shape, dtype)


def piece_start(grid, member, part):
    return (member if part == 0 else grid.F - 1 - member) * grid.R


def table_rows(grid, table_ref, member, part):
    start = pl.multiple_of(piece_start(grid, member, part), grid.R)
    return table_ref[pl.ds(start, grid.R), :]


def dot(left, right, contract):
    return lax.dot_general(
        left, right, (((contract[0],), (contract[1],)), ((), ())), preferred_element_type=F32
    )


def mm(left, right, contract=(1, 0)):
    return dot(left, right, contract)


def project(grid, memory, tables, hidden, gain, weight, moves=()):
    rows, width = hidden.shape
    heads = weight.shape[1] // (3 * HEAD_DIM)
    together = 2
    size = together * HEAD_DIM
    steps = heads // together
    count = 3 if memory else 2

    def body(here, step, ins, outs, held):
        cos_ref, sin_ref, hidden_ref, gain_ref = ins[:4]
        normed_ref, q_out, kv_out = outs[:3]

        @pl.when(step == 0)
        def _():
            normed_ref[...] = norm(hidden_ref[...].astype(F32), gain_ref[...]).astype(BF)

        for part in range(2):
            at = pl.ds(part * grid.R, grid.R)
            cos = table_rows(grid, cos_ref, here.k, part)
            sin = table_rows(grid, sin_ref, here.k, part)
            normed = normed_ref[at, :]
            query, key, value = (dot(normed, w[...], (1, 0)) for w in ins[4:])
            kv_out[1, at, :] = value.astype(BF)
            for h in range(together):
                columns = slice(h * HEAD_DIM, (h + 1) * HEAD_DIM)
                q_out[at, columns] = turn(query[:, columns], cos, sin).astype(BF)
                kv_out[0, at, columns] = turn(key[:, columns], cos, sin).astype(BF)
            if memory:
                kv_out[2, at, :] = key.astype(BF)
                outs[3][at, :] = query.astype(BF)

    piece = columns_spec(rows, size)
    table = whole_spec(SEG, HEAD_DIM)
    flat = kind(rows, heads * HEAD_DIM)
    return host(
        grid,
        body,
        steps,
        [table, table, whole_spec(rows, width), whole_spec(1, width)]
        + [columns_spec(width, size, first=i * steps) for i in range(3)],
        [*tables, hidden, gain, weight, weight, weight],
        [whole_spec(rows, width), piece, columns_spec(count, rows, size)] + [piece] * memory,
        [kind(rows, width), flat, kind(count, rows, heads * HEAD_DIM)] + [flat] * memory,
        moves,
        cost=pl.CostEstimate(
            flops=2 * rows * width * weight.shape[1], bytes_accessed=2 * width * weight.shape[1], transcendentals=0
        ),
    )


def part_scores(grid, here, valid, part, query, keys):
    shape = (grid.R, grid.R)
    apart = lax.broadcasted_iota(jnp.int32, shape, 0) - lax.broadcasted_iota(jnp.int32, shape, 1)
    found = []
    for t in range(grid.U):
        member = (here.k - t + grid.U) % grid.U
        for side in range(part + 1):
            score = dot(keys[t][side * grid.R : (side + 1) * grid.R], query, (1, 1))
            if side == part:
                start = piece_start(grid, member, side)
                allowed = apart <= piece_start(grid, here.k, part) - start
                if side == 1:
                    down = lax.broadcasted_iota(jnp.int32, shape, 0)
                    allowed = allowed & (down < valid - start)
                score = jnp.where(allowed, score, MASKED)
            found.append((t, side, score))
    return found


def softmax_parts(scores):
    top = functools.reduce(jnp.maximum, [jnp.max(s, axis=0, keepdims=True) for s in scores])
    powers = [jnp.exp2((s - top) * (SCALE * LOG2E)) for s in scores]
    inverse = 1.0 / sum(jnp.sum(p, axis=0, keepdims=True) for p in powers)
    return [p * inverse for p in powers]


def attention_cost(grid, heads, memory_rows, products):
    pairs = grid.T * (SEG * 3 // 4 + memory_rows) * heads
    return pl.CostEstimate(
        flops=2 * products * HEAD_DIM * pairs,
        bytes_accessed=2 * HEAD_DIM * heads * 4 * (SEG + memory_rows),
        transcendentals=pairs,
    )


def memory_operands(grid, extra):
    rows = extra["keys"].shape[0]
    piece = columns_spec(grid.T, HEAD_DIM)
    column = columns_spec(rows, HEAD_DIM)
    return [extra["query"], extra["keys"], extra["values"], extra["bias"]], [
        piece, column, column, whole_spec(rows, 1)
    ], rows


def attend(grid, valid, query, pairs, extra, moves=()):
    rows, width = query.shape
    heads = width // HEAD_DIM
    R, U = grid.R, grid.U

    def body(here, step, ins, outs, held):
        valid_ref, q_ref, kv_refs, refs = ins[0], ins[1], ins[2 : 2 + U], ins[2 + U :]
        keys, values = [r[0] for r in kv_refs], [r[1] for r in kv_refs]
        for part in range(2):
            at = pl.ds(part * R, R)
            found = part_scores(grid, here, valid_ref[0], part, q_ref[at, :], keys)
            scores = [s for _, _, s in found]
            mixed = [values[t][side * R : (side + 1) * R] for t, side, _ in found]
            if extra is not None:
                scores.append(dot(refs[1][...], refs[0][at, :], (1, 1)) + refs[3][...])
                mixed.append(refs[2][...])
            total = sum(
                dot(value, p.astype(BF), (0, 0)) for value, p in zip(mixed, softmax_parts(scores))
            )
            outs[0][at, :] = total.T.astype(BF)

    piece = columns_spec(rows, HEAD_DIM)
    operands = [valid, query, *pairs]
    specs = [smem(), piece] + [columns_spec(2, rows, HEAD_DIM)] * U
    memory_rows = 0
    if extra is not None:
        more, more_specs, memory_rows = memory_operands(grid, extra)
        operands, specs = operands + more, specs + more_specs
    outs, got = host(
        grid, body, heads, specs, operands, [piece], [kind(rows, width)], moves,
        cost=attention_cost(grid, heads, memory_rows, 2),
    )
    return outs[0], got


def attend_back(grid, valid, tables, query, grad, pairs, extra, moves=()):
    rows, width = query.shape
    heads = width // HEAD_DIM
    R, U = grid.R, grid.U

    def body(here, step, ins, outs, held):
        valid_ref, cos_ref, sin_ref, q_ref, g_ref = ins[:5]
        kv_refs, refs = ins[5 : 5 + U], ins[5 + U :]
        keys, values = [r[0] for r in kv_refs], [r[1] for r in kv_refs]
        grad_keys, grad_values = {}, {}

        def add(store, at, value):
            store[at] = store[at] + value if at in store else value

        for part in range(2):
            at_rows = pl.ds(part * R, R)
            asked, grads_in = q_ref[at_rows, :], g_ref[at_rows, :]
            found = part_scores(grid, here, valid_ref[0], part, asked, keys)
            places = [(t, side) for t, side, _ in found]
            scores = [s for _, _, s in found]
            part_keys = [keys[t][side * R : (side + 1) * R] for t, side in places]
            part_values = [values[t][side * R : (side + 1) * R] for t, side in places]
            queries = [asked] * len(places)
            if extra is not None:
                places.append("memory")
                queries.append(refs[0][at_rows, :])
                scores.append(dot(refs[1][...], queries[-1], (1, 1)) + refs[3][...])
                part_keys.append(refs[1][...])
                part_values.append(refs[2][...])
            probs = softmax_parts(scores)
            grads = [dot(value, grads_in, (1, 1)) for value in part_values]
            inner = sum(jnp.sum(p * d, axis=0, keepdims=True) for p, d in zip(probs, grads))
            local_query, raw_query = None, None
            for at, p, d, key, by in zip(places, probs, grads, part_keys, queries):
                moved = (p * (d - inner)).astype(BF)
                add(grad_keys, at, dot(moved, by, (1, 0)))
                add(grad_values, at, dot(p.astype(BF), grads_in, (1, 0)))
                back = dot(key, moved, (0, 0))
                if at == "memory":
                    raw_query = back
                else:
                    local_query = back if local_query is None else local_query + back
            cos = table_rows(grid, cos_ref, here.k, part)
            sin = table_rows(grid, sin_ref, here.k, part)
            result = turn(local_query.T, cos, -sin)
            if extra is not None:
                result = result + raw_query.T
            outs[0][at_rows, :] = (result * SCALE).astype(BF)
        for t in range(U):
            member = (here.k - t + U) % U
            for side in range(2):
                at_rows = pl.ds(side * R, R)
                cos = table_rows(grid, cos_ref, member, side)
                sin = table_rows(grid, sin_ref, member, side)
                key = turn(grad_keys[(t, side)], cos, -sin) * SCALE
                if t == 0:
                    outs[1][0, at_rows, :] = key
                    outs[1][1, at_rows, :] = grad_values[(t, side)]
                else:
                    outs[2][t - 1, 0, at_rows, :] = key.astype(BF)
                    outs[2][t - 1, 1, at_rows, :] = grad_values[(t, side)].astype(BF)
        if extra is not None:
            outs[3][0] = (grad_keys["memory"] * SCALE).astype(BF)
            outs[3][1] = grad_values["memory"].astype(BF)

    piece = columns_spec(rows, HEAD_DIM)
    pair = columns_spec(2, rows, HEAD_DIM)
    table = whole_spec(SEG, HEAD_DIM)
    operands = [valid, *tables, query, grad, *pairs]
    specs = [smem(), table, table, piece, piece] + [pair] * U
    out_shape = [kind(rows, width), kind(2, rows, width, dtype=F32), kind(U - 1, 2, rows, width)]
    out_specs = [piece, pair, columns_spec(U - 1, 2, rows, HEAD_DIM)]
    memory_rows = 0
    if extra is not None:
        more, more_specs, memory_rows = memory_operands(grid, extra)
        operands, specs = operands + more, specs + more_specs
        out_shape.append(kind(2, memory_rows, width))
        out_specs.append(columns_spec(2, memory_rows, HEAD_DIM))
    return host(
        grid, body, heads, specs, operands, out_specs, out_shape, moves,
        cost=attention_cost(grid, heads, memory_rows, 5),
    )


def pick_memory(grid, picks, stacked, c):
    heads, topk = picks.shape
    per = heads // 2
    R, U = grid.R, grid.U

    def body(info_ref, picks_ref, *refs):
        chosen_from, out_ref = refs[:U], refs[U]
        here = Here(grid)
        picked = picks_ref[0]
        key, value = 0.0, 0.0
        for t in range(U):
            member = (here.k - t + U) % U
            for side in range(2):
                across = lax.broadcasted_iota(jnp.int32, (picked.shape[0], R), 1)
                chosen = (picked == across + piece_start(grid, member, side)).astype(BF)
                at = pl.ds(side * R, R)
                key = key + dot(chosen, chosen_from[t][2, at, :], (1, 0))
                value = value + dot(chosen, chosen_from[t][1, at, :], (1, 0))
        out_ref[0] = key.astype(BF)
        out_ref[1] = value.astype(BF)

    at = lambda h, info: info[0] * per + h
    piece = pl.BlockSpec((3, grid.T, HEAD_DIM), lambda h, info: (0, 0, at(h, info)))
    return pl.pallas_call(
        body,
        grid_spec=pltpu.PrefetchScalarGridSpec(
            num_scalar_prefetch=1,
            grid=(per,),
            in_specs=[pl.BlockSpec((1, topk, 1), lambda h, info: (at(h, info), 0, 0))] + [piece] * U,
            out_specs=pl.BlockSpec((2, topk, HEAD_DIM), lambda h, info: (0, 0, h)),
        ),
        out_shape=kind(2, topk, per * HEAD_DIM),
        compiler_params=pltpu.CompilerParams(vmem_limit_bytes=VMEM_LIMIT),
        cost_estimate=pl.CostEstimate(
            flops=4 * topk * SEG * HEAD_DIM * per, bytes_accessed=4 * SEG * HEAD_DIM * per, transcendentals=0
        ),
    )(c.reshape(1).astype(jnp.int32), picks[:, :, None], *stacked)


def finish_gradient(grid, grad_query, own, others, picks, memory, moves=()):
    rows, width = grad_query.shape
    heads = width // HEAD_DIM
    R, U = grid.R, grid.U

    def body(here, step, ins, outs, held):
        dq_ref, own_ref, others_ref = ins[:3]
        out_ref = outs[0]

        @pl.when(step == 0)
        def _():
            out_ref[...] = dq_ref[...]

        @pl.when(step > 0)
        def _():
            for side in range(2):
                at = pl.ds(side * R, R)
                for h in range(heads):
                    columns = pl.ds(h * HEAD_DIM, HEAD_DIM)
                    value = own_ref[0, at, columns]
                    for t in range(U - 1):
                        value = value + others_ref[t, 0, at, columns].astype(F32)
                    if memory is not None:
                        picked = ins[3][h]
                        down = lax.broadcasted_iota(jnp.int32, (R, picked.shape[1]), 0)
                        chosen = (down + piece_start(grid, here.k, side) == picked).astype(BF)
                        value = value + dot(chosen, ins[4][0, :, columns], (1, 0))
                    out_ref[at, columns] = value.astype(BF)

    which = lambda b: jnp.maximum(b - 1, 0)
    operands = [grad_query, own, others]
    specs = [
        whole_spec(rows, width),
        pl.BlockSpec((1, rows, width), lambda b: (which(b), 0, 0)),
        pl.BlockSpec((U - 1, 1, rows, width), lambda b: (0, which(b), 0, 0)),
    ]
    if memory is not None:
        topk = picks.shape[1]
        operands += [picks[:, None, :], memory]
        specs += [
            whole_spec(heads, 1, topk),
            pl.BlockSpec((1, topk, width), lambda b: (which(b), 0, 0)),
        ]
    outs, got = host(
        grid, body, 3, specs, operands, [columns_spec(rows, width)], [kind(rows, 3 * width)], moves,
        cost=pl.CostEstimate(flops=2 * rows * width, bytes_accessed=16 * rows * width, transcendentals=0),
    )
    return outs[0], got


FEED_TILE = 256


def feed(grid, middle, gain, w_up, w_down, moves=()):
    rows, width = middle.shape
    hidden = w_down.shape[0]
    steps = hidden // FEED_TILE

    def body(here, step, ins, outs, held):
        middle_ref, gain_ref, gate_w, up_w, down_w = ins
        out_ref, normed_ref, both_ref, inner_ref = outs

        @pl.when(step == 0)
        def _():
            value = middle_ref[...]
            normed_ref[...] = norm(value, gain_ref[...]).astype(BF)
            held[0][...] = value

        normed = normed_ref[...]
        gate, up = dot(normed, gate_w[...], (1, 0)), dot(normed, up_w[...], (1, 0))
        both_ref[0] = gate.astype(BF)
        both_ref[1] = up.astype(BF)
        inner = (gate / (1.0 + jnp.exp(-gate)) * up).astype(BF)
        inner_ref[...] = inner
        held[0][...] += dot(inner, down_w[...], (1, 0))

        @pl.when(step == steps - 1)
        def _():
            out_ref[...] = held[0][...]

    tile = columns_spec(width, FEED_TILE)
    return host(
        grid, body, steps,
        [whole_spec(rows, width), whole_spec(1, width), tile, columns_spec(width, FEED_TILE, first=steps), rows_spec(FEED_TILE, width)],
        [middle, gain, w_up, w_up, w_down],
        [whole_spec(rows, width), whole_spec(rows, width), columns_spec(2, rows, FEED_TILE), columns_spec(rows, FEED_TILE)],
        [kind(rows, width, dtype=F32), kind(rows, width), kind(2, rows, hidden), kind(rows, hidden)],
        moves,
        scratch=[pltpu.VMEM((rows, width), F32)],
        cost=pl.CostEstimate(flops=6 * rows * width * hidden, bytes_accessed=6 * width * hidden, transcendentals=rows * hidden),
    )


def feed_back(grid, grad, middle, gain, both, w_up, w_down, moves=()):
    rows, width = grad.shape
    hidden = w_down.shape[0]
    steps = hidden // FEED_TILE

    def body(here, step, ins, outs, held):
        grad_ref, middle_ref, gain_ref, both_ref, gate_w, up_w, down_w = ins
        out_ref, low_ref, grads_ref, gain_out = outs
        total = held[0]

        @pl.when(step == 0)
        def _():
            held[1][...] = grad_ref[...].astype(BF)
            total[...] = jnp.zeros_like(total)

        grad_inner = dot(held[1][...], down_w[...], (1, 1))
        gate, up = both_ref[0].astype(F32), both_ref[1].astype(F32)
        sigmoid = 1.0 / (1.0 + jnp.exp(-gate))
        scaled = grad_inner * sigmoid
        grad_gate = (scaled * up * (1.0 + gate * (1.0 - sigmoid))).astype(BF)
        grad_up = (scaled * gate).astype(BF)
        grads_ref[0] = grad_gate
        grads_ref[1] = grad_up
        total[...] += dot(grad_gate, gate_w[...], (1, 1)) + dot(grad_up, up_w[...], (1, 1))

        @pl.when(step == steps - 1)
        def _():
            pulled, grad_gain = norm_back(middle_ref[...], gain_ref[...], total[...])
            result = grad_ref[...] + pulled
            out_ref[...] = result
            low_ref[...] = result.astype(BF)
            gain_out[...] = grad_gain

    tile = columns_spec(width, FEED_TILE)
    whole = whole_spec(rows, width)
    return host(
        grid, body, steps,
        [whole, whole, whole_spec(1, width), columns_spec(2, rows, FEED_TILE), tile,
         columns_spec(width, FEED_TILE, first=steps), rows_spec(FEED_TILE, width)],
        [grad, middle, gain, both, w_up, w_up, w_down],
        [whole, whole, columns_spec(2, rows, FEED_TILE), whole_spec(1, width)],
        [kind(rows, width, dtype=F32), kind(rows, width), kind(2, rows, hidden), kind(1, width, dtype=F32)],
        moves,
        scratch=[pltpu.VMEM((rows, width), F32), pltpu.VMEM((rows, width), BF)],
        cost=pl.CostEstimate(flops=6 * rows * width * hidden, bytes_accessed=6 * width * hidden, transcendentals=rows * hidden),
    )


def norm(value, gain):
    return value * lax.rsqrt(jnp.mean(value * value, axis=-1, keepdims=True) + EPSILON) * gain


def norm_back(value, gain, grad):
    inverse = lax.rsqrt(jnp.mean(value * value, axis=-1, keepdims=True) + EPSILON)
    unit = value * inverse
    grad_gain = jnp.sum(grad * unit, axis=0, keepdims=True)
    scaled = grad * gain
    pulled = inverse * (scaled - unit * jnp.mean(scaled * unit, axis=-1, keepdims=True))
    return pulled, grad_gain


def product(grid, left, left_other, right, moves=(), piece=(0, 1)):
    rows, height = left.shape
    stacked = right.ndim == 3
    full = right.shape[-1] if stacked else right.shape[-1] // 2
    half = full // piece[1]
    tile = 512 if height % 512 == 0 else height // 2
    tiles = height // tile
    fetch = left_other is None

    def part(ref, c):
        ref = ref.at[c] if stacked else ref
        start = piece[0] * half if stacked else c * full + piece[0] * half
        return ref.at[:, pl.ds(pl.multiple_of(start, 128), half)]

    def body(here, step, ins, outs, held):
        own_ref, other_ref, right_ref = ins
        own_right, other_right, total, own_sem, sems = held[:5]
        own = pltpu.make_async_copy(part(right_ref, here.c), own_right, own_sem)
        swaps = [remote(part(right_ref, 1 - here.c), other_right, sems, 0, here.swap)]
        if fetch:
            swaps.append(remote(other_ref, held[5], sems, 1, here.swap))

        @pl.when(step == 0)
        def _():
            own.start()
            for swap in swaps:
                swap.start()
            own.wait()

        @pl.when(step < tiles)
        def _():
            total[step] = dot(own_ref[...], own_right[...], (0, 0))

        @pl.when(step == tiles)
        def _():
            for swap in swaps:
                swap.wait()

        @pl.when(step >= tiles)
        def _():
            other = other_ref
            if fetch:
                other = held[5].at[:, pl.ds(pl.multiple_of((step - tiles) * tile, 128), tile)]
            outs[0][...] = (total[step - tiles] + dot(other[...], other_right[...], (0, 0))).astype(BF)

    early = lambda i: jnp.minimum(i, tiles - 1)
    late = lambda i: jnp.maximum(i - tiles, 0)
    other_spec = any_spec() if fetch else pl.BlockSpec((rows, tile), lambda i: (0, late(i)))
    outs, got = host(
        grid, body, 2 * tiles,
        [pl.BlockSpec((rows, tile), lambda i: (0, early(i))), other_spec, any_spec()],
        [left, left if fetch else left_other, right],
        [pl.BlockSpec((tile, half), lambda i: (late(i), 0))],
        [kind(height, half)],
        moves,
        scratch=[
            pltpu.VMEM((rows, half), BF),
            pltpu.VMEM((rows, half), BF),
            pltpu.VMEM((tiles, tile, half), F32),
            pltpu.SemaphoreType.DMA,
            pltpu.SemaphoreType.DMA((2, 2)),
        ] + [pltpu.VMEM((rows, height), BF)] * fetch,
        cost=pl.CostEstimate(flops=4 * rows * height * half, bytes_accessed=2 * height * half, transcendentals=0),
        reaches=True,
    )
    return outs[0], got


class Reduce:
    def __init__(self, grid, total):
        self.grid = grid
        self.parts = total.reshape(grid.J, total.shape[0] // grid.J, total.shape[1])
        self.phase = 0

    def flip(self):
        return flip_move(self.grid, self.parts, self.phase)

    def flipped(self, got):
        grid = self.grid
        if self.phase == 0:
            kept = jnp.stack(
                [
                    lax.dynamic_index_in_dim(self.parts, grid.place(2 * i, grid.c), 0, keepdims=False)
                    for i in range(grid.J // 2)
                ]
            )
        else:
            kept = self.parts[0::2]
        self.parts = (kept.astype(F32) + got.astype(F32)).astype(BF)
        self.phase += 1
        if self.phase == grid.bits:
            self.line = self.parts.reshape(2, grid.F, -1, self.parts.shape[2])

    def ring(self):
        while self.phase < self.grid.bits:
            self.flipped(send(self.grid, [self.flip()])[0])
        return ring_move(self.grid, self.line)

    def arrived(self, got):
        grid = self.grid
        here = lax.dynamic_index_in_dim(self.line, grid.f, 1, keepdims=False)
        self.summed = here.astype(F32) + sum(got[t].astype(F32) for t in range(grid.F - 1))
        give = lax.dynamic_index_in_dim(self.summed, 1 - grid.c, 0, keepdims=False)
        self.give = give.astype(BF)

    def done(self, got):
        grid = self.grid
        mine = lax.dynamic_index_in_dim(self.summed, grid.c, 0, keepdims=False)
        got = got.astype(F32)
        return jnp.concatenate(
            [jnp.where(grid.c == 0, mine, got), jnp.where(grid.c == 0, got, mine)], axis=1
        )


def local(
    n_dp,
    pieces,
    tokens,
    cotangent,
    doc_lengths,
    partner,
    memory_picks,
    attention_in,
    attention_out,
    feed_in,
    feed_out,
    norm_gains,
):
    IDS[0] = 1
    grid = Grid(n_dp, pieces)
    grid.trace()
    layers = attention_in.shape[0]
    width = tokens.shape[2]
    heads = width // HEAD_DIM
    topk = memory_picks.shape[3]
    valid_all, visible_all = jax.vmap(memory_plan)(doc_lengths, partner)
    valid = valid_all[grid.m, grid.slot].reshape(1)
    visible = visible_all[grid.m, grid.slot]
    relative = (grid.slot - jnp.arange(n_dp)) % n_dp
    bias = jnp.repeat(jnp.where(visible[relative], 0.0, MASKED), topk)[:, None].astype(F32)
    tables = rope_tables()
    picks_there = grid.swap(memory_picks)
    picks = jnp.where(grid.r == grid.c, memory_picks[grid.m, 0], picks_there[grid.m, 0])
    zero = grid.c == 0

    def both_halves(mine, other):
        return jnp.where(
            zero, jnp.concatenate([mine, other], axis=-1), jnp.concatenate([other, mine], axis=-1)
        )

    def half(value, c):
        size = value.shape[-1] // 2
        return lax.dynamic_slice_in_dim(value, c * size, size, axis=value.ndim - 1)

    hidden, gains, weights = gather_all(
        grid, tokens, norm_gains, [attention_in, attention_out, feed_in, feed_out]
    )
    gain = lambda l, i: gains[l, i][None]
    flat = lambda w: w.reshape(-1, w.shape[-1])
    saved = []
    cotangent_rows = None
    for l in range(layers):
        w_qkv, w_out = flat(weights[l][0]), flat(weights[l][1])
        memory = l == layers - 1
        coming = weights[l + 1] if l + 1 < layers else None
        moves = []
        if coming is not None:
            moves.append(spread_move(grid, coming[3], [(0, 0, 1)]))
        if later_here(l, 2):
            moves += [
                spread_move(grid, weights[l][2], [(1, 0, 2), (1, 1, 2)]),
                spread_move(grid, weights[l][3], [(2, 0, 1)]),
            ]
        split, got = project(grid, memory, tables, hidden, gain(l, 0), w_qkv, moves)
        if coming is not None:
            coming[3] = got[0]
        if later_here(l, 2):
            weights[l][2:] = got[-2:]
        normed, query = split[:2]
        (others,) = send(grid, [member_move(grid, split[2], False)])
        pairs = [split[2]] + [others[t] for t in range(grid.U - 1)]
        extra = None
        if memory:
            chosen = pick_memory(grid, picks, pairs, grid.c)
            (came,) = send(grid, [slots_move(grid, chosen, False)])
            slots = jnp.concatenate([chosen[None], came])
            slots = jnp.swapaxes(slots, 0, 1).reshape(2, n_dp * topk, -1)
            slots = both_halves(slots, grid.swap(slots))
            extra = {"query": split[3], "keys": slots[0], "values": slots[1], "bias": bias}
        moves = []
        if coming is not None:
            moves.append(spread_move(grid, coming[2], [(0, 0, 2)]))
        if later_here(l, 2):
            moves.append(spread_move(grid, weights[l][2], [(2, 0, 1)]))
        if memory:
            moves.append(regroup_move(grid, cotangent))
        attended, got = attend(grid, valid, query, pairs, extra, moves)
        if coming is not None:
            coming[2] = got[0]
        if later_here(l, 2):
            weights[l][2] = got[-2]
            for stage in range(3, grid.bits + 1):
                weights[l][2:] = send(grid, [spread_move(grid, w, [(stage, 0, 1)]) for w in weights[l][2:]])
        if memory:
            cotangent_rows = got[-1]
        middle = hidden.astype(F32) + mm(attended, w_out)
        moves = []
        if coming is not None:
            moves = [spread_move(grid, coming[2], [(0, 1, 2)]), spread_move(grid, coming[3], [(1, 0, 1)])]
        w_up, w_down = flat(weights[l][2]), flat(weights[l][3])
        (out, normed_feed, both, inner), got = feed(grid, middle, gain(l, 1), w_up, w_down, moves)
        if coming is not None:
            coming[2:] = got
        saved.append((hidden, normed, query, pairs, extra, attended, middle, normed_feed, both, inner))
        hidden = out
    weights = [[flat(w) for w in kinds] for kinds in weights]
    cotangent_rows = cotangent_rows.reshape(-1, width)
    def row_halves(value):
        value = value.astype(BF).reshape(2, grid.R, width)
        return value[:, : grid.R // 2], value[:, grid.R // 2 :]

    out_rows = row_halves(hidden)
    grad = cotangent_rows.astype(F32)
    found = [[None] * 4 for _ in range(layers)]
    grad_gains = [[None, None] for _ in range(layers)]
    layer_output, above, inner_other = [], None, None

    def took(got, reduces):
        for result, (reduce, what) in zip(got, reduces):
            (reduce.flipped if what == "flip" else reduce.arrived)(result)

    def moves_of(reduces):
        return [reduce.flip() if what == "flip" else reduce.ring() for reduce, what in reduces]

    for l in reversed(range(layers)):
        w_qkv, w_out, w_up, w_down = weights[l]
        hidden, normed, query, pairs, extra, attended, middle, normed_feed, both, inner = saved[l]
        low = grad.astype(BF)
        last_layer = above is None

        reduces = [] if last_layer else [(above[1], "flip")]
        total, got = product(grid, inner, inner_other, low, moves_of(reduces))
        took(got, reduces)
        down = Reduce(grid, total)

        reduces = [(down, "flip")]
        if not last_layer:
            reduces += [(above[0], "flip"), (above[1], "flip")] + [(up, "ring") for up in above[2]]
        moves = moves_of(reduces) + [swap_move(normed_feed), swap_move(normed), swap_move(attended)]
        if last_layer:
            moves += [swap_move(saved[l - 1][9]), regroup_back_move(grid, out_rows[0])]
        (grad, grad_low, grads, gain_feed), got = feed_back(
            grid, grad, middle, gain(l, 1), both, w_up, w_down, moves
        )
        took(got, reduces)
        normed_feed_other, normed_other, attended_other = got[len(reduces) : len(reduces) + 3]
        if last_layer:
            inner_other = got[-2]
            layer_output.append(got[-1])

        ups = []
        pieces_of_up = 1 if last_layer else 2
        for piece in range(pieces_of_up):
            if piece == 0:
                reduces = [(down, "flip")]
            else:
                reduces = [(ups[0], "flip"), (above[0], "ring"), (above[1], "ring")]
            total, got = product(
                grid, normed_feed, normed_feed_other, grads, moves_of(reduces), (piece, pieces_of_up)
            )
            took(got, reduces)
            ups.append(Reduce(grid, total))
        grad_heads = mm(grad_low, w_out, (1, 1)).astype(BF)

        reduces = [(ups[-1], "flip"), (down, "ring")]
        if not last_layer:
            reduces.append((ups[0], "flip"))
        outs, got = attend_back(grid, valid, tables, query, grad_heads, pairs, extra, moves_of(reduces))
        took(got, reduces)
        grad_query, own, others = outs[:3]
        memory_grad = None
        moves = [member_move(grid, others, True)]
        if extra is not None:
            moves.append(swap_half_move(outs[3]))
        got = send(grid, moves)
        others = got[0]
        moves = []
        if extra is not None:
            joined = half(outs[3], grid.c).astype(F32) + got[1].astype(F32)
            joined = joined.astype(BF).reshape(2, n_dp, topk, -1)
            moves = [slots_move(grid, joined, True)]
        total, got = product(grid, attended, attended_other, grad_low, moves)
        across = Reduce(grid, total)
        if extra is not None:
            total = joined[:, 0].astype(F32) + sum(got[0][t].astype(F32) for t in range(n_dp - 1))
            for t in range(1, grid.Q):
                total = total + grid.within(total.astype(BF), t).astype(F32)
            total = total.astype(BF)
            memory_grad = both_halves(total, grid.swap(total))
        reduces = [(ups[-1], "flip"), (across, "flip")]
        if not last_layer:
            reduces.append((ups[0], "ring"))
        moves = moves_of(reduces)
        if last_layer:
            moves.append(regroup_back_move(grid, out_rows[1]))
        grad_projected, got = finish_gradient(grid, grad_query, own, others, picks, memory_grad, moves)
        took(got, reduces)
        if last_layer:
            layer_output.append(got[-1])
        pulled, gain_attention = norm_back(
            hidden.astype(F32), gain(l, 0), mm(grad_projected, w_qkv, (1, 1))
        )
        grad = grad + pulled
        grad_gains[l] = [gain_attention[0], gain_feed[0]]
        reduces, moves = [], []
        if l == 0:
            small = GainSum(grid, jnp.stack([jnp.stack(pair) for pair in grad_gains]).reshape(-1, HEAD_DIM))
            reduces = [(ups[-1], "ring"), (across, "flip")]
            moves = [small.move()]
        total, got = product(grid, normed, normed_other, grad_projected, moves_of(reduces) + moves)
        took(got, reduces)
        if l == 0:
            small.took(got[-1])
        last = Reduce(grid, total)
        found[l][3] = down.done(grid.swap(down.give))
        if not last_layer:
            found[l + 1] = [r.done(grid.swap(r.give)) for r in (above[1], above[0])] + [
                feed_parts([r.done(grid.swap(r.give)) for r in above[2]]), found[l + 1][3]
            ]
        above = (across, last, ups)
    across, last, ups = above
    in_rows = row_halves(grad)
    input_grad = []
    for i, reduces in enumerate([[(last, "flip"), (across, "ring")], [(last, "flip")], [(last, "ring")]]):
        moves = moves_of(reduces)
        if i < 2:
            moves.append(regroup_back_move(grid, in_rows[i]))
        got = send(grid, moves + [small.move()])
        took(got, reduces)
        small.took(got[-1])
        if i < 2:
            input_grad.append(got[-2])
    layer_output = jnp.concatenate(layer_output, axis=1)
    input_grad = jnp.concatenate(input_grad, axis=1).astype(F32)
    found[0] = [r.done(grid.swap(r.give)) for r in (last, across)] + [
        feed_parts([r.done(grid.swap(r.give)) for r in ups]), found[0][3]
    ]
    total_gains = small.finish().reshape(layers, 2, n_dp * pieces, -1)
    device = (grid.j * 2 + grid.c) * grid.F + grid.f
    return (
        layer_output,
        input_grad,
        *(jnp.stack([found[l][i] for l in range(layers)]) for i in range(4)),
        lax.dynamic_index_in_dim(total_gains, device, 2, keepdims=False),
    )


def feed_parts(parts):
    sides = [[part[:, : part.shape[1] // 2] for part in parts], [part[:, part.shape[1] // 2 :] for part in parts]]
    return jnp.concatenate(sides[0] + sides[1], axis=1)


def solution(mesh):
    rows = P(None, ("dp", "fsdp"), None)
    in_specs = (rows, rows, P(), P(), P(None, "dp", None, None), rows, rows, rows, rows, P(None, None, ("dp", "fsdp")))
    out_specs = (rows, rows, rows, rows, rows, rows, P(None, None, ("dp", "fsdp")))
    body = functools.partial(local, mesh.shape["dp"], mesh.shape["fsdp"])
    return jax.shard_map(body, mesh=mesh, in_specs=in_specs, out_specs=out_specs, check_vma=False)
```

```python
import functools
import math

import jax
import jax.numpy as jnp
from jax import lax
from jax.experimental import pallas as pl
from jax.experimental.pallas import tpu as pltpu
from jax.sharding import PartitionSpec as P

HEAD_DIM = 128
SEG = 1024
MICRO = 2
EPSILON = 1e-06
MASKED = -1e30
SCALE = HEAD_DIM ** (-0.5)
LOG2E = 1.0 / math.log(2.0)
BF = jnp.bfloat16
F32 = jnp.float32
VMEM_LIMIT = 48 * 1024 * 1024


def slot_layout(lengths):
    slot_total = lengths.shape[0]
    slot_counts = ((lengths + SEG - 1) // SEG).astype(jnp.int32)
    slot_starts = (jnp.cumsum(slot_counts) - slot_counts).astype(jnp.int32)
    slot_index = jnp.arange(slot_total, dtype=jnp.int32)
    started = (slot_starts[None, :] <= slot_index[:, None]) & (slot_counts[None, :] > 0)
    owner_doc = (jnp.sum(started.astype(jnp.int32), axis=1) - 1).astype(jnp.int32)
    owner_pick = slot_index[None, :] == owner_doc[:, None]
    first_slot = jnp.sum(jnp.where(owner_pick, slot_starts[None, :], 0), axis=1).astype(jnp.int32)
    doc_total = jnp.sum(jnp.where(owner_pick, lengths[None, :], 0), axis=1).astype(jnp.int32)
    valid_rows = jnp.clip(doc_total - (slot_index - first_slot) * SEG, 0, SEG).astype(jnp.int32)
    return (valid_rows, owner_doc)


def memory_plan(lengths, partner_row):
    valid_rows, owner_doc = slot_layout(lengths)
    block_ids = jnp.arange(lengths.shape[0], dtype=jnp.int32)
    earlier = (block_ids[None, :] < block_ids[:, None]) & (owner_doc[None, :] == owner_doc[:, None])
    visible = earlier | (block_ids[None, :] == partner_row[:, None])
    return (valid_rows, visible)


class Grid:
    def __init__(self, n_dp, pieces):
        self.n_dp, self.F = n_dp, pieces
        self.J = n_dp // 2
        self.bits = self.J.bit_length() - 1
        self.Q = pieces // 4
        self.U = 2 * self.Q
        self.R = SEG // pieces
        self.T = 2 * self.R

    def trace(self):
        dp = lax.axis_index("dp")
        self.c, self.j, self.f = dp % 2, dp // 2, lax.axis_index("fsdp")
        self.q, self.g = self.f // self.Q, self.f % self.Q
        self.m, self.r = self.q // 2, self.q % 2
        self.k = self.c * self.Q + self.g
        self.slot = 2 * self.j + self.r

    def permute(self, value, target):
        pairs = []
        for j in range(self.J):
            for c in range(2):
                for f in range(self.F):
                    j2, c2, f2 = target(j, c, f)
                    pairs.append(((j * 2 + c) * self.F + f, (j2 * 2 + c2) * self.F + f2))
        return lax.ppermute(value, ("dp", "fsdp"), pairs)

    def swap(self, value):
        return self.permute(value, lambda j, c, f: (j, 1 - c, f))

    def ring(self, value, t):
        return self.permute(value, lambda j, c, f: (j, c, (f + t) % self.F))

    def bit(self, phase, c):
        return phase if c == 0 else self.bits - 1 - phase

    def flip(self, value, phase):
        return self.permute(value, lambda j, c, f: (j ^ (1 << self.bit(phase, c)), c, f))

    def mask(self, key, c):
        return sum(1 << self.bit(p, c) for p in range(self.bits) if key >> p & 1)

    def place(self, key, c):
        return jnp.where(c == 0, self.j ^ self.mask(key, 0), self.j ^ self.mask(key, 1))

    def member(self, value, t):
        def target(j, c, f):
            q, g = f // self.Q, f % self.Q
            k = (c * self.Q + g + t) % self.U
            return (j, k // self.Q, q * self.Q + k % self.Q)

        return self.permute(value, target)

    def within(self, value, t):
        return self.permute(
            value, lambda j, c, f: (j, c, f // self.Q * self.Q + (f % self.Q + t) % self.Q)
        )

    def slots(self, value, t):
        def target(j, c, f):
            q, g = f // self.Q, f % self.Q
            slot = (2 * j + q % 2 + t) % self.n_dp
            return (slot // 2, c, (2 * (q // 2) + slot % 2) * self.Q + g)

        return self.permute(value, target)

    def _spread(self, second):
        def target(j, c, f):
            m = f // (self.F // 2)
            m = 1 - m if second else m
            k = min(f, self.F - 1 - f)
            return (j, k // self.Q, (2 * m + c) * self.Q + k % self.Q)

        return target

    def _collect(self, second):
        there = self._spread(second)
        back = {
            there(0, c, f): (c, f) for c in range(2) for f in range(self.F)
        }
        return lambda j, c, f: (j,) + back[(0, c, f)]

    def to_units(self, value):
        here = self.f // (self.F // 2)
        first = self.permute(jnp.where(here == 0, value[0], value[1]), self._spread(False))
        second = self.permute(jnp.where(here == 0, value[1], value[0]), self._spread(True))
        return jnp.concatenate(
            [jnp.where(self.m == 0, first, second), jnp.where(self.m == 0, second, first)]
        )

    def from_units(self, value):
        low, high = value[: self.R], value[self.R :]
        first = self.permute(jnp.where(self.m == 0, low, high), self._collect(False))
        second = self.permute(jnp.where(self.m == 0, high, low), self._collect(True))
        here = self.f // (self.F // 2)
        return jnp.stack([jnp.where(here == 0, first, second), jnp.where(here == 0, second, first)])


def any_spec():
    return pl.BlockSpec(memory_space=pl.ANY)


MESH = pl.DeviceIdType.MESH


class Here:
    def __init__(self, grid):
        self.grid = grid
        dp = lax.axis_index("dp")
        self.j, self.c, self.f = dp // 2, dp % 2, lax.axis_index("fsdp")
        self.q, self.g = self.f // grid.Q, self.f % grid.Q
        self.m, self.r = self.q // 2, self.q % 2
        self.k = self.c * grid.Q + self.g
        self.swap = self.device(self.j, 1 - self.c, self.f)

    def device(self, j, c, f):
        return {"dp": 2 * j + c, "fsdp": f}

    def ring(self, t):
        return self.device(self.j, self.c, (self.f + t) % self.grid.F)

    def step(self, phase):
        first, second = (1 << self.grid.bit(phase, c) for c in (0, 1))
        return first + self.c * (second - first)

    def moved(self, j, phase):
        step = self.step(phase)
        return j + step * (1 - 2 * ((j // step) % 2))

    def flip(self, phase):
        return self.device(self.moved(self.j, phase), self.c, self.f)

    def slots(self, t):
        grid = self.grid
        slot = (2 * self.j + self.r + t) % grid.n_dp
        return self.device(slot // 2, self.c, (2 * self.m + slot % 2) * grid.Q + self.g)

    def member(self, t):
        grid = self.grid
        k = (self.k + t) % grid.U
        return self.device(self.j, k // grid.Q, self.q * grid.Q + k % grid.Q)

    def place(self, key):
        j = self.j
        for phase in range(self.grid.bits):
            if key >> phase & 1:
                j = self.moved(j, phase)
        return j

    def greet(self):
        grid = self.grid
        barrier = pltpu.get_barrier_semaphore()
        peers = [self.ring(t) for t in range(1, grid.F)]
        peers += [self.device(self.j, 1 - self.c, (self.f + t) % grid.F) for t in range(grid.F)]
        for bit in range(grid.bits):
            step = 1 << bit
            peers.append(self.device(self.j + step * (1 - 2 * ((self.j // step) % 2)), self.c, self.f))
        for peer in peers:
            pl.semaphore_signal(barrier, inc=1, device_id=peer, device_id_type=MESH)
        pl.semaphore_wait(barrier, len(peers))


def remote(source, target, sems, index, device):
    return pltpu.make_async_remote_copy(
        src_ref=source,
        dst_ref=target,
        send_sem=sems.at[0, index],
        recv_sem=sems.at[1, index],
        device_id=device,
        device_id_type=MESH,
    )


class Spread:
    def __init__(self, here, shard, whole, sems, own_sem, split):
        grid = here.grid
        self.here, self.split = here, split
        rows, width = shard.shape
        half = width // 2 if split else width

        def part(ref, c):
            if not split:
                return ref
            return ref.at[(slice(None),) * (len(ref.shape) - 1) + (pl.ds(pl.multiple_of(c * half, 128), half),)]

        j, c, f = here.j, here.c, here.f
        mine = part(whole, c)
        self.own = pltpu.make_async_copy(part(shard, c), part(whole.at[j, c, f], c), own_sem)
        other = 1 - c if split else c
        self.pre = remote(part(shard, other), part(whole.at[j, c, f], other), sems, 0, here.swap)
        at = 1
        self.hops = []
        for h in range(1, grid.F):
            hop = []
            for way in (1, -1):
                origin = f - way * (h - 1)
                inside = lambda place: (place >= 0) & (place < grid.F)
                block = mine.at[j, :, jnp.clip(origin, 0, grid.F - 1)]
                copy = remote(block, block, sems, at, here.device(j, c, (f + way + grid.F) % grid.F))
                hop.append((copy, inside(origin) & inside(f + way), inside(f - way * h)))
                at += 1
            self.hops.append(hop)
        self.flips = []
        for phase in range(grid.bits):
            sent = []
            for key in range(1 << phase):
                block = mine.at[here.place(key)]
                sent.append(remote(block, block, sems, at, here.flip(phase)))
                at += 1
            self.flips.append(sent)
        self.swaps = []
        for key in range(grid.J if split else 0):
            block = mine.at[here.place(key)]
            self.swaps.append(remote(block, block, sems, at, here.swap))
            at += 1

    @staticmethod
    def count(grid):
        return 1 + 2 * (grid.F - 1) + (grid.J - 1) + grid.J

    def begin(self):
        self.own.start()
        self.pre.start()

    def to_line(self):
        self.own.wait()
        self.pre.wait()
        self._hop(0)

    def _hop(self, h):
        for copy, sends, _ in self.hops[h]:
            pl.when(sends)(copy.start)

    def _send(self, keys):
        for key in keys:
            if self.swaps:
                self.swaps[key].start()
        for phase, sent in enumerate(self.flips):
            for key in keys:
                if key < 1 << phase:
                    sent[key].start()

    def steps(self, whole):
        def along(h):
            for copy, _, comes in self.hops[h]:
                pl.when(comes)(copy.wait_recv)
            if h + 1 < len(self.hops):
                self._hop(h + 1)
                return
            for hop in self.hops:
                for copy, sends, _ in hop:
                    pl.when(sends)(copy.wait_send)
            if whole:
                self._send([0])

        def later(phase):
            for copy in self.flips[phase]:
                copy.wait()
            self._send([key + (1 << phase) for key in range(1 << phase)])

        def last():
            for copy in self.swaps:
                copy.wait()

        line = [functools.partial(along, h) for h in range(len(self.hops))]
        if not whole:
            return line
        return line + [functools.partial(later, p) for p in range(len(self.flips))] + [last]


class Regroup:
    def __init__(self, here, source, target, sems, own_sem):
        grid = here.grid
        half = grid.F // 2
        k = jnp.minimum(here.f, grid.F - 1 - here.f)
        side = here.f // half
        self.sends = []
        for m in range(2):
            c2, f2 = k // grid.Q, (2 * m + here.c) * grid.Q + k % grid.Q
            same = (c2 == here.c) & (f2 == here.f)
            own = pltpu.make_async_copy(source.at[m], target.at[side], own_sem)
            away = pltpu.make_async_remote_copy(
                src_ref=source.at[m],
                dst_ref=target.at[side],
                send_sem=sems.at[0, m],
                recv_sem=sems.at[1, side],
                device_id=here.device(here.j, c2, f2),
                device_id_type=MESH,
            )
            self.sends.append((same, own, away))
        self.arrivals = []
        for side in range(2):
            from_f = here.k if side == 0 else grid.F - 1 - here.k
            same = (here.r == here.c) & (from_f == here.f)
            came = pltpu.make_async_remote_copy(
                src_ref=source.at[0],
                dst_ref=target.at[side],
                send_sem=sems.at[0, 0],
                recv_sem=sems.at[1, side],
                device_id=here.swap,
                device_id_type=MESH,
            )
            self.arrivals.append((same, came))

    def start(self):
        for same, own, away in self.sends:
            pl.when(same)(own.start)
            pl.when(jnp.logical_not(same))(away.start)

    def wait(self):
        for same, own, away in self.sends:
            pl.when(same)(own.wait)
            pl.when(jnp.logical_not(same))(away.wait_send)
        for same, came in self.arrivals:
            pl.when(jnp.logical_not(same))(came.wait_recv)


def gather_body(grid, layers, kinds, *refs):
    tokens, gains = refs[:2]
    shards = refs[2 : 2 + kinds]
    outs = refs[2 + kinds :]
    tokens_out, gains_out = outs[:2]
    wholes = outs[2 : 2 + layers * kinds]
    sems, own_sems, regroup_sems = outs[2 + layers * kinds :]
    here = Here(grid)
    here.greet()
    rows = Regroup(here, tokens, tokens_out, regroup_sems, own_sems.at[0])
    moves = []
    for l, i in ORDER:
        n = l * kinds + i
        move = Spread(here, shards[i].at[l], wholes[n], sems.at[n + 1], own_sems.at[n + 2], True)
        moves.append((move, not later_here(l, i)))
    moves.insert(GAINS_AT, (Spread(here, gains, gains_out, sems.at[0], own_sems.at[1], False), True))
    for move, _ in moves:
        move.begin()
    steps = [move.steps(whole) for move, whole in moves]
    count = len(steps[0])
    for at in range(AHEAD):
        moves[at][0].to_line()
    for at in range(len(moves) + count - 1):
        if at == ROWS_AT:
            rows.start()
        if at + AHEAD < len(moves):
            moves[at + AHEAD][0].to_line()
        for back in reversed(range(count)):
            if 0 <= at - back < len(moves) and back < len(steps[at - back]):
                steps[at - back][back]()
    rows.wait()


ORDER = [(0, 1), (0, 3), (0, 2), (0, 0), (1, 0), (1, 1), (1, 3), (1, 2)]
GAINS_AT, ROWS_AT, AHEAD = 3, 6, 1


def later_here(l, i):
    return l > 0 and i >= 2


def gather_all(grid, tokens, gains, shards):
    layers, kinds = shards[0].shape[0], len(shards)
    packed = jnp.zeros((8, 128), F32).at[: layers * 2, : gains.shape[2]].set(
        gains.astype(F32).reshape(layers * 2, -1)
    )
    whole = lambda shard: jax.ShapeDtypeStruct((grid.J, 2, grid.F) + shard.shape[-2:], shard.dtype)
    out_shape = [jax.ShapeDtypeStruct(tokens.shape, BF), whole(packed)]
    out_shape += [whole(shard) for _ in range(layers) for shard in shards]
    moves = 1 + layers * kinds
    outs = pl.pallas_call(
        functools.partial(gather_body, grid, layers, kinds),
        in_specs=[any_spec()] * (2 + kinds),
        out_specs=[any_spec()] * len(out_shape),
        out_shape=out_shape,
        scratch_shapes=[
            pltpu.SemaphoreType.DMA((moves, 2, Spread.count(grid))),
            pltpu.SemaphoreType.DMA((moves + 1,)),
            pltpu.SemaphoreType.DMA((2, 2)),
        ],
        compiler_params=pltpu.CompilerParams(
            collective_id=0, has_side_effects=True, vmem_limit_bytes=VMEM_LIMIT
        ),
    )(tokens, packed, *shards)
    gains_all = outs[1][..., : layers * 2, : gains.shape[2]]
    gains_all = jnp.moveaxis(gains_all, 3, 0).reshape(layers, 2, -1)
    weights = [list(outs[2 + l * kinds : 2 + (l + 1) * kinds]) for l in range(layers)]
    return outs[0].reshape(-1, tokens.shape[2]), gains_all, weights


def unless(condition, act):
    if condition is None:
        act()
    else:
        pl.when(jnp.logical_not(condition))(act)


class Move:
    def __init__(self, array, shape, count, copies, plan=None, in_place=False):
        self.array, self.shape, self.count, self.copies = array, shape, count, copies
        self.plan, self.in_place = plan or self._plain, in_place

    def _plain(self, here, source, target, sends, recvs, base):
        found = []
        for i, (what, where, peer, giver) in enumerate(self.copies(here, source, target)):
            copy = pltpu.make_async_remote_copy(
                src_ref=what,
                dst_ref=where,
                send_sem=sends.at[base + i],
                recv_sem=recvs.at[base + i],
                device_id=peer,
                device_id_type=MESH,
            )
            found.append((copy, None, None, giver, copy, None))
        return found


def flip_move(grid, parts, phase):
    count = parts.shape[0] // 2

    def copies(here, source, target):
        found = []
        for i in range(count):
            at = here.place(2 * i + 1) if phase == 0 else 2 * i + 1
            peer = here.flip(phase)
            found.append((source.at[at], target.at[i], peer, peer))
        return found

    return Move(parts, (count,) + parts.shape[1:], count, copies)


def ring_move(grid, line, distances):
    def copies(here, source, target):
        return [
            (source.at[:, (here.f + t) % grid.F], target.at[i], here.ring(t), here.ring(grid.F - t))
            for i, t in enumerate(distances)
        ]

    return Move(line, (len(distances), 2) + line.shape[2:], len(distances), copies)


def swap_move(array, give=None):
    def copies(here, source, target):
        return [(source if give is None else source.at[give(here)], target, here.swap, here.swap)]

    return Move(array, array.shape if give is None else array.shape[1:], 1, copies)


def swap_half_move(array):
    half = array.shape[-1] // 2

    def copies(here, source, target):
        start = pl.multiple_of((1 - here.c) * half, 128)
        return [(source.at[:, :, pl.ds(start, half)], target, here.swap, here.swap)]

    return Move(array, array.shape[:-1] + (half,), 1, copies)


def slots_move(grid, array, back):
    def copies(here, source, target):
        found = []
        for t in range(1, grid.n_dp):
            ahead, behind = here.slots(t), here.slots(grid.n_dp - t)
            if back:
                found.append((source.at[:, t], target.at[t - 1], behind, ahead))
            else:
                found.append((source, target.at[t - 1], ahead, behind))
        return found

    shape = array.shape if not back else array.shape[:1] + array.shape[2:]
    return Move(array, (grid.n_dp - 1,) + shape, grid.n_dp - 1, copies)


def member_move(grid, array, back):
    def copies(here, source, target):
        found = []
        for t in range(1, grid.U):
            ahead, behind = here.member(t), here.member(grid.U - t)
            if back:
                found.append((source.at[t - 1], target.at[t - 1], behind, ahead))
            else:
                found.append((source, target.at[t - 1], ahead, behind))
        return found

    shape = array.shape[1:] if back else array.shape
    return Move(array, (grid.U - 1,) + shape, grid.U - 1, copies)


def spread_move(grid, whole, stages):
    half = whole.shape[-1] // 2

    def keys_of(stage):
        return [0] if stage == 0 else range(1 << (stage - 1), 1 << stage)

    def copies(here, source, target):
        found = []
        for stage, part, parts in stages:
            size = half // parts
            columns = pl.ds(pl.multiple_of(here.c * half + part * size, 128), size)
            mine = target.at[:, :, :, :, columns]
            for key in keys_of(stage):
                block = mine.at[here.place(key)]
                found.append((block, block, here.swap, here.swap))
                for phase in range(stage, grid.bits):
                    found.append((block, block, here.flip(phase), here.flip(phase)))
        return found

    count = sum(len(keys_of(stage)) * (1 + grid.bits - stage) for stage, _, _ in stages)
    return Move(whole, whole.shape, count, copies, in_place=True)


def peer_move(array, peer):
    return Move(array, array.shape, 1, lambda here, source, target: [(source, target, peer(here), peer(here))])


def line_move(grid, array):
    def copies(here, source, target):
        return [(source, target.at[t - 1], here.ring(t), here.ring(grid.F - t)) for t in range(1, grid.F)]

    return Move(array, (grid.F - 1,) + array.shape, grid.F - 1, copies)


def regroup_move(grid, array):
    def plan(here, source, target, sends, recvs, base):
        found = []
        k = jnp.minimum(here.f, grid.F - 1 - here.f)
        side = here.f // (grid.F // 2)
        for m in range(2):
            c2, f2 = k // grid.Q, (2 * m + here.c) * grid.Q + k % grid.Q
            same = (c2 == here.c) & (f2 == here.f)
            away = pltpu.make_async_remote_copy(
                src_ref=source.at[m],
                dst_ref=target.at[side],
                send_sem=sends.at[base + m],
                recv_sem=recvs.at[base + side],
                device_id=here.device(here.j, c2, f2),
                device_id_type=MESH,
            )
            own = pltpu.make_async_copy(source.at[m], target.at[side], sends.at[base + m])
            from_f = here.k if m == 0 else grid.F - 1 - here.k
            same_in = (here.r == here.c) & (from_f == here.f)
            came = pltpu.make_async_remote_copy(
                src_ref=source.at[0],
                dst_ref=target.at[m],
                send_sem=sends.at[base],
                recv_sem=recvs.at[base + m],
                device_id=here.swap,
                device_id_type=MESH,
            )
            found.append((away, same, own, here.device(here.j, here.r, from_f), came, same_in))
        return found

    return Move(array, array.shape, 2, None, plan)


def regroup_back_move(grid, array):
    def plan(here, source, target, sends, recvs, base):
        found = []
        for piece in range(2):
            f = here.k if piece == 0 else grid.F - 1 - here.k
            same = (here.r == here.c) & (f == here.f)
            away = pltpu.make_async_remote_copy(
                src_ref=source.at[piece],
                dst_ref=target.at[here.m],
                send_sem=sends.at[base + piece],
                recv_sem=recvs.at[base + here.m],
                device_id=here.device(here.j, here.r, f),
                device_id_type=MESH,
            )
            own = pltpu.make_async_copy(source.at[piece], target.at[here.m], sends.at[base + piece])
            k = jnp.minimum(here.f, grid.F - 1 - here.f)
            c2, f2 = k // grid.Q, (2 * piece + here.c) * grid.Q + k % grid.Q
            same_in = (c2 == here.c) & (f2 == here.f)
            came = pltpu.make_async_remote_copy(
                src_ref=source.at[0],
                dst_ref=target.at[piece],
                send_sem=sends.at[base],
                recv_sem=recvs.at[base + piece],
                device_id=here.swap,
                device_id_type=MESH,
            )
            found.append((away, same, own, here.device(here.j, c2, f2), came, same_in))
        return found

    return Move(array, array.shape, 2, None, plan)


IDS = [1]


def host(grid, body, steps, in_specs, operands, out_specs, out_shape, moves=(), scratch=(), cost=None, reaches=None):
    counts = [len(operands), len(moves), len(out_shape), len(moves), len(scratch)]

    def kernel(*refs):
        parts, at = [], 0
        for count in counts:
            parts.append(refs[at : at + count])
            at += count
        ins, sources, outs, targets, held = parts
        here = Here(grid)
        step = pl.program_id(0)
        planned = []
        if moves:
            sends, recvs = refs[at:]
            base = 0
            for move, source, target in zip(moves, sources, targets):
                planned += move.plan(here, source, target, sends, recvs, base)
                base += move.count

        if moves or reaches:

            @pl.when(step == 0)
            def _():
                barrier = pltpu.get_barrier_semaphore()
                givers = reaches(here) if reaches else []
                for giver in givers:
                    pl.semaphore_signal(barrier, inc=1, device_id=giver, device_id_type=MESH)
                for _, _, _, giver, _, same_in in planned:
                    signal = functools.partial(
                        pl.semaphore_signal, barrier, inc=1, device_id=giver, device_id_type=MESH
                    )
                    unless(same_in, signal)
                due = len(givers) + sum(same is None for _, same, _, _, _, _ in planned)
                for _, same, _, _, _, _ in planned:
                    if same is not None:
                        due = due + 1 - same.astype(jnp.int32)
                pl.semaphore_wait(barrier, due)
                for away, same, own, _, _, _ in planned:
                    unless(same, away.start)
                    if same is not None:
                        pl.when(same)(own.start)

        if body is not None:
            body(here, step, ins, outs, held)
        if moves:

            @pl.when(step == steps - 1)
            def _():
                for away, same, own, _, came, same_in in planned:
                    unless(same, away.wait_send)
                    if same is not None:
                        pl.when(same)(own.wait)
                    unless(same_in, came.wait_recv)

    total = sum(move.count for move in moves)
    extra = {}
    sems = []
    if moves or reaches:
        extra = {"collective_id": IDS[0], "has_side_effects": True}
        IDS[0] += 1
    if moves:
        sems = [pltpu.SemaphoreType.DMA((total,)), pltpu.SemaphoreType.DMA((total,))]
    outs = pl.pallas_call(
        kernel,
        grid=(steps,),
        in_specs=list(in_specs) + [any_spec()] * len(moves),
        out_specs=list(out_specs) + [any_spec()] * len(moves),
        out_shape=list(out_shape) + [jax.ShapeDtypeStruct(m.shape, m.array.dtype) for m in moves],
        scratch_shapes=list(scratch) + sems,
        input_output_aliases={
            len(operands) + i: len(out_shape) + i for i, move in enumerate(moves) if move.in_place
        },
        compiler_params=pltpu.CompilerParams(vmem_limit_bytes=VMEM_LIMIT, **extra),
        cost_estimate=cost,
    )(*operands, *[move.array for move in moves])
    return outs[: len(out_shape)], outs[len(out_shape) :]


def send(grid, moves):
    return host(grid, None, 1, [], [], [], [], moves)[1]


class GainSum:
    def __init__(self, grid, total):
        self.grid, self.total, self.stage = grid, total, 0

    def move(self):
        grid, phase = self.grid, self.stage - 1
        if self.stage == 0:
            return swap_move(self.total)
        if phase < grid.bits:
            return peer_move(self.total, lambda here: here.flip(phase))
        return line_move(grid, self.total)

    def took(self, got):
        if self.stage > self.grid.bits:
            got = sum(got[t] for t in range(self.grid.F - 1))
        self.total = self.total + got
        self.stage += 1

    def finish(self):
        while self.stage <= self.grid.bits + 1:
            self.took(send(self.grid, [self.move()])[0])
        return self.total


def rope_tables():
    half_dim = HEAD_DIM // 2
    frequency = jnp.exp(
        jnp.arange(half_dim, dtype=F32) * (-2.0 * math.log(10000.0) / HEAD_DIM)
    )
    angles = jnp.arange(SEG, dtype=jnp.int32).astype(F32)[:, None] * frequency[None, :]
    cos, sin = jnp.cos(angles), jnp.sin(angles)
    return (jnp.concatenate([cos, cos], axis=-1), jnp.concatenate([-sin, sin], axis=-1))


def turn(values, cos, sin):
    return values * cos + pltpu.roll(values, HEAD_DIM // 2, 1) * sin


def smem():
    return pl.BlockSpec(memory_space=pltpu.SMEM)


def whole_spec(*shape):
    return pl.BlockSpec(shape, lambda i: (0,) * len(shape))


def columns_spec(*shape, first=0):
    return pl.BlockSpec(shape, lambda i: (0,) * (len(shape) - 1) + (i + first,))


def rows_spec(*shape):
    return pl.BlockSpec(shape, lambda i: (i,) + (0,) * (len(shape) - 1))


def kind(*shape, dtype=BF):
    return jax.ShapeDtypeStruct(shape, dtype)


def piece_start(grid, member, part):
    return (member if part == 0 else grid.F - 1 - member) * grid.R


def table_rows(grid, table_ref, member, part):
    start = pl.multiple_of(piece_start(grid, member, part), grid.R)
    return table_ref[pl.ds(start, grid.R), :]


def dot(left, right, contract):
    return lax.dot_general(
        left, right, (((contract[0],), (contract[1],)), ((), ())), preferred_element_type=F32
    )


def mm(left, right, contract=(1, 0)):
    return dot(left, right, contract)


def project(grid, memory, tables, hidden, gain, weight, moves=()):
    rows, width = hidden.shape
    heads = weight.shape[1] // (3 * HEAD_DIM)
    together = 2
    size = together * HEAD_DIM
    steps = heads // together
    count = 3 if memory else 2

    width_out = heads * HEAD_DIM

    def sends(here, held, target, step):
        columns = pl.ds(pl.multiple_of(step * size, 128), size)
        return [
            pltpu.make_async_remote_copy(
                src_ref=held[0].at[:, :, columns],
                dst_ref=target.at[t - 1, :, :, columns],
                send_sem=held[1].at[0, t - 1, step],
                recv_sem=held[1].at[1, t - 1, step],
                device_id=here.member(t),
                device_id_type=MESH,
            )
            for t in range(1, grid.U)
        ]

    def body(here, step, ins, outs, held):
        cos_ref, sin_ref, hidden_ref, gain_ref = ins[:4]
        normed_ref, q_out, kv_out, others = outs[:4]

        @pl.when(step == 0)
        def _():
            normed_ref[...] = norm(hidden_ref[...].astype(F32), gain_ref[...]).astype(BF)

        for part in range(2):
            at = pl.ds(part * grid.R, grid.R)
            cos = table_rows(grid, cos_ref, here.k, part)
            sin = table_rows(grid, sin_ref, here.k, part)
            normed = normed_ref[at, :]
            query, key, value = (dot(normed, w[...], (1, 0)) for w in ins[4:])
            kv_out[1, at, :] = value.astype(BF)
            for h in range(together):
                columns = slice(h * HEAD_DIM, (h + 1) * HEAD_DIM)
                q_out[at, columns] = turn(query[:, columns], cos, sin).astype(BF)
                kv_out[0, at, columns] = turn(key[:, columns], cos, sin).astype(BF)
            if memory:
                kv_out[2, at, :] = key.astype(BF)
                outs[4][at, :] = query.astype(BF)
        held[0][:, :, pl.ds(pl.multiple_of(step * size, 128), size)] = kv_out[...]
        for copy in sends(here, held, others, step):
            copy.start()

        @pl.when(step == steps - 1)
        def _():
            for i in range(steps):
                for copy in sends(here, held, others, i):
                    copy.wait()

    piece = columns_spec(rows, size)
    table = whole_spec(SEG, HEAD_DIM)
    flat = kind(rows, width_out)
    return host(
        grid,
        body,
        steps,
        [table, table, whole_spec(rows, width), whole_spec(1, width)]
        + [columns_spec(width, size, first=i * steps) for i in range(3)],
        [*tables, hidden, gain, weight, weight, weight],
        [whole_spec(rows, width), piece, columns_spec(count, rows, size), any_spec()] + [piece] * memory,
        [kind(rows, width), flat, kind(count, rows, width_out), kind(grid.U - 1, count, rows, width_out)]
        + [flat] * memory,
        moves,
        scratch=[
            pltpu.VMEM((count, rows, width_out), BF),
            pltpu.SemaphoreType.DMA((2, grid.U - 1, steps)),
        ],
        cost=pl.CostEstimate(
            flops=2 * rows * width * weight.shape[1], bytes_accessed=2 * width * weight.shape[1], transcendentals=0
        ),
        reaches=lambda here: [here.member(grid.U - t) for t in range(1, grid.U)],
    )


def part_scores(grid, here, valid, part, query, keys):
    shape = (grid.R, grid.R)
    apart = lax.broadcasted_iota(jnp.int32, shape, 0) - lax.broadcasted_iota(jnp.int32, shape, 1)
    found = []
    for t in range(grid.U):
        member = (here.k - t + grid.U) % grid.U
        for side in range(part + 1):
            score = dot(keys[t][side * grid.R : (side + 1) * grid.R], query, (1, 1))
            if side == part:
                start = piece_start(grid, member, side)
                allowed = apart <= piece_start(grid, here.k, part) - start
                if side == 1:
                    down = lax.broadcasted_iota(jnp.int32, shape, 0)
                    allowed = allowed & (down < valid - start)
                score = jnp.where(allowed, score, MASKED)
            found.append((t, side, score))
    return found


def softmax_parts(scores):
    top = functools.reduce(jnp.maximum, [jnp.max(s, axis=0, keepdims=True) for s in scores])
    powers = [jnp.exp2((s - top) * (SCALE * LOG2E)) for s in scores]
    inverse = 1.0 / sum(jnp.sum(p, axis=0, keepdims=True) for p in powers)
    return [p * inverse for p in powers]


def attention_cost(grid, heads, memory_rows, products):
    pairs = grid.T * (SEG * 3 // 4 + memory_rows) * heads
    return pl.CostEstimate(
        flops=2 * products * HEAD_DIM * pairs,
        bytes_accessed=2 * HEAD_DIM * heads * 4 * (SEG + memory_rows),
        transcendentals=pairs,
    )


def memory_operands(grid, extra):
    rows = extra["memory"].shape[1]
    return [extra["query"], extra["memory"], extra["bias"]], [
        columns_spec(grid.T, HEAD_DIM), columns_spec(2, rows, HEAD_DIM), whole_spec(rows, 1)
    ], rows


def attend(grid, valid, query, pairs, extra, moves=()):
    rows, width = query.shape
    heads = width // HEAD_DIM
    R, U = grid.R, grid.U

    def body(here, step, ins, outs, held):
        valid_ref, q_ref, kv_refs, refs = ins[0], ins[1], ins[2 : 2 + U], ins[2 + U :]
        keys, values = [r[0] for r in kv_refs], [r[1] for r in kv_refs]
        for part in range(2):
            at = pl.ds(part * R, R)
            found = part_scores(grid, here, valid_ref[0], part, q_ref[at, :], keys)
            scores = [s for _, _, s in found]
            mixed = [values[t][side * R : (side + 1) * R] for t, side, _ in found]
            if extra is not None:
                scores.append(dot(refs[1][0], refs[0][at, :], (1, 1)) + refs[2][...])
                mixed.append(refs[1][1])
            total = sum(
                dot(value, p.astype(BF), (0, 0)) for value, p in zip(mixed, softmax_parts(scores))
            )
            outs[0][at, :] = total.T.astype(BF)

    piece = columns_spec(rows, HEAD_DIM)
    operands = [valid, query, *pairs]
    specs = [smem(), piece] + [columns_spec(2, rows, HEAD_DIM)] * U
    memory_rows = 0
    if extra is not None:
        more, more_specs, memory_rows = memory_operands(grid, extra)
        operands, specs = operands + more, specs + more_specs
    outs, got = host(
        grid, body, heads, specs, operands, [piece], [kind(rows, width)], moves,
        cost=attention_cost(grid, heads, memory_rows, 2),
    )
    return outs[0], got


def attend_back(grid, valid, tables, query, grad, pairs, extra, moves=()):
    rows, width = query.shape
    heads = width // HEAD_DIM
    R, U = grid.R, grid.U
    per = heads // 2

    def sends(here, held, target, h):
        columns = pl.ds(pl.multiple_of(h * HEAD_DIM, HEAD_DIM), HEAD_DIM)
        return [
            pltpu.make_async_remote_copy(
                src_ref=held[0].at[h, t - 1],
                dst_ref=target.at[t - 1, :, :, columns],
                send_sem=held[1].at[0, t - 1, h],
                recv_sem=held[1].at[1, t - 1, h],
                device_id=here.member(U - t),
                device_id_type=MESH,
            )
            for t in range(1, U)
        ]

    def memory_send(here, held, target, h):
        columns = pl.ds(pl.multiple_of(h * HEAD_DIM, HEAD_DIM), HEAD_DIM)
        return pltpu.make_async_remote_copy(
            src_ref=held[2].at[h],
            dst_ref=target.at[:, :, columns],
            send_sem=held[3].at[0, h],
            recv_sem=held[3].at[1, h],
            device_id=here.swap,
            device_id_type=MESH,
        )

    def body(here, step, ins, outs, held):
        valid_ref, cos_ref, sin_ref, q_ref, g_ref = ins[:5]
        kv_refs, refs = ins[5 : 5 + U], ins[5 + U :]
        keys, values = [r[0] for r in kv_refs], [r[1] for r in kv_refs]
        grad_keys, grad_values = {}, {}

        def add(store, at, value):
            store[at] = store[at] + value if at in store else value

        for part in range(2):
            at_rows = pl.ds(part * R, R)
            asked, grads_in = q_ref[at_rows, :], g_ref[at_rows, :]
            found = part_scores(grid, here, valid_ref[0], part, asked, keys)
            places = [(t, side) for t, side, _ in found]
            scores = [s for _, _, s in found]
            part_keys = [keys[t][side * R : (side + 1) * R] for t, side in places]
            part_values = [values[t][side * R : (side + 1) * R] for t, side in places]
            queries = [asked] * len(places)
            if extra is not None:
                places.append("memory")
                queries.append(refs[0][at_rows, :])
                scores.append(dot(refs[1][0], queries[-1], (1, 1)) + refs[2][...])
                part_keys.append(refs[1][0])
                part_values.append(refs[1][1])
            probs = softmax_parts(scores)
            grads = [dot(value, grads_in, (1, 1)) for value in part_values]
            inner = sum(jnp.sum(p * d, axis=0, keepdims=True) for p, d in zip(probs, grads))
            local_query, raw_query = None, None
            for at, p, d, key, by in zip(places, probs, grads, part_keys, queries):
                moved = (p * (d - inner)).astype(BF)
                add(grad_keys, at, dot(moved, by, (1, 0)))
                add(grad_values, at, dot(p.astype(BF), grads_in, (1, 0)))
                back = dot(key, moved, (0, 0))
                if at == "memory":
                    raw_query = back
                else:
                    local_query = back if local_query is None else local_query + back
            cos = table_rows(grid, cos_ref, here.k, part)
            sin = table_rows(grid, sin_ref, here.k, part)
            result = turn(local_query.T, cos, -sin)
            if extra is not None:
                result = result + raw_query.T
            outs[0][at_rows, :] = (result * SCALE).astype(BF)
        for t in range(U):
            member = (here.k - t + U) % U
            for side in range(2):
                at_rows = pl.ds(side * R, R)
                cos = table_rows(grid, cos_ref, member, side)
                sin = table_rows(grid, sin_ref, member, side)
                key = turn(grad_keys[(t, side)], cos, -sin) * SCALE
                if t == 0:
                    outs[1][0, at_rows, :] = key
                    outs[1][1, at_rows, :] = grad_values[(t, side)]
                else:
                    held[0][step, t - 1, 0, at_rows, :] = key.astype(BF)
                    held[0][step, t - 1, 1, at_rows, :] = grad_values[(t, side)].astype(BF)
        for copy in sends(here, held, outs[2], step):
            copy.start()
        if extra is not None:
            memory_key = (grad_keys["memory"] * SCALE).astype(BF)
            memory_value = grad_values["memory"].astype(BF)
            outs[3][0] = memory_key
            outs[3][1] = memory_value

            @pl.when(step // per == 1 - here.c)
            def _():
                held[2][step % per, 0] = memory_key
                held[2][step % per, 1] = memory_value
                memory_send(here, held, outs[4], step % per).start()

        @pl.when(step == heads - 1)
        def _():
            for h in range(heads):
                for copy in sends(here, held, outs[2], h):
                    copy.wait()
            if extra is not None:
                for h in range(per):
                    memory_send(here, held, outs[4], h).wait()

    piece = columns_spec(rows, HEAD_DIM)
    pair = columns_spec(2, rows, HEAD_DIM)
    table = whole_spec(SEG, HEAD_DIM)
    operands = [valid, *tables, query, grad, *pairs]
    specs = [smem(), table, table, piece, piece] + [pair] * U
    out_shape = [kind(rows, width), kind(2, rows, width, dtype=F32), kind(U - 1, 2, rows, width)]
    out_specs = [piece, pair, any_spec()]
    scratch = [pltpu.VMEM((heads, U - 1, 2, rows, HEAD_DIM), BF), pltpu.SemaphoreType.DMA((2, U - 1, heads))]
    memory_rows = 0
    if extra is not None:
        more, more_specs, memory_rows = memory_operands(grid, extra)
        operands, specs = operands + more, specs + more_specs
        out_shape += [kind(2, memory_rows, width), kind(2, memory_rows, width // 2)]
        out_specs += [columns_spec(2, memory_rows, HEAD_DIM), any_spec()]
        scratch += [pltpu.VMEM((per, 2, memory_rows, HEAD_DIM), BF), pltpu.SemaphoreType.DMA((2, per))]

    def reaches(here):
        return [here.member(t) for t in range(1, U)] + [here.swap] * (extra is not None)

    return host(
        grid, body, heads, specs, operands, out_specs, out_shape, moves,
        scratch=scratch,
        cost=attention_cost(grid, heads, memory_rows, 5),
        reaches=reaches,
    )


def pick_memory(grid, picks, stacked, c):
    heads, topk = picks.shape
    per = heads // 2
    R, U = grid.R, grid.U

    def body(info_ref, picks_ref, *refs):
        chosen_from, out_ref = refs[:U], refs[U]
        here = Here(grid)
        picked = picks_ref[0]
        key, value = 0.0, 0.0
        for t in range(U):
            member = (here.k - t + U) % U
            for side in range(2):
                across = lax.broadcasted_iota(jnp.int32, (picked.shape[0], R), 1)
                chosen = (picked == across + piece_start(grid, member, side)).astype(BF)
                at = pl.ds(side * R, R)
                key = key + dot(chosen, chosen_from[t][2, at, :], (1, 0))
                value = value + dot(chosen, chosen_from[t][1, at, :], (1, 0))
        out_ref[0] = key.astype(BF)
        out_ref[1] = value.astype(BF)

    at = lambda h, info: info[0] * per + h
    piece = pl.BlockSpec((3, grid.T, HEAD_DIM), lambda h, info: (0, 0, at(h, info)))
    return pl.pallas_call(
        body,
        grid_spec=pltpu.PrefetchScalarGridSpec(
            num_scalar_prefetch=1,
            grid=(per,),
            in_specs=[pl.BlockSpec((1, topk, 1), lambda h, info: (at(h, info), 0, 0))] + [piece] * U,
            out_specs=pl.BlockSpec((2, topk, HEAD_DIM), lambda h, info: (0, 0, h)),
        ),
        out_shape=kind(2, topk, per * HEAD_DIM),
        compiler_params=pltpu.CompilerParams(vmem_limit_bytes=VMEM_LIMIT),
        cost_estimate=pl.CostEstimate(
            flops=4 * topk * SEG * HEAD_DIM * per, bytes_accessed=4 * SEG * HEAD_DIM * per, transcendentals=0
        ),
    )(c.reshape(1).astype(jnp.int32), picks[:, :, None], *stacked)


def gather_memory(grid, chosen):
    n = grid.n_dp
    half = chosen.shape[2]

    def body(here, step, ins, outs, held):
        source, target = ins[0], outs[0]
        own_sem, sems = held
        mine = target.at[:, :, :, pl.ds(pl.multiple_of(here.c * half, 128), half)]
        own = pltpu.make_async_copy(source, mine.at[:, 0], own_sem)
        across = [remote(source, mine.at[:, t], sems, t, here.slots(t)) for t in range(1, n)]
        swaps = [remote(source, mine.at[:, 0], sems, n, here.swap)]
        swaps += [remote(mine.at[:, t], mine.at[:, t], sems, n + t, here.swap) for t in range(1, n)]
        for copy in across + [swaps[0], own]:
            copy.start()
        for t in range(1, n):
            across[t - 1].wait_recv()
            swaps[t].start()
        own.wait()
        for copy in across:
            copy.wait_send()
        for copy in swaps:
            copy.wait()

    outs, _ = host(
        grid, body, 1, [any_spec()], [chosen], [any_spec()], [kind(2, n, chosen.shape[1], 2 * half)],
        scratch=[pltpu.SemaphoreType.DMA, pltpu.SemaphoreType.DMA((2, 2 * n))],
        reaches=lambda here: [here.slots(n - t) for t in range(1, n)] + [here.swap],
    )
    return outs[0]


def finish_gradient(grid, grad_query, own, others, picks, memory, moves=()):
    rows, width = grad_query.shape
    heads = width // HEAD_DIM
    R, U = grid.R, grid.U

    def body(here, step, ins, outs, held):
        dq_ref, own_ref, others_ref = ins[:3]
        out_ref = outs[0]

        @pl.when(step == 0)
        def _():
            out_ref[...] = dq_ref[...]

        @pl.when(step > 0)
        def _():
            for side in range(2):
                at = pl.ds(side * R, R)
                for h in range(heads):
                    columns = pl.ds(h * HEAD_DIM, HEAD_DIM)
                    value = own_ref[0, at, columns]
                    for t in range(U - 1):
                        value = value + others_ref[t, 0, at, columns].astype(F32)
                    if memory is not None:
                        picked = ins[3][h]
                        down = lax.broadcasted_iota(jnp.int32, (R, picked.shape[1]), 0)
                        chosen = (down + piece_start(grid, here.k, side) == picked).astype(BF)
                        value = value + dot(chosen, ins[4][0, :, columns], (1, 0))
                    out_ref[at, columns] = value.astype(BF)

    which = lambda b: jnp.maximum(b - 1, 0)
    operands = [grad_query, own, others]
    specs = [
        whole_spec(rows, width),
        pl.BlockSpec((1, rows, width), lambda b: (which(b), 0, 0)),
        pl.BlockSpec((U - 1, 1, rows, width), lambda b: (0, which(b), 0, 0)),
    ]
    if memory is not None:
        topk = picks.shape[1]
        operands += [picks[:, None, :], memory]
        specs += [
            whole_spec(heads, 1, topk),
            pl.BlockSpec((1, topk, width), lambda b: (which(b), 0, 0)),
        ]
    outs, got = host(
        grid, body, 3, specs, operands, [columns_spec(rows, width)], [kind(rows, 3 * width)], moves,
        cost=pl.CostEstimate(flops=2 * rows * width, bytes_accessed=16 * rows * width, transcendentals=0),
    )
    return outs[0], got


FEED_TILE = 256


def feed(grid, middle, gain, w_up, w_down, moves=()):
    rows, width = middle.shape
    hidden = w_down.shape[0]
    steps = hidden // FEED_TILE

    def body(here, step, ins, outs, held):
        middle_ref, gain_ref, gate_w, up_w, down_w = ins
        out_ref, normed_ref, both_ref, inner_ref = outs

        @pl.when(step == 0)
        def _():
            value = middle_ref[...]
            normed_ref[...] = norm(value, gain_ref[...]).astype(BF)
            held[0][...] = value

        normed = normed_ref[...]
        gate, up = dot(normed, gate_w[...], (1, 0)), dot(normed, up_w[...], (1, 0))
        both_ref[0] = gate.astype(BF)
        both_ref[1] = up.astype(BF)
        inner = (gate / (1.0 + jnp.exp(-gate)) * up).astype(BF)
        inner_ref[...] = inner
        held[0][...] += dot(inner, down_w[...], (1, 0))

        @pl.when(step == steps - 1)
        def _():
            out_ref[...] = held[0][...]

    tile = columns_spec(width, FEED_TILE)
    return host(
        grid, body, steps,
        [whole_spec(rows, width), whole_spec(1, width), tile, columns_spec(width, FEED_TILE, first=steps), rows_spec(FEED_TILE, width)],
        [middle, gain, w_up, w_up, w_down],
        [whole_spec(rows, width), whole_spec(rows, width), columns_spec(2, rows, FEED_TILE), columns_spec(rows, FEED_TILE)],
        [kind(rows, width, dtype=F32), kind(rows, width), kind(2, rows, hidden), kind(rows, hidden)],
        moves,
        scratch=[pltpu.VMEM((rows, width), F32)],
        cost=pl.CostEstimate(flops=6 * rows * width * hidden, bytes_accessed=6 * width * hidden, transcendentals=rows * hidden),
    )


def feed_back(grid, grad, middle, gain, both, w_up, w_down, moves=()):
    rows, width = grad.shape
    hidden = w_down.shape[0]
    steps = hidden // FEED_TILE

    def body(here, step, ins, outs, held):
        grad_ref, middle_ref, gain_ref, both_ref, gate_w, up_w, down_w = ins
        out_ref, low_ref, grads_ref, gain_out = outs
        total = held[0]

        @pl.when(step == 0)
        def _():
            held[1][...] = grad_ref[...].astype(BF)
            total[...] = jnp.zeros_like(total)

        grad_inner = dot(held[1][...], down_w[...], (1, 1))
        gate, up = both_ref[0].astype(F32), both_ref[1].astype(F32)
        sigmoid = 1.0 / (1.0 + jnp.exp(-gate))
        scaled = grad_inner * sigmoid
        grad_gate = (scaled * up * (1.0 + gate * (1.0 - sigmoid))).astype(BF)
        grad_up = (scaled * gate).astype(BF)
        grads_ref[0] = grad_gate
        grads_ref[1] = grad_up
        total[...] += dot(grad_gate, gate_w[...], (1, 1)) + dot(grad_up, up_w[...], (1, 1))

        @pl.when(step == steps - 1)
        def _():
            pulled, grad_gain = norm_back(middle_ref[...], gain_ref[...], total[...])
            result = grad_ref[...] + pulled
            out_ref[...] = result
            low_ref[...] = result.astype(BF)
            gain_out[...] = grad_gain

    tile = columns_spec(width, FEED_TILE)
    whole = whole_spec(rows, width)
    return host(
        grid, body, steps,
        [whole, whole, whole_spec(1, width), columns_spec(2, rows, FEED_TILE), tile,
         columns_spec(width, FEED_TILE, first=steps), rows_spec(FEED_TILE, width)],
        [grad, middle, gain, both, w_up, w_up, w_down],
        [whole, whole, columns_spec(2, rows, FEED_TILE), whole_spec(1, width)],
        [kind(rows, width, dtype=F32), kind(rows, width), kind(2, rows, hidden), kind(1, width, dtype=F32)],
        moves,
        scratch=[pltpu.VMEM((rows, width), F32), pltpu.VMEM((rows, width), BF)],
        cost=pl.CostEstimate(flops=6 * rows * width * hidden, bytes_accessed=6 * width * hidden, transcendentals=rows * hidden),
    )


def norm(value, gain):
    return value * lax.rsqrt(jnp.mean(value * value, axis=-1, keepdims=True) + EPSILON) * gain


def norm_back(value, gain, grad):
    inverse = lax.rsqrt(jnp.mean(value * value, axis=-1, keepdims=True) + EPSILON)
    unit = value * inverse
    grad_gain = jnp.sum(grad * unit, axis=0, keepdims=True)
    scaled = grad * gain
    pulled = inverse * (scaled - unit * jnp.mean(scaled * unit, axis=-1, keepdims=True))
    return pulled, grad_gain


def product(grid, left, left_other, right, moves=(), piece=(0, 1)):
    rows, height = left.shape
    stacked = right.ndim == 3
    full = right.shape[-1] if stacked else right.shape[-1] // 2
    half = full // piece[1]
    tile = 512 if height % 512 == 0 else height // 2
    tiles = height // tile
    fetch = left_other is None

    def part(ref, c):
        ref = ref.at[c] if stacked else ref
        start = piece[0] * half if stacked else c * full + piece[0] * half
        return ref.at[:, pl.ds(pl.multiple_of(start, 128), half)]

    def body(here, step, ins, outs, held):
        own_ref, other_ref, right_ref = ins
        own_right, other_right, total, own_sem, sems = held[:5]
        own = pltpu.make_async_copy(part(right_ref, here.c), own_right, own_sem)
        swaps = [remote(part(right_ref, 1 - here.c), other_right, sems, 0, here.swap)]
        if fetch:
            swaps.append(remote(other_ref, held[5], sems, 1, here.swap))

        @pl.when(step == 0)
        def _():
            own.start()
            for swap in swaps:
                swap.start()
            own.wait()

        @pl.when(step < tiles)
        def _():
            total[step] = dot(own_ref[...], own_right[...], (0, 0))

        @pl.when(step == tiles)
        def _():
            for swap in swaps:
                swap.wait()

        @pl.when(step >= tiles)
        def _():
            other = other_ref
            if fetch:
                other = held[5].at[:, pl.ds(pl.multiple_of((step - tiles) * tile, 128), tile)]
            outs[0][...] = (total[step - tiles] + dot(other[...], other_right[...], (0, 0))).astype(BF)

    early = lambda i: jnp.minimum(i, tiles - 1)
    late = lambda i: jnp.maximum(i - tiles, 0)
    other_spec = any_spec() if fetch else pl.BlockSpec((rows, tile), lambda i: (0, late(i)))
    outs, got = host(
        grid, body, 2 * tiles,
        [pl.BlockSpec((rows, tile), lambda i: (0, early(i))), other_spec, any_spec()],
        [left, left if fetch else left_other, right],
        [pl.BlockSpec((tile, half), lambda i: (late(i), 0))],
        [kind(height, half)],
        moves,
        scratch=[
            pltpu.VMEM((rows, half), BF),
            pltpu.VMEM((rows, half), BF),
            pltpu.VMEM((tiles, tile, half), F32),
            pltpu.SemaphoreType.DMA,
            pltpu.SemaphoreType.DMA((2, 2)),
        ] + [pltpu.VMEM((rows, height), BF)] * fetch,
        cost=pl.CostEstimate(flops=4 * rows * height * half, bytes_accessed=2 * height * half, transcendentals=0),
        reaches=lambda here: [here.swap],
    )
    return outs[0], got


class Reduce:
    def __init__(self, grid, total):
        self.grid = grid
        self.parts = total.reshape(grid.J, total.shape[0] // grid.J, total.shape[1])
        self.phase, self.came = 0, []

    def flip(self):
        return flip_move(self.grid, self.parts, self.phase)

    def flipped(self, got):
        grid = self.grid
        if self.phase == 0:
            kept = jnp.stack(
                [
                    lax.dynamic_index_in_dim(self.parts, grid.place(2 * i, grid.c), 0, keepdims=False)
                    for i in range(grid.J // 2)
                ]
            )
        else:
            kept = self.parts[0::2]
        self.parts = (kept.astype(F32) + got.astype(F32)).astype(BF)
        self.phase += 1
        if self.phase == grid.bits:
            self.line = self.parts.reshape(2, grid.F, -1, self.parts.shape[2])

    def ring(self, distances=None):
        grid = self.grid
        while self.phase < grid.bits:
            self.flipped(send(grid, [self.flip()])[0])
        return ring_move(grid, self.line, distances or list(range(1, grid.F)))

    def far(self):
        return self.ring([self.grid.F // 2])

    def near(self):
        return self.ring([t for t in range(1, self.grid.F) if t != self.grid.F // 2])

    def arrived(self, got):
        grid = self.grid
        self.came.append(got)
        if sum(part.shape[0] for part in self.came) < grid.F - 1:
            return
        here = lax.dynamic_index_in_dim(self.line, grid.f, 1, keepdims=False)
        self.summed = here.astype(F32) + sum(
            part[i].astype(F32) for part in self.came for i in range(part.shape[0])
        )
        give = lax.dynamic_index_in_dim(self.summed, 1 - grid.c, 0, keepdims=False)
        self.give = give.astype(BF)

    def done(self, got):
        grid = self.grid
        mine = lax.dynamic_index_in_dim(self.summed, grid.c, 0, keepdims=False)
        got = got.astype(F32)
        return jnp.concatenate(
            [jnp.where(grid.c == 0, mine, got), jnp.where(grid.c == 0, got, mine)], axis=1
        )


def local(
    n_dp,
    pieces,
    tokens,
    cotangent,
    doc_lengths,
    partner,
    memory_picks,
    attention_in,
    attention_out,
    feed_in,
    feed_out,
    norm_gains,
):
    IDS[0] = 1
    grid = Grid(n_dp, pieces)
    grid.trace()
    layers = attention_in.shape[0]
    width = tokens.shape[2]
    heads = width // HEAD_DIM
    topk = memory_picks.shape[3]
    valid_all, visible_all = jax.vmap(memory_plan)(doc_lengths, partner)
    valid = valid_all[grid.m, grid.slot].reshape(1)
    visible = visible_all[grid.m, grid.slot]
    relative = (grid.slot - jnp.arange(n_dp)) % n_dp
    bias = jnp.repeat(jnp.where(visible[relative], 0.0, MASKED), topk)[:, None].astype(F32)
    tables = rope_tables()
    picks_there = grid.swap(memory_picks)
    picks = jnp.where(grid.r == grid.c, memory_picks[grid.m, 0], picks_there[grid.m, 0])
    zero = grid.c == 0

    def both_halves(mine, other):
        return jnp.where(
            zero, jnp.concatenate([mine, other], axis=-1), jnp.concatenate([other, mine], axis=-1)
        )

    def half(value, c):
        size = value.shape[-1] // 2
        return lax.dynamic_slice_in_dim(value, c * size, size, axis=value.ndim - 1)

    hidden, gains, weights = gather_all(
        grid, tokens, norm_gains, [attention_in, attention_out, feed_in, feed_out]
    )
    gain = lambda l, i: gains[l, i][None]
    flat = lambda w: w.reshape(-1, w.shape[-1])
    saved = []
    cotangent_rows = None
    for l in range(layers):
        w_qkv, w_out = flat(weights[l][0]), flat(weights[l][1])
        memory = l == layers - 1
        coming = weights[l + 1] if l + 1 < layers else None
        moves = []
        if coming is not None:
            moves.append(spread_move(grid, coming[3], [(0, 0, 1)]))
        if later_here(l, 2):
            moves += [
                spread_move(grid, weights[l][2], [(1, 0, 2), (1, 1, 2)]),
                spread_move(grid, weights[l][3], [(2, 0, 1)]),
            ]
        split, got = project(grid, memory, tables, hidden, gain(l, 0), w_qkv, moves)
        if coming is not None:
            coming[3] = got[0]
        if later_here(l, 2):
            weights[l][2:] = got[-2:]
        normed, query = split[:2]
        pairs = [split[2]] + [split[3][t] for t in range(grid.U - 1)]
        extra = None
        if memory:
            chosen = pick_memory(grid, picks, pairs, grid.c)
            slots = gather_memory(grid, chosen).reshape(2, n_dp * topk, -1)
            extra = {"query": split[4], "memory": slots, "bias": bias}
        moves = []
        if coming is not None:
            moves.append(spread_move(grid, coming[2], [(0, 0, 2)]))
        if later_here(l, 2):
            moves.append(spread_move(grid, weights[l][2], [(2, 0, 1)]))
        if memory:
            moves.append(regroup_move(grid, cotangent))
        attended, got = attend(grid, valid, query, pairs, extra, moves)
        if coming is not None:
            coming[2] = got[0]
        if later_here(l, 2):
            weights[l][2] = got[-2]
            for stage in range(3, grid.bits + 1):
                weights[l][2:] = send(grid, [spread_move(grid, w, [(stage, 0, 1)]) for w in weights[l][2:]])
        if memory:
            cotangent_rows = got[-1]
        middle = hidden.astype(F32) + mm(attended, w_out)
        moves = []
        if coming is not None:
            moves = [spread_move(grid, coming[2], [(0, 1, 2)]), spread_move(grid, coming[3], [(1, 0, 1)])]
        w_up, w_down = flat(weights[l][2]), flat(weights[l][3])
        (out, normed_feed, both, inner), got = feed(grid, middle, gain(l, 1), w_up, w_down, moves)
        if coming is not None:
            coming[2:] = got
        saved.append((hidden, normed, query, pairs, extra, attended, middle, normed_feed, both, inner))
        hidden = out
    weights = [[flat(w) for w in kinds] for kinds in weights]
    cotangent_rows = cotangent_rows.reshape(-1, width)
    def row_halves(value):
        value = value.astype(BF).reshape(2, grid.R, width)
        return value[:, : grid.R // 2], value[:, grid.R // 2 :]

    out_rows = row_halves(hidden)
    grad = cotangent_rows.astype(F32)
    found = [[None] * 4 for _ in range(layers)]
    grad_gains = [[None, None] for _ in range(layers)]
    layer_output, above, inner_other = [], None, None

    def took(got, reduces):
        for result, (reduce, what) in zip(got, reduces):
            (reduce.flipped if what == "flip" else reduce.arrived)(result)

    def moves_of(reduces):
        return [getattr(reduce, what)() for reduce, what in reduces]

    for l in reversed(range(layers)):
        w_qkv, w_out, w_up, w_down = weights[l]
        hidden, normed, query, pairs, extra, attended, middle, normed_feed, both, inner = saved[l]
        low = grad.astype(BF)
        last_layer = above is None

        reduces = [] if last_layer else [(above[1], "flip"), (above[2][0], "far")]
        total, got = product(grid, inner, inner_other, low, moves_of(reduces))
        took(got, reduces)
        down = Reduce(grid, total)

        reduces = [(down, "flip")]
        if not last_layer:
            reduces += [(above[0], "flip"), (above[1], "flip"), (above[2][0], "near")]
        moves = moves_of(reduces) + [swap_move(normed_feed), swap_move(normed), swap_move(attended)]
        if last_layer:
            moves += [swap_move(saved[l - 1][9]), regroup_back_move(grid, out_rows[0])]
        (grad, grad_low, grads, gain_feed), got = feed_back(
            grid, grad, middle, gain(l, 1), both, w_up, w_down, moves
        )
        took(got, reduces)
        normed_feed_other, normed_other, attended_other = got[len(reduces) : len(reduces) + 3]
        if last_layer:
            inner_other = got[-2]
            layer_output.append(got[-1])

        ups = []
        pieces_of_up = 1 if last_layer else 2
        for piece in range(pieces_of_up):
            if piece == 0:
                reduces = [(down, "flip")] if last_layer else [(down, "flip"), (above[1], "far")]
            else:
                reduces = [(ups[0], "flip"), (above[1], "near")]
            total, got = product(
                grid, normed_feed, normed_feed_other, grads, moves_of(reduces), (piece, pieces_of_up)
            )
            took(got, reduces)
            ups.append(Reduce(grid, total))
        grad_heads = mm(grad_low, w_out, (1, 1)).astype(BF)

        reduces = [(ups[-1], "flip"), (down, "ring")]
        if not last_layer:
            reduces += [(ups[0], "flip"), (above[0], "ring")]
        outs, got = attend_back(grid, valid, tables, query, grad_heads, pairs, extra, moves_of(reduces))
        took(got, reduces)
        grad_query, own, others = outs[:3]
        memory_grad = None
        moves = []
        if extra is not None:
            joined = half(outs[3], grid.c).astype(F32) + outs[4].astype(F32)
            joined = joined.astype(BF).reshape(2, n_dp, topk, -1)
            moves = [slots_move(grid, joined, True)]
        total, got = product(grid, attended, attended_other, grad_low, moves)
        across = Reduce(grid, total)
        if extra is not None:
            total = joined[:, 0].astype(F32) + sum(got[0][t].astype(F32) for t in range(n_dp - 1))
            for t in range(1, grid.Q):
                total = total + grid.within(total.astype(BF), t).astype(F32)
            total = total.astype(BF)
            memory_grad = both_halves(total, grid.swap(total))
        reduces = [(ups[-1], "flip"), (across, "flip")]
        if not last_layer:
            reduces.append((ups[0], "ring"))
        moves = moves_of(reduces)
        if last_layer:
            moves.append(regroup_back_move(grid, out_rows[1]))
        grad_projected, got = finish_gradient(grid, grad_query, own, others, picks, memory_grad, moves)
        took(got, reduces)
        if last_layer:
            layer_output.append(got[-1])
        pulled, gain_attention = norm_back(
            hidden.astype(F32), gain(l, 0), mm(grad_projected, w_qkv, (1, 1))
        )
        grad = grad + pulled
        grad_gains[l] = [gain_attention[0], gain_feed[0]]
        reduces, moves = [], []
        if l == 0:
            small = GainSum(grid, jnp.stack([jnp.stack(pair) for pair in grad_gains]).reshape(-1, HEAD_DIM))
            reduces = [(ups[-1], "ring"), (across, "flip")]
            moves = [small.move()]
        total, got = product(grid, normed, normed_other, grad_projected, moves_of(reduces) + moves)
        took(got, reduces)
        if l == 0:
            small.took(got[-1])
        last = Reduce(grid, total)
        found[l][3] = down.done(grid.swap(down.give))
        if not last_layer:
            found[l + 1] = [r.done(grid.swap(r.give)) for r in (above[1], above[0])] + [
                feed_parts([r.done(grid.swap(r.give)) for r in above[2]]), found[l + 1][3]
            ]
        above = (across, last, ups)
    across, last, ups = above
    in_rows = row_halves(grad)
    input_grad = []
    for i, reduces in enumerate([[(last, "flip"), (across, "ring")], [(last, "flip")], [(last, "ring")]]):
        moves = moves_of(reduces)
        if i < 2:
            moves.append(regroup_back_move(grid, in_rows[i]))
        got = send(grid, moves + [small.move()])
        took(got, reduces)
        small.took(got[-1])
        if i < 2:
            input_grad.append(got[-2])
    layer_output = jnp.concatenate(layer_output, axis=1)
    input_grad = jnp.concatenate(input_grad, axis=1).astype(F32)
    found[0] = [r.done(grid.swap(r.give)) for r in (last, across)] + [
        feed_parts([r.done(grid.swap(r.give)) for r in ups]), found[0][3]
    ]
    total_gains = small.finish().reshape(layers, 2, n_dp * pieces, -1)
    device = (grid.j * 2 + grid.c) * grid.F + grid.f
    return (
        layer_output,
        input_grad,
        *(jnp.stack([found[l][i] for l in range(layers)]) for i in range(4)),
        lax.dynamic_index_in_dim(total_gains, device, 2, keepdims=False),
    )


def feed_parts(parts):
    sides = [[part[:, : part.shape[1] // 2] for part in parts], [part[:, part.shape[1] // 2 :] for part in parts]]
    return jnp.concatenate(sides[0] + sides[1], axis=1)


def solution(mesh):
    rows = P(None, ("dp", "fsdp"), None)
    in_specs = (rows, rows, P(), P(), P(None, "dp", None, None), rows, rows, rows, rows, P(None, None, ("dp", "fsdp")))
    out_specs = (rows, rows, rows, rows, rows, rows, P(None, None, ("dp", "fsdp")))
    body = functools.partial(local, mesh.shape["dp"], mesh.shape["fsdp"])
    return jax.shard_map(body, mesh=mesh, in_specs=in_specs, out_specs=out_specs, check_vma=False)
```

```python
import functools
import math

import jax
import jax.numpy as jnp
from jax import lax
from jax.experimental import pallas as pl
from jax.experimental.pallas import tpu as pltpu
from jax.sharding import PartitionSpec as P

HEAD_DIM = 128
SEG = 1024
MICRO = 2
EPSILON = 1e-06
MASKED = -1e30
SCALE = HEAD_DIM ** (-0.5)
LOG2E = 1.0 / math.log(2.0)
BF = jnp.bfloat16
F32 = jnp.float32
VMEM_LIMIT = 44 * 1024 * 1024


def slot_layout(lengths):
    slot_total = lengths.shape[0]
    slot_counts = ((lengths + SEG - 1) // SEG).astype(jnp.int32)
    slot_starts = (jnp.cumsum(slot_counts) - slot_counts).astype(jnp.int32)
    slot_index = jnp.arange(slot_total, dtype=jnp.int32)
    started = (slot_starts[None, :] <= slot_index[:, None]) & (slot_counts[None, :] > 0)
    owner_doc = (jnp.sum(started.astype(jnp.int32), axis=1) - 1).astype(jnp.int32)
    owner_pick = slot_index[None, :] == owner_doc[:, None]
    first_slot = jnp.sum(jnp.where(owner_pick, slot_starts[None, :], 0), axis=1).astype(jnp.int32)
    doc_total = jnp.sum(jnp.where(owner_pick, lengths[None, :], 0), axis=1).astype(jnp.int32)
    valid_rows = jnp.clip(doc_total - (slot_index - first_slot) * SEG, 0, SEG).astype(jnp.int32)
    return (valid_rows, owner_doc)


def memory_plan(lengths, partner_row):
    valid_rows, owner_doc = slot_layout(lengths)
    block_ids = jnp.arange(lengths.shape[0], dtype=jnp.int32)
    earlier = (block_ids[None, :] < block_ids[:, None]) & (owner_doc[None, :] == owner_doc[:, None])
    visible = earlier | (block_ids[None, :] == partner_row[:, None])
    return (valid_rows, visible)


class Grid:
    def __init__(self, n_dp, pieces):
        self.n_dp, self.F = n_dp, pieces
        self.J = n_dp // 2
        self.bits = self.J.bit_length() - 1
        self.Q = pieces // 4
        self.U = 2 * self.Q
        self.R = SEG // pieces
        self.T = 2 * self.R

    def trace(self):
        dp = lax.axis_index("dp")
        self.c, self.j, self.f = dp % 2, dp // 2, lax.axis_index("fsdp")
        self.q, self.g = self.f // self.Q, self.f % self.Q
        self.m, self.r = self.q // 2, self.q % 2
        self.k = self.c * self.Q + self.g
        self.slot = 2 * self.j + self.r

    def permute(self, value, target):
        pairs = []
        for j in range(self.J):
            for c in range(2):
                for f in range(self.F):
                    j2, c2, f2 = target(j, c, f)
                    pairs.append(((j * 2 + c) * self.F + f, (j2 * 2 + c2) * self.F + f2))
        return lax.ppermute(value, ("dp", "fsdp"), pairs)

    def swap(self, value):
        return self.permute(value, lambda j, c, f: (j, 1 - c, f))

    def ring(self, value, t):
        return self.permute(value, lambda j, c, f: (j, c, (f + t) % self.F))

    def bit(self, phase, c):
        return phase if c == 0 else self.bits - 1 - phase

    def flip(self, value, phase):
        return self.permute(value, lambda j, c, f: (j ^ (1 << self.bit(phase, c)), c, f))

    def mask(self, key, c):
        return sum(1 << self.bit(p, c) for p in range(self.bits) if key >> p & 1)

    def place(self, key, c):
        return jnp.where(c == 0, self.j ^ self.mask(key, 0), self.j ^ self.mask(key, 1))

    def member(self, value, t):
        def target(j, c, f):
            q, g = f // self.Q, f % self.Q
            k = (c * self.Q + g + t) % self.U
            return (j, k // self.Q, q * self.Q + k % self.Q)

        return self.permute(value, target)

    def within(self, value, t):
        return self.permute(
            value, lambda j, c, f: (j, c, f // self.Q * self.Q + (f % self.Q + t) % self.Q)
        )

    def slots(self, value, t):
        def target(j, c, f):
            q, g = f // self.Q, f % self.Q
            slot = (2 * j + q % 2 + t) % self.n_dp
            return (slot // 2, c, (2 * (q // 2) + slot % 2) * self.Q + g)

        return self.permute(value, target)

    def _spread(self, second):
        def target(j, c, f):
            m = f // (self.F // 2)
            m = 1 - m if second else m
            k = min(f, self.F - 1 - f)
            return (j, k // self.Q, (2 * m + c) * self.Q + k % self.Q)

        return target

    def _collect(self, second):
        there = self._spread(second)
        back = {
            there(0, c, f): (c, f) for c in range(2) for f in range(self.F)
        }
        return lambda j, c, f: (j,) + back[(0, c, f)]

    def to_units(self, value):
        here = self.f // (self.F // 2)
        first = self.permute(jnp.where(here == 0, value[0], value[1]), self._spread(False))
        second = self.permute(jnp.where(here == 0, value[1], value[0]), self._spread(True))
        return jnp.concatenate(
            [jnp.where(self.m == 0, first, second), jnp.where(self.m == 0, second, first)]
        )

    def from_units(self, value):
        low, high = value[: self.R], value[self.R :]
        first = self.permute(jnp.where(self.m == 0, low, high), self._collect(False))
        second = self.permute(jnp.where(self.m == 0, high, low), self._collect(True))
        here = self.f // (self.F // 2)
        return jnp.stack([jnp.where(here == 0, first, second), jnp.where(here == 0, second, first)])


def any_spec():
    return pl.BlockSpec(memory_space=pl.ANY)


MESH = pl.DeviceIdType.MESH


class Here:
    def __init__(self, grid):
        self.grid = grid
        dp = lax.axis_index("dp")
        self.j, self.c, self.f = dp // 2, dp % 2, lax.axis_index("fsdp")
        self.q, self.g = self.f // grid.Q, self.f % grid.Q
        self.m, self.r = self.q // 2, self.q % 2
        self.k = self.c * grid.Q + self.g
        self.swap = self.device(self.j, 1 - self.c, self.f)

    def device(self, j, c, f):
        return {"dp": 2 * j + c, "fsdp": f}

    def ring(self, t):
        return self.device(self.j, self.c, (self.f + t) % self.grid.F)

    def step(self, phase):
        first, second = (1 << self.grid.bit(phase, c) for c in (0, 1))
        return first + self.c * (second - first)

    def moved(self, j, phase):
        step = self.step(phase)
        return j + step * (1 - 2 * ((j // step) % 2))

    def flip(self, phase):
        return self.device(self.moved(self.j, phase), self.c, self.f)

    def slots(self, t):
        grid = self.grid
        slot = (2 * self.j + self.r + t) % grid.n_dp
        return self.device(slot // 2, self.c, (2 * self.m + slot % 2) * grid.Q + self.g)

    def member(self, t):
        grid = self.grid
        k = (self.k + t) % grid.U
        return self.device(self.j, k // grid.Q, self.q * grid.Q + k % grid.Q)

    def place(self, key):
        j = self.j
        for phase in range(self.grid.bits):
            if key >> phase & 1:
                j = self.moved(j, phase)
        return j

    def greet(self):
        grid = self.grid
        barrier = pltpu.get_barrier_semaphore()
        peers = [self.ring(t) for t in range(1, grid.F)]
        peers += [self.device(self.j, 1 - self.c, (self.f + t) % grid.F) for t in range(grid.F)]
        for bit in range(grid.bits):
            step = 1 << bit
            peers.append(self.device(self.j + step * (1 - 2 * ((self.j // step) % 2)), self.c, self.f))
        for peer in peers:
            pl.semaphore_signal(barrier, inc=1, device_id=peer, device_id_type=MESH)
        pl.semaphore_wait(barrier, len(peers))


def remote(source, target, sems, index, device):
    return pltpu.make_async_remote_copy(
        src_ref=source,
        dst_ref=target,
        send_sem=sems.at[0, index],
        recv_sem=sems.at[1, index],
        device_id=device,
        device_id_type=MESH,
    )


class Spread:
    def __init__(self, here, shard, whole, sems, own_sem, split):
        grid = here.grid
        self.here, self.split = here, split
        rows, width = shard.shape
        half = width // 2 if split else width

        def part(ref, c):
            if not split:
                return ref
            return ref.at[(slice(None),) * (len(ref.shape) - 1) + (pl.ds(pl.multiple_of(c * half, 128), half),)]

        j, c, f = here.j, here.c, here.f
        mine = part(whole, c)
        self.own = pltpu.make_async_copy(part(shard, c), part(whole.at[j, c, f], c), own_sem)
        other = 1 - c if split else c
        self.pre = remote(part(shard, other), part(whole.at[j, c, f], other), sems, 0, here.swap)
        at = 1
        self.hops = []
        for h in range(1, grid.F):
            hop = []
            for way in (1, -1):
                origin = f - way * (h - 1)
                inside = lambda place: (place >= 0) & (place < grid.F)
                block = mine.at[j, :, jnp.clip(origin, 0, grid.F - 1)]
                copy = remote(block, block, sems, at, here.device(j, c, (f + way + grid.F) % grid.F))
                hop.append((copy, inside(origin) & inside(f + way), inside(f - way * h)))
                at += 1
            self.hops.append(hop)
        self.flips = []
        for phase in range(grid.bits):
            sent = []
            for key in range(1 << phase):
                block = mine.at[here.place(key)]
                sent.append(remote(block, block, sems, at, here.flip(phase)))
                at += 1
            self.flips.append(sent)
        self.swaps = []
        for key in range(grid.J if split else 0):
            block = mine.at[here.place(key)]
            self.swaps.append(remote(block, block, sems, at, here.swap))
            at += 1

    @staticmethod
    def count(grid):
        return 1 + 2 * (grid.F - 1) + (grid.J - 1) + grid.J

    def begin(self):
        self.own.start()
        self.pre.start()

    def to_line(self):
        self.own.wait()
        self.pre.wait()
        self._hop(0)

    def _hop(self, h):
        for copy, sends, _ in self.hops[h]:
            pl.when(sends)(copy.start)

    def _send(self, keys):
        for key in keys:
            if self.swaps:
                self.swaps[key].start()
        for phase, sent in enumerate(self.flips):
            for key in keys:
                if key < 1 << phase:
                    sent[key].start()

    def steps(self, whole):
        def along(h):
            for copy, _, comes in self.hops[h]:
                pl.when(comes)(copy.wait_recv)
            if h + 1 < len(self.hops):
                self._hop(h + 1)
                return
            for hop in self.hops:
                for copy, sends, _ in hop:
                    pl.when(sends)(copy.wait_send)
            if whole:
                self._send([0])

        def later(phase):
            for copy in self.flips[phase]:
                copy.wait()
            self._send([key + (1 << phase) for key in range(1 << phase)])

        def last():
            for copy in self.swaps:
                copy.wait()

        line = [functools.partial(along, h) for h in range(len(self.hops))]
        if not whole:
            return line
        return line + [functools.partial(later, p) for p in range(len(self.flips))] + [last]


class Regroup:
    def __init__(self, here, source, target, sems, own_sem):
        grid = here.grid
        half = grid.F // 2
        k = jnp.minimum(here.f, grid.F - 1 - here.f)
        side = here.f // half
        self.sends = []
        for m in range(2):
            c2, f2 = k // grid.Q, (2 * m + here.c) * grid.Q + k % grid.Q
            same = (c2 == here.c) & (f2 == here.f)
            own = pltpu.make_async_copy(source.at[m], target.at[side], own_sem)
            away = pltpu.make_async_remote_copy(
                src_ref=source.at[m],
                dst_ref=target.at[side],
                send_sem=sems.at[0, m],
                recv_sem=sems.at[1, side],
                device_id=here.device(here.j, c2, f2),
                device_id_type=MESH,
            )
            self.sends.append((same, own, away))
        self.arrivals = []
        for side in range(2):
            from_f = here.k if side == 0 else grid.F - 1 - here.k
            same = (here.r == here.c) & (from_f == here.f)
            came = pltpu.make_async_remote_copy(
                src_ref=source.at[0],
                dst_ref=target.at[side],
                send_sem=sems.at[0, 0],
                recv_sem=sems.at[1, side],
                device_id=here.swap,
                device_id_type=MESH,
            )
            self.arrivals.append((same, came))

    def start(self):
        for same, own, away in self.sends:
            pl.when(same)(own.start)
            pl.when(jnp.logical_not(same))(away.start)

    def wait(self):
        for same, own, away in self.sends:
            pl.when(same)(own.wait)
            pl.when(jnp.logical_not(same))(away.wait_send)
        for same, came in self.arrivals:
            pl.when(jnp.logical_not(same))(came.wait_recv)


def gather_body(grid, layers, kinds, *refs):
    tokens, gains = refs[:2]
    shards = refs[2 : 2 + kinds]
    outs = refs[2 + kinds :]
    tokens_out, gains_out = outs[:2]
    wholes = outs[2 : 2 + layers * kinds]
    sems, own_sems, regroup_sems = outs[2 + layers * kinds :]
    here = Here(grid)
    here.greet()
    rows = Regroup(here, tokens, tokens_out, regroup_sems, own_sems.at[0])
    moves = []
    for l, i in ORDER:
        n = l * kinds + i
        move = Spread(here, shards[i].at[l], wholes[n], sems.at[n + 1], own_sems.at[n + 2], True)
        moves.append((move, not later_here(l, i)))
    moves.insert(GAINS_AT, (Spread(here, gains, gains_out, sems.at[0], own_sems.at[1], False), True))
    for move, _ in moves:
        move.begin()
    steps = [move.steps(whole) for move, whole in moves]
    count = len(steps[0])
    for at in range(AHEAD):
        moves[at][0].to_line()
    for at in range(len(moves) + count - 1):
        if at == ROWS_AT:
            rows.start()
        if at + AHEAD < len(moves):
            moves[at + AHEAD][0].to_line()
        for back in reversed(range(count)):
            if 0 <= at - back < len(moves) and back < len(steps[at - back]):
                steps[at - back][back]()
    rows.wait()


ORDER = [(0, 1), (0, 3), (0, 2), (0, 0), (1, 0), (1, 1), (1, 3), (1, 2)]
GAINS_AT, ROWS_AT, AHEAD = 3, 6, 1


def later_here(l, i):
    return l > 0 and i >= 2


def gather_all(grid, tokens, gains, shards):
    layers, kinds = shards[0].shape[0], len(shards)
    packed = jnp.zeros((8, 128), F32).at[: layers * 2, : gains.shape[2]].set(
        gains.astype(F32).reshape(layers * 2, -1)
    )
    whole = lambda shard: jax.ShapeDtypeStruct((grid.J, 2, grid.F) + shard.shape[-2:], shard.dtype)
    out_shape = [jax.ShapeDtypeStruct(tokens.shape, BF), whole(packed)]
    out_shape += [whole(shard) for _ in range(layers) for shard in shards]
    moves = 1 + layers * kinds
    outs = pl.pallas_call(
        functools.partial(gather_body, grid, layers, kinds),
        in_specs=[any_spec()] * (2 + kinds),
        out_specs=[any_spec()] * len(out_shape),
        out_shape=out_shape,
        scratch_shapes=[
            pltpu.SemaphoreType.DMA((moves, 2, Spread.count(grid))),
            pltpu.SemaphoreType.DMA((moves + 1,)),
            pltpu.SemaphoreType.DMA((2, 2)),
        ],
        compiler_params=pltpu.CompilerParams(
            collective_id=0, has_side_effects=True, vmem_limit_bytes=VMEM_LIMIT
        ),
    )(tokens, packed, *shards)
    gains_all = outs[1][..., : layers * 2, : gains.shape[2]]
    gains_all = jnp.moveaxis(gains_all, 3, 0).reshape(layers, 2, -1)
    weights = [list(outs[2 + l * kinds : 2 + (l + 1) * kinds]) for l in range(layers)]
    return outs[0].reshape(-1, tokens.shape[2]), gains_all, weights


def unless(condition, act):
    if condition is None:
        act()
    else:
        pl.when(jnp.logical_not(condition))(act)


class Move:
    def __init__(self, array, shape, count, copies, plan=None, in_place=False):
        self.array, self.shape, self.count, self.copies = array, shape, count, copies
        self.plan, self.in_place = plan or self._plain, in_place

    def _plain(self, here, source, target, sends, recvs, base):
        found = []
        for i, (what, where, peer, giver) in enumerate(self.copies(here, source, target)):
            copy = pltpu.make_async_remote_copy(
                src_ref=what,
                dst_ref=where,
                send_sem=sends.at[base + i],
                recv_sem=recvs.at[base + i],
                device_id=peer,
                device_id_type=MESH,
            )
            found.append((copy, None, None, giver, copy, None))
        return found


def flip_move(grid, parts, phase):
    count = parts.shape[0] // 2

    def copies(here, source, target):
        found = []
        for i in range(count):
            at = here.place(2 * i + 1) if phase == 0 else 2 * i + 1
            peer = here.flip(phase)
            found.append((source.at[at], target.at[i], peer, peer))
        return found

    return Move(parts, (count,) + parts.shape[1:], count, copies)


def ring_move(grid, line, distances):
    def copies(here, source, target):
        return [
            (source.at[:, (here.f + t) % grid.F], target.at[i], here.ring(t), here.ring(grid.F - t))
            for i, t in enumerate(distances)
        ]

    return Move(line, (len(distances), 2) + line.shape[2:], len(distances), copies)


def swap_move(array, give=None):
    def copies(here, source, target):
        return [(source if give is None else source.at[give(here)], target, here.swap, here.swap)]

    return Move(array, array.shape if give is None else array.shape[1:], 1, copies)


def swap_half_move(array):
    half = array.shape[-1] // 2

    def copies(here, source, target):
        start = pl.multiple_of((1 - here.c) * half, 128)
        return [(source.at[:, :, pl.ds(start, half)], target, here.swap, here.swap)]

    return Move(array, array.shape[:-1] + (half,), 1, copies)


def slots_move(grid, array, back):
    def copies(here, source, target):
        found = []
        for t in range(1, grid.n_dp):
            ahead, behind = here.slots(t), here.slots(grid.n_dp - t)
            if back:
                found.append((source.at[:, t], target.at[t - 1], behind, ahead))
            else:
                found.append((source, target.at[t - 1], ahead, behind))
        return found

    shape = array.shape if not back else array.shape[:1] + array.shape[2:]
    return Move(array, (grid.n_dp - 1,) + shape, grid.n_dp - 1, copies)


def member_move(grid, array, back):
    def copies(here, source, target):
        found = []
        for t in range(1, grid.U):
            ahead, behind = here.member(t), here.member(grid.U - t)
            if back:
                found.append((source.at[t - 1], target.at[t - 1], behind, ahead))
            else:
                found.append((source, target.at[t - 1], ahead, behind))
        return found

    shape = array.shape[1:] if back else array.shape
    return Move(array, (grid.U - 1,) + shape, grid.U - 1, copies)


def spread_move(grid, whole, stages):
    half = whole.shape[-1] // 2

    def keys_of(stage):
        return [0] if stage == 0 else range(1 << (stage - 1), 1 << stage)

    def copies(here, source, target):
        found = []
        for stage, part, parts in stages:
            size = half // parts
            columns = pl.ds(pl.multiple_of(here.c * half + part * size, 128), size)
            mine = target.at[:, :, :, :, columns]
            for key in keys_of(stage):
                block = mine.at[here.place(key)]
                found.append((block, block, here.swap, here.swap))
                for phase in range(stage, grid.bits):
                    found.append((block, block, here.flip(phase), here.flip(phase)))
        return found

    count = sum(len(keys_of(stage)) * (1 + grid.bits - stage) for stage, _, _ in stages)
    return Move(whole, whole.shape, count, copies, in_place=True)


def peer_move(array, peer):
    return Move(array, array.shape, 1, lambda here, source, target: [(source, target, peer(here), peer(here))])


def line_move(grid, array):
    def copies(here, source, target):
        return [(source, target.at[t - 1], here.ring(t), here.ring(grid.F - t)) for t in range(1, grid.F)]

    return Move(array, (grid.F - 1,) + array.shape, grid.F - 1, copies)


def regroup_move(grid, array):
    def plan(here, source, target, sends, recvs, base):
        found = []
        k = jnp.minimum(here.f, grid.F - 1 - here.f)
        side = here.f // (grid.F // 2)
        for m in range(2):
            c2, f2 = k // grid.Q, (2 * m + here.c) * grid.Q + k % grid.Q
            same = (c2 == here.c) & (f2 == here.f)
            away = pltpu.make_async_remote_copy(
                src_ref=source.at[m],
                dst_ref=target.at[side],
                send_sem=sends.at[base + m],
                recv_sem=recvs.at[base + side],
                device_id=here.device(here.j, c2, f2),
                device_id_type=MESH,
            )
            own = pltpu.make_async_copy(source.at[m], target.at[side], sends.at[base + m])
            from_f = here.k if m == 0 else grid.F - 1 - here.k
            same_in = (here.r == here.c) & (from_f == here.f)
            came = pltpu.make_async_remote_copy(
                src_ref=source.at[0],
                dst_ref=target.at[m],
                send_sem=sends.at[base],
                recv_sem=recvs.at[base + m],
                device_id=here.swap,
                device_id_type=MESH,
            )
            found.append((away, same, own, here.device(here.j, here.r, from_f), came, same_in))
        return found

    return Move(array, array.shape, 2, None, plan)


def regroup_back_move(grid, array):
    def plan(here, source, target, sends, recvs, base):
        found = []
        for piece in range(2):
            f = here.k if piece == 0 else grid.F - 1 - here.k
            same = (here.r == here.c) & (f == here.f)
            away = pltpu.make_async_remote_copy(
                src_ref=source.at[piece],
                dst_ref=target.at[here.m],
                send_sem=sends.at[base + piece],
                recv_sem=recvs.at[base + here.m],
                device_id=here.device(here.j, here.r, f),
                device_id_type=MESH,
            )
            own = pltpu.make_async_copy(source.at[piece], target.at[here.m], sends.at[base + piece])
            k = jnp.minimum(here.f, grid.F - 1 - here.f)
            c2, f2 = k // grid.Q, (2 * piece + here.c) * grid.Q + k % grid.Q
            same_in = (c2 == here.c) & (f2 == here.f)
            came = pltpu.make_async_remote_copy(
                src_ref=source.at[0],
                dst_ref=target.at[piece],
                send_sem=sends.at[base],
                recv_sem=recvs.at[base + piece],
                device_id=here.swap,
                device_id_type=MESH,
            )
            found.append((away, same, own, here.device(here.j, c2, f2), came, same_in))
        return found

    return Move(array, array.shape, 2, None, plan)


IDS = [1]


def host(grid, body, steps, in_specs, operands, out_specs, out_shape, moves=(), scratch=(), cost=None, reaches=None):
    counts = [len(operands), len(moves), len(out_shape), len(moves), len(scratch)]

    def kernel(*refs):
        parts, at = [], 0
        for count in counts:
            parts.append(refs[at : at + count])
            at += count
        ins, sources, outs, targets, held = parts
        here = Here(grid)
        step = pl.program_id(0)
        planned = []
        if moves:
            sends, recvs = refs[at:]
            base = 0
            for move, source, target in zip(moves, sources, targets):
                planned += move.plan(here, source, target, sends, recvs, base)
                base += move.count

        if moves or reaches:

            @pl.when(step == 0)
            def _():
                barrier = pltpu.get_barrier_semaphore()
                givers = reaches(here) if reaches else []
                for giver in givers:
                    pl.semaphore_signal(barrier, inc=1, device_id=giver, device_id_type=MESH)
                for _, _, _, giver, _, same_in in planned:
                    signal = functools.partial(
                        pl.semaphore_signal, barrier, inc=1, device_id=giver, device_id_type=MESH
                    )
                    unless(same_in, signal)
                due = len(givers) + sum(same is None for _, same, _, _, _, _ in planned)
                for _, same, _, _, _, _ in planned:
                    if same is not None:
                        due = due + 1 - same.astype(jnp.int32)
                pl.semaphore_wait(barrier, due)
                for away, same, own, _, _, _ in planned:
                    unless(same, away.start)
                    if same is not None:
                        pl.when(same)(own.start)

        if body is not None:
            body(here, step, ins, outs, held)
        if moves:

            @pl.when(step == steps - 1)
            def _():
                for away, same, own, _, came, same_in in planned:
                    unless(same, away.wait_send)
                    if same is not None:
                        pl.when(same)(own.wait)
                    unless(same_in, came.wait_recv)

    total = sum(move.count for move in moves)
    extra = {}
    sems = []
    if moves or reaches:
        extra = {"collective_id": IDS[0], "has_side_effects": True}
        IDS[0] += 1
    if moves:
        sems = [pltpu.SemaphoreType.DMA((total,)), pltpu.SemaphoreType.DMA((total,))]
    outs = pl.pallas_call(
        kernel,
        grid=(steps,),
        in_specs=list(in_specs) + [any_spec()] * len(moves),
        out_specs=list(out_specs) + [any_spec()] * len(moves),
        out_shape=list(out_shape) + [jax.ShapeDtypeStruct(m.shape, m.array.dtype) for m in moves],
        scratch_shapes=list(scratch) + sems,
        input_output_aliases={
            len(operands) + i: len(out_shape) + i for i, move in enumerate(moves) if move.in_place
        },
        compiler_params=pltpu.CompilerParams(vmem_limit_bytes=VMEM_LIMIT, **extra),
        cost_estimate=cost,
    )(*operands, *[move.array for move in moves])
    return outs[: len(out_shape)], outs[len(out_shape) :]


def send(grid, moves):
    return host(grid, None, 1, [], [], [], [], moves)[1]


class GainSum:
    def __init__(self, grid, total):
        self.grid, self.total, self.stage = grid, total, 0

    def move(self):
        grid, phase = self.grid, self.stage - 1
        if self.stage == 0:
            return swap_move(self.total)
        if phase < grid.bits:
            return peer_move(self.total, lambda here: here.flip(phase))
        return line_move(grid, self.total)

    def took(self, got):
        if self.stage > self.grid.bits:
            got = sum(got[t] for t in range(self.grid.F - 1))
        self.total = self.total + got
        self.stage += 1

    def finish(self):
        while self.stage <= self.grid.bits + 1:
            self.took(send(self.grid, [self.move()])[0])
        return self.total


def rope_tables():
    half_dim = HEAD_DIM // 2
    frequency = jnp.exp(
        jnp.arange(half_dim, dtype=F32) * (-2.0 * math.log(10000.0) / HEAD_DIM)
    )
    angles = jnp.arange(SEG, dtype=jnp.int32).astype(F32)[:, None] * frequency[None, :]
    cos, sin = jnp.cos(angles), jnp.sin(angles)
    return (jnp.concatenate([cos, cos], axis=-1), jnp.concatenate([-sin, sin], axis=-1))


def turn(values, cos, sin):
    return values * cos + pltpu.roll(values, HEAD_DIM // 2, 1) * sin


def smem():
    return pl.BlockSpec(memory_space=pltpu.SMEM)


def whole_spec(*shape):
    return pl.BlockSpec(shape, lambda i: (0,) * len(shape))


def columns_spec(*shape, first=0):
    return pl.BlockSpec(shape, lambda i: (0,) * (len(shape) - 1) + (i + first,))


def rows_spec(*shape):
    return pl.BlockSpec(shape, lambda i: (i,) + (0,) * (len(shape) - 1))


def kind(*shape, dtype=BF):
    return jax.ShapeDtypeStruct(shape, dtype)


def piece_start(grid, member, part):
    return (member if part == 0 else grid.F - 1 - member) * grid.R


def table_rows(grid, table_ref, member, part):
    start = pl.multiple_of(piece_start(grid, member, part), grid.R)
    return table_ref[pl.ds(start, grid.R), :]


def dot(left, right, contract):
    return lax.dot_general(
        left, right, (((contract[0],), (contract[1],)), ((), ())), preferred_element_type=F32
    )


def mm(left, right, contract=(1, 0)):
    return dot(left, right, contract)


def project(grid, memory, tables, hidden, gain, weight, moves=()):
    rows, width = hidden.shape
    heads = weight.shape[1] // (3 * HEAD_DIM)
    together = 2
    size = together * HEAD_DIM
    steps = heads // together
    count = 3 if memory else 2

    width_out = heads * HEAD_DIM

    def sends(here, held, target, step):
        columns = pl.ds(pl.multiple_of(step * size, 128), size)
        return [
            pltpu.make_async_remote_copy(
                src_ref=held[0].at[:, :, columns],
                dst_ref=target.at[t - 1, :, :, columns],
                send_sem=held[1].at[0, t - 1, step],
                recv_sem=held[1].at[1, t - 1, step],
                device_id=here.member(t),
                device_id_type=MESH,
            )
            for t in range(1, grid.U)
        ]

    def body(here, step, ins, outs, held):
        cos_ref, sin_ref, hidden_ref, gain_ref = ins[:4]
        normed_ref, q_out, kv_out, others = outs[:4]

        @pl.when(step == 0)
        def _():
            normed_ref[...] = norm(hidden_ref[...].astype(F32), gain_ref[...]).astype(BF)

        for part in range(2):
            at = pl.ds(part * grid.R, grid.R)
            cos = table_rows(grid, cos_ref, here.k, part)
            sin = table_rows(grid, sin_ref, here.k, part)
            normed = normed_ref[at, :]
            query, key, value = (dot(normed, w[...], (1, 0)) for w in ins[4:])
            kv_out[1, at, :] = value.astype(BF)
            for h in range(together):
                columns = slice(h * HEAD_DIM, (h + 1) * HEAD_DIM)
                q_out[at, columns] = turn(query[:, columns], cos, sin).astype(BF)
                kv_out[0, at, columns] = turn(key[:, columns], cos, sin).astype(BF)
            if memory:
                kv_out[2, at, :] = key.astype(BF)
                outs[4][at, :] = query.astype(BF)
        held[0][:, :, pl.ds(pl.multiple_of(step * size, 128), size)] = kv_out[...]
        for copy in sends(here, held, others, step):
            copy.start()

        @pl.when(step == steps - 1)
        def _():
            for i in range(steps):
                for copy in sends(here, held, others, i):
                    copy.wait()

    piece = columns_spec(rows, size)
    table = whole_spec(SEG, HEAD_DIM)
    flat = kind(rows, width_out)
    return host(
        grid,
        body,
        steps,
        [table, table, whole_spec(rows, width), whole_spec(1, width)]
        + [columns_spec(width, size, first=i * steps) for i in range(3)],
        [*tables, hidden, gain, weight, weight, weight],
        [whole_spec(rows, width), piece, columns_spec(count, rows, size), any_spec()] + [piece] * memory,
        [kind(rows, width), flat, kind(count, rows, width_out), kind(grid.U - 1, count, rows, width_out)]
        + [flat] * memory,
        moves,
        scratch=[
            pltpu.VMEM((count, rows, width_out), BF),
            pltpu.SemaphoreType.DMA((2, grid.U - 1, steps)),
        ],
        cost=pl.CostEstimate(
            flops=2 * rows * width * weight.shape[1], bytes_accessed=2 * width * weight.shape[1], transcendentals=0
        ),
        reaches=lambda here: [here.member(grid.U - t) for t in range(1, grid.U)],
    )


def part_scores(grid, here, valid, part, query, keys):
    shape = (grid.R, grid.R)
    apart = lax.broadcasted_iota(jnp.int32, shape, 0) - lax.broadcasted_iota(jnp.int32, shape, 1)
    found = []
    for t in range(grid.U):
        member = (here.k - t + grid.U) % grid.U
        for side in range(part + 1):
            score = dot(keys[t][side * grid.R : (side + 1) * grid.R], query, (1, 1))
            if side == part:
                start = piece_start(grid, member, side)
                allowed = apart <= piece_start(grid, here.k, part) - start
                if side == 1:
                    down = lax.broadcasted_iota(jnp.int32, shape, 0)
                    allowed = allowed & (down < valid - start)
                score = jnp.where(allowed, score, MASKED)
            found.append((t, side, score))
    return found


def softmax_parts(scores, stat=None):
    top = functools.reduce(jnp.maximum, [jnp.max(s, axis=0, keepdims=True) for s in scores])
    powers = [jnp.exp2((s - top) * (SCALE * LOG2E)) for s in scores]
    total = sum(jnp.sum(p, axis=0, keepdims=True) for p in powers)
    if stat is not None:
        stat(top * (SCALE * LOG2E) + jnp.log(total) * LOG2E)
    inverse = 1.0 / total
    return [p * inverse for p in powers]


def attention_cost(grid, heads, memory_rows, products):
    pairs = grid.T * (SEG * 3 // 4 + memory_rows) * heads
    return pl.CostEstimate(
        flops=2 * products * HEAD_DIM * pairs,
        bytes_accessed=2 * HEAD_DIM * heads * 4 * (SEG + memory_rows),
        transcendentals=pairs,
    )


def memory_operands(grid, extra):
    rows = extra["memory"].shape[1]
    return [extra["query"], extra["memory"], extra["bias"]], [
        columns_spec(grid.T, HEAD_DIM), columns_spec(2, rows, HEAD_DIM), whole_spec(rows, 1)
    ], rows


def attend(grid, valid, query, pairs, extra, moves=()):
    rows, width = query.shape
    heads = width // HEAD_DIM
    R, U = grid.R, grid.U

    def body(here, step, ins, outs, held):
        valid_ref, q_ref, kv_refs, refs = ins[0], ins[1], ins[2 : 2 + U], ins[2 + U :]
        keys, values = [r[0] for r in kv_refs], [r[1] for r in kv_refs]
        for part in range(2):
            at = pl.ds(part * R, R)
            found = part_scores(grid, here, valid_ref[0], part, q_ref[at, :], keys)
            scores = [s for _, _, s in found]
            mixed = [values[t][side * R : (side + 1) * R] for t, side, _ in found]
            if extra is not None:
                scores.append(dot(refs[1][0], refs[0][at, :], (1, 1)) + refs[2][...])
                mixed.append(refs[1][1])

            def stat(row):
                outs[1][0, :, at] = row

            probs = softmax_parts(scores, stat)
            total = sum(dot(value, p.astype(BF), (0, 0)) for value, p in zip(mixed, probs))
            outs[0][at, :] = total.T.astype(BF)

    piece = columns_spec(rows, HEAD_DIM)
    operands = [valid, query, *pairs]
    specs = [smem(), piece] + [columns_spec(2, rows, HEAD_DIM)] * U
    memory_rows = 0
    if extra is not None:
        more, more_specs, memory_rows = memory_operands(grid, extra)
        operands, specs = operands + more, specs + more_specs
    outs, got = host(
        grid, body, heads, specs, operands,
        [piece, rows_spec(1, 1, rows)], [kind(rows, width), kind(heads, 1, rows, dtype=F32)], moves,
        cost=attention_cost(grid, heads, memory_rows, 2),
    )
    return outs[0], outs[1], got


def inner_row(grads, mixed):
    return jnp.sum((grads.astype(F32) * mixed.astype(F32)).T, axis=0, keepdims=True)


def memory_back(grid, grad_heads, attended, extra, moves=()):
    rows, width = grad_heads.shape
    heads = width // HEAD_DIM
    per = heads // 2
    memory_rows = extra["memory"].shape[1]

    def memory_send(here, held, target, h):
        columns = pl.ds(pl.multiple_of(h * HEAD_DIM, HEAD_DIM), HEAD_DIM)
        return pltpu.make_async_remote_copy(
            src_ref=held[0].at[h],
            dst_ref=target.at[:, :, columns],
            send_sem=held[1].at[0, h],
            recv_sem=held[1].at[1, h],
            device_id=here.swap,
            device_id_type=MESH,
        )

    def body(here, step, ins, outs, held):
        g_ref, mixed_ref, stat_ref, q_ref, memory_ref, bias_ref = ins
        grad_key, grad_value = 0.0, 0.0
        for part in range(2):
            at = pl.ds(part * grid.R, grid.R)
            grads, query = g_ref[at, :], q_ref[at, :]
            inner = inner_row(grads, mixed_ref[at, :])
            score = dot(memory_ref[0], query, (1, 1)) + bias_ref[...]
            prob = jnp.exp2(score * (SCALE * LOG2E) - stat_ref[0, :, at])
            moved = (prob * (dot(memory_ref[1], grads, (1, 1)) - inner)).astype(BF)
            grad_key = grad_key + dot(moved, query, (1, 0))
            grad_value = grad_value + dot(prob.astype(BF), grads, (1, 0))
            outs[0][at, :] = dot(memory_ref[0], moved, (0, 0)).T
        grad_key, grad_value = (grad_key * SCALE).astype(BF), grad_value.astype(BF)
        outs[1][0] = grad_key
        outs[1][1] = grad_value

        @pl.when(step // per == 1 - here.c)
        def _():
            held[0][step % per, 0] = grad_key
            held[0][step % per, 1] = grad_value
            memory_send(here, held, outs[2], step % per).start()

        @pl.when(step == heads - 1)
        def _():
            for h in range(per):
                memory_send(here, held, outs[2], h).wait()

    piece = columns_spec(rows, HEAD_DIM)
    column = columns_spec(2, memory_rows, HEAD_DIM)
    return host(
        grid, body, heads,
        [piece, piece, rows_spec(1, 1, rows), piece, column, whole_spec(memory_rows, 1)],
        [grad_heads, attended, extra["logsum"], extra["query"], extra["memory"], extra["bias"]],
        [piece, column, any_spec()],
        [kind(rows, width, dtype=F32), kind(2, memory_rows, width), kind(2, memory_rows, width // 2)],
        moves,
        scratch=[pltpu.VMEM((per, 2, memory_rows, HEAD_DIM), BF), pltpu.SemaphoreType.DMA((2, per))],
        cost=pl.CostEstimate(
            flops=10 * HEAD_DIM * rows * memory_rows * heads,
            bytes_accessed=12 * memory_rows * width,
            transcendentals=rows * memory_rows * heads,
        ),
        reaches=lambda here: [here.swap],
    )


def attend_back(grid, valid, tables, query, grad, w_out, pairs, moves=(), memory=None):
    rows, width = query.shape
    heads = width // HEAD_DIM
    R, U = grid.R, grid.U

    def sends(here, held, target, h):
        columns = pl.ds(pl.multiple_of(h * HEAD_DIM, HEAD_DIM), HEAD_DIM)
        return [
            pltpu.make_async_remote_copy(
                src_ref=held[0].at[h, t - 1],
                dst_ref=target.at[t - 1, :, :, columns],
                send_sem=held[1].at[0, t - 1, h],
                recv_sem=held[1].at[1, t - 1, h],
                device_id=here.member(U - t),
                device_id_type=MESH,
            )
            for t in range(1, U)
        ]

    def body(here, step, ins, outs, held):
        valid_ref, cos_ref, sin_ref, q_ref, g_ref = ins[:5]
        kv_refs, refs = ins[5 : 5 + U], ins[5 + U :]
        keys, values = [r[0] for r in kv_refs], [r[1] for r in kv_refs]
        grad_keys, grad_values = {}, {}

        def add(store, at, value):
            store[at] = store[at] + value if at in store else value

        if memory is None:

            @pl.when(step == 0)
            def _():
                held[2][...] = dot(g_ref[...], refs[0][...], (1, 1)).astype(BF)

        for part in range(2):
            at_rows = pl.ds(part * R, R)
            asked = q_ref[at_rows, :]
            if memory is None:
                grads_in = held[2][at_rows, pl.ds(pl.multiple_of(step * HEAD_DIM, HEAD_DIM), HEAD_DIM)]
            else:
                grads_in = g_ref[at_rows, :]
            found = part_scores(grid, here, valid_ref[0], part, asked, keys)
            places = [(t, side) for t, side, _ in found]
            scores = [s for _, _, s in found]
            part_keys = [keys[t][side * R : (side + 1) * R] for t, side in places]
            part_values = [values[t][side * R : (side + 1) * R] for t, side in places]
            grads = [dot(value, grads_in, (1, 1)) for value in part_values]
            if memory is None:
                probs = softmax_parts(scores)
                inner = sum(jnp.sum(p * d, axis=0, keepdims=True) for p, d in zip(probs, grads))
            else:
                probs = [jnp.exp2(s * (SCALE * LOG2E) - refs[1][0, :, at_rows]) for s in scores]
                inner = inner_row(grads_in, refs[0][at_rows, :])
            back = None
            for at, p, d, key in zip(places, probs, grads, part_keys):
                moved = (p * (d - inner)).astype(BF)
                add(grad_keys, at, dot(moved, asked, (1, 0)))
                add(grad_values, at, dot(p.astype(BF), grads_in, (1, 0)))
                share = dot(key, moved, (0, 0))
                back = share if back is None else back + share
            cos = table_rows(grid, cos_ref, here.k, part)
            sin = table_rows(grid, sin_ref, here.k, part)
            result = turn(back.T, cos, -sin)
            if memory is not None:
                result = result + refs[2][at_rows, :]
            outs[0][at_rows, :] = (result * SCALE).astype(BF)
        for t in range(U):
            member = (here.k - t + U) % U
            for side in range(2):
                at_rows = pl.ds(side * R, R)
                cos = table_rows(grid, cos_ref, member, side)
                sin = table_rows(grid, sin_ref, member, side)
                key = turn(grad_keys[(t, side)], cos, -sin) * SCALE
                if t == 0:
                    outs[1][0, at_rows, :] = key
                    outs[1][1, at_rows, :] = grad_values[(t, side)]
                else:
                    held[0][step, t - 1, 0, at_rows, :] = key.astype(BF)
                    held[0][step, t - 1, 1, at_rows, :] = grad_values[(t, side)].astype(BF)
        for copy in sends(here, held, outs[2], step):
            copy.start()

        @pl.when(step == heads - 1)
        def _():
            for h in range(heads):
                for copy in sends(here, held, outs[2], h):
                    copy.wait()

    piece = columns_spec(rows, HEAD_DIM)
    pair = columns_spec(2, rows, HEAD_DIM)
    table = whole_spec(SEG, HEAD_DIM)
    operands = [valid, *tables, query, grad, *pairs]
    scratch = [pltpu.VMEM((heads, U - 1, 2, rows, HEAD_DIM), BF), pltpu.SemaphoreType.DMA((2, U - 1, heads))]
    if memory is None:
        specs = [smem(), table, table, piece, whole_spec(rows, width)] + [pair] * U + [whole_spec(width, width)]
        operands.append(w_out)
        scratch.append(pltpu.VMEM((rows, width), BF))
    else:
        specs = [smem(), table, table, piece, piece] + [pair] * U + [piece, rows_spec(1, 1, rows), piece]
        operands += memory
    return host(
        grid, body, heads, specs, operands,
        [piece, pair, any_spec()],
        [kind(rows, width), kind(2, rows, width, dtype=F32), kind(U - 1, 2, rows, width)],
        moves,
        scratch=scratch,
        cost=attention_cost(grid, heads, 0, 5),
        reaches=lambda here: [here.member(t) for t in range(1, U)],
    )


def gather_memory(grid, picks, pairs):
    n, U, R = grid.n_dp, grid.U, grid.R
    heads, topk = picks.shape
    per = heads // 2
    half = per * HEAD_DIM

    def body(here, step, ins, outs, held):
        picks_ref, sources, target = ins[0], ins[1:], outs[0]
        rows, chosen, load_sems, own_sem, sems = held
        columns = pl.ds(pl.multiple_of(here.c * half, 128), half)
        loads = [
            pltpu.make_async_copy(source.at[1:3, :, columns], rows.at[t], load_sems.at[t])
            for t, source in enumerate(sources)
        ]
        for load in loads:
            load.start()
        for load in loads:
            load.wait()
        for h in range(per):
            picked = picks_ref[here.c * per + h]
            at_columns = slice(h * HEAD_DIM, (h + 1) * HEAD_DIM)
            totals = [0.0, 0.0]
            for t in range(U):
                member = (here.k - t + U) % U
                for side in range(2):
                    across = lax.broadcasted_iota(jnp.int32, (topk, R), 1)
                    mask = (picked == across + piece_start(grid, member, side)).astype(BF)
                    for i in range(2):
                        block = rows[t, i, side * R : (side + 1) * R, at_columns]
                        totals[i] = totals[i] + dot(mask, block, (1, 0))
            chosen[0, :, at_columns] = totals[1].astype(BF)
            chosen[1, :, at_columns] = totals[0].astype(BF)
        mine = target.at[:, :, :, columns]
        own = pltpu.make_async_copy(chosen, mine.at[:, 0], own_sem)
        across = [remote(chosen, mine.at[:, t], sems, t, here.slots(t)) for t in range(1, n)]
        swaps = [remote(chosen, mine.at[:, 0], sems, n, here.swap)]
        swaps += [remote(mine.at[:, t], mine.at[:, t], sems, n + t, here.swap) for t in range(1, n)]
        for copy in across + [swaps[0], own]:
            copy.start()
        for t in range(1, n):
            across[t - 1].wait_recv()
            swaps[t].start()
        own.wait()
        for copy in across:
            copy.wait_send()
        for copy in swaps:
            copy.wait()

    outs, _ = host(
        grid, body, 1,
        [whole_spec(heads, topk, 1)] + [any_spec()] * U,
        [picks[:, :, None], *pairs],
        [any_spec()], [kind(2, n, topk, 2 * half)],
        scratch=[
            pltpu.VMEM((U, 2, grid.T, half), BF),
            pltpu.VMEM((2, topk, half), BF),
            pltpu.SemaphoreType.DMA((U,)),
            pltpu.SemaphoreType.DMA,
            pltpu.SemaphoreType.DMA((2, 2 * n)),
        ],
        reaches=lambda here: [here.slots(n - t) for t in range(1, n)] + [here.swap],
    )
    return outs[0]


def finish_gradient(grid, grad_query, own, others, picks, memory, moves=()):
    rows, width = grad_query.shape
    heads = width // HEAD_DIM
    R, U = grid.R, grid.U

    def body(here, step, ins, outs, held):
        dq_ref, own_ref, others_ref = ins[:3]
        out_ref = outs[0]

        @pl.when(step == 0)
        def _():
            out_ref[...] = dq_ref[...]

        @pl.when(step > 0)
        def _():
            for side in range(2):
                at = pl.ds(side * R, R)
                for h in range(heads):
                    columns = pl.ds(h * HEAD_DIM, HEAD_DIM)
                    value = own_ref[0, at, columns]
                    for t in range(U - 1):
                        value = value + others_ref[t, 0, at, columns].astype(F32)
                    if memory is not None:
                        picked = ins[3][h]
                        down = lax.broadcasted_iota(jnp.int32, (R, picked.shape[1]), 0)
                        chosen = (down + piece_start(grid, here.k, side) == picked).astype(BF)
                        value = value + dot(chosen, ins[4][0, :, columns], (1, 0))
                    out_ref[at, columns] = value.astype(BF)

    which = lambda b: jnp.maximum(b - 1, 0)
    operands = [grad_query, own, others]
    specs = [
        whole_spec(rows, width),
        pl.BlockSpec((1, rows, width), lambda b: (which(b), 0, 0)),
        pl.BlockSpec((U - 1, 1, rows, width), lambda b: (0, which(b), 0, 0)),
    ]
    if memory is not None:
        topk = picks.shape[1]
        operands += [picks[:, None, :], memory]
        specs += [
            whole_spec(heads, 1, topk),
            pl.BlockSpec((1, topk, width), lambda b: (which(b), 0, 0)),
        ]
    outs, got = host(
        grid, body, 3, specs, operands, [columns_spec(rows, width)], [kind(rows, 3 * width)], moves,
        cost=pl.CostEstimate(flops=2 * rows * width, bytes_accessed=16 * rows * width, transcendentals=0),
    )
    return outs[0], got


FEED_TILE = 256


def feed(grid, hidden_rows, attended, gain, w_out, w_up, w_down, moves=()):
    rows, width = hidden_rows.shape
    hidden = w_down.shape[0]
    steps = hidden // FEED_TILE

    def body(here, step, ins, outs, held):
        hidden_ref, attended_ref, gain_ref, out_w, gate_w, up_w, down_w = ins
        out_ref, middle_ref, normed_ref, both_ref, inner_ref = outs

        @pl.when(step == 0)
        def _():
            value = hidden_ref[...].astype(F32) + dot(attended_ref[...], out_w[...], (1, 0))
            middle_ref[...] = value
            normed_ref[...] = norm(value, gain_ref[...]).astype(BF)
            held[0][...] = value

        normed = normed_ref[...]
        gate, up = dot(normed, gate_w[...], (1, 0)), dot(normed, up_w[...], (1, 0))
        both_ref[0] = gate.astype(BF)
        both_ref[1] = up.astype(BF)
        inner = (gate / (1.0 + jnp.exp(-gate)) * up).astype(BF)
        inner_ref[...] = inner
        held[0][...] += dot(inner, down_w[...], (1, 0))

        @pl.when(step == steps - 1)
        def _():
            out_ref[...] = held[0][...]

    tile = columns_spec(width, FEED_TILE)
    return host(
        grid, body, steps,
        [whole_spec(rows, width), whole_spec(rows, width), whole_spec(1, width), whole_spec(width, width), tile,
         columns_spec(width, FEED_TILE, first=steps), rows_spec(FEED_TILE, width)],
        [hidden_rows, attended, gain, w_out, w_up, w_up, w_down],
        [whole_spec(rows, width)] * 3 + [columns_spec(2, rows, FEED_TILE), columns_spec(rows, FEED_TILE)],
        [kind(rows, width, dtype=F32), kind(rows, width, dtype=F32), kind(rows, width), kind(2, rows, hidden), kind(rows, hidden)],
        moves,
        scratch=[pltpu.VMEM((rows, width), F32)],
        cost=pl.CostEstimate(flops=6 * rows * width * hidden, bytes_accessed=6 * width * hidden, transcendentals=rows * hidden),
    )


def feed_back(grid, grad, middle, gain, both, w_up, w_down, moves=()):
    rows, width = grad.shape
    hidden = w_down.shape[0]
    steps = hidden // FEED_TILE

    def body(here, step, ins, outs, held):
        grad_ref, middle_ref, gain_ref, both_ref, gate_w, up_w, down_w = ins
        out_ref, low_ref, grads_ref, gain_out = outs
        total = held[0]

        @pl.when(step == 0)
        def _():
            held[1][...] = grad_ref[...].astype(BF)
            total[...] = jnp.zeros_like(total)

        grad_inner = dot(held[1][...], down_w[...], (1, 1))
        gate, up = both_ref[0].astype(F32), both_ref[1].astype(F32)
        sigmoid = 1.0 / (1.0 + jnp.exp(-gate))
        scaled = grad_inner * sigmoid
        grad_gate = (scaled * up * (1.0 + gate * (1.0 - sigmoid))).astype(BF)
        grad_up = (scaled * gate).astype(BF)
        grads_ref[0] = grad_gate
        grads_ref[1] = grad_up
        total[...] += dot(grad_gate, gate_w[...], (1, 1)) + dot(grad_up, up_w[...], (1, 1))

        @pl.when(step == steps - 1)
        def _():
            pulled, grad_gain = norm_back(middle_ref[...], gain_ref[...], total[...])
            result = grad_ref[...] + pulled
            out_ref[...] = result
            low_ref[...] = result.astype(BF)
            gain_out[...] = grad_gain

    tile = columns_spec(width, FEED_TILE)
    whole = whole_spec(rows, width)
    return host(
        grid, body, steps,
        [whole, whole, whole_spec(1, width), columns_spec(2, rows, FEED_TILE), tile,
         columns_spec(width, FEED_TILE, first=steps), rows_spec(FEED_TILE, width)],
        [grad, middle, gain, both, w_up, w_up, w_down],
        [whole, whole, columns_spec(2, rows, FEED_TILE), whole_spec(1, width)],
        [kind(rows, width, dtype=F32), kind(rows, width), kind(2, rows, hidden), kind(1, width, dtype=F32)],
        moves,
        scratch=[pltpu.VMEM((rows, width), F32), pltpu.VMEM((rows, width), BF)],
        cost=pl.CostEstimate(flops=6 * rows * width * hidden, bytes_accessed=6 * width * hidden, transcendentals=rows * hidden),
    )


def norm(value, gain):
    return value * lax.rsqrt(jnp.mean(value * value, axis=-1, keepdims=True) + EPSILON) * gain


def norm_back(value, gain, grad):
    inverse = lax.rsqrt(jnp.mean(value * value, axis=-1, keepdims=True) + EPSILON)
    unit = value * inverse
    grad_gain = jnp.sum(grad * unit, axis=0, keepdims=True)
    scaled = grad * gain
    pulled = inverse * (scaled - unit * jnp.mean(scaled * unit, axis=-1, keepdims=True))
    return pulled, grad_gain


def product(grid, left, left_other, right, moves=(), piece=(0, 1)):
    rows, height = left.shape
    stacked = right.ndim == 3
    full = right.shape[-1] if stacked else right.shape[-1] // 2
    half = full // piece[1]
    tile = 512 if height % 512 == 0 else height // 2
    tiles = height // tile
    fetch = left_other is None

    def part(ref, c):
        ref = ref.at[c] if stacked else ref
        start = piece[0] * half if stacked else c * full + piece[0] * half
        return ref.at[:, pl.ds(pl.multiple_of(start, 128), half)]

    def body(here, step, ins, outs, held):
        own_ref, other_ref, right_ref = ins
        own_right, other_right, total, own_sem, sems = held[:5]
        own = pltpu.make_async_copy(part(right_ref, here.c), own_right, own_sem)
        swaps = [remote(part(right_ref, 1 - here.c), other_right, sems, 0, here.swap)]
        if fetch:
            swaps.append(remote(other_ref, held[5], sems, 1, here.swap))

        @pl.when(step == 0)
        def _():
            own.start()
            for swap in swaps:
                swap.start()
            own.wait()

        @pl.when(step < tiles)
        def _():
            total[step] = dot(own_ref[...], own_right[...], (0, 0))

        @pl.when(step == tiles)
        def _():
            for swap in swaps:
                swap.wait()

        @pl.when(step >= tiles)
        def _():
            other = other_ref
            if fetch:
                other = held[5].at[:, pl.ds(pl.multiple_of((step - tiles) * tile, 128), tile)]
            outs[0][...] = (total[step - tiles] + dot(other[...], other_right[...], (0, 0))).astype(BF)

    early = lambda i: jnp.minimum(i, tiles - 1)
    late = lambda i: jnp.maximum(i - tiles, 0)
    other_spec = any_spec() if fetch else pl.BlockSpec((rows, tile), lambda i: (0, late(i)))
    outs, got = host(
        grid, body, 2 * tiles,
        [pl.BlockSpec((rows, tile), lambda i: (0, early(i))), other_spec, any_spec()],
        [left, left if fetch else left_other, right],
        [pl.BlockSpec((tile, half), lambda i: (late(i), 0))],
        [kind(height, half)],
        moves,
        scratch=[
            pltpu.VMEM((rows, half), BF),
            pltpu.VMEM((rows, half), BF),
            pltpu.VMEM((tiles, tile, half), F32),
            pltpu.SemaphoreType.DMA,
            pltpu.SemaphoreType.DMA((2, 2)),
        ] + [pltpu.VMEM((rows, height), BF)] * fetch,
        cost=pl.CostEstimate(flops=4 * rows * height * half, bytes_accessed=2 * height * half, transcendentals=0),
        reaches=lambda here: [here.swap],
    )
    return outs[0], got


class Reduce:
    def __init__(self, grid, total):
        self.grid = grid
        self.parts = total.reshape(grid.J, total.shape[0] // grid.J, total.shape[1])
        self.phase, self.came = 0, []

    def flip(self):
        return flip_move(self.grid, self.parts, self.phase)

    def flipped(self, got):
        grid = self.grid
        if self.phase == 0:
            kept = jnp.stack(
                [
                    lax.dynamic_index_in_dim(self.parts, grid.place(2 * i, grid.c), 0, keepdims=False)
                    for i in range(grid.J // 2)
                ]
            )
        else:
            kept = self.parts[0::2]
        self.parts = (kept.astype(F32) + got.astype(F32)).astype(BF)
        self.phase += 1
        if self.phase == grid.bits:
            self.line = self.parts.reshape(2, grid.F, -1, self.parts.shape[2])

    def ring(self, distances=None):
        grid = self.grid
        while self.phase < grid.bits:
            self.flipped(send(grid, [self.flip()])[0])
        return ring_move(grid, self.line, distances or list(range(1, grid.F)))

    def far(self):
        return self.ring([self.grid.F // 2])

    def near(self):
        return self.ring([t for t in range(1, self.grid.F) if t != self.grid.F // 2])

    def arrived(self, got):
        grid = self.grid
        self.came.append(got)
        if sum(part.shape[0] for part in self.came) < grid.F - 1:
            return
        here = lax.dynamic_index_in_dim(self.line, grid.f, 1, keepdims=False)
        self.summed = here.astype(F32) + sum(
            part[i].astype(F32) for part in self.came for i in range(part.shape[0])
        )
        give = lax.dynamic_index_in_dim(self.summed, 1 - grid.c, 0, keepdims=False)
        self.give = give.astype(BF)

    def done(self, got):
        grid = self.grid
        mine = lax.dynamic_index_in_dim(self.summed, grid.c, 0, keepdims=False)
        got = got.astype(F32)
        return jnp.concatenate(
            [jnp.where(grid.c == 0, mine, got), jnp.where(grid.c == 0, got, mine)], axis=1
        )


def local(
    n_dp,
    pieces,
    tokens,
    cotangent,
    doc_lengths,
    partner,
    memory_picks,
    attention_in,
    attention_out,
    feed_in,
    feed_out,
    norm_gains,
):
    IDS[0] = 1
    grid = Grid(n_dp, pieces)
    grid.trace()
    layers = attention_in.shape[0]
    width = tokens.shape[2]
    heads = width // HEAD_DIM
    topk = memory_picks.shape[3]
    valid_all, visible_all = jax.vmap(memory_plan)(doc_lengths, partner)
    valid = valid_all[grid.m, grid.slot].reshape(1)
    visible = visible_all[grid.m, grid.slot]
    relative = (grid.slot - jnp.arange(n_dp)) % n_dp
    bias = jnp.repeat(jnp.where(visible[relative], 0.0, MASKED), topk)[:, None].astype(F32)
    tables = rope_tables()
    picks_there = grid.swap(memory_picks)
    picks = jnp.where(grid.r == grid.c, memory_picks[grid.m, 0], picks_there[grid.m, 0])
    zero = grid.c == 0

    def both_halves(mine, other):
        return jnp.where(
            zero, jnp.concatenate([mine, other], axis=-1), jnp.concatenate([other, mine], axis=-1)
        )

    def half(value, c):
        size = value.shape[-1] // 2
        return lax.dynamic_slice_in_dim(value, c * size, size, axis=value.ndim - 1)

    tokens, *tables = lax.optimization_barrier((tokens, *tables))
    hidden, gains, weights = gather_all(
        grid, tokens, norm_gains, [attention_in, attention_out, feed_in, feed_out]
    )
    gain = lambda l, i: gains[l, i][None]
    flat = lambda w: w.reshape(-1, w.shape[-1])
    saved = []
    cotangent_rows = None
    for l in range(layers):
        w_qkv, w_out = flat(weights[l][0]), flat(weights[l][1])
        memory = l == layers - 1
        coming = weights[l + 1] if l + 1 < layers else None
        moves = []
        if coming is not None:
            moves.append(spread_move(grid, coming[3], [(0, 0, 1)]))
        if later_here(l, 2):
            moves += [
                spread_move(grid, weights[l][2], [(1, 0, 2), (1, 1, 2)]),
                spread_move(grid, weights[l][3], [(2, 0, 1)]),
            ]
        split, got = project(grid, memory, tables, hidden, gain(l, 0), w_qkv, moves)
        if coming is not None:
            coming[3] = got[0]
        if later_here(l, 2):
            weights[l][2:] = got[-2:]
        normed, query = split[:2]
        pairs = [split[2]] + [split[3][t] for t in range(grid.U - 1)]
        extra = None
        if memory:
            slots = gather_memory(grid, picks, pairs).reshape(2, n_dp * topk, -1)
            extra = {"query": split[4], "memory": slots, "bias": bias}
        moves = []
        if coming is not None:
            moves.append(spread_move(grid, coming[2], [(0, 0, 2)]))
        if later_here(l, 2):
            moves.append(spread_move(grid, weights[l][2], [(2, 0, 1)]))
        if memory:
            moves.append(regroup_move(grid, cotangent))
        attended, logsum, got = attend(grid, valid, query, pairs, extra, moves)
        if coming is not None:
            coming[2] = got[0]
        if later_here(l, 2):
            weights[l][2] = got[-2]
            for stage in range(3, grid.bits + 1):
                weights[l][2:] = send(grid, [spread_move(grid, w, [(stage, 0, 1)]) for w in weights[l][2:]])
        if memory:
            cotangent_rows = got[-1]
            extra["logsum"] = logsum
        moves = []
        if coming is not None:
            moves = [spread_move(grid, coming[2], [(0, 1, 2)]), spread_move(grid, coming[3], [(1, 0, 1)])]
        w_up, w_down = flat(weights[l][2]), flat(weights[l][3])
        (out, middle, normed_feed, both, inner), got = feed(
            grid, hidden, attended, gain(l, 1), w_out, w_up, w_down, moves
        )
        if coming is not None:
            coming[2:] = got
        saved.append((hidden, normed, query, pairs, extra, attended, middle, normed_feed, both, inner))
        hidden = out
    weights = [[flat(w) for w in kinds] for kinds in weights]
    cotangent_rows = cotangent_rows.reshape(-1, width)
    def row_halves(value):
        value = value.astype(BF).reshape(2, grid.R, width)
        return value[:, : grid.R // 2], value[:, grid.R // 2 :]

    out_rows = row_halves(hidden)
    grad = cotangent_rows.astype(F32)
    found = [[None] * 4 for _ in range(layers)]
    grad_gains = [[None, None] for _ in range(layers)]
    layer_output, above, inner_other = [], None, None

    def took(got, reduces):
        for result, (reduce, what) in zip(got, reduces):
            (reduce.flipped if what == "flip" else reduce.arrived)(result)

    def moves_of(reduces):
        return [getattr(reduce, what)() for reduce, what in reduces]

    for l in reversed(range(layers)):
        w_qkv, w_out, w_up, w_down = weights[l]
        hidden, normed, query, pairs, extra, attended, middle, normed_feed, both, inner = saved[l]
        low = grad.astype(BF)
        last_layer = above is None

        reduces = [] if last_layer else [(above[1], "flip"), (above[2][0], "far")]
        total, got = product(grid, inner, inner_other, low, moves_of(reduces))
        took(got, reduces)
        down = Reduce(grid, total)

        reduces = [(down, "flip")]
        if not last_layer:
            reduces += [(above[0], "flip"), (above[1], "flip"), (above[2][0], "near")]
        moves = moves_of(reduces) + [swap_move(normed_feed), swap_move(normed), swap_move(attended)]
        if last_layer:
            moves += [swap_move(saved[l - 1][9]), regroup_back_move(grid, out_rows[0])]
        (grad, grad_low, grads, gain_feed), got = feed_back(
            grid, grad, middle, gain(l, 1), both, w_up, w_down, moves
        )
        took(got, reduces)
        normed_feed_other, normed_other, attended_other = got[len(reduces) : len(reduces) + 3]
        if last_layer:
            inner_other = got[-2]
            layer_output.append(got[-1])

        ups = []
        pieces_of_up = 1 if last_layer else 2
        for piece in range(pieces_of_up):
            if piece == 0:
                reduces = [(down, "flip")] if last_layer else [(down, "flip"), (above[1], "far")]
            else:
                reduces = [(ups[0], "flip"), (above[1], "near")]
            total, got = product(
                grid, normed_feed, normed_feed_other, grads, moves_of(reduces), (piece, pieces_of_up)
            )
            took(got, reduces)
            ups.append(Reduce(grid, total))

        reduces = [(ups[-1], "flip"), (down, "ring")]
        if not last_layer:
            reduces += [(ups[0], "flip"), (above[0], "ring")]
        memory_grad = None
        if extra is None:
            outs, got = attend_back(grid, valid, tables, query, grad_low, w_out, pairs, moves_of(reduces))
            took(got, reduces)
        else:
            grad_heads = mm(grad_low, w_out, (1, 1)).astype(BF)
            moves = moves_of(reduces)
            if last_layer:
                moves.append(regroup_back_move(grid, out_rows[1]))
            outs, got = memory_back(grid, grad_heads, attended, extra, moves)
            took(got, reduces)
            if last_layer:
                layer_output.append(got[-1])
            joined = half(outs[1], grid.c).astype(F32) + outs[2].astype(F32)
            joined = joined.astype(BF).reshape(2, n_dp, topk, -1)
            outs, got = attend_back(
                grid, valid, tables, query, grad_heads, w_out, pairs, [slots_move(grid, joined, True)],
                [attended, extra["logsum"], outs[0]],
            )
            total = joined[:, 0].astype(F32) + sum(got[0][t].astype(F32) for t in range(n_dp - 1))
            for t in range(1, grid.Q):
                total = total + grid.within(total.astype(BF), t).astype(F32)
            total = total.astype(BF)
            memory_grad = both_halves(total, grid.swap(total))
        grad_query, own, others = outs[:3]
        total, got = product(grid, attended, attended_other, grad_low)
        across = Reduce(grid, total)
        reduces = [(ups[-1], "flip")]
        if not last_layer:
            reduces += [(across, "flip"), (ups[0], "ring")]
        grad_projected, got = finish_gradient(
            grid, grad_query, own, others, picks, memory_grad, moves_of(reduces)
        )
        took(got, reduces)
        pulled, gain_attention = norm_back(
            hidden.astype(F32), gain(l, 0), mm(grad_projected, w_qkv, (1, 1))
        )
        grad = grad + pulled
        grad_gains[l] = [gain_attention[0], gain_feed[0]]
        reduces, moves = [(across, "flip")], []
        if l == 0:
            small = GainSum(grid, jnp.stack([jnp.stack(pair) for pair in grad_gains]).reshape(-1, HEAD_DIM))
            reduces = [(ups[-1], "ring"), (across, "flip")]
            moves = [small.move()]
        total, got = product(grid, normed, normed_other, grad_projected, moves_of(reduces) + moves)
        took(got, reduces)
        if l == 0:
            small.took(got[-1])
        last = Reduce(grid, total)
        found[l][3] = down.done(grid.swap(down.give))
        if not last_layer:
            found[l + 1] = [r.done(grid.swap(r.give)) for r in (above[1], above[0])] + [
                feed_parts([r.done(grid.swap(r.give)) for r in above[2]]), found[l + 1][3]
            ]
        above = (across, last, ups)
    across, last, ups = above
    in_rows = row_halves(grad)
    input_grad = []
    for i, reduces in enumerate([[(last, "flip"), (across, "ring")], [(last, "flip")], [(last, "ring")]]):
        moves = moves_of(reduces)
        if i < 2:
            moves.append(regroup_back_move(grid, in_rows[i]))
        got = send(grid, moves + [small.move()])
        took(got, reduces)
        small.took(got[-1])
        if i < 2:
            input_grad.append(got[-2])
    layer_output = jnp.concatenate(layer_output, axis=1)
    input_grad = jnp.concatenate(input_grad, axis=1).astype(F32)
    found[0] = [r.done(grid.swap(r.give)) for r in (last, across)] + [
        feed_parts([r.done(grid.swap(r.give)) for r in ups]), found[0][3]
    ]
    total_gains = small.finish().reshape(layers, 2, n_dp * pieces, -1)
    device = (grid.j * 2 + grid.c) * grid.F + grid.f
    return (
        layer_output,
        input_grad,
        *(jnp.stack([found[l][i] for l in range(layers)]) for i in range(4)),
        lax.dynamic_index_in_dim(total_gains, device, 2, keepdims=False),
    )


def feed_parts(parts):
    sides = [[part[:, : part.shape[1] // 2] for part in parts], [part[:, part.shape[1] // 2 :] for part in parts]]
    return jnp.concatenate(sides[0] + sides[1], axis=1)


def solution(mesh):
    rows = P(None, ("dp", "fsdp"), None)
    in_specs = (rows, rows, P(), P(), P(None, "dp", None, None), rows, rows, rows, rows, P(None, None, ("dp", "fsdp")))
    out_specs = (rows, rows, rows, rows, rows, rows, P(None, None, ("dp", "fsdp")))
    body = functools.partial(local, mesh.shape["dp"], mesh.shape["fsdp"])
    return jax.shard_map(body, mesh=mesh, in_specs=in_specs, out_specs=out_specs, check_vma=False)
```

```python
import functools
import math

import jax
import jax.numpy as jnp
from jax import lax
from jax.experimental import pallas as pl
from jax.experimental.pallas import tpu as pltpu
from jax.sharding import PartitionSpec as P

HEAD_DIM = 128
SEG = 1024
MICRO = 2
EPSILON = 1e-06
MASKED = -1e30
SCALE = HEAD_DIM ** (-0.5)
LOG2E = 1.0 / math.log(2.0)
BF = jnp.bfloat16
F32 = jnp.float32
VMEM_LIMIT = 44 * 1024 * 1024


def slot_layout(lengths):
    slot_total = lengths.shape[0]
    slot_counts = ((lengths + SEG - 1) // SEG).astype(jnp.int32)
    slot_starts = (jnp.cumsum(slot_counts) - slot_counts).astype(jnp.int32)
    slot_index = jnp.arange(slot_total, dtype=jnp.int32)
    started = (slot_starts[None, :] <= slot_index[:, None]) & (slot_counts[None, :] > 0)
    owner_doc = (jnp.sum(started.astype(jnp.int32), axis=1) - 1).astype(jnp.int32)
    owner_pick = slot_index[None, :] == owner_doc[:, None]
    first_slot = jnp.sum(jnp.where(owner_pick, slot_starts[None, :], 0), axis=1).astype(jnp.int32)
    doc_total = jnp.sum(jnp.where(owner_pick, lengths[None, :], 0), axis=1).astype(jnp.int32)
    valid_rows = jnp.clip(doc_total - (slot_index - first_slot) * SEG, 0, SEG).astype(jnp.int32)
    return (valid_rows, owner_doc)


def memory_plan(lengths, partner_row):
    valid_rows, owner_doc = slot_layout(lengths)
    block_ids = jnp.arange(lengths.shape[0], dtype=jnp.int32)
    earlier = (block_ids[None, :] < block_ids[:, None]) & (owner_doc[None, :] == owner_doc[:, None])
    visible = earlier | (block_ids[None, :] == partner_row[:, None])
    return (valid_rows, visible)


class Grid:
    def __init__(self, n_dp, pieces):
        self.n_dp, self.F = n_dp, pieces
        self.J = n_dp // 2
        self.bits = self.J.bit_length() - 1
        self.Q = pieces // 4
        self.U = 2 * self.Q
        self.R = SEG // pieces
        self.T = 2 * self.R

    def trace(self):
        dp = lax.axis_index("dp")
        self.c, self.j, self.f = dp % 2, dp // 2, lax.axis_index("fsdp")
        self.q, self.g = self.f // self.Q, self.f % self.Q
        self.m, self.r = self.q // 2, self.q % 2
        self.k = self.c * self.Q + self.g
        self.slot = 2 * self.j + self.r

    def permute(self, value, target):
        pairs = []
        for j in range(self.J):
            for c in range(2):
                for f in range(self.F):
                    j2, c2, f2 = target(j, c, f)
                    pairs.append(((j * 2 + c) * self.F + f, (j2 * 2 + c2) * self.F + f2))
        return lax.ppermute(value, ("dp", "fsdp"), pairs)

    def swap(self, value):
        return self.permute(value, lambda j, c, f: (j, 1 - c, f))

    def ring(self, value, t):
        return self.permute(value, lambda j, c, f: (j, c, (f + t) % self.F))

    def bit(self, phase, c):
        return phase if c == 0 else self.bits - 1 - phase

    def flip(self, value, phase):
        return self.permute(value, lambda j, c, f: (j ^ (1 << self.bit(phase, c)), c, f))

    def mask(self, key, c):
        return sum(1 << self.bit(p, c) for p in range(self.bits) if key >> p & 1)

    def place(self, key, c):
        return jnp.where(c == 0, self.j ^ self.mask(key, 0), self.j ^ self.mask(key, 1))

    def member(self, value, t):
        def target(j, c, f):
            q, g = f // self.Q, f % self.Q
            k = (c * self.Q + g + t) % self.U
            return (j, k // self.Q, q * self.Q + k % self.Q)

        return self.permute(value, target)

    def within(self, value, t):
        return self.permute(
            value, lambda j, c, f: (j, c, f // self.Q * self.Q + (f % self.Q + t) % self.Q)
        )

    def slots(self, value, t):
        def target(j, c, f):
            q, g = f // self.Q, f % self.Q
            slot = (2 * j + q % 2 + t) % self.n_dp
            return (slot // 2, c, (2 * (q // 2) + slot % 2) * self.Q + g)

        return self.permute(value, target)

    def _spread(self, second):
        def target(j, c, f):
            m = f // (self.F // 2)
            m = 1 - m if second else m
            k = min(f, self.F - 1 - f)
            return (j, k // self.Q, (2 * m + c) * self.Q + k % self.Q)

        return target

    def _collect(self, second):
        there = self._spread(second)
        back = {
            there(0, c, f): (c, f) for c in range(2) for f in range(self.F)
        }
        return lambda j, c, f: (j,) + back[(0, c, f)]

    def to_units(self, value):
        here = self.f // (self.F // 2)
        first = self.permute(jnp.where(here == 0, value[0], value[1]), self._spread(False))
        second = self.permute(jnp.where(here == 0, value[1], value[0]), self._spread(True))
        return jnp.concatenate(
            [jnp.where(self.m == 0, first, second), jnp.where(self.m == 0, second, first)]
        )

    def from_units(self, value):
        low, high = value[: self.R], value[self.R :]
        first = self.permute(jnp.where(self.m == 0, low, high), self._collect(False))
        second = self.permute(jnp.where(self.m == 0, high, low), self._collect(True))
        here = self.f // (self.F // 2)
        return jnp.stack([jnp.where(here == 0, first, second), jnp.where(here == 0, second, first)])


def any_spec():
    return pl.BlockSpec(memory_space=pl.ANY)


MESH = pl.DeviceIdType.MESH


class Here:
    def __init__(self, grid):
        self.grid = grid
        dp = lax.axis_index("dp")
        self.j, self.c, self.f = dp // 2, dp % 2, lax.axis_index("fsdp")
        self.q, self.g = self.f // grid.Q, self.f % grid.Q
        self.m, self.r = self.q // 2, self.q % 2
        self.k = self.c * grid.Q + self.g
        self.swap = self.device(self.j, 1 - self.c, self.f)

    def device(self, j, c, f):
        return {"dp": 2 * j + c, "fsdp": f}

    def ring(self, t):
        return self.device(self.j, self.c, (self.f + t) % self.grid.F)

    def step(self, phase):
        first, second = (1 << self.grid.bit(phase, c) for c in (0, 1))
        return first + self.c * (second - first)

    def moved(self, j, phase):
        step = self.step(phase)
        return j + step * (1 - 2 * ((j // step) % 2))

    def flip(self, phase):
        return self.device(self.moved(self.j, phase), self.c, self.f)

    def slots(self, t):
        grid = self.grid
        slot = (2 * self.j + self.r + t) % grid.n_dp
        return self.device(slot // 2, self.c, (2 * self.m + slot % 2) * grid.Q + self.g)

    def member(self, t):
        grid = self.grid
        k = (self.k + t) % grid.U
        return self.device(self.j, k // grid.Q, self.q * grid.Q + k % grid.Q)

    def place(self, key):
        j = self.j
        for phase in range(self.grid.bits):
            if key >> phase & 1:
                j = self.moved(j, phase)
        return j

    def greet(self):
        grid = self.grid
        barrier = pltpu.get_barrier_semaphore()
        peers = [self.ring(t) for t in range(1, grid.F)]
        peers += [self.device(self.j, 1 - self.c, (self.f + t) % grid.F) for t in range(grid.F)]
        for bit in range(grid.bits):
            step = 1 << bit
            peers.append(self.device(self.j + step * (1 - 2 * ((self.j // step) % 2)), self.c, self.f))
        for peer in peers:
            pl.semaphore_signal(barrier, inc=1, device_id=peer, device_id_type=MESH)
        pl.semaphore_wait(barrier, len(peers))


def remote(source, target, sems, index, device):
    return pltpu.make_async_remote_copy(
        src_ref=source,
        dst_ref=target,
        send_sem=sems.at[0, index],
        recv_sem=sems.at[1, index],
        device_id=device,
        device_id_type=MESH,
    )


class Spread:
    def __init__(self, here, shard, whole, sems, own_sem, split):
        grid = here.grid
        self.here, self.split = here, split
        rows, width = shard.shape
        half = width // 2 if split else width

        def part(ref, c):
            if not split:
                return ref
            return ref.at[(slice(None),) * (len(ref.shape) - 1) + (pl.ds(pl.multiple_of(c * half, 128), half),)]

        j, c, f = here.j, here.c, here.f
        mine = part(whole, c)
        self.own = pltpu.make_async_copy(part(shard, c), part(whole.at[j, c, f], c), own_sem)
        other = 1 - c if split else c
        self.pre = remote(part(shard, other), part(whole.at[j, c, f], other), sems, 0, here.swap)
        at = 1
        self.hops = []
        for h in range(1, grid.F):
            hop = []
            for way in (1, -1):
                origin = f - way * (h - 1)
                inside = lambda place: (place >= 0) & (place < grid.F)
                block = mine.at[j, :, jnp.clip(origin, 0, grid.F - 1)]
                copy = remote(block, block, sems, at, here.device(j, c, (f + way + grid.F) % grid.F))
                hop.append((copy, inside(origin) & inside(f + way), inside(f - way * h)))
                at += 1
            self.hops.append(hop)
        self.flips = []
        for phase in range(grid.bits):
            sent = []
            for key in range(1 << phase):
                block = mine.at[here.place(key)]
                sent.append(remote(block, block, sems, at, here.flip(phase)))
                at += 1
            self.flips.append(sent)
        self.swaps = []
        for key in range(grid.J if split else 0):
            block = mine.at[here.place(key)]
            self.swaps.append(remote(block, block, sems, at, here.swap))
            at += 1

    @staticmethod
    def count(grid):
        return 1 + 2 * (grid.F - 1) + (grid.J - 1) + grid.J

    def begin(self):
        self.own.start()
        self.pre.start()

    def to_line(self):
        self.own.wait()
        self.pre.wait()
        self._hop(0)

    def _hop(self, h):
        for copy, sends, _ in self.hops[h]:
            pl.when(sends)(copy.start)

    def _send(self, keys):
        for key in keys:
            if self.swaps:
                self.swaps[key].start()
        for phase, sent in enumerate(self.flips):
            for key in keys:
                if key < 1 << phase:
                    sent[key].start()

    def steps(self, whole):
        def along(h):
            for copy, _, comes in self.hops[h]:
                pl.when(comes)(copy.wait_recv)
            if h + 1 < len(self.hops):
                self._hop(h + 1)
                return
            for hop in self.hops:
                for copy, sends, _ in hop:
                    pl.when(sends)(copy.wait_send)
            if whole:
                self._send([0])

        def later(phase):
            for copy in self.flips[phase]:
                copy.wait()
            self._send([key + (1 << phase) for key in range(1 << phase)])

        def last():
            for copy in self.swaps:
                copy.wait()

        line = [functools.partial(along, h) for h in range(len(self.hops))]
        if not whole:
            return line
        return line + [functools.partial(later, p) for p in range(len(self.flips))] + [last]


class Regroup:
    def __init__(self, here, source, target, sems, own_sem):
        grid = here.grid
        half = grid.F // 2
        k = jnp.minimum(here.f, grid.F - 1 - here.f)
        side = here.f // half
        self.sends = []
        for m in range(2):
            c2, f2 = k // grid.Q, (2 * m + here.c) * grid.Q + k % grid.Q
            same = (c2 == here.c) & (f2 == here.f)
            own = pltpu.make_async_copy(source.at[m], target.at[side], own_sem)
            away = pltpu.make_async_remote_copy(
                src_ref=source.at[m],
                dst_ref=target.at[side],
                send_sem=sems.at[0, m],
                recv_sem=sems.at[1, side],
                device_id=here.device(here.j, c2, f2),
                device_id_type=MESH,
            )
            self.sends.append((same, own, away))
        self.arrivals = []
        for side in range(2):
            from_f = here.k if side == 0 else grid.F - 1 - here.k
            same = (here.r == here.c) & (from_f == here.f)
            came = pltpu.make_async_remote_copy(
                src_ref=source.at[0],
                dst_ref=target.at[side],
                send_sem=sems.at[0, 0],
                recv_sem=sems.at[1, side],
                device_id=here.swap,
                device_id_type=MESH,
            )
            self.arrivals.append((same, came))

    def start(self):
        for same, own, away in self.sends:
            pl.when(same)(own.start)
            pl.when(jnp.logical_not(same))(away.start)

    def wait(self):
        for same, own, away in self.sends:
            pl.when(same)(own.wait)
            pl.when(jnp.logical_not(same))(away.wait_send)
        for same, came in self.arrivals:
            pl.when(jnp.logical_not(same))(came.wait_recv)


def gather_body(grid, layers, kinds, *refs):
    tokens, gains = refs[:2]
    shards = refs[2 : 2 + kinds]
    outs = refs[2 + kinds :]
    tokens_out, gains_out = outs[:2]
    wholes = outs[2 : 2 + layers * kinds]
    sems, own_sems, regroup_sems = outs[2 + layers * kinds :]
    here = Here(grid)
    here.greet()
    rows = Regroup(here, tokens, tokens_out, regroup_sems, own_sems.at[0])
    moves = []
    for l, i in ORDER:
        n = l * kinds + i
        move = Spread(here, shards[i].at[l], wholes[n], sems.at[n + 1], own_sems.at[n + 2], True)
        moves.append((move, not later_here(l, i)))
    moves.insert(GAINS_AT, (Spread(here, gains, gains_out, sems.at[0], own_sems.at[1], False), True))
    for move, _ in moves:
        move.begin()
    steps = [move.steps(whole) for move, whole in moves]
    count = len(steps[0])
    for at in range(AHEAD):
        moves[at][0].to_line()
    for at in range(len(moves) + count - 1):
        if at == ROWS_AT:
            rows.start()
        if at + AHEAD < len(moves):
            moves[at + AHEAD][0].to_line()
        for back in reversed(range(count)):
            if 0 <= at - back < len(moves) and back < len(steps[at - back]):
                steps[at - back][back]()
    rows.wait()


ORDER = [(0, 1), (0, 3), (0, 2), (0, 0), (1, 0), (1, 1), (1, 3), (1, 2)]
GAINS_AT, ROWS_AT, AHEAD = 3, 6, 1


def later_here(l, i):
    return l > 0 and i >= 2


def gather_all(grid, tokens, gains, shards):
    layers, kinds = shards[0].shape[0], len(shards)
    packed = jnp.zeros((8, 128), F32).at[: layers * 2, : gains.shape[2]].set(
        gains.astype(F32).reshape(layers * 2, -1)
    )
    whole = lambda shard: jax.ShapeDtypeStruct((grid.J, 2, grid.F) + shard.shape[-2:], shard.dtype)
    out_shape = [jax.ShapeDtypeStruct(tokens.shape, BF), whole(packed)]
    out_shape += [whole(shard) for _ in range(layers) for shard in shards]
    moves = 1 + layers * kinds
    outs = pl.pallas_call(
        functools.partial(gather_body, grid, layers, kinds),
        in_specs=[any_spec()] * (2 + kinds),
        out_specs=[any_spec()] * len(out_shape),
        out_shape=out_shape,
        scratch_shapes=[
            pltpu.SemaphoreType.DMA((moves, 2, Spread.count(grid))),
            pltpu.SemaphoreType.DMA((moves + 1,)),
            pltpu.SemaphoreType.DMA((2, 2)),
        ],
        compiler_params=pltpu.CompilerParams(
            collective_id=0, has_side_effects=True, vmem_limit_bytes=VMEM_LIMIT
        ),
    )(tokens, packed, *shards)
    gains_all = outs[1][..., : layers * 2, : gains.shape[2]]
    gains_all = jnp.moveaxis(gains_all, 3, 0).reshape(layers, 2, -1)
    weights = [list(outs[2 + l * kinds : 2 + (l + 1) * kinds]) for l in range(layers)]
    return outs[0].reshape(-1, tokens.shape[2]), gains_all, weights


def unless(condition, act):
    if condition is None:
        act()
    else:
        pl.when(jnp.logical_not(condition))(act)


class Move:
    def __init__(self, array, shape, count, copies, plan=None, in_place=False):
        self.array, self.shape, self.count, self.copies = array, shape, count, copies
        self.plan, self.in_place = plan or self._plain, in_place

    def _plain(self, here, source, target, sends, recvs, base):
        found = []
        for i, (what, where, peer, giver) in enumerate(self.copies(here, source, target)):
            copy = pltpu.make_async_remote_copy(
                src_ref=what,
                dst_ref=where,
                send_sem=sends.at[base + i],
                recv_sem=recvs.at[base + i],
                device_id=peer,
                device_id_type=MESH,
            )
            found.append((copy, None, None, giver, copy, None))
        return found


def flip_move(grid, parts, phase):
    count = parts.shape[0] // 2

    def copies(here, source, target):
        found = []
        for i in range(count):
            at = here.place(2 * i + 1) if phase == 0 else 2 * i + 1
            peer = here.flip(phase)
            found.append((source.at[at], target.at[i], peer, peer))
        return found

    return Move(parts, (count,) + parts.shape[1:], count, copies)


def ring_move(grid, line, distances):
    def copies(here, source, target):
        return [
            (source.at[:, (here.f + t) % grid.F], target.at[i], here.ring(t), here.ring(grid.F - t))
            for i, t in enumerate(distances)
        ]

    return Move(line, (len(distances), 2) + line.shape[2:], len(distances), copies)


def swap_move(array, give=None):
    def copies(here, source, target):
        return [(source if give is None else source.at[give(here)], target, here.swap, here.swap)]

    return Move(array, array.shape if give is None else array.shape[1:], 1, copies)


def swap_half_move(array):
    half = array.shape[-1] // 2

    def copies(here, source, target):
        start = pl.multiple_of((1 - here.c) * half, 128)
        return [(source.at[:, :, pl.ds(start, half)], target, here.swap, here.swap)]

    return Move(array, array.shape[:-1] + (half,), 1, copies)


def slots_move(grid, array, back):
    def copies(here, source, target):
        found = []
        for t in range(1, grid.n_dp):
            ahead, behind = here.slots(t), here.slots(grid.n_dp - t)
            if back:
                found.append((source.at[:, t], target.at[t - 1], behind, ahead))
            else:
                found.append((source, target.at[t - 1], ahead, behind))
        return found

    shape = array.shape if not back else array.shape[:1] + array.shape[2:]
    return Move(array, (grid.n_dp - 1,) + shape, grid.n_dp - 1, copies)


def member_move(grid, array, back):
    def copies(here, source, target):
        found = []
        for t in range(1, grid.U):
            ahead, behind = here.member(t), here.member(grid.U - t)
            if back:
                found.append((source.at[t - 1], target.at[t - 1], behind, ahead))
            else:
                found.append((source, target.at[t - 1], ahead, behind))
        return found

    shape = array.shape[1:] if back else array.shape
    return Move(array, (grid.U - 1,) + shape, grid.U - 1, copies)


def spread_move(grid, whole, stages):
    half = whole.shape[-1] // 2

    def keys_of(stage):
        return [0] if stage == 0 else range(1 << (stage - 1), 1 << stage)

    def copies(here, source, target):
        found = []
        for stage, part, parts in stages:
            size = half // parts
            columns = pl.ds(pl.multiple_of(here.c * half + part * size, 128), size)
            mine = target.at[:, :, :, :, columns]
            for key in keys_of(stage):
                block = mine.at[here.place(key)]
                found.append((block, block, here.swap, here.swap))
                for phase in range(stage, grid.bits):
                    found.append((block, block, here.flip(phase), here.flip(phase)))
        return found

    count = sum(len(keys_of(stage)) * (1 + grid.bits - stage) for stage, _, _ in stages)
    return Move(whole, whole.shape, count, copies, in_place=True)


def peer_move(array, peer):
    return Move(array, array.shape, 1, lambda here, source, target: [(source, target, peer(here), peer(here))])


def line_move(grid, array):
    def copies(here, source, target):
        return [(source, target.at[t - 1], here.ring(t), here.ring(grid.F - t)) for t in range(1, grid.F)]

    return Move(array, (grid.F - 1,) + array.shape, grid.F - 1, copies)


def regroup_move(grid, array):
    def plan(here, source, target, sends, recvs, base):
        found = []
        k = jnp.minimum(here.f, grid.F - 1 - here.f)
        side = here.f // (grid.F // 2)
        for m in range(2):
            c2, f2 = k // grid.Q, (2 * m + here.c) * grid.Q + k % grid.Q
            same = (c2 == here.c) & (f2 == here.f)
            away = pltpu.make_async_remote_copy(
                src_ref=source.at[m],
                dst_ref=target.at[side],
                send_sem=sends.at[base + m],
                recv_sem=recvs.at[base + side],
                device_id=here.device(here.j, c2, f2),
                device_id_type=MESH,
            )
            own = pltpu.make_async_copy(source.at[m], target.at[side], sends.at[base + m])
            from_f = here.k if m == 0 else grid.F - 1 - here.k
            same_in = (here.r == here.c) & (from_f == here.f)
            came = pltpu.make_async_remote_copy(
                src_ref=source.at[0],
                dst_ref=target.at[m],
                send_sem=sends.at[base],
                recv_sem=recvs.at[base + m],
                device_id=here.swap,
                device_id_type=MESH,
            )
            found.append((away, same, own, here.device(here.j, here.r, from_f), came, same_in))
        return found

    return Move(array, array.shape, 2, None, plan)


def regroup_back_move(grid, array):
    def plan(here, source, target, sends, recvs, base):
        found = []
        for piece in range(2):
            f = here.k if piece == 0 else grid.F - 1 - here.k
            same = (here.r == here.c) & (f == here.f)
            away = pltpu.make_async_remote_copy(
                src_ref=source.at[piece],
                dst_ref=target.at[here.m],
                send_sem=sends.at[base + piece],
                recv_sem=recvs.at[base + here.m],
                device_id=here.device(here.j, here.r, f),
                device_id_type=MESH,
            )
            own = pltpu.make_async_copy(source.at[piece], target.at[here.m], sends.at[base + piece])
            k = jnp.minimum(here.f, grid.F - 1 - here.f)
            c2, f2 = k // grid.Q, (2 * piece + here.c) * grid.Q + k % grid.Q
            same_in = (c2 == here.c) & (f2 == here.f)
            came = pltpu.make_async_remote_copy(
                src_ref=source.at[0],
                dst_ref=target.at[piece],
                send_sem=sends.at[base],
                recv_sem=recvs.at[base + piece],
                device_id=here.swap,
                device_id_type=MESH,
            )
            found.append((away, same, own, here.device(here.j, c2, f2), came, same_in))
        return found

    return Move(array, array.shape, 2, None, plan)


IDS = [1]


def host(grid, body, steps, in_specs, operands, out_specs, out_shape, moves=(), scratch=(), cost=None, reaches=None):
    counts = [len(operands), len(moves), len(out_shape), len(moves), len(scratch)]

    def kernel(*refs):
        parts, at = [], 0
        for count in counts:
            parts.append(refs[at : at + count])
            at += count
        ins, sources, outs, targets, held = parts
        here = Here(grid)
        step = pl.program_id(0)
        planned = []
        if moves:
            sends, recvs = refs[at:]
            base = 0
            for move, source, target in zip(moves, sources, targets):
                planned += move.plan(here, source, target, sends, recvs, base)
                base += move.count

        if moves or reaches:

            @pl.when(step == 0)
            def _():
                barrier = pltpu.get_barrier_semaphore()
                givers = reaches(here) if reaches else []
                for giver in givers:
                    pl.semaphore_signal(barrier, inc=1, device_id=giver, device_id_type=MESH)
                for _, _, _, giver, _, same_in in planned:
                    signal = functools.partial(
                        pl.semaphore_signal, barrier, inc=1, device_id=giver, device_id_type=MESH
                    )
                    unless(same_in, signal)
                due = len(givers) + sum(same is None for _, same, _, _, _, _ in planned)
                for _, same, _, _, _, _ in planned:
                    if same is not None:
                        due = due + 1 - same.astype(jnp.int32)
                pl.semaphore_wait(barrier, due)
                for away, same, own, _, _, _ in planned:
                    unless(same, away.start)
                    if same is not None:
                        pl.when(same)(own.start)

        if body is not None:
            body(here, step, ins, outs, held)
        if moves:

            @pl.when(step == steps - 1)
            def _():
                for away, same, own, _, came, same_in in planned:
                    unless(same, away.wait_send)
                    if same is not None:
                        pl.when(same)(own.wait)
                    unless(same_in, came.wait_recv)

    total = sum(move.count for move in moves)
    extra = {}
    sems = []
    if moves or reaches:
        extra = {"collective_id": IDS[0], "has_side_effects": True}
        IDS[0] += 1
    if moves:
        sems = [pltpu.SemaphoreType.DMA((total,)), pltpu.SemaphoreType.DMA((total,))]
    outs = pl.pallas_call(
        kernel,
        grid=(steps,),
        in_specs=list(in_specs) + [any_spec()] * len(moves),
        out_specs=list(out_specs) + [any_spec()] * len(moves),
        out_shape=list(out_shape) + [jax.ShapeDtypeStruct(m.shape, m.array.dtype) for m in moves],
        scratch_shapes=list(scratch) + sems,
        input_output_aliases={
            len(operands) + i: len(out_shape) + i for i, move in enumerate(moves) if move.in_place
        },
        compiler_params=pltpu.CompilerParams(vmem_limit_bytes=VMEM_LIMIT, **extra),
        cost_estimate=cost,
    )(*operands, *[move.array for move in moves])
    return outs[: len(out_shape)], outs[len(out_shape) :]


def send(grid, moves):
    return host(grid, None, 1, [], [], [], [], moves)[1]


class GainSum:
    def __init__(self, grid, total):
        self.grid, self.total, self.stage = grid, total, 0

    def move(self):
        grid, phase = self.grid, self.stage - 1
        if self.stage == 0:
            return swap_move(self.total)
        if phase < grid.bits:
            return peer_move(self.total, lambda here: here.flip(phase))
        return line_move(grid, self.total)

    def took(self, got):
        if self.stage > self.grid.bits:
            got = sum(got[t] for t in range(self.grid.F - 1))
        self.total = self.total + got
        self.stage += 1

    def finish(self):
        while self.stage <= self.grid.bits + 1:
            self.took(send(self.grid, [self.move()])[0])
        return self.total


def rope_tables():
    half_dim = HEAD_DIM // 2
    frequency = jnp.exp(
        jnp.arange(half_dim, dtype=F32) * (-2.0 * math.log(10000.0) / HEAD_DIM)
    )
    angles = jnp.arange(SEG, dtype=jnp.int32).astype(F32)[:, None] * frequency[None, :]
    cos, sin = jnp.cos(angles), jnp.sin(angles)
    return (jnp.concatenate([cos, cos], axis=-1), jnp.concatenate([-sin, sin], axis=-1))


def turn(values, cos, sin):
    return values * cos + pltpu.roll(values, HEAD_DIM // 2, 1) * sin


def smem():
    return pl.BlockSpec(memory_space=pltpu.SMEM)


def whole_spec(*shape):
    return pl.BlockSpec(shape, lambda i: (0,) * len(shape))


def columns_spec(*shape, first=0):
    return pl.BlockSpec(shape, lambda i: (0,) * (len(shape) - 1) + (i + first,))


def rows_spec(*shape):
    return pl.BlockSpec(shape, lambda i: (i,) + (0,) * (len(shape) - 1))


def kind(*shape, dtype=BF):
    return jax.ShapeDtypeStruct(shape, dtype)


def piece_start(grid, member, part):
    return (member if part == 0 else grid.F - 1 - member) * grid.R


def table_rows(grid, table_ref, member, part):
    start = pl.multiple_of(piece_start(grid, member, part), grid.R)
    return table_ref[pl.ds(start, grid.R), :]


def dot(left, right, contract):
    return lax.dot_general(
        left, right, (((contract[0],), (contract[1],)), ((), ())), preferred_element_type=F32
    )


def mm(left, right, contract=(1, 0)):
    return dot(left, right, contract)


def project(grid, memory, tables, hidden, gain, weight, moves=()):
    rows, width = hidden.shape
    heads = weight.shape[1] // (3 * HEAD_DIM)
    together = 2
    size = together * HEAD_DIM
    steps = heads // together
    count = 3 if memory else 2

    width_out = heads * HEAD_DIM

    def sends(here, held, target, step):
        columns = pl.ds(pl.multiple_of(step * size, 128), size)
        return [
            pltpu.make_async_remote_copy(
                src_ref=held[0].at[:, :, columns],
                dst_ref=target.at[t - 1, :, :, columns],
                send_sem=held[1].at[0, t - 1, step],
                recv_sem=held[1].at[1, t - 1, step],
                device_id=here.member(t),
                device_id_type=MESH,
            )
            for t in range(1, grid.U)
        ]

    def body(here, step, ins, outs, held):
        cos_ref, sin_ref, hidden_ref, gain_ref = ins[:4]
        normed_ref, q_out, kv_out, others = outs[:4]

        @pl.when(step == 0)
        def _():
            normed_ref[...] = norm(hidden_ref[...].astype(F32), gain_ref[...]).astype(BF)

        for part in range(2):
            at = pl.ds(part * grid.R, grid.R)
            cos = table_rows(grid, cos_ref, here.k, part)
            sin = table_rows(grid, sin_ref, here.k, part)
            normed = normed_ref[at, :]
            query, key, value = (dot(normed, w[...], (1, 0)) for w in ins[4:])
            kv_out[1, at, :] = value.astype(BF)
            for h in range(together):
                columns = slice(h * HEAD_DIM, (h + 1) * HEAD_DIM)
                q_out[at, columns] = turn(query[:, columns], cos, sin).astype(BF)
                kv_out[0, at, columns] = turn(key[:, columns], cos, sin).astype(BF)
            if memory:
                kv_out[2, at, :] = key.astype(BF)
                outs[4][at, :] = query.astype(BF)
        held[0][:, :, pl.ds(pl.multiple_of(step * size, 128), size)] = kv_out[...]
        for copy in sends(here, held, others, step):
            copy.start()

        @pl.when(step == steps - 1)
        def _():
            for i in range(steps):
                for copy in sends(here, held, others, i):
                    copy.wait()

    piece = columns_spec(rows, size)
    table = whole_spec(SEG, HEAD_DIM)
    flat = kind(rows, width_out)
    return host(
        grid,
        body,
        steps,
        [table, table, whole_spec(rows, width), whole_spec(1, width)]
        + [columns_spec(width, size, first=i * steps) for i in range(3)],
        [*tables, hidden, gain, weight, weight, weight],
        [whole_spec(rows, width), piece, columns_spec(count, rows, size), any_spec()] + [piece] * memory,
        [kind(rows, width), flat, kind(count, rows, width_out), kind(grid.U - 1, count, rows, width_out)]
        + [flat] * memory,
        moves,
        scratch=[
            pltpu.VMEM((count, rows, width_out), BF),
            pltpu.SemaphoreType.DMA((2, grid.U - 1, steps)),
        ],
        cost=pl.CostEstimate(
            flops=2 * rows * width * weight.shape[1], bytes_accessed=2 * width * weight.shape[1], transcendentals=0
        ),
        reaches=lambda here: [here.member(grid.U - t) for t in range(1, grid.U)],
    )


def part_scores(grid, here, valid, part, query, keys):
    shape = (grid.R, grid.R)
    apart = lax.broadcasted_iota(jnp.int32, shape, 0) - lax.broadcasted_iota(jnp.int32, shape, 1)
    found = []
    for t in range(grid.U):
        member = (here.k - t + grid.U) % grid.U
        for side in range(part + 1):
            score = dot(keys[t][side * grid.R : (side + 1) * grid.R], query, (1, 1))
            if side == part:
                start = piece_start(grid, member, side)
                allowed = apart <= piece_start(grid, here.k, part) - start
                if side == 1:
                    down = lax.broadcasted_iota(jnp.int32, shape, 0)
                    allowed = allowed & (down < valid - start)
                score = jnp.where(allowed, score, MASKED)
            found.append((t, side, score))
    return found


def softmax_parts(scores, stat=None):
    top = functools.reduce(jnp.maximum, [jnp.max(s, axis=0, keepdims=True) for s in scores])
    powers = [jnp.exp2((s - top) * (SCALE * LOG2E)) for s in scores]
    total = sum(jnp.sum(p, axis=0, keepdims=True) for p in powers)
    if stat is not None:
        stat(top * (SCALE * LOG2E) + jnp.log(total) * LOG2E)
    inverse = 1.0 / total
    return [p * inverse for p in powers]


def attention_cost(grid, heads, memory_rows, products):
    pairs = grid.T * (SEG * 3 // 4 + memory_rows) * heads
    return pl.CostEstimate(
        flops=2 * products * HEAD_DIM * pairs,
        bytes_accessed=2 * HEAD_DIM * heads * 4 * (SEG + memory_rows),
        transcendentals=pairs,
    )


def memory_operands(grid, extra):
    rows = extra["memory"].shape[1]
    return [extra["query"], extra["memory"], extra["bias"]], [
        columns_spec(grid.T, HEAD_DIM), columns_spec(2, rows, HEAD_DIM), whole_spec(rows, 1)
    ], rows


def attend(grid, valid, query, pairs, extra, moves=()):
    rows, width = query.shape
    heads = width // HEAD_DIM
    R, U = grid.R, grid.U

    def body(here, step, ins, outs, held):
        valid_ref, q_ref, kv_refs, refs = ins[0], ins[1], ins[2 : 2 + U], ins[2 + U :]
        keys, values = [r[0] for r in kv_refs], [r[1] for r in kv_refs]
        for part in range(2):
            at = pl.ds(part * R, R)
            found = part_scores(grid, here, valid_ref[0], part, q_ref[at, :], keys)
            scores = [s for _, _, s in found]
            mixed = [values[t][side * R : (side + 1) * R] for t, side, _ in found]
            if extra is not None:
                scores.append(dot(refs[1][0], refs[0][at, :], (1, 1)) + refs[2][...])
                mixed.append(refs[1][1])

            def stat(row):
                outs[1][0, :, at] = row

            probs = softmax_parts(scores, stat)
            total = sum(dot(value, p.astype(BF), (0, 0)) for value, p in zip(mixed, probs))
            outs[0][at, :] = total.T.astype(BF)

    piece = columns_spec(rows, HEAD_DIM)
    operands = [valid, query, *pairs]
    specs = [smem(), piece] + [columns_spec(2, rows, HEAD_DIM)] * U
    memory_rows = 0
    if extra is not None:
        more, more_specs, memory_rows = memory_operands(grid, extra)
        operands, specs = operands + more, specs + more_specs
    outs, got = host(
        grid, body, heads, specs, operands,
        [piece, rows_spec(1, 1, rows)], [kind(rows, width), kind(heads, 1, rows, dtype=F32)], moves,
        cost=attention_cost(grid, heads, memory_rows, 2),
    )
    return outs[0], outs[1], got


def inner_row(grads, mixed):
    return jnp.sum((grads.astype(F32) * mixed.astype(F32)).T, axis=0, keepdims=True)


def memory_back(grid, grad_heads, attended, extra, moves=()):
    rows, width = grad_heads.shape
    heads = width // HEAD_DIM
    per = heads // 2
    memory_rows = extra["memory"].shape[1]

    def memory_send(here, held, target, h):
        columns = pl.ds(pl.multiple_of(h * HEAD_DIM, HEAD_DIM), HEAD_DIM)
        return pltpu.make_async_remote_copy(
            src_ref=held[0].at[h],
            dst_ref=target.at[:, :, columns],
            send_sem=held[1].at[0, h],
            recv_sem=held[1].at[1, h],
            device_id=here.swap,
            device_id_type=MESH,
        )

    def body(here, step, ins, outs, held):
        g_ref, mixed_ref, stat_ref, q_ref, memory_ref, bias_ref = ins
        grad_key, grad_value = 0.0, 0.0
        for part in range(2):
            at = pl.ds(part * grid.R, grid.R)
            grads, query = g_ref[at, :], q_ref[at, :]
            inner = inner_row(grads, mixed_ref[at, :])
            score = dot(memory_ref[0], query, (1, 1)) + bias_ref[...]
            prob = jnp.exp2(score * (SCALE * LOG2E) - stat_ref[0, :, at])
            moved = (prob * (dot(memory_ref[1], grads, (1, 1)) - inner)).astype(BF)
            grad_key = grad_key + dot(moved, query, (1, 0))
            grad_value = grad_value + dot(prob.astype(BF), grads, (1, 0))
            outs[0][at, :] = dot(memory_ref[0], moved, (0, 0)).T
        grad_key, grad_value = (grad_key * SCALE).astype(BF), grad_value.astype(BF)
        outs[1][0] = grad_key
        outs[1][1] = grad_value

        @pl.when(step // per == 1 - here.c)
        def _():
            held[0][step % per, 0] = grad_key
            held[0][step % per, 1] = grad_value
            memory_send(here, held, outs[2], step % per).start()

        @pl.when(step == heads - 1)
        def _():
            for h in range(per):
                memory_send(here, held, outs[2], h).wait()

    piece = columns_spec(rows, HEAD_DIM)
    column = columns_spec(2, memory_rows, HEAD_DIM)
    return host(
        grid, body, heads,
        [piece, piece, rows_spec(1, 1, rows), piece, column, whole_spec(memory_rows, 1)],
        [grad_heads, attended, extra["logsum"], extra["query"], extra["memory"], extra["bias"]],
        [piece, column, any_spec()],
        [kind(rows, width, dtype=F32), kind(2, memory_rows, width), kind(2, memory_rows, width // 2)],
        moves,
        scratch=[pltpu.VMEM((per, 2, memory_rows, HEAD_DIM), BF), pltpu.SemaphoreType.DMA((2, per))],
        cost=pl.CostEstimate(
            flops=10 * HEAD_DIM * rows * memory_rows * heads,
            bytes_accessed=12 * memory_rows * width,
            transcendentals=rows * memory_rows * heads,
        ),
        reaches=lambda here: [here.swap],
    )


def attend_back(grid, valid, tables, query, grad, w_out, pairs, moves=(), memory=None):
    rows, width = query.shape
    heads = width // HEAD_DIM
    R, U = grid.R, grid.U

    def sends(here, held, target, h):
        columns = pl.ds(pl.multiple_of(h * HEAD_DIM, HEAD_DIM), HEAD_DIM)
        return [
            pltpu.make_async_remote_copy(
                src_ref=held[0].at[h, t - 1],
                dst_ref=target.at[t - 1, :, :, columns],
                send_sem=held[1].at[0, t - 1, h],
                recv_sem=held[1].at[1, t - 1, h],
                device_id=here.member(U - t),
                device_id_type=MESH,
            )
            for t in range(1, U)
        ]

    def body(here, step, ins, outs, held):
        valid_ref, cos_ref, sin_ref, q_ref, g_ref = ins[:5]
        kv_refs, refs = ins[5 : 5 + U], ins[5 + U :]
        keys, values = [r[0] for r in kv_refs], [r[1] for r in kv_refs]
        grad_keys, grad_values = {}, {}

        def add(store, at, value):
            store[at] = store[at] + value if at in store else value

        if memory is None:

            @pl.when(step == 0)
            def _():
                held[2][...] = dot(g_ref[...], refs[0][...], (1, 1)).astype(BF)

        for part in range(2):
            at_rows = pl.ds(part * R, R)
            asked = q_ref[at_rows, :]
            if memory is None:
                grads_in = held[2][at_rows, pl.ds(pl.multiple_of(step * HEAD_DIM, HEAD_DIM), HEAD_DIM)]
            else:
                grads_in = g_ref[at_rows, :]
            found = part_scores(grid, here, valid_ref[0], part, asked, keys)
            places = [(t, side) for t, side, _ in found]
            scores = [s for _, _, s in found]
            part_keys = [keys[t][side * R : (side + 1) * R] for t, side in places]
            part_values = [values[t][side * R : (side + 1) * R] for t, side in places]
            grads = [dot(value, grads_in, (1, 1)) for value in part_values]
            if memory is None:
                probs = softmax_parts(scores)
                inner = sum(jnp.sum(p * d, axis=0, keepdims=True) for p, d in zip(probs, grads))
            else:
                probs = [jnp.exp2(s * (SCALE * LOG2E) - refs[1][0, :, at_rows]) for s in scores]
                inner = inner_row(grads_in, refs[0][at_rows, :])
            back = None
            for at, p, d, key in zip(places, probs, grads, part_keys):
                moved = (p * (d - inner)).astype(BF)
                add(grad_keys, at, dot(moved, asked, (1, 0)))
                add(grad_values, at, dot(p.astype(BF), grads_in, (1, 0)))
                share = dot(key, moved, (0, 0))
                back = share if back is None else back + share
            cos = table_rows(grid, cos_ref, here.k, part)
            sin = table_rows(grid, sin_ref, here.k, part)
            result = turn(back.T, cos, -sin)
            if memory is not None:
                result = result + refs[2][at_rows, :]
            outs[0][at_rows, :] = (result * SCALE).astype(BF)
        for t in range(U):
            member = (here.k - t + U) % U
            for side in range(2):
                at_rows = pl.ds(side * R, R)
                cos = table_rows(grid, cos_ref, member, side)
                sin = table_rows(grid, sin_ref, member, side)
                key = turn(grad_keys[(t, side)], cos, -sin) * SCALE
                if t == 0:
                    outs[1][0, at_rows, :] = key
                    outs[1][1, at_rows, :] = grad_values[(t, side)]
                else:
                    held[0][step, t - 1, 0, at_rows, :] = key.astype(BF)
                    held[0][step, t - 1, 1, at_rows, :] = grad_values[(t, side)].astype(BF)
        for copy in sends(here, held, outs[2], step):
            copy.start()

        @pl.when(step == heads - 1)
        def _():
            for h in range(heads):
                for copy in sends(here, held, outs[2], h):
                    copy.wait()

    piece = columns_spec(rows, HEAD_DIM)
    pair = columns_spec(2, rows, HEAD_DIM)
    table = whole_spec(SEG, HEAD_DIM)
    operands = [valid, *tables, query, grad, *pairs]
    scratch = [pltpu.VMEM((heads, U - 1, 2, rows, HEAD_DIM), BF), pltpu.SemaphoreType.DMA((2, U - 1, heads))]
    if memory is None:
        specs = [smem(), table, table, piece, whole_spec(rows, width)] + [pair] * U + [whole_spec(width, width)]
        operands.append(w_out)
        scratch.append(pltpu.VMEM((rows, width), BF))
    else:
        specs = [smem(), table, table, piece, piece] + [pair] * U + [piece, rows_spec(1, 1, rows), piece]
        operands += memory
    return host(
        grid, body, heads, specs, operands,
        [piece, pair, any_spec()],
        [kind(rows, width), kind(2, rows, width, dtype=F32), kind(U - 1, 2, rows, width)],
        moves,
        scratch=scratch,
        cost=attention_cost(grid, heads, 0, 5),
        reaches=lambda here: [here.member(t) for t in range(1, U)],
    )


def gather_memory(grid, picks, pairs):
    n, U, R = grid.n_dp, grid.U, grid.R
    heads, topk = picks.shape
    per = heads // 2
    half = per * HEAD_DIM

    def body(here, step, ins, outs, held):
        picks_ref, sources, target = ins[0], ins[1:], outs[0]
        rows, chosen, load_sems, own_sem, sems = held
        columns = pl.ds(pl.multiple_of(here.c * half, 128), half)
        loads = [
            pltpu.make_async_copy(source.at[1:3, :, columns], rows.at[t], load_sems.at[t])
            for t, source in enumerate(sources)
        ]
        for load in loads:
            load.start()
        for load in loads:
            load.wait()
        for h in range(per):
            picked = picks_ref[here.c * per + h]
            at_columns = slice(h * HEAD_DIM, (h + 1) * HEAD_DIM)
            totals = [0.0, 0.0]
            for t in range(U):
                member = (here.k - t + U) % U
                for side in range(2):
                    across = lax.broadcasted_iota(jnp.int32, (topk, R), 1)
                    mask = (picked == across + piece_start(grid, member, side)).astype(BF)
                    for i in range(2):
                        block = rows[t, i, side * R : (side + 1) * R, at_columns]
                        totals[i] = totals[i] + dot(mask, block, (1, 0))
            chosen[0, :, at_columns] = totals[1].astype(BF)
            chosen[1, :, at_columns] = totals[0].astype(BF)
        mine = target.at[:, :, :, columns]
        own = pltpu.make_async_copy(chosen, mine.at[:, 0], own_sem)
        across = [remote(chosen, mine.at[:, t], sems, t, here.slots(t)) for t in range(1, n)]
        swaps = [remote(chosen, mine.at[:, 0], sems, n, here.swap)]
        swaps += [remote(mine.at[:, t], mine.at[:, t], sems, n + t, here.swap) for t in range(1, n)]
        for copy in across + [swaps[0], own]:
            copy.start()
        for t in range(1, n):
            across[t - 1].wait_recv()
            swaps[t].start()
        own.wait()
        for copy in across:
            copy.wait_send()
        for copy in swaps:
            copy.wait()

    outs, _ = host(
        grid, body, 1,
        [whole_spec(heads, topk, 1)] + [any_spec()] * U,
        [picks[:, :, None], *pairs],
        [any_spec()], [kind(2, n, topk, 2 * half)],
        scratch=[
            pltpu.VMEM((U, 2, grid.T, half), BF),
            pltpu.VMEM((2, topk, half), BF),
            pltpu.SemaphoreType.DMA((U,)),
            pltpu.SemaphoreType.DMA,
            pltpu.SemaphoreType.DMA((2, 2 * n)),
        ],
        reaches=lambda here: [here.slots(n - t) for t in range(1, n)] + [here.swap],
    )
    return outs[0]


def finish_gradient(grid, grad_query, own, others, picks, memory, moves=()):
    rows, width = grad_query.shape
    heads = width // HEAD_DIM
    R, U = grid.R, grid.U

    def body(here, step, ins, outs, held):
        dq_ref, own_ref, others_ref = ins[:3]
        out_ref = outs[0]

        @pl.when(step == 0)
        def _():
            out_ref[...] = dq_ref[...]

        @pl.when(step > 0)
        def _():
            for side in range(2):
                at = pl.ds(side * R, R)
                for h in range(heads):
                    columns = pl.ds(h * HEAD_DIM, HEAD_DIM)
                    value = own_ref[0, at, columns]
                    for t in range(U - 1):
                        value = value + others_ref[t, 0, at, columns].astype(F32)
                    if memory is not None:
                        picked = ins[3][h]
                        down = lax.broadcasted_iota(jnp.int32, (R, picked.shape[1]), 0)
                        chosen = (down + piece_start(grid, here.k, side) == picked).astype(BF)
                        value = value + dot(chosen, ins[4][0, :, columns], (1, 0))
                    out_ref[at, columns] = value.astype(BF)

    which = lambda b: jnp.maximum(b - 1, 0)
    operands = [grad_query, own, others]
    specs = [
        whole_spec(rows, width),
        pl.BlockSpec((1, rows, width), lambda b: (which(b), 0, 0)),
        pl.BlockSpec((U - 1, 1, rows, width), lambda b: (0, which(b), 0, 0)),
    ]
    if memory is not None:
        topk = picks.shape[1]
        operands += [picks[:, None, :], memory]
        specs += [
            whole_spec(heads, 1, topk),
            pl.BlockSpec((1, topk, width), lambda b: (which(b), 0, 0)),
        ]
    outs, got = host(
        grid, body, 3, specs, operands, [columns_spec(rows, width)], [kind(rows, 3 * width)], moves,
        cost=pl.CostEstimate(flops=2 * rows * width, bytes_accessed=16 * rows * width, transcendentals=0),
    )
    return outs[0], got


FEED_TILE = 256


def feed(grid, hidden_rows, attended, gain, w_out, w_up, w_down, moves=()):
    rows, width = hidden_rows.shape
    hidden = w_down.shape[0]
    steps = hidden // FEED_TILE

    def body(here, step, ins, outs, held):
        hidden_ref, attended_ref, gain_ref, out_w, gate_w, up_w, down_w = ins
        out_ref, middle_ref, normed_ref, both_ref, inner_ref = outs

        @pl.when(step == 0)
        def _():
            value = hidden_ref[...].astype(F32) + dot(attended_ref[...], out_w[...], (1, 0))
            middle_ref[...] = value
            normed_ref[...] = norm(value, gain_ref[...]).astype(BF)
            held[0][...] = value

        normed = normed_ref[...]
        gate, up = dot(normed, gate_w[...], (1, 0)), dot(normed, up_w[...], (1, 0))
        both_ref[0] = gate.astype(BF)
        both_ref[1] = up.astype(BF)
        inner = (gate / (1.0 + jnp.exp(-gate)) * up).astype(BF)
        inner_ref[...] = inner
        held[0][...] += dot(inner, down_w[...], (1, 0))

        @pl.when(step == steps - 1)
        def _():
            out_ref[...] = held[0][...]

    tile = columns_spec(width, FEED_TILE)
    return host(
        grid, body, steps,
        [whole_spec(rows, width), whole_spec(rows, width), whole_spec(1, width), whole_spec(width, width), tile,
         columns_spec(width, FEED_TILE, first=steps), rows_spec(FEED_TILE, width)],
        [hidden_rows, attended, gain, w_out, w_up, w_up, w_down],
        [whole_spec(rows, width)] * 3 + [columns_spec(2, rows, FEED_TILE), columns_spec(rows, FEED_TILE)],
        [kind(rows, width, dtype=F32), kind(rows, width, dtype=F32), kind(rows, width), kind(2, rows, hidden), kind(rows, hidden)],
        moves,
        scratch=[pltpu.VMEM((rows, width), F32)],
        cost=pl.CostEstimate(flops=6 * rows * width * hidden, bytes_accessed=6 * width * hidden, transcendentals=rows * hidden),
    )


def feed_back(grid, grad, middle, gain, both, w_up, w_down, moves=()):
    rows, width = grad.shape
    hidden = w_down.shape[0]
    steps = hidden // FEED_TILE

    def body(here, step, ins, outs, held):
        grad_ref, middle_ref, gain_ref, both_ref, gate_w, up_w, down_w = ins
        out_ref, low_ref, grads_ref, gain_out = outs
        total = held[0]

        @pl.when(step == 0)
        def _():
            held[1][...] = grad_ref[...].astype(BF)
            total[...] = jnp.zeros_like(total)

        grad_inner = dot(held[1][...], down_w[...], (1, 1))
        gate, up = both_ref[0].astype(F32), both_ref[1].astype(F32)
        sigmoid = 1.0 / (1.0 + jnp.exp(-gate))
        scaled = grad_inner * sigmoid
        grad_gate = (scaled * up * (1.0 + gate * (1.0 - sigmoid))).astype(BF)
        grad_up = (scaled * gate).astype(BF)
        grads_ref[0] = grad_gate
        grads_ref[1] = grad_up
        total[...] += dot(grad_gate, gate_w[...], (1, 1)) + dot(grad_up, up_w[...], (1, 1))

        @pl.when(step == steps - 1)
        def _():
            pulled, grad_gain = norm_back(middle_ref[...], gain_ref[...], total[...])
            result = grad_ref[...] + pulled
            out_ref[...] = result
            low_ref[...] = result.astype(BF)
            gain_out[...] = grad_gain

    tile = columns_spec(width, FEED_TILE)
    whole = whole_spec(rows, width)
    return host(
        grid, body, steps,
        [whole, whole, whole_spec(1, width), columns_spec(2, rows, FEED_TILE), tile,
         columns_spec(width, FEED_TILE, first=steps), rows_spec(FEED_TILE, width)],
        [grad, middle, gain, both, w_up, w_up, w_down],
        [whole, whole, columns_spec(2, rows, FEED_TILE), whole_spec(1, width)],
        [kind(rows, width, dtype=F32), kind(rows, width), kind(2, rows, hidden), kind(1, width, dtype=F32)],
        moves,
        scratch=[pltpu.VMEM((rows, width), F32), pltpu.VMEM((rows, width), BF)],
        cost=pl.CostEstimate(flops=6 * rows * width * hidden, bytes_accessed=6 * width * hidden, transcendentals=rows * hidden),
    )


def norm(value, gain):
    return value * lax.rsqrt(jnp.mean(value * value, axis=-1, keepdims=True) + EPSILON) * gain


def norm_back(value, gain, grad):
    inverse = lax.rsqrt(jnp.mean(value * value, axis=-1, keepdims=True) + EPSILON)
    unit = value * inverse
    grad_gain = jnp.sum(grad * unit, axis=0, keepdims=True)
    scaled = grad * gain
    pulled = inverse * (scaled - unit * jnp.mean(scaled * unit, axis=-1, keepdims=True))
    return pulled, grad_gain


def product(grid, left, left_other, right, moves=(), piece=(0, 1)):
    rows, height = left.shape
    stacked = right.ndim == 3
    full = right.shape[-1] if stacked else right.shape[-1] // 2
    half = full // piece[1]
    tile = 512 if height % 512 == 0 else height // 2
    tiles = height // tile
    fetch = left_other is None

    def part(ref, c):
        ref = ref.at[c] if stacked else ref
        start = piece[0] * half if stacked else c * full + piece[0] * half
        return ref.at[:, pl.ds(pl.multiple_of(start, 128), half)]

    def body(here, step, ins, outs, held):
        own_ref, other_ref, right_ref = ins
        own_right, other_right, total, own_sem, sems = held[:5]
        own = pltpu.make_async_copy(part(right_ref, here.c), own_right, own_sem)
        swaps = [remote(part(right_ref, 1 - here.c), other_right, sems, 0, here.swap)]
        if fetch:
            swaps.append(remote(other_ref, held[5], sems, 1, here.swap))

        @pl.when(step == 0)
        def _():
            own.start()
            for swap in swaps:
                swap.start()
            own.wait()

        @pl.when(step < tiles)
        def _():
            total[step] = dot(own_ref[...], own_right[...], (0, 0))

        @pl.when(step == tiles)
        def _():
            for swap in swaps:
                swap.wait()

        @pl.when(step >= tiles)
        def _():
            other = other_ref
            if fetch:
                other = held[5].at[:, pl.ds(pl.multiple_of((step - tiles) * tile, 128), tile)]
            outs[0][...] = (total[step - tiles] + dot(other[...], other_right[...], (0, 0))).astype(BF)

    early = lambda i: jnp.minimum(i, tiles - 1)
    late = lambda i: jnp.maximum(i - tiles, 0)
    other_spec = any_spec() if fetch else pl.BlockSpec((rows, tile), lambda i: (0, late(i)))
    outs, got = host(
        grid, body, 2 * tiles,
        [pl.BlockSpec((rows, tile), lambda i: (0, early(i))), other_spec, any_spec()],
        [left, left if fetch else left_other, right],
        [pl.BlockSpec((tile, half), lambda i: (late(i), 0))],
        [kind(height, half)],
        moves,
        scratch=[
            pltpu.VMEM((rows, half), BF),
            pltpu.VMEM((rows, half), BF),
            pltpu.VMEM((tiles, tile, half), F32),
            pltpu.SemaphoreType.DMA,
            pltpu.SemaphoreType.DMA((2, 2)),
        ] + [pltpu.VMEM((rows, height), BF)] * fetch,
        cost=pl.CostEstimate(flops=4 * rows * height * half, bytes_accessed=2 * height * half, transcendentals=0),
        reaches=lambda here: [here.swap],
    )
    return outs[0], got


class Reduce:
    def __init__(self, grid, total):
        self.grid = grid
        self.parts = total.reshape(grid.J, total.shape[0] // grid.J, total.shape[1])
        self.phase, self.came = 0, []

    def flip(self):
        return flip_move(self.grid, self.parts, self.phase)

    def flipped(self, got):
        grid = self.grid
        if self.phase == 0:
            kept = jnp.stack(
                [
                    lax.dynamic_index_in_dim(self.parts, grid.place(2 * i, grid.c), 0, keepdims=False)
                    for i in range(grid.J // 2)
                ]
            )
        else:
            kept = self.parts[0::2]
        self.parts = (kept.astype(F32) + got.astype(F32)).astype(BF)
        self.phase += 1
        if self.phase == grid.bits:
            self.line = self.parts.reshape(2, grid.F, -1, self.parts.shape[2])

    def ring(self, distances=None):
        grid = self.grid
        while self.phase < grid.bits:
            self.flipped(send(grid, [self.flip()])[0])
        return ring_move(grid, self.line, distances or list(range(1, grid.F)))

    def far(self):
        return self.ring([self.grid.F // 2])

    def near(self):
        return self.ring([t for t in range(1, self.grid.F) if t != self.grid.F // 2])

    def arrived(self, got):
        grid = self.grid
        self.came.append(got)

    def done(self):
        grid = self.grid
        here = lax.dynamic_index_in_dim(self.line, grid.f, 1, keepdims=False)
        summed = here.astype(F32) + sum(
            part[i].astype(F32) for part in self.came for i in range(part.shape[0])
        )
        mine = lax.dynamic_index_in_dim(summed, grid.c, 0, keepdims=False)
        give = lax.dynamic_index_in_dim(summed, 1 - grid.c, 0, keepdims=False)
        got = grid.swap(give.astype(BF)).astype(F32)
        return jnp.concatenate(
            [jnp.where(grid.c == 0, mine, got), jnp.where(grid.c == 0, got, mine)], axis=1
        )


def settle(grid, wanted, row_halves, moves):
    flat, ins, specs, scratch, out_shape = [], [], [], [], []
    for o, by_layer in enumerate(wanted):
        for layer, parts in enumerate(by_layer):
            for piece, reduce in enumerate(parts):
                flat.append((o, layer, piece, len(parts), reduce))
        rows, size = wanted[o][0][0].line.shape[2:]
        out_shape.append(kind(len(by_layer), rows, 2 * size * len(by_layer[0]), dtype=F32))
    for _, _, _, _, reduce in flat:
        _, F, rows, size = reduce.line.shape
        ins += [reduce.line, *reduce.came]
        scratch += [
            pltpu.VMEM((F, 2, rows, size), BF),
            pltpu.VMEM((2, rows, size), F32),
            pltpu.VMEM((rows, size), BF),
            pltpu.VMEM((rows, size), BF),
        ]
    count = len(flat)
    ins += row_halves
    high, width = row_halves[0].shape[1:]
    scratch += [pltpu.VMEM((2, 2, high, width), BF)]
    scratch += [pltpu.SemaphoreType.DMA((len(ins),)), pltpu.SemaphoreType.DMA((2, count))]
    out_shape.append(kind(2, 2 * high, width, dtype=F32))

    def body(here, step, refs, outs, held):
        rows_held, load_sems, sems = held[4 * count :]
        loads, swaps, at = [], [], 0
        for i, (_, _, _, _, reduce) in enumerate(flat):
            blocks, _, give, got = held[4 * i : 4 * i + 4]
            mine = [pltpu.make_async_copy(refs[at].at[:, here.f], blocks.at[0], load_sems.at[at])]
            at, filled = at + 1, 1
            for part in reduce.came:
                size = part.shape[0]
                mine.append(
                    pltpu.make_async_copy(refs[at], blocks.at[pl.ds(filled, size)], load_sems.at[at])
                )
                at, filled = at + 1, filled + size
            loads.append(mine)
            swaps.append(remote(give, got, sems, i, here.swap))
        loads.append(
            [pltpu.make_async_copy(refs[at + i], rows_held.at[i], load_sems.at[at + i]) for i in range(2)]
        )
        for mine in loads:
            for copy in mine:
                copy.start()
        for i in range(count):
            blocks, summed, give, _ = held[4 * i : 4 * i + 4]
            for copy in loads[i]:
                copy.wait()
            total = blocks[0].astype(F32)
            for t in range(1, blocks.shape[0]):
                total = total + blocks[t].astype(F32)
            summed[...] = total
            give[...] = summed[1 - here.c].astype(BF)
            swaps[i].start()
        for copy in loads[count]:
            copy.wait()
        for i in range(2):
            outs[-1][:, i * high : (i + 1) * high, :] = rows_held[i].astype(F32)
        for i, (o, layer, piece, pieces, _) in enumerate(flat):
            _, summed, _, got = held[4 * i : 4 * i + 4]
            swaps[i].wait()
            size = got.shape[1]

            def columns(c):
                return pl.ds(pl.multiple_of((c * pieces + piece) * size, 128), size)

            outs[o][layer, :, columns(here.c)] = summed[here.c]
            outs[o][layer, :, columns(1 - here.c)] = got[...].astype(F32)

    return host(
        grid, body, 1, [any_spec()] * len(ins), ins,
        [whole_spec(*o.shape) for o in out_shape], out_shape, moves,
        scratch=scratch,
        reaches=lambda here: [here.swap],
    )


def local(
    n_dp,
    pieces,
    tokens,
    cotangent,
    doc_lengths,
    partner,
    memory_picks,
    attention_in,
    attention_out,
    feed_in,
    feed_out,
    norm_gains,
):
    IDS[0] = 1
    grid = Grid(n_dp, pieces)
    grid.trace()
    layers = attention_in.shape[0]
    width = tokens.shape[2]
    heads = width // HEAD_DIM
    topk = memory_picks.shape[3]
    valid_all, visible_all = jax.vmap(memory_plan)(doc_lengths, partner)
    valid = valid_all[grid.m, grid.slot].reshape(1)
    visible = visible_all[grid.m, grid.slot]
    relative = (grid.slot - jnp.arange(n_dp)) % n_dp
    bias = jnp.repeat(jnp.where(visible[relative], 0.0, MASKED), topk)[:, None].astype(F32)
    tables = rope_tables()
    picks_there = grid.swap(memory_picks)
    picks = jnp.where(grid.r == grid.c, memory_picks[grid.m, 0], picks_there[grid.m, 0])
    zero = grid.c == 0

    def both_halves(mine, other):
        return jnp.where(
            zero, jnp.concatenate([mine, other], axis=-1), jnp.concatenate([other, mine], axis=-1)
        )

    def half(value, c):
        size = value.shape[-1] // 2
        return lax.dynamic_slice_in_dim(value, c * size, size, axis=value.ndim - 1)

    tokens, *tables = lax.optimization_barrier((tokens, *tables))
    hidden, gains, weights = gather_all(
        grid, tokens, norm_gains, [attention_in, attention_out, feed_in, feed_out]
    )
    gain = lambda l, i: gains[l, i][None]
    flat = lambda w: w.reshape(-1, w.shape[-1])
    saved = []
    cotangent_rows = None
    for l in range(layers):
        w_qkv, w_out = flat(weights[l][0]), flat(weights[l][1])
        memory = l == layers - 1
        coming = weights[l + 1] if l + 1 < layers else None
        moves = []
        if coming is not None:
            moves.append(spread_move(grid, coming[3], [(0, 0, 1)]))
        if later_here(l, 2):
            moves += [
                spread_move(grid, weights[l][2], [(1, 0, 2), (1, 1, 2)]),
                spread_move(grid, weights[l][3], [(2, 0, 1)]),
            ]
        split, got = project(grid, memory, tables, hidden, gain(l, 0), w_qkv, moves)
        if coming is not None:
            coming[3] = got[0]
        if later_here(l, 2):
            weights[l][2:] = got[-2:]
        normed, query = split[:2]
        pairs = [split[2]] + [split[3][t] for t in range(grid.U - 1)]
        extra = None
        if memory:
            slots = gather_memory(grid, picks, pairs).reshape(2, n_dp * topk, -1)
            extra = {"query": split[4], "memory": slots, "bias": bias}
        moves = []
        if coming is not None:
            moves.append(spread_move(grid, coming[2], [(0, 0, 2)]))
        if later_here(l, 2):
            moves.append(spread_move(grid, weights[l][2], [(2, 0, 1)]))
        if memory:
            moves.append(regroup_move(grid, cotangent))
        attended, logsum, got = attend(grid, valid, query, pairs, extra, moves)
        if coming is not None:
            coming[2] = got[0]
        if later_here(l, 2):
            weights[l][2] = got[-2]
            for stage in range(3, grid.bits + 1):
                weights[l][2:] = send(grid, [spread_move(grid, w, [(stage, 0, 1)]) for w in weights[l][2:]])
        if memory:
            cotangent_rows = got[-1]
            extra["logsum"] = logsum
        moves = []
        if coming is not None:
            moves = [spread_move(grid, coming[2], [(0, 1, 2)]), spread_move(grid, coming[3], [(1, 0, 1)])]
        w_up, w_down = flat(weights[l][2]), flat(weights[l][3])
        (out, middle, normed_feed, both, inner), got = feed(
            grid, hidden, attended, gain(l, 1), w_out, w_up, w_down, moves
        )
        if coming is not None:
            coming[2:] = got
        saved.append((hidden, normed, query, pairs, extra, attended, middle, normed_feed, both, inner))
        hidden = out
    weights = [[flat(w) for w in kinds] for kinds in weights]
    cotangent_rows = cotangent_rows.reshape(-1, width)
    def row_halves(value):
        value = value.astype(BF).reshape(2, grid.R, width)
        return value[:, : grid.R // 2], value[:, grid.R // 2 :]

    out_rows = row_halves(hidden)
    grad = cotangent_rows.astype(F32)
    found = [[None] * 4 for _ in range(layers)]
    grad_gains = [[None, None] for _ in range(layers)]
    layer_output, above, inner_other = [], None, None

    def took(got, reduces):
        for result, (reduce, what) in zip(got, reduces):
            (reduce.flipped if what == "flip" else reduce.arrived)(result)

    def moves_of(reduces):
        return [getattr(reduce, what)() for reduce, what in reduces]

    for l in reversed(range(layers)):
        w_qkv, w_out, w_up, w_down = weights[l]
        hidden, normed, query, pairs, extra, attended, middle, normed_feed, both, inner = saved[l]
        low = grad.astype(BF)
        last_layer = above is None

        reduces = [] if last_layer else [(above[1], "flip"), (above[2][0], "far")]
        total, got = product(grid, inner, inner_other, low, moves_of(reduces))
        took(got, reduces)
        down = Reduce(grid, total)

        reduces = [(down, "flip")]
        if not last_layer:
            reduces += [(above[0], "flip"), (above[1], "flip"), (above[2][0], "near")]
        moves = moves_of(reduces) + [swap_move(normed_feed), swap_move(normed), swap_move(attended)]
        if last_layer:
            moves += [swap_move(saved[l - 1][9]), regroup_back_move(grid, out_rows[0])]
        (grad, grad_low, grads, gain_feed), got = feed_back(
            grid, grad, middle, gain(l, 1), both, w_up, w_down, moves
        )
        took(got, reduces)
        normed_feed_other, normed_other, attended_other = got[len(reduces) : len(reduces) + 3]
        if last_layer:
            inner_other = got[-2]
            layer_output.append(got[-1])

        ups = []
        pieces_of_up = 1 if last_layer else 2
        for piece in range(pieces_of_up):
            if piece == 0:
                reduces = [(down, "flip")] if last_layer else [(down, "flip"), (above[1], "far")]
            else:
                reduces = [(ups[0], "flip"), (above[1], "near")]
            total, got = product(
                grid, normed_feed, normed_feed_other, grads, moves_of(reduces), (piece, pieces_of_up)
            )
            took(got, reduces)
            ups.append(Reduce(grid, total))

        reduces = [(ups[-1], "flip"), (down, "ring")]
        if not last_layer:
            reduces += [(ups[0], "flip"), (above[0], "ring")]
        memory_grad = None
        if extra is None:
            outs, got = attend_back(grid, valid, tables, query, grad_low, w_out, pairs, moves_of(reduces))
            took(got, reduces)
        else:
            grad_heads = mm(grad_low, w_out, (1, 1)).astype(BF)
            moves = moves_of(reduces)
            if last_layer:
                moves.append(regroup_back_move(grid, out_rows[1]))
            outs, got = memory_back(grid, grad_heads, attended, extra, moves)
            took(got, reduces)
            if last_layer:
                layer_output.append(got[-1])
            joined = half(outs[1], grid.c).astype(F32) + outs[2].astype(F32)
            joined = joined.astype(BF).reshape(2, n_dp, topk, -1)
            outs, got = attend_back(
                grid, valid, tables, query, grad_heads, w_out, pairs, [slots_move(grid, joined, True)],
                [attended, extra["logsum"], outs[0]],
            )
            total = joined[:, 0].astype(F32) + sum(got[0][t].astype(F32) for t in range(n_dp - 1))
            for t in range(1, grid.Q):
                total = total + grid.within(total.astype(BF), t).astype(F32)
            total = total.astype(BF)
            memory_grad = both_halves(total, grid.swap(total))
        grad_query, own, others = outs[:3]
        total, got = product(grid, attended, attended_other, grad_low)
        across = Reduce(grid, total)
        reduces = [(ups[-1], "flip")]
        if not last_layer:
            reduces += [(across, "flip"), (ups[0], "ring")]
        grad_projected, got = finish_gradient(
            grid, grad_query, own, others, picks, memory_grad, moves_of(reduces)
        )
        took(got, reduces)
        pulled, gain_attention = norm_back(
            hidden.astype(F32), gain(l, 0), mm(grad_projected, w_qkv, (1, 1))
        )
        grad = grad + pulled
        grad_gains[l] = [gain_attention[0], gain_feed[0]]
        reduces, moves = [(across, "flip")], []
        if l == 0:
            small = GainSum(grid, jnp.stack([jnp.stack(pair) for pair in grad_gains]).reshape(-1, HEAD_DIM))
            reduces = [(ups[-1], "ring"), (across, "flip")]
            moves = [small.move()]
        total, got = product(grid, normed, normed_other, grad_projected, moves_of(reduces) + moves)
        took(got, reduces)
        if l == 0:
            small.took(got[-1])
        last = Reduce(grid, total)
        found[l] = [[last], [across], ups, [down]]
        above = (across, last, ups)
    across, last, ups = above
    in_rows = row_halves(grad)
    input_grad = []
    for i, reduces in enumerate([[(last, "flip"), (across, "ring")], [(last, "flip")]]):
        got = send(grid, moves_of(reduces) + [regroup_back_move(grid, in_rows[i]), small.move()])
        took(got, reduces)
        small.took(got[-1])
        input_grad.append(got[-2])
    wanted = [[found[l][0] for l in range(1, layers)]]
    wanted += [[found[l][i] for l in range(layers)] for i in range(1, 4)]
    outs, got = settle(grid, wanted, input_grad, [last.ring(), small.move()])
    last.arrived(got[0])
    small.took(got[1])
    grad_in, grad_out, grad_up, grad_down, input_grad = outs
    grad_in = jnp.concatenate([last.done()[None], grad_in])
    layer_output = jnp.concatenate(layer_output, axis=1)
    total_gains = small.finish().reshape(layers, 2, n_dp * pieces, -1)
    device = (grid.j * 2 + grid.c) * grid.F + grid.f
    return (
        layer_output,
        input_grad,
        grad_in,
        grad_out,
        grad_up,
        grad_down,
        lax.dynamic_index_in_dim(total_gains, device, 2, keepdims=False),
    )


def solution(mesh):
    rows = P(None, ("dp", "fsdp"), None)
    in_specs = (rows, rows, P(), P(), P(None, "dp", None, None), rows, rows, rows, rows, P(None, None, ("dp", "fsdp")))
    out_specs = (rows, rows, rows, rows, rows, rows, P(None, None, ("dp", "fsdp")))
    body = functools.partial(local, mesh.shape["dp"], mesh.shape["fsdp"])
    return jax.shard_map(body, mesh=mesh, in_specs=in_specs, out_specs=out_specs, check_vma=False)
```

```python
import functools
import math

import jax
import jax.numpy as jnp
from jax import lax
from jax.experimental import pallas as pl
from jax.experimental.pallas import tpu as pltpu
from jax.sharding import PartitionSpec as P

HEAD_DIM = 128
SEG = 1024
MICRO = 2
EPSILON = 1e-06
MASKED = -1e30
SCALE = HEAD_DIM ** (-0.5)
LOG2E = 1.0 / math.log(2.0)
BF = jnp.bfloat16
F32 = jnp.float32
VMEM_LIMIT = 42 * 1024 * 1024


def slot_layout(lengths):
    slot_total = lengths.shape[0]
    slot_counts = ((lengths + SEG - 1) // SEG).astype(jnp.int32)
    slot_starts = (jnp.cumsum(slot_counts) - slot_counts).astype(jnp.int32)
    slot_index = jnp.arange(slot_total, dtype=jnp.int32)
    started = (slot_starts[None, :] <= slot_index[:, None]) & (slot_counts[None, :] > 0)
    owner_doc = (jnp.sum(started.astype(jnp.int32), axis=1) - 1).astype(jnp.int32)
    owner_pick = slot_index[None, :] == owner_doc[:, None]
    first_slot = jnp.sum(jnp.where(owner_pick, slot_starts[None, :], 0), axis=1).astype(jnp.int32)
    doc_total = jnp.sum(jnp.where(owner_pick, lengths[None, :], 0), axis=1).astype(jnp.int32)
    valid_rows = jnp.clip(doc_total - (slot_index - first_slot) * SEG, 0, SEG).astype(jnp.int32)
    return (valid_rows, owner_doc)


def memory_plan(lengths, partner_row):
    valid_rows, owner_doc = slot_layout(lengths)
    block_ids = jnp.arange(lengths.shape[0], dtype=jnp.int32)
    earlier = (block_ids[None, :] < block_ids[:, None]) & (owner_doc[None, :] == owner_doc[:, None])
    visible = earlier | (block_ids[None, :] == partner_row[:, None])
    return (valid_rows, visible)


class Grid:
    def __init__(self, n_dp, pieces):
        self.n_dp, self.F = n_dp, pieces
        self.J = n_dp // 2
        self.bits = self.J.bit_length() - 1
        self.Q = pieces // 4
        self.U = 2 * self.Q
        self.R = SEG // pieces
        self.T = 2 * self.R

    def trace(self):
        dp = lax.axis_index("dp")
        self.c, self.j, self.f = dp % 2, dp // 2, lax.axis_index("fsdp")
        self.q, self.g = self.f // self.Q, self.f % self.Q
        self.m, self.r = self.q // 2, self.q % 2
        self.k = self.c * self.Q + self.g
        self.slot = 2 * self.j + self.r

    def permute(self, value, target):
        pairs = []
        for j in range(self.J):
            for c in range(2):
                for f in range(self.F):
                    j2, c2, f2 = target(j, c, f)
                    pairs.append(((j * 2 + c) * self.F + f, (j2 * 2 + c2) * self.F + f2))
        return lax.ppermute(value, ("dp", "fsdp"), pairs)

    def swap(self, value):
        return self.permute(value, lambda j, c, f: (j, 1 - c, f))

    def ring(self, value, t):
        return self.permute(value, lambda j, c, f: (j, c, (f + t) % self.F))

    def bit(self, phase, c):
        return phase if c == 0 else self.bits - 1 - phase

    def flip(self, value, phase):
        return self.permute(value, lambda j, c, f: (j ^ (1 << self.bit(phase, c)), c, f))

    def mask(self, key, c):
        return sum(1 << self.bit(p, c) for p in range(self.bits) if key >> p & 1)

    def place(self, key, c):
        return jnp.where(c == 0, self.j ^ self.mask(key, 0), self.j ^ self.mask(key, 1))

    def member(self, value, t):
        def target(j, c, f):
            q, g = f // self.Q, f % self.Q
            k = (c * self.Q + g + t) % self.U
            return (j, k // self.Q, q * self.Q + k % self.Q)

        return self.permute(value, target)

    def within(self, value, t):
        return self.permute(
            value, lambda j, c, f: (j, c, f // self.Q * self.Q + (f % self.Q + t) % self.Q)
        )

    def slots(self, value, t):
        def target(j, c, f):
            q, g = f // self.Q, f % self.Q
            slot = (2 * j + q % 2 + t) % self.n_dp
            return (slot // 2, c, (2 * (q // 2) + slot % 2) * self.Q + g)

        return self.permute(value, target)

    def _spread(self, second):
        def target(j, c, f):
            m = f // (self.F // 2)
            m = 1 - m if second else m
            k = min(f, self.F - 1 - f)
            return (j, k // self.Q, (2 * m + c) * self.Q + k % self.Q)

        return target

    def _collect(self, second):
        there = self._spread(second)
        back = {
            there(0, c, f): (c, f) for c in range(2) for f in range(self.F)
        }
        return lambda j, c, f: (j,) + back[(0, c, f)]

    def to_units(self, value):
        here = self.f // (self.F // 2)
        first = self.permute(jnp.where(here == 0, value[0], value[1]), self._spread(False))
        second = self.permute(jnp.where(here == 0, value[1], value[0]), self._spread(True))
        return jnp.concatenate(
            [jnp.where(self.m == 0, first, second), jnp.where(self.m == 0, second, first)]
        )

    def from_units(self, value):
        low, high = value[: self.R], value[self.R :]
        first = self.permute(jnp.where(self.m == 0, low, high), self._collect(False))
        second = self.permute(jnp.where(self.m == 0, high, low), self._collect(True))
        here = self.f // (self.F // 2)
        return jnp.stack([jnp.where(here == 0, first, second), jnp.where(here == 0, second, first)])


def any_spec():
    return pl.BlockSpec(memory_space=pl.ANY)


MESH = pl.DeviceIdType.MESH


class Here:
    def __init__(self, grid):
        self.grid = grid
        dp = lax.axis_index("dp")
        self.j, self.c, self.f = dp // 2, dp % 2, lax.axis_index("fsdp")
        self.q, self.g = self.f // grid.Q, self.f % grid.Q
        self.m, self.r = self.q // 2, self.q % 2
        self.k = self.c * grid.Q + self.g
        self.swap = self.device(self.j, 1 - self.c, self.f)

    def device(self, j, c, f):
        return {"dp": 2 * j + c, "fsdp": f}

    def ring(self, t):
        return self.device(self.j, self.c, (self.f + t) % self.grid.F)

    def step(self, phase):
        first, second = (1 << self.grid.bit(phase, c) for c in (0, 1))
        return first + self.c * (second - first)

    def moved(self, j, phase):
        step = self.step(phase)
        return j + step * (1 - 2 * ((j // step) % 2))

    def flip(self, phase):
        return self.device(self.moved(self.j, phase), self.c, self.f)

    def slots(self, t):
        grid = self.grid
        slot = (2 * self.j + self.r + t) % grid.n_dp
        return self.device(slot // 2, self.c, (2 * self.m + slot % 2) * grid.Q + self.g)

    def member(self, t):
        grid = self.grid
        k = (self.k + t) % grid.U
        return self.device(self.j, k // grid.Q, self.q * grid.Q + k % grid.Q)

    def place(self, key):
        j = self.j
        for phase in range(self.grid.bits):
            if key >> phase & 1:
                j = self.moved(j, phase)
        return j

    def greet(self):
        grid = self.grid
        barrier = pltpu.get_barrier_semaphore()
        peers = [self.ring(t) for t in range(1, grid.F)]
        peers += [self.device(self.j, 1 - self.c, (self.f + t) % grid.F) for t in range(grid.F)]
        for bit in range(grid.bits):
            step = 1 << bit
            peers.append(self.device(self.j + step * (1 - 2 * ((self.j // step) % 2)), self.c, self.f))
        for peer in peers:
            pl.semaphore_signal(barrier, inc=1, device_id=peer, device_id_type=MESH)
        pl.semaphore_wait(barrier, len(peers))


def remote(source, target, sems, index, device):
    return pltpu.make_async_remote_copy(
        src_ref=source,
        dst_ref=target,
        send_sem=sems.at[0, index],
        recv_sem=sems.at[1, index],
        device_id=device,
        device_id_type=MESH,
    )


class Spread:
    def __init__(self, here, shard, whole, sems, own_sem, split):
        grid = here.grid
        self.here, self.split = here, split
        rows, width = shard.shape
        half = width // 2 if split else width

        def part(ref, c):
            if not split:
                return ref
            return ref.at[(slice(None),) * (len(ref.shape) - 1) + (pl.ds(pl.multiple_of(c * half, 128), half),)]

        j, c, f = here.j, here.c, here.f
        mine = part(whole, c)
        self.own = pltpu.make_async_copy(part(shard, c), part(whole.at[j, c, f], c), own_sem)
        other = 1 - c if split else c
        self.pre = remote(part(shard, other), part(whole.at[j, c, f], other), sems, 0, here.swap)
        at = 1
        self.hops = []
        for h in range(1, grid.F):
            hop = []
            for way in (1, -1):
                origin = f - way * (h - 1)
                inside = lambda place: (place >= 0) & (place < grid.F)
                block = mine.at[j, :, jnp.clip(origin, 0, grid.F - 1)]
                copy = remote(block, block, sems, at, here.device(j, c, (f + way + grid.F) % grid.F))
                hop.append((copy, inside(origin) & inside(f + way), inside(f - way * h)))
                at += 1
            self.hops.append(hop)
        self.flips = []
        for phase in range(grid.bits):
            sent = []
            for key in range(1 << phase):
                block = mine.at[here.place(key)]
                sent.append(remote(block, block, sems, at, here.flip(phase)))
                at += 1
            self.flips.append(sent)
        self.swaps = []
        for key in range(grid.J if split else 0):
            block = mine.at[here.place(key)]
            self.swaps.append(remote(block, block, sems, at, here.swap))
            at += 1

    @staticmethod
    def count(grid):
        return 1 + 2 * (grid.F - 1) + (grid.J - 1) + grid.J

    def begin(self):
        self.own.start()
        self.pre.start()

    def to_line(self):
        self.own.wait()
        self.pre.wait()
        self._hop(0)

    def _hop(self, h):
        for copy, sends, _ in self.hops[h]:
            pl.when(sends)(copy.start)

    def _send(self, keys):
        for key in keys:
            if self.swaps:
                self.swaps[key].start()
        for phase, sent in enumerate(self.flips):
            for key in keys:
                if key < 1 << phase:
                    sent[key].start()

    def steps(self, whole):
        def along(h):
            for copy, _, comes in self.hops[h]:
                pl.when(comes)(copy.wait_recv)
            if h + 1 < len(self.hops):
                self._hop(h + 1)
                return
            for hop in self.hops:
                for copy, sends, _ in hop:
                    pl.when(sends)(copy.wait_send)
            if whole:
                self._send([0])

        def later(phase):
            for copy in self.flips[phase]:
                copy.wait()
            self._send([key + (1 << phase) for key in range(1 << phase)])

        def last():
            for copy in self.swaps:
                copy.wait()

        line = [functools.partial(along, h) for h in range(len(self.hops))]
        if not whole:
            return line
        return line + [functools.partial(later, p) for p in range(len(self.flips))] + [last]


class Regroup:
    def __init__(self, here, source, target, sems, own_sem):
        grid = here.grid
        half = grid.F // 2
        k = jnp.minimum(here.f, grid.F - 1 - here.f)
        side = here.f // half
        self.sends = []
        for m in range(2):
            c2, f2 = k // grid.Q, (2 * m + here.c) * grid.Q + k % grid.Q
            same = (c2 == here.c) & (f2 == here.f)
            own = pltpu.make_async_copy(source.at[m], target.at[side], own_sem)
            away = pltpu.make_async_remote_copy(
                src_ref=source.at[m],
                dst_ref=target.at[side],
                send_sem=sems.at[0, m],
                recv_sem=sems.at[1, side],
                device_id=here.device(here.j, c2, f2),
                device_id_type=MESH,
            )
            self.sends.append((same, own, away))
        self.arrivals = []
        for side in range(2):
            from_f = here.k if side == 0 else grid.F - 1 - here.k
            same = (here.r == here.c) & (from_f == here.f)
            came = pltpu.make_async_remote_copy(
                src_ref=source.at[0],
                dst_ref=target.at[side],
                send_sem=sems.at[0, 0],
                recv_sem=sems.at[1, side],
                device_id=here.swap,
                device_id_type=MESH,
            )
            self.arrivals.append((same, came))

    def start(self):
        for same, own, away in self.sends:
            pl.when(same)(own.start)
            pl.when(jnp.logical_not(same))(away.start)

    def wait(self):
        for same, own, away in self.sends:
            pl.when(same)(own.wait)
            pl.when(jnp.logical_not(same))(away.wait_send)
        for same, came in self.arrivals:
            pl.when(jnp.logical_not(same))(came.wait_recv)


def gather_body(grid, layers, kinds, *refs):
    tokens, gains = refs[:2]
    shards = refs[2 : 2 + kinds]
    outs = refs[2 + kinds :]
    tokens_out, gains_out = outs[:2]
    wholes = outs[2 : 2 + layers * kinds]
    sems, own_sems, regroup_sems = outs[2 + layers * kinds :]
    here = Here(grid)
    here.greet()
    rows = Regroup(here, tokens, tokens_out, regroup_sems, own_sems.at[0])
    moves = []
    for l, i in ORDER:
        n = l * kinds + i
        move = Spread(here, shards[i].at[l], wholes[n], sems.at[n + 1], own_sems.at[n + 2], True)
        moves.append((move, not later_here(l, i)))
    moves.insert(GAINS_AT, (Spread(here, gains, gains_out, sems.at[0], own_sems.at[1], False), True))
    for move, _ in moves:
        move.begin()
    steps = [move.steps(whole) for move, whole in moves]
    count = len(steps[0])
    for at in range(AHEAD):
        moves[at][0].to_line()
    for at in range(len(moves) + count - 1):
        if at == ROWS_AT:
            rows.start()
        if at + AHEAD < len(moves):
            moves[at + AHEAD][0].to_line()
        for back in reversed(range(count)):
            if 0 <= at - back < len(moves) and back < len(steps[at - back]):
                steps[at - back][back]()
    rows.wait()


ORDER = [(0, 1), (0, 3), (0, 0), (0, 2), (1, 0), (1, 1), (1, 3), (1, 2)]
GAINS_AT, ROWS_AT, AHEAD = 3, 4, 1


def later_here(l, i):
    return l > 0 and i >= 2


def gather_all(grid, tokens, gains, shards):
    layers, kinds = shards[0].shape[0], len(shards)
    packed = jnp.zeros((8, 128), F32).at[: layers * 2, : gains.shape[2]].set(
        gains.astype(F32).reshape(layers * 2, -1)
    )
    whole = lambda shard: jax.ShapeDtypeStruct((grid.J, 2, grid.F) + shard.shape[-2:], shard.dtype)
    out_shape = [jax.ShapeDtypeStruct(tokens.shape, BF), whole(packed)]
    out_shape += [whole(shard) for _ in range(layers) for shard in shards]
    moves = 1 + layers * kinds
    outs = pl.pallas_call(
        functools.partial(gather_body, grid, layers, kinds),
        in_specs=[any_spec()] * (2 + kinds),
        out_specs=[any_spec()] * len(out_shape),
        out_shape=out_shape,
        scratch_shapes=[
            pltpu.SemaphoreType.DMA((moves, 2, Spread.count(grid))),
            pltpu.SemaphoreType.DMA((moves + 1,)),
            pltpu.SemaphoreType.DMA((2, 2)),
        ],
        compiler_params=pltpu.CompilerParams(
            collective_id=0, has_side_effects=True, vmem_limit_bytes=VMEM_LIMIT
        ),
    )(tokens, packed, *shards)
    gains_all = outs[1][..., : layers * 2, : gains.shape[2]]
    gains_all = jnp.moveaxis(gains_all, 3, 0).reshape(layers, 2, -1)
    weights = [list(outs[2 + l * kinds : 2 + (l + 1) * kinds]) for l in range(layers)]
    return outs[0].reshape(-1, tokens.shape[2]), gains_all, weights


def unless(condition, act):
    if condition is None:
        act()
    else:
        pl.when(jnp.logical_not(condition))(act)


class Move:
    def __init__(self, array, shape, count, copies, plan=None, in_place=False):
        self.array, self.shape, self.count, self.copies = array, shape, count, copies
        self.plan, self.in_place = plan or self._plain, in_place

    def _plain(self, here, source, target, sends, recvs, base):
        found = []
        for i, (what, where, peer, giver) in enumerate(self.copies(here, source, target)):
            copy = pltpu.make_async_remote_copy(
                src_ref=what,
                dst_ref=where,
                send_sem=sends.at[base + i],
                recv_sem=recvs.at[base + i],
                device_id=peer,
                device_id_type=MESH,
            )
            found.append((copy, None, None, giver, copy, None))
        return found


def flip_move(grid, parts, phase):
    count = parts.shape[0] // 2

    def copies(here, source, target):
        found = []
        for i in range(count):
            at = here.place(2 * i + 1) if phase == 0 else 2 * i + 1
            peer = here.flip(phase)
            found.append((source.at[at], target.at[i], peer, peer))
        return found

    return Move(parts, (count,) + parts.shape[1:], count, copies)


def ring_move(grid, line, distances):
    def copies(here, source, target):
        return [
            (source.at[:, (here.f + t) % grid.F], target.at[i], here.ring(t), here.ring(grid.F - t))
            for i, t in enumerate(distances)
        ]

    return Move(line, (len(distances), 2) + line.shape[2:], len(distances), copies)


def swap_move(array, give=None):
    def copies(here, source, target):
        return [(source if give is None else source.at[give(here)], target, here.swap, here.swap)]

    return Move(array, array.shape if give is None else array.shape[1:], 1, copies)


def swap_half_move(array):
    half = array.shape[-1] // 2

    def copies(here, source, target):
        start = pl.multiple_of((1 - here.c) * half, 128)
        return [(source.at[:, :, pl.ds(start, half)], target, here.swap, here.swap)]

    return Move(array, array.shape[:-1] + (half,), 1, copies)


def slots_move(grid, array, back):
    def copies(here, source, target):
        found = []
        for t in range(1, grid.n_dp):
            ahead, behind = here.slots(t), here.slots(grid.n_dp - t)
            if back:
                found.append((source.at[:, t], target.at[t - 1], behind, ahead))
            else:
                found.append((source, target.at[t - 1], ahead, behind))
        return found

    shape = array.shape if not back else array.shape[:1] + array.shape[2:]
    return Move(array, (grid.n_dp - 1,) + shape, grid.n_dp - 1, copies)


def member_move(grid, array, back):
    def copies(here, source, target):
        found = []
        for t in range(1, grid.U):
            ahead, behind = here.member(t), here.member(grid.U - t)
            if back:
                found.append((source.at[t - 1], target.at[t - 1], behind, ahead))
            else:
                found.append((source, target.at[t - 1], ahead, behind))
        return found

    shape = array.shape[1:] if back else array.shape
    return Move(array, (grid.U - 1,) + shape, grid.U - 1, copies)


def spread_move(grid, whole, stages):
    half = whole.shape[-1] // 2

    def keys_of(stage):
        return [0] if stage == 0 else range(1 << (stage - 1), 1 << stage)

    def copies(here, source, target):
        found = []
        for stage, part, parts in stages:
            size = half // parts
            columns = pl.ds(pl.multiple_of(here.c * half + part * size, 128), size)
            mine = target.at[:, :, :, :, columns]
            for key in keys_of(stage):
                block = mine.at[here.place(key)]
                found.append((block, block, here.swap, here.swap))
                for phase in range(stage, grid.bits):
                    found.append((block, block, here.flip(phase), here.flip(phase)))
        return found

    count = sum(len(keys_of(stage)) * (1 + grid.bits - stage) for stage, _, _ in stages)
    return Move(whole, whole.shape, count, copies, in_place=True)


def peer_move(array, peer):
    return Move(array, array.shape, 1, lambda here, source, target: [(source, target, peer(here), peer(here))])


def line_move(grid, array):
    def copies(here, source, target):
        return [(source, target.at[t - 1], here.ring(t), here.ring(grid.F - t)) for t in range(1, grid.F)]

    return Move(array, (grid.F - 1,) + array.shape, grid.F - 1, copies)


def regroup_move(grid, array):
    def plan(here, source, target, sends, recvs, base):
        found = []
        k = jnp.minimum(here.f, grid.F - 1 - here.f)
        side = here.f // (grid.F // 2)
        for m in range(2):
            c2, f2 = k // grid.Q, (2 * m + here.c) * grid.Q + k % grid.Q
            same = (c2 == here.c) & (f2 == here.f)
            away = pltpu.make_async_remote_copy(
                src_ref=source.at[m],
                dst_ref=target.at[side],
                send_sem=sends.at[base + m],
                recv_sem=recvs.at[base + side],
                device_id=here.device(here.j, c2, f2),
                device_id_type=MESH,
            )
            own = pltpu.make_async_copy(source.at[m], target.at[side], sends.at[base + m])
            from_f = here.k if m == 0 else grid.F - 1 - here.k
            same_in = (here.r == here.c) & (from_f == here.f)
            came = pltpu.make_async_remote_copy(
                src_ref=source.at[0],
                dst_ref=target.at[m],
                send_sem=sends.at[base],
                recv_sem=recvs.at[base + m],
                device_id=here.swap,
                device_id_type=MESH,
            )
            found.append((away, same, own, here.device(here.j, here.r, from_f), came, same_in))
        return found

    return Move(array, array.shape, 2, None, plan)


def regroup_back_move(grid, array):
    def plan(here, source, target, sends, recvs, base):
        found = []
        for piece in range(2):
            f = here.k if piece == 0 else grid.F - 1 - here.k
            same = (here.r == here.c) & (f == here.f)
            away = pltpu.make_async_remote_copy(
                src_ref=source.at[piece],
                dst_ref=target.at[here.m],
                send_sem=sends.at[base + piece],
                recv_sem=recvs.at[base + here.m],
                device_id=here.device(here.j, here.r, f),
                device_id_type=MESH,
            )
            own = pltpu.make_async_copy(source.at[piece], target.at[here.m], sends.at[base + piece])
            k = jnp.minimum(here.f, grid.F - 1 - here.f)
            c2, f2 = k // grid.Q, (2 * piece + here.c) * grid.Q + k % grid.Q
            same_in = (c2 == here.c) & (f2 == here.f)
            came = pltpu.make_async_remote_copy(
                src_ref=source.at[0],
                dst_ref=target.at[piece],
                send_sem=sends.at[base],
                recv_sem=recvs.at[base + piece],
                device_id=here.swap,
                device_id_type=MESH,
            )
            found.append((away, same, own, here.device(here.j, c2, f2), came, same_in))
        return found

    return Move(array, array.shape, 2, None, plan)


IDS = [1]


def host(grid, body, steps, in_specs, operands, out_specs, out_shape, moves=(), scratch=(), cost=None, reaches=None):
    counts = [len(operands), len(moves), len(out_shape), len(moves), len(scratch)]

    def kernel(*refs):
        parts, at = [], 0
        for count in counts:
            parts.append(refs[at : at + count])
            at += count
        ins, sources, outs, targets, held = parts
        here = Here(grid)
        step = pl.program_id(0)
        planned = []
        if moves:
            sends, recvs = refs[at:]
            base = 0
            for move, source, target in zip(moves, sources, targets):
                planned += move.plan(here, source, target, sends, recvs, base)
                base += move.count

        if moves or reaches:

            @pl.when(step == 0)
            def _():
                barrier = pltpu.get_barrier_semaphore()
                givers = reaches(here) if reaches else []
                for giver in givers:
                    pl.semaphore_signal(barrier, inc=1, device_id=giver, device_id_type=MESH)
                for _, _, _, giver, _, same_in in planned:
                    signal = functools.partial(
                        pl.semaphore_signal, barrier, inc=1, device_id=giver, device_id_type=MESH
                    )
                    unless(same_in, signal)
                due = len(givers) + sum(same is None for _, same, _, _, _, _ in planned)
                for _, same, _, _, _, _ in planned:
                    if same is not None:
                        due = due + 1 - same.astype(jnp.int32)
                pl.semaphore_wait(barrier, due)
                for away, same, own, _, _, _ in planned:
                    unless(same, away.start)
                    if same is not None:
                        pl.when(same)(own.start)

        if body is not None:
            body(here, step, ins, outs, held)
        if moves:

            @pl.when(step == steps - 1)
            def _():
                for away, same, own, _, came, same_in in planned:
                    unless(same, away.wait_send)
                    if same is not None:
                        pl.when(same)(own.wait)
                    unless(same_in, came.wait_recv)

    total = sum(move.count for move in moves)
    extra = {}
    sems = []
    if moves or reaches:
        extra = {"collective_id": IDS[0], "has_side_effects": True}
        IDS[0] += 1
    if moves:
        sems = [pltpu.SemaphoreType.DMA((total,)), pltpu.SemaphoreType.DMA((total,))]
    outs = pl.pallas_call(
        kernel,
        grid=(steps,),
        in_specs=list(in_specs) + [any_spec()] * len(moves),
        out_specs=list(out_specs) + [any_spec()] * len(moves),
        out_shape=list(out_shape) + [jax.ShapeDtypeStruct(m.shape, m.array.dtype) for m in moves],
        scratch_shapes=list(scratch) + sems,
        input_output_aliases={
            len(operands) + i: len(out_shape) + i for i, move in enumerate(moves) if move.in_place
        },
        compiler_params=pltpu.CompilerParams(vmem_limit_bytes=VMEM_LIMIT, **extra),
        cost_estimate=cost,
    )(*operands, *[move.array for move in moves])
    return outs[: len(out_shape)], outs[len(out_shape) :]


def send(grid, moves):
    return host(grid, None, 1, [], [], [], [], moves)[1]


class GainSum:
    def __init__(self, grid, total):
        self.grid, self.total, self.stage = grid, total, 0

    def move(self):
        grid, phase = self.grid, self.stage - 1
        if self.stage == 0:
            return swap_move(self.total)
        if phase < grid.bits:
            return peer_move(self.total, lambda here: here.flip(phase))
        return line_move(grid, self.total)

    def took(self, got):
        if self.stage > self.grid.bits:
            got = sum(got[t] for t in range(self.grid.F - 1))
        self.total = self.total + got
        self.stage += 1

    def finish(self):
        while self.stage <= self.grid.bits + 1:
            self.took(send(self.grid, [self.move()])[0])
        return self.total


def rope_tables():
    half_dim = HEAD_DIM // 2
    frequency = jnp.exp(
        jnp.arange(half_dim, dtype=F32) * (-2.0 * math.log(10000.0) / HEAD_DIM)
    )
    angles = jnp.arange(SEG, dtype=jnp.int32).astype(F32)[:, None] * frequency[None, :]
    cos, sin = jnp.cos(angles), jnp.sin(angles)
    return (jnp.concatenate([cos, cos], axis=-1), jnp.concatenate([-sin, sin], axis=-1))


def turn(values, cos, sin):
    return values * cos + pltpu.roll(values, HEAD_DIM // 2, 1) * sin


def smem():
    return pl.BlockSpec(memory_space=pltpu.SMEM)


def whole_spec(*shape):
    return pl.BlockSpec(shape, lambda i: (0,) * len(shape))


def columns_spec(*shape, first=0):
    return pl.BlockSpec(shape, lambda i: (0,) * (len(shape) - 1) + (i + first,))


def rows_spec(*shape):
    return pl.BlockSpec(shape, lambda i: (i,) + (0,) * (len(shape) - 1))


def kind(*shape, dtype=BF):
    return jax.ShapeDtypeStruct(shape, dtype)


def piece_start(grid, member, part):
    return (member if part == 0 else grid.F - 1 - member) * grid.R


def table_rows(grid, table_ref, member, part):
    start = pl.multiple_of(piece_start(grid, member, part), grid.R)
    return table_ref[pl.ds(start, grid.R), :]


def dot(left, right, contract):
    return lax.dot_general(
        left, right, (((contract[0],), (contract[1],)), ((), ())), preferred_element_type=F32
    )


def mm(left, right, contract=(1, 0)):
    return dot(left, right, contract)


def project(grid, memory, tables, hidden, gain, weight, moves=()):
    rows, width = hidden.shape
    heads = weight.shape[1] // (3 * HEAD_DIM)
    together = 2
    size = together * HEAD_DIM
    steps = heads // together
    count = 3 if memory else 2

    width_out = heads * HEAD_DIM

    def sends(here, held, target, step):
        columns = pl.ds(pl.multiple_of(step * size, 128), size)
        return [
            pltpu.make_async_remote_copy(
                src_ref=held[0].at[:, :, columns],
                dst_ref=target.at[t - 1, :, :, columns],
                send_sem=held[1].at[0, t - 1, step],
                recv_sem=held[1].at[1, t - 1, step],
                device_id=here.member(t),
                device_id_type=MESH,
            )
            for t in range(1, grid.U)
        ]

    def body(here, step, ins, outs, held):
        cos_ref, sin_ref, hidden_ref, gain_ref = ins[:4]
        normed_ref, q_out, kv_out, others = outs[:4]

        @pl.when(step == 0)
        def _():
            normed_ref[...] = norm(hidden_ref[...].astype(F32), gain_ref[...]).astype(BF)

        for part in range(2):
            at = pl.ds(part * grid.R, grid.R)
            cos = table_rows(grid, cos_ref, here.k, part)
            sin = table_rows(grid, sin_ref, here.k, part)
            normed = normed_ref[at, :]
            query, key, value = (dot(normed, w[...], (1, 0)) for w in ins[4:])
            kv_out[1, at, :] = value.astype(BF)
            for h in range(together):
                columns = slice(h * HEAD_DIM, (h + 1) * HEAD_DIM)
                q_out[at, columns] = turn(query[:, columns], cos, sin).astype(BF)
                kv_out[0, at, columns] = turn(key[:, columns], cos, sin).astype(BF)
            if memory:
                kv_out[2, at, :] = key.astype(BF)
                outs[4][at, :] = query.astype(BF)
        held[0][:, :, pl.ds(pl.multiple_of(step * size, 128), size)] = kv_out[...]
        for copy in sends(here, held, others, step):
            copy.start()

        @pl.when(step == steps - 1)
        def _():
            for i in range(steps):
                for copy in sends(here, held, others, i):
                    copy.wait()

    piece = columns_spec(rows, size)
    table = whole_spec(SEG, HEAD_DIM)
    flat = kind(rows, width_out)
    return host(
        grid,
        body,
        steps,
        [table, table, whole_spec(rows, width), whole_spec(1, width)]
        + [columns_spec(width, size, first=i * steps) for i in range(3)],
        [*tables, hidden, gain, weight, weight, weight],
        [whole_spec(rows, width), piece, columns_spec(count, rows, size), any_spec()] + [piece] * memory,
        [kind(rows, width), flat, kind(count, rows, width_out), kind(grid.U - 1, count, rows, width_out)]
        + [flat] * memory,
        moves,
        scratch=[
            pltpu.VMEM((count, rows, width_out), BF),
            pltpu.SemaphoreType.DMA((2, grid.U - 1, steps)),
        ],
        cost=pl.CostEstimate(
            flops=2 * rows * width * weight.shape[1], bytes_accessed=2 * width * weight.shape[1], transcendentals=0
        ),
        reaches=lambda here: [here.member(grid.U - t) for t in range(1, grid.U)],
    )


def part_scores(grid, here, valid, part, query, keys):
    shape = (grid.R, grid.R)
    apart = lax.broadcasted_iota(jnp.int32, shape, 0) - lax.broadcasted_iota(jnp.int32, shape, 1)
    found = []
    for t in range(grid.U):
        member = (here.k - t + grid.U) % grid.U
        for side in range(part + 1):
            score = dot(keys[t][side * grid.R : (side + 1) * grid.R], query, (1, 1))
            if side == part:
                start = piece_start(grid, member, side)
                allowed = apart <= piece_start(grid, here.k, part) - start
                if side == 1:
                    down = lax.broadcasted_iota(jnp.int32, shape, 0)
                    allowed = allowed & (down < valid - start)
                score = jnp.where(allowed, score, MASKED)
            found.append((t, side, score))
    return found


def softmax_parts(scores, stat=None):
    top = functools.reduce(jnp.maximum, [jnp.max(s, axis=0, keepdims=True) for s in scores])
    powers = [jnp.exp2((s - top) * (SCALE * LOG2E)) for s in scores]
    total = sum(jnp.sum(p, axis=0, keepdims=True) for p in powers)
    if stat is not None:
        stat(top * (SCALE * LOG2E) + jnp.log(total) * LOG2E)
    inverse = 1.0 / total
    return [p * inverse for p in powers]


def attention_cost(grid, heads, memory_rows, products):
    pairs = grid.T * (SEG * 3 // 4 + memory_rows) * heads
    return pl.CostEstimate(
        flops=2 * products * HEAD_DIM * pairs,
        bytes_accessed=2 * HEAD_DIM * heads * 4 * (SEG + memory_rows),
        transcendentals=pairs,
    )


def memory_operands(grid, extra):
    rows = extra["memory"].shape[1]
    return [extra["query"], extra["memory"], extra["bias"]], [
        columns_spec(grid.T, HEAD_DIM), columns_spec(2, rows, HEAD_DIM), whole_spec(rows, 1)
    ], rows


def attend(grid, valid, query, pairs, extra, moves=()):
    rows, width = query.shape
    heads = width // HEAD_DIM
    R, U = grid.R, grid.U

    def body(here, step, ins, outs, held):
        valid_ref, q_ref, kv_refs, refs = ins[0], ins[1], ins[2 : 2 + U], ins[2 + U :]
        keys, values = [r[0] for r in kv_refs], [r[1] for r in kv_refs]
        for part in range(2):
            at = pl.ds(part * R, R)
            found = part_scores(grid, here, valid_ref[0], part, q_ref[at, :], keys)
            scores = [s for _, _, s in found]
            mixed = [values[t][side * R : (side + 1) * R] for t, side, _ in found]
            if extra is not None:
                scores.append(dot(refs[1][0], refs[0][at, :], (1, 1)) + refs[2][...])
                mixed.append(refs[1][1])

            def stat(row):
                outs[1][0, :, at] = row

            probs = softmax_parts(scores, stat)
            total = sum(dot(value, p.astype(BF), (0, 0)) for value, p in zip(mixed, probs))
            outs[0][at, :] = total.T.astype(BF)

    piece = columns_spec(rows, HEAD_DIM)
    operands = [valid, query, *pairs]
    specs = [smem(), piece] + [columns_spec(2, rows, HEAD_DIM)] * U
    memory_rows = 0
    if extra is not None:
        more, more_specs, memory_rows = memory_operands(grid, extra)
        operands, specs = operands + more, specs + more_specs
    outs, got = host(
        grid, body, heads, specs, operands,
        [piece, rows_spec(1, 1, rows)], [kind(rows, width), kind(heads, 1, rows, dtype=F32)], moves,
        cost=attention_cost(grid, heads, memory_rows, 2),
    )
    return outs[0], outs[1], got


def inner_row(grads, mixed):
    return jnp.sum((grads.astype(F32) * mixed.astype(F32)).T, axis=0, keepdims=True)


def memory_back(grid, grad_heads, attended, extra, moves=()):
    rows, width = grad_heads.shape
    heads = width // HEAD_DIM
    per = heads // 2
    memory_rows = extra["memory"].shape[1]

    def memory_send(here, held, target, h):
        columns = pl.ds(pl.multiple_of(h * HEAD_DIM, HEAD_DIM), HEAD_DIM)
        return pltpu.make_async_remote_copy(
            src_ref=held[0].at[h],
            dst_ref=target.at[:, :, columns],
            send_sem=held[1].at[0, h],
            recv_sem=held[1].at[1, h],
            device_id=here.swap,
            device_id_type=MESH,
        )

    def body(here, step, ins, outs, held):
        g_ref, mixed_ref, stat_ref, q_ref, memory_ref, bias_ref = ins
        grad_key, grad_value = 0.0, 0.0
        for part in range(2):
            at = pl.ds(part * grid.R, grid.R)
            grads, query = g_ref[at, :], q_ref[at, :]
            inner = inner_row(grads, mixed_ref[at, :])
            score = dot(memory_ref[0], query, (1, 1)) + bias_ref[...]
            prob = jnp.exp2(score * (SCALE * LOG2E) - stat_ref[0, :, at])
            moved = (prob * (dot(memory_ref[1], grads, (1, 1)) - inner)).astype(BF)
            grad_key = grad_key + dot(moved, query, (1, 0))
            grad_value = grad_value + dot(prob.astype(BF), grads, (1, 0))
            outs[0][at, :] = dot(memory_ref[0], moved, (0, 0)).T
        grad_key, grad_value = (grad_key * SCALE).astype(BF), grad_value.astype(BF)
        outs[1][0] = grad_key
        outs[1][1] = grad_value

        @pl.when(step // per == 1 - here.c)
        def _():
            held[0][step % per, 0] = grad_key
            held[0][step % per, 1] = grad_value
            memory_send(here, held, outs[2], step % per).start()

        @pl.when(step == heads - 1)
        def _():
            for h in range(per):
                memory_send(here, held, outs[2], h).wait()

    piece = columns_spec(rows, HEAD_DIM)
    column = columns_spec(2, memory_rows, HEAD_DIM)
    return host(
        grid, body, heads,
        [piece, piece, rows_spec(1, 1, rows), piece, column, whole_spec(memory_rows, 1)],
        [grad_heads, attended, extra["logsum"], extra["query"], extra["memory"], extra["bias"]],
        [piece, column, any_spec()],
        [kind(rows, width, dtype=F32), kind(2, memory_rows, width), kind(2, memory_rows, width // 2)],
        moves,
        scratch=[pltpu.VMEM((per, 2, memory_rows, HEAD_DIM), BF), pltpu.SemaphoreType.DMA((2, per))],
        cost=pl.CostEstimate(
            flops=10 * HEAD_DIM * rows * memory_rows * heads,
            bytes_accessed=12 * memory_rows * width,
            transcendentals=rows * memory_rows * heads,
        ),
        reaches=lambda here: [here.swap],
    )


def attend_back(grid, valid, tables, query, grad, w_out, pairs, moves=(), memory=None):
    rows, width = query.shape
    heads = width // HEAD_DIM
    R, U = grid.R, grid.U

    def sends(here, held, target, h):
        columns = pl.ds(pl.multiple_of(h * HEAD_DIM, HEAD_DIM), HEAD_DIM)
        return [
            pltpu.make_async_remote_copy(
                src_ref=held[0].at[h, t - 1],
                dst_ref=target.at[t - 1, :, :, columns],
                send_sem=held[1].at[0, t - 1, h],
                recv_sem=held[1].at[1, t - 1, h],
                device_id=here.member(U - t),
                device_id_type=MESH,
            )
            for t in range(1, U)
        ]

    def body(here, step, ins, outs, held):
        valid_ref, cos_ref, sin_ref, q_ref, g_ref = ins[:5]
        kv_refs, refs = ins[5 : 5 + U], ins[5 + U :]
        keys, values = [r[0] for r in kv_refs], [r[1] for r in kv_refs]
        grad_keys, grad_values = {}, {}

        def add(store, at, value):
            store[at] = store[at] + value if at in store else value

        if memory is None:

            @pl.when(step == 0)
            def _():
                held[2][...] = dot(g_ref[...], refs[0][...], (1, 1)).astype(BF)

        for part in range(2):
            at_rows = pl.ds(part * R, R)
            asked = q_ref[at_rows, :]
            if memory is None:
                grads_in = held[2][at_rows, pl.ds(pl.multiple_of(step * HEAD_DIM, HEAD_DIM), HEAD_DIM)]
            else:
                grads_in = g_ref[at_rows, :]
            found = part_scores(grid, here, valid_ref[0], part, asked, keys)
            places = [(t, side) for t, side, _ in found]
            scores = [s for _, _, s in found]
            part_keys = [keys[t][side * R : (side + 1) * R] for t, side in places]
            part_values = [values[t][side * R : (side + 1) * R] for t, side in places]
            grads = [dot(value, grads_in, (1, 1)) for value in part_values]
            if memory is None:
                probs = softmax_parts(scores)
                inner = sum(jnp.sum(p * d, axis=0, keepdims=True) for p, d in zip(probs, grads))
            else:
                probs = [jnp.exp2(s * (SCALE * LOG2E) - refs[1][0, :, at_rows]) for s in scores]
                inner = inner_row(grads_in, refs[0][at_rows, :])
            back = None
            for at, p, d, key in zip(places, probs, grads, part_keys):
                moved = (p * (d - inner)).astype(BF)
                add(grad_keys, at, dot(moved, asked, (1, 0)))
                add(grad_values, at, dot(p.astype(BF), grads_in, (1, 0)))
                share = dot(key, moved, (0, 0))
                back = share if back is None else back + share
            cos = table_rows(grid, cos_ref, here.k, part)
            sin = table_rows(grid, sin_ref, here.k, part)
            result = turn(back.T, cos, -sin)
            if memory is not None:
                result = result + refs[2][at_rows, :]
            outs[0][at_rows, :] = (result * SCALE).astype(BF)
        for t in range(U):
            member = (here.k - t + U) % U
            for side in range(2):
                at_rows = pl.ds(side * R, R)
                cos = table_rows(grid, cos_ref, member, side)
                sin = table_rows(grid, sin_ref, member, side)
                key = turn(grad_keys[(t, side)], cos, -sin) * SCALE
                if t == 0:
                    outs[1][0, at_rows, :] = key
                    outs[1][1, at_rows, :] = grad_values[(t, side)]
                else:
                    held[0][step, t - 1, 0, at_rows, :] = key.astype(BF)
                    held[0][step, t - 1, 1, at_rows, :] = grad_values[(t, side)].astype(BF)
        for copy in sends(here, held, outs[2], step):
            copy.start()

        @pl.when(step == heads - 1)
        def _():
            for h in range(heads):
                for copy in sends(here, held, outs[2], h):
                    copy.wait()

    piece = columns_spec(rows, HEAD_DIM)
    pair = columns_spec(2, rows, HEAD_DIM)
    table = whole_spec(SEG, HEAD_DIM)
    operands = [valid, *tables, query, grad, *pairs]
    scratch = [pltpu.VMEM((heads, U - 1, 2, rows, HEAD_DIM), BF), pltpu.SemaphoreType.DMA((2, U - 1, heads))]
    if memory is None:
        specs = [smem(), table, table, piece, whole_spec(rows, width)] + [pair] * U + [whole_spec(width, width)]
        operands.append(w_out)
        scratch.append(pltpu.VMEM((rows, width), BF))
    else:
        specs = [smem(), table, table, piece, piece] + [pair] * U + [piece, rows_spec(1, 1, rows), piece]
        operands += memory
    return host(
        grid, body, heads, specs, operands,
        [piece, pair, any_spec()],
        [kind(rows, width), kind(2, rows, width, dtype=F32), kind(U - 1, 2, rows, width)],
        moves,
        scratch=scratch,
        cost=attention_cost(grid, heads, 0, 5),
        reaches=lambda here: [here.member(t) for t in range(1, U)],
    )


def gather_memory(grid, picks, pairs):
    n, U, R = grid.n_dp, grid.U, grid.R
    heads, topk = picks.shape
    per = heads // 2
    half = per * HEAD_DIM

    def body(here, step, ins, outs, held):
        picks_ref, sources, target = ins[0], ins[1:], outs[0]
        rows, chosen, load_sems, own_sem, sems = held
        columns = pl.ds(pl.multiple_of(here.c * half, 128), half)
        loads = [
            pltpu.make_async_copy(source.at[1:3, :, columns], rows.at[t], load_sems.at[t])
            for t, source in enumerate(sources)
        ]
        for load in loads:
            load.start()
        for load in loads:
            load.wait()
        for h in range(per):
            picked = picks_ref[here.c * per + h]
            at_columns = slice(h * HEAD_DIM, (h + 1) * HEAD_DIM)
            totals = [0.0, 0.0]
            for t in range(U):
                member = (here.k - t + U) % U
                for side in range(2):
                    across = lax.broadcasted_iota(jnp.int32, (topk, R), 1)
                    mask = (picked == across + piece_start(grid, member, side)).astype(BF)
                    for i in range(2):
                        block = rows[t, i, side * R : (side + 1) * R, at_columns]
                        totals[i] = totals[i] + dot(mask, block, (1, 0))
            chosen[0, :, at_columns] = totals[1].astype(BF)
            chosen[1, :, at_columns] = totals[0].astype(BF)
        mine = target.at[:, :, :, columns]
        own = pltpu.make_async_copy(chosen, mine.at[:, 0], own_sem)
        across = [remote(chosen, mine.at[:, t], sems, t, here.slots(t)) for t in range(1, n)]
        swaps = [remote(chosen, mine.at[:, 0], sems, n, here.swap)]
        swaps += [remote(mine.at[:, t], mine.at[:, t], sems, n + t, here.swap) for t in range(1, n)]
        for copy in across + [swaps[0], own]:
            copy.start()
        for t in range(1, n):
            across[t - 1].wait_recv()
            swaps[t].start()
        own.wait()
        for copy in across:
            copy.wait_send()
        for copy in swaps:
            copy.wait()

    outs, _ = host(
        grid, body, 1,
        [whole_spec(heads, topk, 1)] + [any_spec()] * U,
        [picks[:, :, None], *pairs],
        [any_spec()], [kind(2, n, topk, 2 * half)],
        scratch=[
            pltpu.VMEM((U, 2, grid.T, half), BF),
            pltpu.VMEM((2, topk, half), BF),
            pltpu.SemaphoreType.DMA((U,)),
            pltpu.SemaphoreType.DMA,
            pltpu.SemaphoreType.DMA((2, 2 * n)),
        ],
        reaches=lambda here: [here.slots(n - t) for t in range(1, n)] + [here.swap],
    )
    return outs[0]


def finish_gradient(grid, grad_query, own, others, picks, memory, moves=()):
    rows, width = grad_query.shape
    heads = width // HEAD_DIM
    R, U = grid.R, grid.U

    def body(here, step, ins, outs, held):
        dq_ref, own_ref, others_ref = ins[:3]
        out_ref = outs[0]

        @pl.when(step == 0)
        def _():
            out_ref[...] = dq_ref[...]

        @pl.when(step > 0)
        def _():
            for side in range(2):
                at = pl.ds(side * R, R)
                for h in range(heads):
                    columns = pl.ds(h * HEAD_DIM, HEAD_DIM)
                    value = own_ref[0, at, columns]
                    for t in range(U - 1):
                        value = value + others_ref[t, 0, at, columns].astype(F32)
                    if memory is not None:
                        picked = ins[3][h]
                        down = lax.broadcasted_iota(jnp.int32, (R, picked.shape[1]), 0)
                        chosen = (down + piece_start(grid, here.k, side) == picked).astype(BF)
                        value = value + dot(chosen, ins[4][0, :, columns], (1, 0))
                    out_ref[at, columns] = value.astype(BF)

    which = lambda b: jnp.maximum(b - 1, 0)
    operands = [grad_query, own, others]
    specs = [
        whole_spec(rows, width),
        pl.BlockSpec((1, rows, width), lambda b: (which(b), 0, 0)),
        pl.BlockSpec((U - 1, 1, rows, width), lambda b: (0, which(b), 0, 0)),
    ]
    if memory is not None:
        topk = picks.shape[1]
        operands += [picks[:, None, :], memory]
        specs += [
            whole_spec(heads, 1, topk),
            pl.BlockSpec((1, topk, width), lambda b: (which(b), 0, 0)),
        ]
    outs, got = host(
        grid, body, 3, specs, operands, [columns_spec(rows, width)], [kind(rows, 3 * width)], moves,
        cost=pl.CostEstimate(flops=2 * rows * width, bytes_accessed=16 * rows * width, transcendentals=0),
    )
    return outs[0], got


FEED_TILE = 256


def feed(grid, hidden_rows, attended, gain, w_out, w_up, w_down, moves=()):
    rows, width = hidden_rows.shape
    hidden = w_down.shape[0]
    steps = hidden // FEED_TILE

    def body(here, step, ins, outs, held):
        hidden_ref, attended_ref, gain_ref, out_w, gate_w, up_w, down_w = ins
        out_ref, middle_ref, normed_ref, both_ref, inner_ref = outs

        @pl.when(step == 0)
        def _():
            value = hidden_ref[...].astype(F32) + dot(attended_ref[...], out_w[...], (1, 0))
            middle_ref[...] = value
            normed_ref[...] = norm(value, gain_ref[...]).astype(BF)
            held[0][...] = value

        normed = normed_ref[...]
        gate, up = dot(normed, gate_w[...], (1, 0)), dot(normed, up_w[...], (1, 0))
        both_ref[0] = gate.astype(BF)
        both_ref[1] = up.astype(BF)
        inner = (gate / (1.0 + jnp.exp(-gate)) * up).astype(BF)
        inner_ref[...] = inner
        held[0][...] += dot(inner, down_w[...], (1, 0))

        @pl.when(step == steps - 1)
        def _():
            out_ref[...] = held[0][...]

    tile = columns_spec(width, FEED_TILE)
    return host(
        grid, body, steps,
        [whole_spec(rows, width), whole_spec(rows, width), whole_spec(1, width), whole_spec(width, width), tile,
         columns_spec(width, FEED_TILE, first=steps), rows_spec(FEED_TILE, width)],
        [hidden_rows, attended, gain, w_out, w_up, w_up, w_down],
        [whole_spec(rows, width)] * 3 + [columns_spec(2, rows, FEED_TILE), columns_spec(rows, FEED_TILE)],
        [kind(rows, width, dtype=F32), kind(rows, width, dtype=F32), kind(rows, width), kind(2, rows, hidden), kind(rows, hidden)],
        moves,
        scratch=[pltpu.VMEM((rows, width), F32)],
        cost=pl.CostEstimate(flops=6 * rows * width * hidden, bytes_accessed=6 * width * hidden, transcendentals=rows * hidden),
    )


def feed_back(grid, grad, middle, gain, both, w_up, w_down, moves=()):
    rows, width = grad.shape
    hidden = w_down.shape[0]
    steps = hidden // FEED_TILE

    def body(here, step, ins, outs, held):
        grad_ref, middle_ref, gain_ref, both_ref, gate_w, up_w, down_w = ins
        out_ref, low_ref, grads_ref, gain_out = outs
        total = held[0]

        @pl.when(step == 0)
        def _():
            held[1][...] = grad_ref[...].astype(BF)
            total[...] = jnp.zeros_like(total)

        grad_inner = dot(held[1][...], down_w[...], (1, 1))
        gate, up = both_ref[0].astype(F32), both_ref[1].astype(F32)
        sigmoid = 1.0 / (1.0 + jnp.exp(-gate))
        scaled = grad_inner * sigmoid
        grad_gate = (scaled * up * (1.0 + gate * (1.0 - sigmoid))).astype(BF)
        grad_up = (scaled * gate).astype(BF)
        grads_ref[0] = grad_gate
        grads_ref[1] = grad_up
        total[...] += dot(grad_gate, gate_w[...], (1, 1)) + dot(grad_up, up_w[...], (1, 1))

        @pl.when(step == steps - 1)
        def _():
            pulled, grad_gain = norm_back(middle_ref[...], gain_ref[...], total[...])
            result = grad_ref[...] + pulled
            out_ref[...] = result
            low_ref[...] = result.astype(BF)
            gain_out[...] = grad_gain

    tile = columns_spec(width, FEED_TILE)
    whole = whole_spec(rows, width)
    return host(
        grid, body, steps,
        [whole, whole, whole_spec(1, width), columns_spec(2, rows, FEED_TILE), tile,
         columns_spec(width, FEED_TILE, first=steps), rows_spec(FEED_TILE, width)],
        [grad, middle, gain, both, w_up, w_up, w_down],
        [whole, whole, columns_spec(2, rows, FEED_TILE), whole_spec(1, width)],
        [kind(rows, width, dtype=F32), kind(rows, width), kind(2, rows, hidden), kind(1, width, dtype=F32)],
        moves,
        scratch=[pltpu.VMEM((rows, width), F32), pltpu.VMEM((rows, width), BF)],
        cost=pl.CostEstimate(flops=6 * rows * width * hidden, bytes_accessed=6 * width * hidden, transcendentals=rows * hidden),
    )


def norm(value, gain):
    return value * lax.rsqrt(jnp.mean(value * value, axis=-1, keepdims=True) + EPSILON) * gain


def norm_back(value, gain, grad):
    inverse = lax.rsqrt(jnp.mean(value * value, axis=-1, keepdims=True) + EPSILON)
    unit = value * inverse
    grad_gain = jnp.sum(grad * unit, axis=0, keepdims=True)
    scaled = grad * gain
    pulled = inverse * (scaled - unit * jnp.mean(scaled * unit, axis=-1, keepdims=True))
    return pulled, grad_gain


def product(grid, left, left_other, right, moves=(), piece=(0, 1)):
    rows, height = left.shape
    stacked = right.ndim == 3
    full = right.shape[-1] if stacked else right.shape[-1] // 2
    half = full // piece[1]
    tile = 512 if height % 512 == 0 else height // 2
    tiles = height // tile
    fetch = left_other is None

    def part(ref, c):
        ref = ref.at[c] if stacked else ref
        start = piece[0] * half if stacked else c * full + piece[0] * half
        return ref.at[:, pl.ds(pl.multiple_of(start, 128), half)]

    def body(here, step, ins, outs, held):
        own_ref, other_ref, right_ref = ins
        own_right, other_right, total, own_sem, sems = held[:5]
        own = pltpu.make_async_copy(part(right_ref, here.c), own_right, own_sem)
        swaps = [remote(part(right_ref, 1 - here.c), other_right, sems, 0, here.swap)]
        if fetch:
            swaps.append(remote(other_ref, held[5], sems, 1, here.swap))

        @pl.when(step == 0)
        def _():
            own.start()
            for swap in swaps:
                swap.start()
            own.wait()

        @pl.when(step < tiles)
        def _():
            total[step] = dot(own_ref[...], own_right[...], (0, 0))

        @pl.when(step == tiles)
        def _():
            for swap in swaps:
                swap.wait()

        @pl.when(step >= tiles)
        def _():
            other = other_ref
            if fetch:
                other = held[5].at[:, pl.ds(pl.multiple_of((step - tiles) * tile, 128), tile)]
            outs[0][...] = (total[step - tiles] + dot(other[...], other_right[...], (0, 0))).astype(BF)

    early = lambda i: jnp.minimum(i, tiles - 1)
    late = lambda i: jnp.maximum(i - tiles, 0)
    other_spec = any_spec() if fetch else pl.BlockSpec((rows, tile), lambda i: (0, late(i)))
    outs, got = host(
        grid, body, 2 * tiles,
        [pl.BlockSpec((rows, tile), lambda i: (0, early(i))), other_spec, any_spec()],
        [left, left if fetch else left_other, right],
        [pl.BlockSpec((tile, half), lambda i: (late(i), 0))],
        [kind(height, half)],
        moves,
        scratch=[
            pltpu.VMEM((rows, half), BF),
            pltpu.VMEM((rows, half), BF),
            pltpu.VMEM((tiles, tile, half), F32),
            pltpu.SemaphoreType.DMA,
            pltpu.SemaphoreType.DMA((2, 2)),
        ] + [pltpu.VMEM((rows, height), BF)] * fetch,
        cost=pl.CostEstimate(flops=4 * rows * height * half, bytes_accessed=2 * height * half, transcendentals=0),
        reaches=lambda here: [here.swap],
    )
    return outs[0], got


class Reduce:
    def __init__(self, grid, total):
        self.grid = grid
        self.parts = total.reshape(grid.J, total.shape[0] // grid.J, total.shape[1])
        self.phase, self.came = 0, []

    def flip(self):
        return flip_move(self.grid, self.parts, self.phase)

    def flipped(self, got):
        grid = self.grid
        if self.phase == 0:
            kept = jnp.stack(
                [
                    lax.dynamic_index_in_dim(self.parts, grid.place(2 * i, grid.c), 0, keepdims=False)
                    for i in range(grid.J // 2)
                ]
            )
        else:
            kept = self.parts[0::2]
        self.parts = (kept.astype(F32) + got.astype(F32)).astype(BF)
        self.phase += 1
        if self.phase == grid.bits:
            self.line = self.parts.reshape(2, grid.F, -1, self.parts.shape[2])

    def ring(self, distances=None):
        grid = self.grid
        while self.phase < grid.bits:
            self.flipped(send(grid, [self.flip()])[0])
        return ring_move(grid, self.line, distances or list(range(1, grid.F)))

    def far(self):
        return self.ring([self.grid.F // 2])

    def near(self):
        return self.ring([t for t in range(1, self.grid.F) if t != self.grid.F // 2])

    def arrived(self, got):
        grid = self.grid
        self.came.append(got)

    def done(self):
        grid = self.grid
        here = lax.dynamic_index_in_dim(self.line, grid.f, 1, keepdims=False)
        summed = here.astype(F32) + sum(
            part[i].astype(F32) for part in self.came for i in range(part.shape[0])
        )
        mine = lax.dynamic_index_in_dim(summed, grid.c, 0, keepdims=False)
        give = lax.dynamic_index_in_dim(summed, 1 - grid.c, 0, keepdims=False)
        got = grid.swap(give.astype(BF)).astype(F32)
        return jnp.concatenate(
            [jnp.where(grid.c == 0, mine, got), jnp.where(grid.c == 0, got, mine)], axis=1
        )


def settle(grid, wanted, row_halves, moves):
    flat, ins, specs, scratch, out_shape = [], [], [], [], []
    for o, by_layer in enumerate(wanted):
        for layer, parts in enumerate(by_layer):
            for piece, reduce in enumerate(parts):
                flat.append((o, layer, piece, len(parts), reduce))
        rows, size = wanted[o][0][0].line.shape[2:]
        out_shape.append(kind(len(by_layer), rows, 2 * size * len(by_layer[0]), dtype=F32))
    for _, _, _, _, reduce in flat:
        _, F, rows, size = reduce.line.shape
        ins += [reduce.line, *reduce.came]
        scratch += [
            pltpu.VMEM((F, 2, rows, size), BF),
            pltpu.VMEM((2, rows, size), F32),
            pltpu.VMEM((rows, size), BF),
            pltpu.VMEM((rows, size), BF),
        ]
    count = len(flat)
    ins += row_halves
    high, width = row_halves[0].shape[1:]
    scratch += [pltpu.VMEM((2, 2, high, width), BF)]
    scratch += [pltpu.SemaphoreType.DMA((len(ins),)), pltpu.SemaphoreType.DMA((2, count))]
    out_shape.append(kind(2, 2 * high, width, dtype=F32))

    def body(here, step, refs, outs, held):
        rows_held, load_sems, sems = held[4 * count :]
        loads, swaps, at = [], [], 0
        for i, (_, _, _, _, reduce) in enumerate(flat):
            blocks, _, give, got = held[4 * i : 4 * i + 4]
            mine = [pltpu.make_async_copy(refs[at].at[:, here.f], blocks.at[0], load_sems.at[at])]
            at, filled = at + 1, 1
            for part in reduce.came:
                size = part.shape[0]
                mine.append(
                    pltpu.make_async_copy(refs[at], blocks.at[pl.ds(filled, size)], load_sems.at[at])
                )
                at, filled = at + 1, filled + size
            loads.append(mine)
            swaps.append(remote(give, got, sems, i, here.swap))
        loads.append(
            [pltpu.make_async_copy(refs[at + i], rows_held.at[i], load_sems.at[at + i]) for i in range(2)]
        )
        for mine in loads:
            for copy in mine:
                copy.start()
        for i in range(count):
            blocks, summed, give, _ = held[4 * i : 4 * i + 4]
            for copy in loads[i]:
                copy.wait()
            total = blocks[0].astype(F32)
            for t in range(1, blocks.shape[0]):
                total = total + blocks[t].astype(F32)
            summed[...] = total
            give[...] = summed[1 - here.c].astype(BF)
            swaps[i].start()
        for copy in loads[count]:
            copy.wait()
        for i in range(2):
            outs[-1][:, i * high : (i + 1) * high, :] = rows_held[i].astype(F32)
        for i, (o, layer, piece, pieces, _) in enumerate(flat):
            _, summed, _, got = held[4 * i : 4 * i + 4]
            swaps[i].wait()
            size = got.shape[1]

            def columns(c):
                return pl.ds(pl.multiple_of((c * pieces + piece) * size, 128), size)

            outs[o][layer, :, columns(here.c)] = summed[here.c]
            outs[o][layer, :, columns(1 - here.c)] = got[...].astype(F32)

    return host(
        grid, body, 1, [any_spec()] * len(ins), ins,
        [whole_spec(*o.shape) for o in out_shape], out_shape, moves,
        scratch=scratch,
        reaches=lambda here: [here.swap],
    )


def local(
    n_dp,
    pieces,
    tokens,
    cotangent,
    doc_lengths,
    partner,
    memory_picks,
    attention_in,
    attention_out,
    feed_in,
    feed_out,
    norm_gains,
):
    IDS[0] = 1
    grid = Grid(n_dp, pieces)
    grid.trace()
    layers = attention_in.shape[0]
    width = tokens.shape[2]
    heads = width // HEAD_DIM
    topk = memory_picks.shape[3]
    valid_all, visible_all = jax.vmap(memory_plan)(doc_lengths, partner)
    valid = valid_all[grid.m, grid.slot].reshape(1)
    visible = visible_all[grid.m, grid.slot]
    relative = (grid.slot - jnp.arange(n_dp)) % n_dp
    bias = jnp.repeat(jnp.where(visible[relative], 0.0, MASKED), topk)[:, None].astype(F32)
    tables = rope_tables()
    picks_there = grid.swap(memory_picks)
    picks = jnp.where(grid.r == grid.c, memory_picks[grid.m, 0], picks_there[grid.m, 0])
    zero = grid.c == 0

    def both_halves(mine, other):
        return jnp.where(
            zero, jnp.concatenate([mine, other], axis=-1), jnp.concatenate([other, mine], axis=-1)
        )

    def half(value, c):
        size = value.shape[-1] // 2
        return lax.dynamic_slice_in_dim(value, c * size, size, axis=value.ndim - 1)

    tokens, *tables = lax.optimization_barrier((tokens, *tables))
    hidden, gains, weights = gather_all(
        grid, tokens, norm_gains, [attention_in, attention_out, feed_in, feed_out]
    )
    gain = lambda l, i: gains[l, i][None]
    flat = lambda w: w.reshape(-1, w.shape[-1])
    saved = []
    cotangent_rows = None
    for l in range(layers):
        w_qkv, w_out = flat(weights[l][0]), flat(weights[l][1])
        memory = l == layers - 1
        coming = weights[l + 1] if l + 1 < layers else None
        moves = []
        if coming is not None:
            moves.append(spread_move(grid, coming[3], [(0, 0, 1)]))
        if later_here(l, 2):
            moves += [
                spread_move(grid, weights[l][2], [(1, 0, 2), (1, 1, 2)]),
                spread_move(grid, weights[l][3], [(2, 0, 1)]),
            ]
        split, got = project(grid, memory, tables, hidden, gain(l, 0), w_qkv, moves)
        if coming is not None:
            coming[3] = got[0]
        if later_here(l, 2):
            weights[l][2:] = got[-2:]
        normed, query = split[:2]
        pairs = [split[2]] + [split[3][t] for t in range(grid.U - 1)]
        extra = None
        if memory:
            slots = gather_memory(grid, picks, pairs).reshape(2, n_dp * topk, -1)
            extra = {"query": split[4], "memory": slots, "bias": bias}
        moves = []
        if coming is not None:
            moves.append(spread_move(grid, coming[2], [(0, 0, 2)]))
        if later_here(l, 2):
            moves.append(spread_move(grid, weights[l][2], [(2, 0, 1)]))
        if memory:
            moves.append(regroup_move(grid, cotangent))
        attended, logsum, got = attend(grid, valid, query, pairs, extra, moves)
        if coming is not None:
            coming[2] = got[0]
        if later_here(l, 2):
            weights[l][2] = got[-2]
            for stage in range(3, grid.bits + 1):
                weights[l][2:] = send(grid, [spread_move(grid, w, [(stage, 0, 1)]) for w in weights[l][2:]])
        if memory:
            cotangent_rows = got[-1]
            extra["logsum"] = logsum
        moves = []
        if coming is not None:
            moves = [spread_move(grid, coming[2], [(0, 1, 2)]), spread_move(grid, coming[3], [(1, 0, 1)])]
        w_up, w_down = flat(weights[l][2]), flat(weights[l][3])
        (out, middle, normed_feed, both, inner), got = feed(
            grid, hidden, attended, gain(l, 1), w_out, w_up, w_down, moves
        )
        if coming is not None:
            coming[2:] = got
        saved.append((hidden, normed, query, pairs, extra, attended, middle, normed_feed, both, inner))
        hidden = out
    weights = [[flat(w) for w in kinds] for kinds in weights]
    cotangent_rows = cotangent_rows.reshape(-1, width)
    def row_halves(value):
        value = value.astype(BF).reshape(2, grid.R, width)
        return value[:, : grid.R // 2], value[:, grid.R // 2 :]

    out_rows = row_halves(hidden)
    grad = cotangent_rows.astype(F32)
    found = [[None] * 4 for _ in range(layers)]
    grad_gains = [[None, None] for _ in range(layers)]
    layer_output, above, inner_other = [], None, None

    def took(got, reduces):
        for result, (reduce, what) in zip(got, reduces):
            (reduce.flipped if what == "flip" else reduce.arrived)(result)

    def moves_of(reduces):
        return [getattr(reduce, what)() for reduce, what in reduces]

    for l in reversed(range(layers)):
        w_qkv, w_out, w_up, w_down = weights[l]
        hidden, normed, query, pairs, extra, attended, middle, normed_feed, both, inner = saved[l]
        low = grad.astype(BF)
        last_layer = above is None

        reduces = [] if last_layer else [(above[1], "flip"), (above[2][0], "far")]
        total, got = product(grid, inner, inner_other, low, moves_of(reduces))
        took(got, reduces)
        down = Reduce(grid, total)

        reduces = [(down, "flip")]
        if not last_layer:
            reduces += [(above[0], "flip"), (above[1], "flip"), (above[2][0], "near")]
        moves = moves_of(reduces) + [swap_move(normed_feed), swap_move(normed), swap_move(attended)]
        if last_layer:
            moves += [swap_move(saved[l - 1][9]), regroup_back_move(grid, out_rows[0])]
        (grad, grad_low, grads, gain_feed), got = feed_back(
            grid, grad, middle, gain(l, 1), both, w_up, w_down, moves
        )
        took(got, reduces)
        normed_feed_other, normed_other, attended_other = got[len(reduces) : len(reduces) + 3]
        if last_layer:
            inner_other = got[-2]
            layer_output.append(got[-1])

        ups = []
        pieces_of_up = 1 if last_layer else 2
        for piece in range(pieces_of_up):
            if piece == 0:
                reduces = [(down, "flip")] if last_layer else [(down, "flip"), (above[1], "far")]
            else:
                reduces = [(ups[0], "flip"), (above[1], "near")]
            total, got = product(
                grid, normed_feed, normed_feed_other, grads, moves_of(reduces), (piece, pieces_of_up)
            )
            took(got, reduces)
            ups.append(Reduce(grid, total))

        reduces = [(ups[-1], "flip"), (down, "ring")]
        if not last_layer:
            reduces += [(ups[0], "flip"), (above[0], "ring")]
        memory_grad = None
        if extra is None:
            outs, got = attend_back(grid, valid, tables, query, grad_low, w_out, pairs, moves_of(reduces))
            took(got, reduces)
        else:
            grad_heads = mm(grad_low, w_out, (1, 1)).astype(BF)
            moves = moves_of(reduces)
            if last_layer:
                moves.append(regroup_back_move(grid, out_rows[1]))
            outs, got = memory_back(grid, grad_heads, attended, extra, moves)
            took(got, reduces)
            if last_layer:
                layer_output.append(got[-1])
            joined = half(outs[1], grid.c).astype(F32) + outs[2].astype(F32)
            joined = joined.astype(BF).reshape(2, n_dp, topk, -1)
            outs, got = attend_back(
                grid, valid, tables, query, grad_heads, w_out, pairs, [slots_move(grid, joined, True)],
                [attended, extra["logsum"], outs[0]],
            )
            total = joined[:, 0].astype(F32) + sum(got[0][t].astype(F32) for t in range(n_dp - 1))
            for t in range(1, grid.Q):
                total = total + grid.within(total.astype(BF), t).astype(F32)
            total = total.astype(BF)
            memory_grad = both_halves(total, grid.swap(total))
        grad_query, own, others = outs[:3]
        total, got = product(grid, attended, attended_other, grad_low)
        across = Reduce(grid, total)
        reduces = [(ups[-1], "flip")]
        if not last_layer:
            reduces += [(across, "flip"), (ups[0], "ring")]
        grad_projected, got = finish_gradient(
            grid, grad_query, own, others, picks, memory_grad, moves_of(reduces)
        )
        took(got, reduces)
        pulled, gain_attention = norm_back(
            hidden.astype(F32), gain(l, 0), mm(grad_projected, w_qkv, (1, 1))
        )
        grad = grad + pulled
        grad_gains[l] = [gain_attention[0], gain_feed[0]]
        reduces, moves = [(across, "flip")], []
        if l == 0:
            small = GainSum(grid, jnp.stack([jnp.stack(pair) for pair in grad_gains]).reshape(-1, HEAD_DIM))
            reduces = [(ups[-1], "ring"), (across, "flip")]
            moves = [small.move()]
        total, got = product(grid, normed, normed_other, grad_projected, moves_of(reduces) + moves)
        took(got, reduces)
        if l == 0:
            small.took(got[-1])
        last = Reduce(grid, total)
        found[l] = [[last], [across], ups, [down]]
        above = (across, last, ups)
    across, last, ups = above
    in_rows = row_halves(grad)
    input_grad = []
    for i, reduces in enumerate([[(last, "flip"), (across, "ring")], [(last, "flip")]]):
        got = send(grid, moves_of(reduces) + [regroup_back_move(grid, in_rows[i]), small.move()])
        took(got, reduces)
        small.took(got[-1])
        input_grad.append(got[-2])
    wanted = [[found[l][0] for l in range(1, layers)]]
    wanted += [[found[l][i] for l in range(layers)] for i in range(1, 4)]
    outs, got = settle(grid, wanted, input_grad, [last.ring(), small.move()])
    last.arrived(got[0])
    small.took(got[1])
    grad_in, grad_out, grad_up, grad_down, input_grad = outs
    grad_in = jnp.concatenate([last.done()[None], grad_in])
    layer_output = jnp.concatenate(layer_output, axis=1)
    total_gains = small.finish().reshape(layers, 2, n_dp * pieces, -1)
    device = (grid.j * 2 + grid.c) * grid.F + grid.f
    return (
        layer_output,
        input_grad,
        grad_in,
        grad_out,
        grad_up,
        grad_down,
        lax.dynamic_index_in_dim(total_gains, device, 2, keepdims=False),
    )


def solution(mesh):
    rows = P(None, ("dp", "fsdp"), None)
    in_specs = (rows, rows, P(), P(), P(None, "dp", None, None), rows, rows, rows, rows, P(None, None, ("dp", "fsdp")))
    out_specs = (rows, rows, rows, rows, rows, rows, P(None, None, ("dp", "fsdp")))
    body = functools.partial(local, mesh.shape["dp"], mesh.shape["fsdp"])
    return jax.shard_map(body, mesh=mesh, in_specs=in_specs, out_specs=out_specs, check_vma=False)
```

```python
import functools
import math

import jax
import jax.numpy as jnp
from jax import lax
from jax.experimental import pallas as pl
from jax.experimental.pallas import tpu as pltpu
from jax.sharding import PartitionSpec as P

HEAD_DIM = 128
SEG = 1024
MICRO = 2
EPSILON = 1e-06
MASKED = -1e30
SCALE = HEAD_DIM ** (-0.5)
LOG2E = 1.0 / math.log(2.0)
BF = jnp.bfloat16
F32 = jnp.float32
VMEM_LIMIT = 40 * 1024 * 1024


def slot_layout(lengths):
    slot_total = lengths.shape[0]
    slot_counts = ((lengths + SEG - 1) // SEG).astype(jnp.int32)
    slot_starts = (jnp.cumsum(slot_counts) - slot_counts).astype(jnp.int32)
    slot_index = jnp.arange(slot_total, dtype=jnp.int32)
    started = (slot_starts[None, :] <= slot_index[:, None]) & (slot_counts[None, :] > 0)
    owner_doc = (jnp.sum(started.astype(jnp.int32), axis=1) - 1).astype(jnp.int32)
    owner_pick = slot_index[None, :] == owner_doc[:, None]
    first_slot = jnp.sum(jnp.where(owner_pick, slot_starts[None, :], 0), axis=1).astype(jnp.int32)
    doc_total = jnp.sum(jnp.where(owner_pick, lengths[None, :], 0), axis=1).astype(jnp.int32)
    valid_rows = jnp.clip(doc_total - (slot_index - first_slot) * SEG, 0, SEG).astype(jnp.int32)
    return (valid_rows, owner_doc)


def memory_plan(lengths, partner_row):
    valid_rows, owner_doc = slot_layout(lengths)
    block_ids = jnp.arange(lengths.shape[0], dtype=jnp.int32)
    earlier = (block_ids[None, :] < block_ids[:, None]) & (owner_doc[None, :] == owner_doc[:, None])
    visible = earlier | (block_ids[None, :] == partner_row[:, None])
    return (valid_rows, visible)


class Grid:
    def __init__(self, n_dp, pieces):
        self.n_dp, self.F = n_dp, pieces
        self.J = n_dp // 2
        self.bits = self.J.bit_length() - 1
        self.Q = pieces // 4
        self.U = 2 * self.Q
        self.R = SEG // pieces
        self.T = 2 * self.R

    def trace(self):
        dp = lax.axis_index("dp")
        self.c, self.j, self.f = dp % 2, dp // 2, lax.axis_index("fsdp")
        self.q, self.g = self.f // self.Q, self.f % self.Q
        self.m, self.r = self.q // 2, self.q % 2
        self.k = self.c * self.Q + self.g
        self.slot = 2 * self.j + self.r

    def permute(self, value, target):
        pairs = []
        for j in range(self.J):
            for c in range(2):
                for f in range(self.F):
                    j2, c2, f2 = target(j, c, f)
                    pairs.append(((j * 2 + c) * self.F + f, (j2 * 2 + c2) * self.F + f2))
        return lax.ppermute(value, ("dp", "fsdp"), pairs)

    def swap(self, value):
        return self.permute(value, lambda j, c, f: (j, 1 - c, f))

    def ring(self, value, t):
        return self.permute(value, lambda j, c, f: (j, c, (f + t) % self.F))

    def bit(self, phase, c):
        return phase if c == 0 else self.bits - 1 - phase

    def flip(self, value, phase):
        return self.permute(value, lambda j, c, f: (j ^ (1 << self.bit(phase, c)), c, f))

    def mask(self, key, c):
        return sum(1 << self.bit(p, c) for p in range(self.bits) if key >> p & 1)

    def place(self, key, c):
        return jnp.where(c == 0, self.j ^ self.mask(key, 0), self.j ^ self.mask(key, 1))

    def member(self, value, t):
        def target(j, c, f):
            q, g = f // self.Q, f % self.Q
            k = (c * self.Q + g + t) % self.U
            return (j, k // self.Q, q * self.Q + k % self.Q)

        return self.permute(value, target)

    def within(self, value, t):
        return self.permute(
            value, lambda j, c, f: (j, c, f // self.Q * self.Q + (f % self.Q + t) % self.Q)
        )

    def slots(self, value, t):
        def target(j, c, f):
            q, g = f // self.Q, f % self.Q
            slot = (2 * j + q % 2 + t) % self.n_dp
            return (slot // 2, c, (2 * (q // 2) + slot % 2) * self.Q + g)

        return self.permute(value, target)

    def _spread(self, second):
        def target(j, c, f):
            m = f // (self.F // 2)
            m = 1 - m if second else m
            k = min(f, self.F - 1 - f)
            return (j, k // self.Q, (2 * m + c) * self.Q + k % self.Q)

        return target

    def _collect(self, second):
        there = self._spread(second)
        back = {
            there(0, c, f): (c, f) for c in range(2) for f in range(self.F)
        }
        return lambda j, c, f: (j,) + back[(0, c, f)]

    def to_units(self, value):
        here = self.f // (self.F // 2)
        first = self.permute(jnp.where(here == 0, value[0], value[1]), self._spread(False))
        second = self.permute(jnp.where(here == 0, value[1], value[0]), self._spread(True))
        return jnp.concatenate(
            [jnp.where(self.m == 0, first, second), jnp.where(self.m == 0, second, first)]
        )

    def from_units(self, value):
        low, high = value[: self.R], value[self.R :]
        first = self.permute(jnp.where(self.m == 0, low, high), self._collect(False))
        second = self.permute(jnp.where(self.m == 0, high, low), self._collect(True))
        here = self.f // (self.F // 2)
        return jnp.stack([jnp.where(here == 0, first, second), jnp.where(here == 0, second, first)])


def any_spec():
    return pl.BlockSpec(memory_space=pl.ANY)


MESH = pl.DeviceIdType.MESH


class Here:
    def __init__(self, grid):
        self.grid = grid
        dp = lax.axis_index("dp")
        self.j, self.c, self.f = dp // 2, dp % 2, lax.axis_index("fsdp")
        self.q, self.g = self.f // grid.Q, self.f % grid.Q
        self.m, self.r = self.q // 2, self.q % 2
        self.k = self.c * grid.Q + self.g
        self.swap = self.device(self.j, 1 - self.c, self.f)

    def device(self, j, c, f):
        return {"dp": 2 * j + c, "fsdp": f}

    def ring(self, t):
        return self.device(self.j, self.c, (self.f + t) % self.grid.F)

    def step(self, phase):
        first, second = (1 << self.grid.bit(phase, c) for c in (0, 1))
        return first + self.c * (second - first)

    def moved(self, j, phase):
        step = self.step(phase)
        return j + step * (1 - 2 * ((j // step) % 2))

    def flip(self, phase):
        return self.device(self.moved(self.j, phase), self.c, self.f)

    def slots(self, t):
        grid = self.grid
        slot = (2 * self.j + self.r + t) % grid.n_dp
        return self.device(slot // 2, self.c, (2 * self.m + slot % 2) * grid.Q + self.g)

    def member(self, t):
        grid = self.grid
        k = (self.k + t) % grid.U
        return self.device(self.j, k // grid.Q, self.q * grid.Q + k % grid.Q)

    def place(self, key):
        j = self.j
        for phase in range(self.grid.bits):
            if key >> phase & 1:
                j = self.moved(j, phase)
        return j

    def greet(self):
        grid = self.grid
        barrier = pltpu.get_barrier_semaphore()
        peers = [self.ring(t) for t in range(1, grid.F)]
        peers += [self.device(self.j, 1 - self.c, (self.f + t) % grid.F) for t in range(grid.F)]
        for bit in range(grid.bits):
            step = 1 << bit
            peers.append(self.device(self.j + step * (1 - 2 * ((self.j // step) % 2)), self.c, self.f))
        for peer in peers:
            pl.semaphore_signal(barrier, inc=1, device_id=peer, device_id_type=MESH)
        pl.semaphore_wait(barrier, len(peers))


def remote(source, target, sems, index, device):
    return pltpu.make_async_remote_copy(
        src_ref=source,
        dst_ref=target,
        send_sem=sems.at[0, index],
        recv_sem=sems.at[1, index],
        device_id=device,
        device_id_type=MESH,
    )


class Spread:
    def __init__(self, here, shard, whole, sems, own_sem, split):
        grid = here.grid
        self.here, self.split = here, split
        rows, width = shard.shape
        half = width // 2 if split else width

        def part(ref, c):
            if not split:
                return ref
            return ref.at[(slice(None),) * (len(ref.shape) - 1) + (pl.ds(pl.multiple_of(c * half, 128), half),)]

        j, c, f = here.j, here.c, here.f
        mine = part(whole, c)
        self.own = pltpu.make_async_copy(part(shard, c), part(whole.at[j, c, f], c), own_sem)
        other = 1 - c if split else c
        self.pre = remote(part(shard, other), part(whole.at[j, c, f], other), sems, 0, here.swap)
        at = 1
        self.hops = []
        for h in range(1, grid.F):
            hop = []
            for way in (1, -1):
                origin = f - way * (h - 1)
                inside = lambda place: (place >= 0) & (place < grid.F)
                block = mine.at[j, :, jnp.clip(origin, 0, grid.F - 1)]
                copy = remote(block, block, sems, at, here.device(j, c, (f + way + grid.F) % grid.F))
                hop.append((copy, inside(origin) & inside(f + way), inside(f - way * h)))
                at += 1
            self.hops.append(hop)
        self.flips = []
        for phase in range(grid.bits):
            sent = []
            for key in range(1 << phase):
                block = mine.at[here.place(key)]
                sent.append(remote(block, block, sems, at, here.flip(phase)))
                at += 1
            self.flips.append(sent)
        self.swaps = []
        for key in range(grid.J if split else 0):
            block = mine.at[here.place(key)]
            self.swaps.append(remote(block, block, sems, at, here.swap))
            at += 1

    @staticmethod
    def count(grid):
        return 1 + 2 * (grid.F - 1) + (grid.J - 1) + grid.J

    def begin(self):
        self.own.start()
        self.pre.start()

    def to_line(self):
        self.own.wait()
        self.pre.wait()
        self._hop(0)

    def _hop(self, h):
        for copy, sends, _ in self.hops[h]:
            pl.when(sends)(copy.start)

    def _send(self, keys):
        for key in keys:
            if self.swaps:
                self.swaps[key].start()
        for phase, sent in enumerate(self.flips):
            for key in keys:
                if key < 1 << phase:
                    sent[key].start()

    def steps(self, whole):
        def along(h):
            for copy, _, comes in self.hops[h]:
                pl.when(comes)(copy.wait_recv)
            if h + 1 < len(self.hops):
                self._hop(h + 1)
                return
            for hop in self.hops:
                for copy, sends, _ in hop:
                    pl.when(sends)(copy.wait_send)
            if whole:
                self._send([0])

        def later(phase):
            for copy in self.flips[phase]:
                copy.wait()
            self._send([key + (1 << phase) for key in range(1 << phase)])

        def last():
            for copy in self.swaps:
                copy.wait()

        line = [functools.partial(along, h) for h in range(len(self.hops))]
        if not whole:
            return line
        return line + [functools.partial(later, p) for p in range(len(self.flips))] + [last]


class Regroup:
    def __init__(self, here, source, target, sems, own_sem):
        grid = here.grid
        half = grid.F // 2
        k = jnp.minimum(here.f, grid.F - 1 - here.f)
        side = here.f // half
        self.sends = []
        for m in range(2):
            c2, f2 = k // grid.Q, (2 * m + here.c) * grid.Q + k % grid.Q
            same = (c2 == here.c) & (f2 == here.f)
            own = pltpu.make_async_copy(source.at[m], target.at[side], own_sem)
            away = pltpu.make_async_remote_copy(
                src_ref=source.at[m],
                dst_ref=target.at[side],
                send_sem=sems.at[0, m],
                recv_sem=sems.at[1, side],
                device_id=here.device(here.j, c2, f2),
                device_id_type=MESH,
            )
            self.sends.append((same, own, away))
        self.arrivals = []
        for side in range(2):
            from_f = here.k if side == 0 else grid.F - 1 - here.k
            same = (here.r == here.c) & (from_f == here.f)
            came = pltpu.make_async_remote_copy(
                src_ref=source.at[0],
                dst_ref=target.at[side],
                send_sem=sems.at[0, 0],
                recv_sem=sems.at[1, side],
                device_id=here.swap,
                device_id_type=MESH,
            )
            self.arrivals.append((same, came))

    def start(self):
        for same, own, away in self.sends:
            pl.when(same)(own.start)
            pl.when(jnp.logical_not(same))(away.start)

    def wait(self):
        for same, own, away in self.sends:
            pl.when(same)(own.wait)
            pl.when(jnp.logical_not(same))(away.wait_send)
        for same, came in self.arrivals:
            pl.when(jnp.logical_not(same))(came.wait_recv)


def gather_body(grid, layers, kinds, *refs):
    tokens, gains = refs[:2]
    shards = refs[2 : 2 + kinds]
    outs = refs[2 + kinds :]
    tokens_out, gains_out = outs[:2]
    wholes = outs[2 : 2 + layers * kinds]
    sems, own_sems, regroup_sems = outs[2 + layers * kinds :]
    here = Here(grid)
    here.greet()
    rows = Regroup(here, tokens, tokens_out, regroup_sems, own_sems.at[0])
    moves = []
    for l, i in ORDER:
        n = l * kinds + i
        move = Spread(here, shards[i].at[l], wholes[n], sems.at[n + 1], own_sems.at[n + 2], True)
        moves.append((move, not later_here(l, i)))
    moves.insert(GAINS_AT, (Spread(here, gains, gains_out, sems.at[0], own_sems.at[1], False), True))
    for move, _ in moves:
        move.begin()
    steps = [move.steps(whole) for move, whole in moves]
    count = len(steps[0])
    for at in range(AHEAD):
        moves[at][0].to_line()
    for at in range(len(moves) + count - 1):
        if at == ROWS_AT:
            rows.start()
        if at + AHEAD < len(moves):
            moves[at + AHEAD][0].to_line()
        for back in reversed(range(count)):
            if 0 <= at - back < len(moves) and back < len(steps[at - back]):
                steps[at - back][back]()
    rows.wait()


ORDER = [(0, 1), (0, 3), (0, 0), (0, 2), (1, 0), (1, 1), (1, 3), (1, 2)]
GAINS_AT, ROWS_AT, AHEAD = 3, 4, 1


def later_here(l, i):
    return l > 0 and i >= 2


def gather_all(grid, tokens, gains, shards):
    layers, kinds = shards[0].shape[0], len(shards)
    packed = jnp.zeros((8, 128), F32).at[: layers * 2, : gains.shape[2]].set(
        gains.astype(F32).reshape(layers * 2, -1)
    )
    whole = lambda shard: jax.ShapeDtypeStruct((grid.J, 2, grid.F) + shard.shape[-2:], shard.dtype)
    out_shape = [jax.ShapeDtypeStruct(tokens.shape, BF), whole(packed)]
    out_shape += [whole(shard) for _ in range(layers) for shard in shards]
    moves = 1 + layers * kinds
    outs = pl.pallas_call(
        functools.partial(gather_body, grid, layers, kinds),
        in_specs=[any_spec()] * (2 + kinds),
        out_specs=[any_spec()] * len(out_shape),
        out_shape=out_shape,
        scratch_shapes=[
            pltpu.SemaphoreType.DMA((moves, 2, Spread.count(grid))),
            pltpu.SemaphoreType.DMA((moves + 1,)),
            pltpu.SemaphoreType.DMA((2, 2)),
        ],
        compiler_params=pltpu.CompilerParams(
            collective_id=0, has_side_effects=True, vmem_limit_bytes=VMEM_LIMIT
        ),
    )(tokens, packed, *shards)
    gains_all = outs[1][..., : layers * 2, : gains.shape[2]]
    gains_all = jnp.moveaxis(gains_all, 3, 0).reshape(layers, 2, -1)
    weights = [list(outs[2 + l * kinds : 2 + (l + 1) * kinds]) for l in range(layers)]
    return outs[0].reshape(-1, tokens.shape[2]), gains_all, weights


def unless(condition, act):
    if condition is None:
        act()
    else:
        pl.when(jnp.logical_not(condition))(act)


class Move:
    def __init__(self, array, shape, count, copies, plan=None, in_place=False):
        self.array, self.shape, self.count, self.copies = array, shape, count, copies
        self.plan, self.in_place = plan or self._plain, in_place

    def _plain(self, here, source, target, sends, recvs, base):
        found = []
        for i, (what, where, peer, giver) in enumerate(self.copies(here, source, target)):
            copy = pltpu.make_async_remote_copy(
                src_ref=what,
                dst_ref=where,
                send_sem=sends.at[base + i],
                recv_sem=recvs.at[base + i],
                device_id=peer,
                device_id_type=MESH,
            )
            found.append((copy, None, None, giver, copy, None))
        return found


def flip_move(grid, parts, phase):
    count = parts.shape[0] // 2

    def copies(here, source, target):
        found = []
        for i in range(count):
            at = here.place(2 * i + 1) if phase == 0 else 2 * i + 1
            peer = here.flip(phase)
            found.append((source.at[at], target.at[i], peer, peer))
        return found

    return Move(parts, (count,) + parts.shape[1:], count, copies)


def ring_move(grid, line, distances):
    def copies(here, source, target):
        return [
            (source.at[:, (here.f + t) % grid.F], target.at[i], here.ring(t), here.ring(grid.F - t))
            for i, t in enumerate(distances)
        ]

    return Move(line, (len(distances), 2) + line.shape[2:], len(distances), copies)


def swap_move(array, give=None):
    def copies(here, source, target):
        return [(source if give is None else source.at[give(here)], target, here.swap, here.swap)]

    return Move(array, array.shape if give is None else array.shape[1:], 1, copies)


def swap_half_move(array):
    half = array.shape[-1] // 2

    def copies(here, source, target):
        start = pl.multiple_of((1 - here.c) * half, 128)
        return [(source.at[:, :, pl.ds(start, half)], target, here.swap, here.swap)]

    return Move(array, array.shape[:-1] + (half,), 1, copies)


def slots_move(grid, array, back):
    def copies(here, source, target):
        found = []
        for t in range(1, grid.n_dp):
            ahead, behind = here.slots(t), here.slots(grid.n_dp - t)
            if back:
                found.append((source.at[:, t], target.at[t - 1], behind, ahead))
            else:
                found.append((source, target.at[t - 1], ahead, behind))
        return found

    shape = array.shape if not back else array.shape[:1] + array.shape[2:]
    return Move(array, (grid.n_dp - 1,) + shape, grid.n_dp - 1, copies)


def member_move(grid, array, back):
    def copies(here, source, target):
        found = []
        for t in range(1, grid.U):
            ahead, behind = here.member(t), here.member(grid.U - t)
            if back:
                found.append((source.at[t - 1], target.at[t - 1], behind, ahead))
            else:
                found.append((source, target.at[t - 1], ahead, behind))
        return found

    shape = array.shape[1:] if back else array.shape
    return Move(array, (grid.U - 1,) + shape, grid.U - 1, copies)


def spread_move(grid, whole, stages):
    half = whole.shape[-1] // 2

    def keys_of(stage):
        return [0] if stage == 0 else range(1 << (stage - 1), 1 << stage)

    def copies(here, source, target):
        found = []
        for stage, part, parts in stages:
            size = half // parts
            columns = pl.ds(pl.multiple_of(here.c * half + part * size, 128), size)
            mine = target.at[:, :, :, :, columns]
            for key in keys_of(stage):
                block = mine.at[here.place(key)]
                found.append((block, block, here.swap, here.swap))
                for phase in range(stage, grid.bits):
                    found.append((block, block, here.flip(phase), here.flip(phase)))
        return found

    count = sum(len(keys_of(stage)) * (1 + grid.bits - stage) for stage, _, _ in stages)
    return Move(whole, whole.shape, count, copies, in_place=True)


def peer_move(array, peer):
    return Move(array, array.shape, 1, lambda here, source, target: [(source, target, peer(here), peer(here))])


def line_move(grid, array):
    def copies(here, source, target):
        return [(source, target.at[t - 1], here.ring(t), here.ring(grid.F - t)) for t in range(1, grid.F)]

    return Move(array, (grid.F - 1,) + array.shape, grid.F - 1, copies)


def regroup_move(grid, array):
    def plan(here, source, target, sends, recvs, base):
        found = []
        k = jnp.minimum(here.f, grid.F - 1 - here.f)
        side = here.f // (grid.F // 2)
        for m in range(2):
            c2, f2 = k // grid.Q, (2 * m + here.c) * grid.Q + k % grid.Q
            same = (c2 == here.c) & (f2 == here.f)
            away = pltpu.make_async_remote_copy(
                src_ref=source.at[m],
                dst_ref=target.at[side],
                send_sem=sends.at[base + m],
                recv_sem=recvs.at[base + side],
                device_id=here.device(here.j, c2, f2),
                device_id_type=MESH,
            )
            own = pltpu.make_async_copy(source.at[m], target.at[side], sends.at[base + m])
            from_f = here.k if m == 0 else grid.F - 1 - here.k
            same_in = (here.r == here.c) & (from_f == here.f)
            came = pltpu.make_async_remote_copy(
                src_ref=source.at[0],
                dst_ref=target.at[m],
                send_sem=sends.at[base],
                recv_sem=recvs.at[base + m],
                device_id=here.swap,
                device_id_type=MESH,
            )
            found.append((away, same, own, here.device(here.j, here.r, from_f), came, same_in))
        return found

    return Move(array, array.shape, 2, None, plan)


def regroup_back_move(grid, array):
    def plan(here, source, target, sends, recvs, base):
        found = []
        for piece in range(2):
            f = here.k if piece == 0 else grid.F - 1 - here.k
            same = (here.r == here.c) & (f == here.f)
            away = pltpu.make_async_remote_copy(
                src_ref=source.at[piece],
                dst_ref=target.at[here.m],
                send_sem=sends.at[base + piece],
                recv_sem=recvs.at[base + here.m],
                device_id=here.device(here.j, here.r, f),
                device_id_type=MESH,
            )
            own = pltpu.make_async_copy(source.at[piece], target.at[here.m], sends.at[base + piece])
            k = jnp.minimum(here.f, grid.F - 1 - here.f)
            c2, f2 = k // grid.Q, (2 * piece + here.c) * grid.Q + k % grid.Q
            same_in = (c2 == here.c) & (f2 == here.f)
            came = pltpu.make_async_remote_copy(
                src_ref=source.at[0],
                dst_ref=target.at[piece],
                send_sem=sends.at[base],
                recv_sem=recvs.at[base + piece],
                device_id=here.swap,
                device_id_type=MESH,
            )
            found.append((away, same, own, here.device(here.j, c2, f2), came, same_in))
        return found

    return Move(array, array.shape, 2, None, plan)


IDS = [1]


def host(grid, body, steps, in_specs, operands, out_specs, out_shape, moves=(), scratch=(), cost=None, reaches=None):
    counts = [len(operands), len(moves), len(out_shape), len(moves), len(scratch)]

    def kernel(*refs):
        parts, at = [], 0
        for count in counts:
            parts.append(refs[at : at + count])
            at += count
        ins, sources, outs, targets, held = parts
        here = Here(grid)
        step = pl.program_id(0)
        planned = []
        if moves:
            sends, recvs = refs[at:]
            base = 0
            for move, source, target in zip(moves, sources, targets):
                planned += move.plan(here, source, target, sends, recvs, base)
                base += move.count

        if moves or reaches:

            @pl.when(step == 0)
            def _():
                barrier = pltpu.get_barrier_semaphore()
                givers = reaches(here) if reaches else []
                for giver in givers:
                    pl.semaphore_signal(barrier, inc=1, device_id=giver, device_id_type=MESH)
                for _, _, _, giver, _, same_in in planned:
                    signal = functools.partial(
                        pl.semaphore_signal, barrier, inc=1, device_id=giver, device_id_type=MESH
                    )
                    unless(same_in, signal)
                due = len(givers) + sum(same is None for _, same, _, _, _, _ in planned)
                for _, same, _, _, _, _ in planned:
                    if same is not None:
                        due = due + 1 - same.astype(jnp.int32)
                pl.semaphore_wait(barrier, due)
                for away, same, own, _, _, _ in planned:
                    unless(same, away.start)
                    if same is not None:
                        pl.when(same)(own.start)

        if body is not None:
            body(here, step, ins, outs, held)
        if moves:

            @pl.when(step == steps - 1)
            def _():
                for away, same, own, _, came, same_in in planned:
                    unless(same, away.wait_send)
                    if same is not None:
                        pl.when(same)(own.wait)
                    unless(same_in, came.wait_recv)

    total = sum(move.count for move in moves)
    extra = {}
    sems = []
    if moves or reaches:
        extra = {"collective_id": IDS[0], "has_side_effects": True}
        IDS[0] += 1
    if moves:
        sems = [pltpu.SemaphoreType.DMA((total,)), pltpu.SemaphoreType.DMA((total,))]
    outs = pl.pallas_call(
        kernel,
        grid=(steps,),
        in_specs=list(in_specs) + [any_spec()] * len(moves),
        out_specs=list(out_specs) + [any_spec()] * len(moves),
        out_shape=list(out_shape) + [jax.ShapeDtypeStruct(m.shape, m.array.dtype) for m in moves],
        scratch_shapes=list(scratch) + sems,
        input_output_aliases={
            len(operands) + i: len(out_shape) + i for i, move in enumerate(moves) if move.in_place
        },
        compiler_params=pltpu.CompilerParams(vmem_limit_bytes=VMEM_LIMIT, **extra),
        cost_estimate=cost,
    )(*operands, *[move.array for move in moves])
    return outs[: len(out_shape)], outs[len(out_shape) :]


def send(grid, moves):
    return host(grid, None, 1, [], [], [], [], moves)[1]


class GainSum:
    def __init__(self, grid, total):
        self.grid, self.total, self.stage = grid, total, 0

    def move(self):
        grid, phase = self.grid, self.stage - 1
        if self.stage == 0:
            return swap_move(self.total)
        if phase < grid.bits:
            return peer_move(self.total, lambda here: here.flip(phase))
        return line_move(grid, self.total)

    def took(self, got):
        if self.stage > self.grid.bits:
            got = sum(got[t] for t in range(self.grid.F - 1))
        self.total = self.total + got
        self.stage += 1

    def finish(self):
        while self.stage <= self.grid.bits + 1:
            self.took(send(self.grid, [self.move()])[0])
        return self.total


def rope_tables():
    half_dim = HEAD_DIM // 2
    frequency = jnp.exp(
        jnp.arange(half_dim, dtype=F32) * (-2.0 * math.log(10000.0) / HEAD_DIM)
    )
    angles = jnp.arange(SEG, dtype=jnp.int32).astype(F32)[:, None] * frequency[None, :]
    cos, sin = jnp.cos(angles), jnp.sin(angles)
    return (jnp.concatenate([cos, cos], axis=-1), jnp.concatenate([-sin, sin], axis=-1))


def turn(values, cos, sin):
    return values * cos + pltpu.roll(values, HEAD_DIM // 2, 1) * sin


def smem():
    return pl.BlockSpec(memory_space=pltpu.SMEM)


def whole_spec(*shape):
    return pl.BlockSpec(shape, lambda i: (0,) * len(shape))


def columns_spec(*shape, first=0):
    return pl.BlockSpec(shape, lambda i: (0,) * (len(shape) - 1) + (i + first,))


def rows_spec(*shape):
    return pl.BlockSpec(shape, lambda i: (i,) + (0,) * (len(shape) - 1))


def kind(*shape, dtype=BF):
    return jax.ShapeDtypeStruct(shape, dtype)


def piece_start(grid, member, part):
    return (member if part == 0 else grid.F - 1 - member) * grid.R


def table_rows(grid, table_ref, member, part):
    start = pl.multiple_of(piece_start(grid, member, part), grid.R)
    return table_ref[pl.ds(start, grid.R), :]


def dot(left, right, contract):
    return lax.dot_general(
        left, right, (((contract[0],), (contract[1],)), ((), ())), preferred_element_type=F32
    )


def mm(left, right, contract=(1, 0)):
    return dot(left, right, contract)


def project(grid, memory, tables, hidden, gain, weight, moves=()):
    rows, width = hidden.shape
    heads = weight.shape[1] // (3 * HEAD_DIM)
    together = 2
    size = together * HEAD_DIM
    steps = heads // together
    count = 3 if memory else 2

    width_out = heads * HEAD_DIM

    def sends(here, held, target, step):
        columns = pl.ds(pl.multiple_of(step * size, 128), size)
        return [
            pltpu.make_async_remote_copy(
                src_ref=held[0].at[:, :, columns],
                dst_ref=target.at[t - 1, :, :, columns],
                send_sem=held[1].at[0, t - 1, step],
                recv_sem=held[1].at[1, t - 1, step],
                device_id=here.member(t),
                device_id_type=MESH,
            )
            for t in range(1, grid.U)
        ]

    def body(here, step, ins, outs, held):
        cos_ref, sin_ref, hidden_ref, gain_ref = ins[:4]
        normed_ref, q_out, kv_out, others = outs[:4]

        @pl.when(step == 0)
        def _():
            normed_ref[...] = norm(hidden_ref[...].astype(F32), gain_ref[...]).astype(BF)

        for part in range(2):
            at = pl.ds(part * grid.R, grid.R)
            cos = table_rows(grid, cos_ref, here.k, part)
            sin = table_rows(grid, sin_ref, here.k, part)
            normed = normed_ref[at, :]
            query, key, value = (dot(normed, w[...], (1, 0)) for w in ins[4:])
            kv_out[1, at, :] = value.astype(BF)
            for h in range(together):
                columns = slice(h * HEAD_DIM, (h + 1) * HEAD_DIM)
                q_out[at, columns] = turn(query[:, columns], cos, sin).astype(BF)
                kv_out[0, at, columns] = turn(key[:, columns], cos, sin).astype(BF)
            if memory:
                kv_out[2, at, :] = key.astype(BF)
                outs[4][at, :] = query.astype(BF)
        held[0][:, :, pl.ds(pl.multiple_of(step * size, 128), size)] = kv_out[...]
        for copy in sends(here, held, others, step):
            copy.start()

        @pl.when(step == steps - 1)
        def _():
            for i in range(steps):
                for copy in sends(here, held, others, i):
                    copy.wait()

    piece = columns_spec(rows, size)
    table = whole_spec(SEG, HEAD_DIM)
    flat = kind(rows, width_out)
    return host(
        grid,
        body,
        steps,
        [table, table, whole_spec(rows, width), whole_spec(1, width)]
        + [columns_spec(width, size, first=i * steps) for i in range(3)],
        [*tables, hidden, gain, weight, weight, weight],
        [whole_spec(rows, width), piece, columns_spec(count, rows, size), any_spec()] + [piece] * memory,
        [kind(rows, width), flat, kind(count, rows, width_out), kind(grid.U - 1, count, rows, width_out)]
        + [flat] * memory,
        moves,
        scratch=[
            pltpu.VMEM((count, rows, width_out), BF),
            pltpu.SemaphoreType.DMA((2, grid.U - 1, steps)),
        ],
        cost=pl.CostEstimate(
            flops=2 * rows * width * weight.shape[1], bytes_accessed=2 * width * weight.shape[1], transcendentals=0
        ),
        reaches=lambda here: [here.member(grid.U - t) for t in range(1, grid.U)],
    )


def part_scores(grid, here, valid, part, query, keys):
    shape = (grid.R, grid.R)
    apart = lax.broadcasted_iota(jnp.int32, shape, 0) - lax.broadcasted_iota(jnp.int32, shape, 1)
    found = []
    for t in range(grid.U):
        member = (here.k - t + grid.U) % grid.U
        for side in range(part + 1):
            score = dot(keys[t][side * grid.R : (side + 1) * grid.R], query, (1, 1))
            if side == part:
                start = piece_start(grid, member, side)
                allowed = apart <= piece_start(grid, here.k, part) - start
                if side == 1:
                    down = lax.broadcasted_iota(jnp.int32, shape, 0)
                    allowed = allowed & (down < valid - start)
                score = jnp.where(allowed, score, MASKED)
            found.append((t, side, score))
    return found


def softmax_parts(scores, stat=None):
    top = functools.reduce(jnp.maximum, [jnp.max(s, axis=0, keepdims=True) for s in scores])
    powers = [jnp.exp2((s - top) * (SCALE * LOG2E)) for s in scores]
    total = sum(jnp.sum(p, axis=0, keepdims=True) for p in powers)
    if stat is not None:
        stat(top * (SCALE * LOG2E) + jnp.log(total) * LOG2E)
    inverse = 1.0 / total
    return [p * inverse for p in powers]


def attention_cost(grid, heads, memory_rows, products):
    pairs = grid.T * (SEG * 3 // 4 + memory_rows) * heads
    return pl.CostEstimate(
        flops=2 * products * HEAD_DIM * pairs,
        bytes_accessed=2 * HEAD_DIM * heads * 4 * (SEG + memory_rows),
        transcendentals=pairs,
    )


def memory_operands(grid, extra):
    rows = extra["memory"].shape[1]
    return [extra["query"], extra["memory"], extra["bias"]], [
        columns_spec(grid.T, HEAD_DIM), columns_spec(2, rows, HEAD_DIM), whole_spec(rows, 1)
    ], rows


def attend(grid, valid, query, pairs, extra, moves=()):
    rows, width = query.shape
    heads = width // HEAD_DIM
    R, U = grid.R, grid.U

    def body(here, step, ins, outs, held):
        valid_ref, q_ref, kv_refs, refs = ins[0], ins[1], ins[2 : 2 + U], ins[2 + U :]
        keys, values = [r[0] for r in kv_refs], [r[1] for r in kv_refs]
        for part in range(2):
            at = pl.ds(part * R, R)
            found = part_scores(grid, here, valid_ref[0], part, q_ref[at, :], keys)
            scores = [s for _, _, s in found]
            mixed = [values[t][side * R : (side + 1) * R] for t, side, _ in found]
            if extra is not None:
                scores.append(dot(refs[1][0], refs[0][at, :], (1, 1)) + refs[2][...])
                mixed.append(refs[1][1])

            def stat(row):
                outs[1][0, :, at] = row

            probs = softmax_parts(scores, stat)
            total = sum(dot(value, p.astype(BF), (0, 0)) for value, p in zip(mixed, probs))
            outs[0][at, :] = total.T.astype(BF)

    piece = columns_spec(rows, HEAD_DIM)
    operands = [valid, query, *pairs]
    specs = [smem(), piece] + [columns_spec(2, rows, HEAD_DIM)] * U
    memory_rows = 0
    if extra is not None:
        more, more_specs, memory_rows = memory_operands(grid, extra)
        operands, specs = operands + more, specs + more_specs
    outs, got = host(
        grid, body, heads, specs, operands,
        [piece, rows_spec(1, 1, rows)], [kind(rows, width), kind(heads, 1, rows, dtype=F32)], moves,
        cost=attention_cost(grid, heads, memory_rows, 2),
    )
    return outs[0], outs[1], got


def inner_row(grads, mixed):
    return jnp.sum((grads.astype(F32) * mixed.astype(F32)).T, axis=0, keepdims=True)


def memory_back(grid, grad_heads, attended, extra, moves=()):
    rows, width = grad_heads.shape
    heads = width // HEAD_DIM
    per = heads // 2
    memory_rows = extra["memory"].shape[1]

    def memory_send(here, held, target, h):
        columns = pl.ds(pl.multiple_of(h * HEAD_DIM, HEAD_DIM), HEAD_DIM)
        return pltpu.make_async_remote_copy(
            src_ref=held[0].at[h],
            dst_ref=target.at[:, :, columns],
            send_sem=held[1].at[0, h],
            recv_sem=held[1].at[1, h],
            device_id=here.swap,
            device_id_type=MESH,
        )

    def body(here, step, ins, outs, held):
        g_ref, mixed_ref, stat_ref, q_ref, memory_ref, bias_ref = ins
        grad_key, grad_value = 0.0, 0.0
        for part in range(2):
            at = pl.ds(part * grid.R, grid.R)
            grads, query = g_ref[at, :], q_ref[at, :]
            inner = inner_row(grads, mixed_ref[at, :])
            score = dot(memory_ref[0], query, (1, 1)) + bias_ref[...]
            prob = jnp.exp2(score * (SCALE * LOG2E) - stat_ref[0, :, at])
            moved = (prob * (dot(memory_ref[1], grads, (1, 1)) - inner)).astype(BF)
            grad_key = grad_key + dot(moved, query, (1, 0))
            grad_value = grad_value + dot(prob.astype(BF), grads, (1, 0))
            outs[0][at, :] = dot(memory_ref[0], moved, (0, 0)).T
        grad_key, grad_value = (grad_key * SCALE).astype(BF), grad_value.astype(BF)
        outs[1][0] = grad_key
        outs[1][1] = grad_value

        @pl.when(step // per == 1 - here.c)
        def _():
            held[0][step % per, 0] = grad_key
            held[0][step % per, 1] = grad_value
            memory_send(here, held, outs[2], step % per).start()

        @pl.when(step == heads - 1)
        def _():
            for h in range(per):
                memory_send(here, held, outs[2], h).wait()

    piece = columns_spec(rows, HEAD_DIM)
    column = columns_spec(2, memory_rows, HEAD_DIM)
    return host(
        grid, body, heads,
        [piece, piece, rows_spec(1, 1, rows), piece, column, whole_spec(memory_rows, 1)],
        [grad_heads, attended, extra["logsum"], extra["query"], extra["memory"], extra["bias"]],
        [piece, column, any_spec()],
        [kind(rows, width, dtype=F32), kind(2, memory_rows, width), kind(2, memory_rows, width // 2)],
        moves,
        scratch=[pltpu.VMEM((per, 2, memory_rows, HEAD_DIM), BF), pltpu.SemaphoreType.DMA((2, per))],
        cost=pl.CostEstimate(
            flops=10 * HEAD_DIM * rows * memory_rows * heads,
            bytes_accessed=12 * memory_rows * width,
            transcendentals=rows * memory_rows * heads,
        ),
        reaches=lambda here: [here.swap],
    )


def attend_back(grid, valid, tables, query, grad, w_out, pairs, moves=(), memory=None):
    rows, width = query.shape
    heads = width // HEAD_DIM
    R, U = grid.R, grid.U

    def sends(here, held, target, h):
        columns = pl.ds(pl.multiple_of(h * HEAD_DIM, HEAD_DIM), HEAD_DIM)
        return [
            pltpu.make_async_remote_copy(
                src_ref=held[0].at[h, t - 1],
                dst_ref=target.at[t - 1, :, :, columns],
                send_sem=held[1].at[0, t - 1, h],
                recv_sem=held[1].at[1, t - 1, h],
                device_id=here.member(U - t),
                device_id_type=MESH,
            )
            for t in range(1, U)
        ]

    def body(here, step, ins, outs, held):
        valid_ref, cos_ref, sin_ref, q_ref, g_ref = ins[:5]
        kv_refs, refs = ins[5 : 5 + U], ins[5 + U :]
        keys, values = [r[0] for r in kv_refs], [r[1] for r in kv_refs]
        grad_keys, grad_values = {}, {}

        def add(store, at, value):
            store[at] = store[at] + value if at in store else value

        if memory is None:

            @pl.when(step == 0)
            def _():
                held[2][...] = dot(g_ref[...], refs[0][...], (1, 1)).astype(BF)

        for part in range(2):
            at_rows = pl.ds(part * R, R)
            asked = q_ref[at_rows, :]
            if memory is None:
                grads_in = held[2][at_rows, pl.ds(pl.multiple_of(step * HEAD_DIM, HEAD_DIM), HEAD_DIM)]
            else:
                grads_in = g_ref[at_rows, :]
            found = part_scores(grid, here, valid_ref[0], part, asked, keys)
            places = [(t, side) for t, side, _ in found]
            scores = [s for _, _, s in found]
            part_keys = [keys[t][side * R : (side + 1) * R] for t, side in places]
            part_values = [values[t][side * R : (side + 1) * R] for t, side in places]
            grads = [dot(value, grads_in, (1, 1)) for value in part_values]
            if memory is None:
                probs = softmax_parts(scores)
                inner = sum(jnp.sum(p * d, axis=0, keepdims=True) for p, d in zip(probs, grads))
            else:
                probs = [jnp.exp2(s * (SCALE * LOG2E) - refs[1][0, :, at_rows]) for s in scores]
                inner = inner_row(grads_in, refs[0][at_rows, :])
            back = None
            for at, p, d, key in zip(places, probs, grads, part_keys):
                moved = (p * (d - inner)).astype(BF)
                add(grad_keys, at, dot(moved, asked, (1, 0)))
                add(grad_values, at, dot(p.astype(BF), grads_in, (1, 0)))
                share = dot(key, moved, (0, 0))
                back = share if back is None else back + share
            cos = table_rows(grid, cos_ref, here.k, part)
            sin = table_rows(grid, sin_ref, here.k, part)
            result = turn(back.T, cos, -sin)
            if memory is not None:
                result = result + refs[2][at_rows, :]
            outs[0][at_rows, :] = (result * SCALE).astype(BF)
        for t in range(U):
            member = (here.k - t + U) % U
            for side in range(2):
                at_rows = pl.ds(side * R, R)
                cos = table_rows(grid, cos_ref, member, side)
                sin = table_rows(grid, sin_ref, member, side)
                key = turn(grad_keys[(t, side)], cos, -sin) * SCALE
                if t == 0:
                    outs[1][0, at_rows, :] = key
                    outs[1][1, at_rows, :] = grad_values[(t, side)]
                else:
                    held[0][step, t - 1, 0, at_rows, :] = key.astype(BF)
                    held[0][step, t - 1, 1, at_rows, :] = grad_values[(t, side)].astype(BF)
        for copy in sends(here, held, outs[2], step):
            copy.start()

        @pl.when(step == heads - 1)
        def _():
            for h in range(heads):
                for copy in sends(here, held, outs[2], h):
                    copy.wait()

    piece = columns_spec(rows, HEAD_DIM)
    pair = columns_spec(2, rows, HEAD_DIM)
    table = whole_spec(SEG, HEAD_DIM)
    operands = [valid, *tables, query, grad, *pairs]
    scratch = [pltpu.VMEM((heads, U - 1, 2, rows, HEAD_DIM), BF), pltpu.SemaphoreType.DMA((2, U - 1, heads))]
    if memory is None:
        specs = [smem(), table, table, piece, whole_spec(rows, width)] + [pair] * U + [whole_spec(width, width)]
        operands.append(w_out)
        scratch.append(pltpu.VMEM((rows, width), BF))
    else:
        specs = [smem(), table, table, piece, piece] + [pair] * U + [piece, rows_spec(1, 1, rows), piece]
        operands += memory
    return host(
        grid, body, heads, specs, operands,
        [piece, pair, any_spec()],
        [kind(rows, width), kind(2, rows, width, dtype=F32), kind(U - 1, 2, rows, width)],
        moves,
        scratch=scratch,
        cost=attention_cost(grid, heads, 0, 5),
        reaches=lambda here: [here.member(t) for t in range(1, U)],
    )


def gather_memory(grid, picks, pairs):
    n, U, R = grid.n_dp, grid.U, grid.R
    heads, topk = picks.shape
    per = heads // 2
    half = per * HEAD_DIM

    def body(here, step, ins, outs, held):
        picks_ref, sources, target = ins[0], ins[1:], outs[0]
        rows, chosen, load_sems, own_sem, sems = held
        columns = pl.ds(pl.multiple_of(here.c * half, 128), half)
        loads = [
            pltpu.make_async_copy(source.at[1:3, :, columns], rows.at[t], load_sems.at[t])
            for t, source in enumerate(sources)
        ]
        for load in loads:
            load.start()
        for load in loads:
            load.wait()
        for h in range(per):
            picked = picks_ref[here.c * per + h]
            at_columns = slice(h * HEAD_DIM, (h + 1) * HEAD_DIM)
            totals = [0.0, 0.0]
            for t in range(U):
                member = (here.k - t + U) % U
                for side in range(2):
                    across = lax.broadcasted_iota(jnp.int32, (topk, R), 1)
                    mask = (picked == across + piece_start(grid, member, side)).astype(BF)
                    for i in range(2):
                        block = rows[t, i, side * R : (side + 1) * R, at_columns]
                        totals[i] = totals[i] + dot(mask, block, (1, 0))
            chosen[0, :, at_columns] = totals[1].astype(BF)
            chosen[1, :, at_columns] = totals[0].astype(BF)
        mine = target.at[:, :, :, columns]
        own = pltpu.make_async_copy(chosen, mine.at[:, 0], own_sem)
        across = [remote(chosen, mine.at[:, t], sems, t, here.slots(t)) for t in range(1, n)]
        swaps = [remote(chosen, mine.at[:, 0], sems, n, here.swap)]
        swaps += [remote(mine.at[:, t], mine.at[:, t], sems, n + t, here.swap) for t in range(1, n)]
        for copy in across + [swaps[0], own]:
            copy.start()
        for t in range(1, n):
            across[t - 1].wait_recv()
            swaps[t].start()
        own.wait()
        for copy in across:
            copy.wait_send()
        for copy in swaps:
            copy.wait()

    outs, _ = host(
        grid, body, 1,
        [whole_spec(heads, topk, 1)] + [any_spec()] * U,
        [picks[:, :, None], *pairs],
        [any_spec()], [kind(2, n, topk, 2 * half)],
        scratch=[
            pltpu.VMEM((U, 2, grid.T, half), BF),
            pltpu.VMEM((2, topk, half), BF),
            pltpu.SemaphoreType.DMA((U,)),
            pltpu.SemaphoreType.DMA,
            pltpu.SemaphoreType.DMA((2, 2 * n)),
        ],
        reaches=lambda here: [here.slots(n - t) for t in range(1, n)] + [here.swap],
    )
    return outs[0]


def finish_gradient(grid, grad_query, own, others, picks, memory, moves=()):
    rows, width = grad_query.shape
    heads = width // HEAD_DIM
    R, U = grid.R, grid.U

    def body(here, step, ins, outs, held):
        dq_ref, own_ref, others_ref = ins[:3]
        out_ref = outs[0]

        @pl.when(step == 0)
        def _():
            out_ref[...] = dq_ref[...]

        @pl.when(step > 0)
        def _():
            for side in range(2):
                at = pl.ds(side * R, R)
                for h in range(heads):
                    columns = pl.ds(h * HEAD_DIM, HEAD_DIM)
                    value = own_ref[0, at, columns]
                    for t in range(U - 1):
                        value = value + others_ref[t, 0, at, columns].astype(F32)
                    if memory is not None:
                        picked = ins[3][h]
                        down = lax.broadcasted_iota(jnp.int32, (R, picked.shape[1]), 0)
                        chosen = (down + piece_start(grid, here.k, side) == picked).astype(BF)
                        value = value + dot(chosen, ins[4][0, :, columns], (1, 0))
                    out_ref[at, columns] = value.astype(BF)

    which = lambda b: jnp.maximum(b - 1, 0)
    operands = [grad_query, own, others]
    specs = [
        whole_spec(rows, width),
        pl.BlockSpec((1, rows, width), lambda b: (which(b), 0, 0)),
        pl.BlockSpec((U - 1, 1, rows, width), lambda b: (0, which(b), 0, 0)),
    ]
    if memory is not None:
        topk = picks.shape[1]
        operands += [picks[:, None, :], memory]
        specs += [
            whole_spec(heads, 1, topk),
            pl.BlockSpec((1, topk, width), lambda b: (which(b), 0, 0)),
        ]
    outs, got = host(
        grid, body, 3, specs, operands, [columns_spec(rows, width)], [kind(rows, 3 * width)], moves,
        cost=pl.CostEstimate(flops=2 * rows * width, bytes_accessed=16 * rows * width, transcendentals=0),
    )
    return outs[0], got


FEED_TILE = 256


def feed(grid, hidden_rows, attended, gain, w_out, w_up, w_down, moves=()):
    rows, width = hidden_rows.shape
    hidden = w_down.shape[0]
    steps = hidden // FEED_TILE

    def body(here, step, ins, outs, held):
        hidden_ref, attended_ref, gain_ref, out_w, gate_w, up_w, down_w = ins
        out_ref, middle_ref, normed_ref, both_ref, inner_ref = outs

        @pl.when(step == 0)
        def _():
            value = hidden_ref[...].astype(F32) + dot(attended_ref[...], out_w[...], (1, 0))
            middle_ref[...] = value
            normed_ref[...] = norm(value, gain_ref[...]).astype(BF)
            held[0][...] = value

        normed = normed_ref[...]
        gate, up = dot(normed, gate_w[...], (1, 0)), dot(normed, up_w[...], (1, 0))
        both_ref[0] = gate.astype(BF)
        both_ref[1] = up.astype(BF)
        inner = (gate / (1.0 + jnp.exp(-gate)) * up).astype(BF)
        inner_ref[...] = inner
        held[0][...] += dot(inner, down_w[...], (1, 0))

        @pl.when(step == steps - 1)
        def _():
            out_ref[...] = held[0][...]

    tile = columns_spec(width, FEED_TILE)
    return host(
        grid, body, steps,
        [whole_spec(rows, width), whole_spec(rows, width), whole_spec(1, width), whole_spec(width, width), tile,
         columns_spec(width, FEED_TILE, first=steps), rows_spec(FEED_TILE, width)],
        [hidden_rows, attended, gain, w_out, w_up, w_up, w_down],
        [whole_spec(rows, width)] * 3 + [columns_spec(2, rows, FEED_TILE), columns_spec(rows, FEED_TILE)],
        [kind(rows, width, dtype=F32), kind(rows, width, dtype=F32), kind(rows, width), kind(2, rows, hidden), kind(rows, hidden)],
        moves,
        scratch=[pltpu.VMEM((rows, width), F32)],
        cost=pl.CostEstimate(flops=6 * rows * width * hidden, bytes_accessed=6 * width * hidden, transcendentals=rows * hidden),
    )


def feed_back(grid, grad, middle, gain, both, w_up, w_down, moves=()):
    rows, width = grad.shape
    hidden = w_down.shape[0]
    steps = hidden // FEED_TILE

    def body(here, step, ins, outs, held):
        grad_ref, middle_ref, gain_ref, both_ref, gate_w, up_w, down_w = ins
        out_ref, low_ref, grads_ref, gain_out = outs
        total = held[0]

        @pl.when(step == 0)
        def _():
            held[1][...] = grad_ref[...].astype(BF)
            total[...] = jnp.zeros_like(total)

        grad_inner = dot(held[1][...], down_w[...], (1, 1))
        gate, up = both_ref[0].astype(F32), both_ref[1].astype(F32)
        sigmoid = 1.0 / (1.0 + jnp.exp(-gate))
        scaled = grad_inner * sigmoid
        grad_gate = (scaled * up * (1.0 + gate * (1.0 - sigmoid))).astype(BF)
        grad_up = (scaled * gate).astype(BF)
        grads_ref[0] = grad_gate
        grads_ref[1] = grad_up
        total[...] += dot(grad_gate, gate_w[...], (1, 1)) + dot(grad_up, up_w[...], (1, 1))

        @pl.when(step == steps - 1)
        def _():
            pulled, grad_gain = norm_back(middle_ref[...], gain_ref[...], total[...])
            result = grad_ref[...] + pulled
            out_ref[...] = result
            low_ref[...] = result.astype(BF)
            gain_out[...] = grad_gain

    tile = columns_spec(width, FEED_TILE)
    whole = whole_spec(rows, width)
    return host(
        grid, body, steps,
        [whole, whole, whole_spec(1, width), columns_spec(2, rows, FEED_TILE), tile,
         columns_spec(width, FEED_TILE, first=steps), rows_spec(FEED_TILE, width)],
        [grad, middle, gain, both, w_up, w_up, w_down],
        [whole, whole, columns_spec(2, rows, FEED_TILE), whole_spec(1, width)],
        [kind(rows, width, dtype=F32), kind(rows, width), kind(2, rows, hidden), kind(1, width, dtype=F32)],
        moves,
        scratch=[pltpu.VMEM((rows, width), F32), pltpu.VMEM((rows, width), BF)],
        cost=pl.CostEstimate(flops=6 * rows * width * hidden, bytes_accessed=6 * width * hidden, transcendentals=rows * hidden),
    )


def norm(value, gain):
    return value * lax.rsqrt(jnp.mean(value * value, axis=-1, keepdims=True) + EPSILON) * gain


def norm_back(value, gain, grad):
    inverse = lax.rsqrt(jnp.mean(value * value, axis=-1, keepdims=True) + EPSILON)
    unit = value * inverse
    grad_gain = jnp.sum(grad * unit, axis=0, keepdims=True)
    scaled = grad * gain
    pulled = inverse * (scaled - unit * jnp.mean(scaled * unit, axis=-1, keepdims=True))
    return pulled, grad_gain


def product(grid, left, left_other, right, moves=(), piece=(0, 1)):
    rows, height = left.shape
    stacked = right.ndim == 3
    full = right.shape[-1] if stacked else right.shape[-1] // 2
    half = full // piece[1]
    tile = 512 if height % 512 == 0 else height // 2
    tiles = height // tile
    fetch = left_other is None

    def part(ref, c):
        ref = ref.at[c] if stacked else ref
        start = piece[0] * half if stacked else c * full + piece[0] * half
        return ref.at[:, pl.ds(pl.multiple_of(start, 128), half)]

    def body(here, step, ins, outs, held):
        own_ref, other_ref, right_ref = ins
        own_right, other_right, total, own_sem, sems = held[:5]
        own = pltpu.make_async_copy(part(right_ref, here.c), own_right, own_sem)
        swaps = [remote(part(right_ref, 1 - here.c), other_right, sems, 0, here.swap)]
        if fetch:
            swaps.append(remote(other_ref, held[5], sems, 1, here.swap))

        @pl.when(step == 0)
        def _():
            own.start()
            for swap in swaps:
                swap.start()
            own.wait()

        @pl.when(step < tiles)
        def _():
            total[step] = dot(own_ref[...], own_right[...], (0, 0))

        @pl.when(step == tiles)
        def _():
            for swap in swaps:
                swap.wait()

        @pl.when(step >= tiles)
        def _():
            other = other_ref
            if fetch:
                other = held[5].at[:, pl.ds(pl.multiple_of((step - tiles) * tile, 128), tile)]
            outs[0][...] = (total[step - tiles] + dot(other[...], other_right[...], (0, 0))).astype(BF)

    early = lambda i: jnp.minimum(i, tiles - 1)
    late = lambda i: jnp.maximum(i - tiles, 0)
    other_spec = any_spec() if fetch else pl.BlockSpec((rows, tile), lambda i: (0, late(i)))
    outs, got = host(
        grid, body, 2 * tiles,
        [pl.BlockSpec((rows, tile), lambda i: (0, early(i))), other_spec, any_spec()],
        [left, left if fetch else left_other, right],
        [pl.BlockSpec((tile, half), lambda i: (late(i), 0))],
        [kind(height, half)],
        moves,
        scratch=[
            pltpu.VMEM((rows, half), BF),
            pltpu.VMEM((rows, half), BF),
            pltpu.VMEM((tiles, tile, half), F32),
            pltpu.SemaphoreType.DMA,
            pltpu.SemaphoreType.DMA((2, 2)),
        ] + [pltpu.VMEM((rows, height), BF)] * fetch,
        cost=pl.CostEstimate(flops=4 * rows * height * half, bytes_accessed=2 * height * half, transcendentals=0),
        reaches=lambda here: [here.swap],
    )
    return outs[0], got


class Reduce:
    def __init__(self, grid, total):
        self.grid = grid
        self.parts = total.reshape(grid.J, total.shape[0] // grid.J, total.shape[1])
        self.phase, self.came = 0, []

    def flip(self):
        return flip_move(self.grid, self.parts, self.phase)

    def flipped(self, got):
        grid = self.grid
        if self.phase == 0:
            kept = jnp.stack(
                [
                    lax.dynamic_index_in_dim(self.parts, grid.place(2 * i, grid.c), 0, keepdims=False)
                    for i in range(grid.J // 2)
                ]
            )
        else:
            kept = self.parts[0::2]
        self.parts = (kept.astype(F32) + got.astype(F32)).astype(BF)
        self.phase += 1
        if self.phase == grid.bits:
            self.line = self.parts.reshape(2, grid.F, -1, self.parts.shape[2])

    def ring(self, distances=None):
        grid = self.grid
        while self.phase < grid.bits:
            self.flipped(send(grid, [self.flip()])[0])
        return ring_move(grid, self.line, distances or list(range(1, grid.F)))

    def far(self):
        return self.ring([self.grid.F // 2])

    def near(self):
        return self.ring([t for t in range(1, self.grid.F) if t != self.grid.F // 2])

    def arrived(self, got):
        grid = self.grid
        self.came.append(got)

    def done(self):
        grid = self.grid
        here = lax.dynamic_index_in_dim(self.line, grid.f, 1, keepdims=False)
        summed = here.astype(F32) + sum(
            part[i].astype(F32) for part in self.came for i in range(part.shape[0])
        )
        mine = lax.dynamic_index_in_dim(summed, grid.c, 0, keepdims=False)
        give = lax.dynamic_index_in_dim(summed, 1 - grid.c, 0, keepdims=False)
        got = grid.swap(give.astype(BF)).astype(F32)
        return jnp.concatenate(
            [jnp.where(grid.c == 0, mine, got), jnp.where(grid.c == 0, got, mine)], axis=1
        )


def settle(grid, wanted, row_halves, moves):
    flat, ins, specs, scratch, out_shape = [], [], [], [], []
    for o, by_layer in enumerate(wanted):
        for layer, parts in enumerate(by_layer):
            for piece, reduce in enumerate(parts):
                flat.append((o, layer, piece, len(parts), reduce))
        rows, size = wanted[o][0][0].line.shape[2:]
        out_shape.append(kind(len(by_layer), rows, 2 * size * len(by_layer[0]), dtype=F32))
    for _, _, _, _, reduce in flat:
        _, F, rows, size = reduce.line.shape
        ins += [reduce.line, *reduce.came]
        scratch += [
            pltpu.VMEM((F, 2, rows, size), BF),
            pltpu.VMEM((2, rows, size), F32),
            pltpu.VMEM((rows, size), BF),
            pltpu.VMEM((rows, size), BF),
        ]
    count = len(flat)
    ins += row_halves
    high, width = row_halves[0].shape[1:]
    scratch += [pltpu.VMEM((2, 2, high, width), BF)]
    scratch += [pltpu.SemaphoreType.DMA((len(ins),)), pltpu.SemaphoreType.DMA((2, count))]
    out_shape.append(kind(2, 2 * high, width, dtype=F32))

    def body(here, step, refs, outs, held):
        rows_held, load_sems, sems = held[4 * count :]
        loads, swaps, at = [], [], 0
        for i, (_, _, _, _, reduce) in enumerate(flat):
            blocks, _, give, got = held[4 * i : 4 * i + 4]
            mine = [pltpu.make_async_copy(refs[at].at[:, here.f], blocks.at[0], load_sems.at[at])]
            at, filled = at + 1, 1
            for part in reduce.came:
                size = part.shape[0]
                mine.append(
                    pltpu.make_async_copy(refs[at], blocks.at[pl.ds(filled, size)], load_sems.at[at])
                )
                at, filled = at + 1, filled + size
            loads.append(mine)
            swaps.append(remote(give, got, sems, i, here.swap))
        loads.append(
            [pltpu.make_async_copy(refs[at + i], rows_held.at[i], load_sems.at[at + i]) for i in range(2)]
        )
        for mine in loads:
            for copy in mine:
                copy.start()
        for i in range(count):
            blocks, summed, give, _ = held[4 * i : 4 * i + 4]
            for copy in loads[i]:
                copy.wait()
            total = blocks[0].astype(F32)
            for t in range(1, blocks.shape[0]):
                total = total + blocks[t].astype(F32)
            summed[...] = total
            give[...] = summed[1 - here.c].astype(BF)
            swaps[i].start()
        for copy in loads[count]:
            copy.wait()
        for i in range(2):
            outs[-1][:, i * high : (i + 1) * high, :] = rows_held[i].astype(F32)
        for i, (o, layer, piece, pieces, _) in enumerate(flat):
            _, summed, _, got = held[4 * i : 4 * i + 4]
            swaps[i].wait()
            size = got.shape[1]

            def columns(c):
                return pl.ds(pl.multiple_of((c * pieces + piece) * size, 128), size)

            outs[o][layer, :, columns(here.c)] = summed[here.c]
            outs[o][layer, :, columns(1 - here.c)] = got[...].astype(F32)

    return host(
        grid, body, 1, [any_spec()] * len(ins), ins,
        [whole_spec(*o.shape) for o in out_shape], out_shape, moves,
        scratch=scratch,
        reaches=lambda here: [here.swap],
    )


def local(
    n_dp,
    pieces,
    tokens,
    cotangent,
    doc_lengths,
    partner,
    memory_picks,
    attention_in,
    attention_out,
    feed_in,
    feed_out,
    norm_gains,
):
    IDS[0] = 1
    grid = Grid(n_dp, pieces)
    grid.trace()
    layers = attention_in.shape[0]
    width = tokens.shape[2]
    heads = width // HEAD_DIM
    topk = memory_picks.shape[3]
    valid_all, visible_all = jax.vmap(memory_plan)(doc_lengths, partner)
    valid = valid_all[grid.m, grid.slot].reshape(1)
    visible = visible_all[grid.m, grid.slot]
    relative = (grid.slot - jnp.arange(n_dp)) % n_dp
    bias = jnp.repeat(jnp.where(visible[relative], 0.0, MASKED), topk)[:, None].astype(F32)
    tables = rope_tables()
    picks_there = grid.swap(memory_picks)
    picks = jnp.where(grid.r == grid.c, memory_picks[grid.m, 0], picks_there[grid.m, 0])
    zero = grid.c == 0

    def both_halves(mine, other):
        return jnp.where(
            zero, jnp.concatenate([mine, other], axis=-1), jnp.concatenate([other, mine], axis=-1)
        )

    def half(value, c):
        size = value.shape[-1] // 2
        return lax.dynamic_slice_in_dim(value, c * size, size, axis=value.ndim - 1)

    tokens, *tables = lax.optimization_barrier((tokens, *tables))
    hidden, gains, weights = gather_all(
        grid, tokens, norm_gains, [attention_in, attention_out, feed_in, feed_out]
    )
    gain = lambda l, i: gains[l, i][None]
    flat = lambda w: w.reshape(-1, w.shape[-1])
    saved = []
    cotangent_rows = None
    for l in range(layers):
        w_qkv, w_out = flat(weights[l][0]), flat(weights[l][1])
        memory = l == layers - 1
        coming = weights[l + 1] if l + 1 < layers else None
        moves = []
        if coming is not None:
            moves.append(spread_move(grid, coming[3], [(0, 0, 1)]))
        if later_here(l, 2):
            moves += [
                spread_move(grid, weights[l][2], [(1, 0, 2), (1, 1, 2)]),
                spread_move(grid, weights[l][3], [(2, 0, 1)]),
            ]
        split, got = project(grid, memory, tables, hidden, gain(l, 0), w_qkv, moves)
        if coming is not None:
            coming[3] = got[0]
        if later_here(l, 2):
            weights[l][2:] = got[-2:]
        normed, query = split[:2]
        pairs = [split[2]] + [split[3][t] for t in range(grid.U - 1)]
        extra = None
        if memory:
            slots = gather_memory(grid, picks, pairs).reshape(2, n_dp * topk, -1)
            extra = {"query": split[4], "memory": slots, "bias": bias}
        moves = []
        if coming is not None:
            moves.append(spread_move(grid, coming[2], [(0, 0, 2)]))
        if later_here(l, 2):
            moves.append(spread_move(grid, weights[l][2], [(2, 0, 1)]))
        if memory:
            moves.append(regroup_move(grid, cotangent))
        attended, logsum, got = attend(grid, valid, query, pairs, extra, moves)
        if coming is not None:
            coming[2] = got[0]
        if later_here(l, 2):
            weights[l][2] = got[-2]
            for stage in range(3, grid.bits + 1):
                weights[l][2:] = send(grid, [spread_move(grid, w, [(stage, 0, 1)]) for w in weights[l][2:]])
        if memory:
            cotangent_rows = got[-1]
            extra["logsum"] = logsum
        moves = []
        if coming is not None:
            moves = [spread_move(grid, coming[2], [(0, 1, 2)]), spread_move(grid, coming[3], [(1, 0, 1)])]
        w_up, w_down = flat(weights[l][2]), flat(weights[l][3])
        (out, middle, normed_feed, both, inner), got = feed(
            grid, hidden, attended, gain(l, 1), w_out, w_up, w_down, moves
        )
        if coming is not None:
            coming[2:] = got
        saved.append((hidden, normed, query, pairs, extra, attended, middle, normed_feed, both, inner))
        hidden = out
    weights = [[flat(w) for w in kinds] for kinds in weights]
    cotangent_rows = cotangent_rows.reshape(-1, width)
    def row_halves(value):
        value = value.astype(BF).reshape(2, grid.R, width)
        return value[:, : grid.R // 2], value[:, grid.R // 2 :]

    out_rows = row_halves(hidden)
    grad = cotangent_rows.astype(F32)
    found = [[None] * 4 for _ in range(layers)]
    grad_gains = [[None, None] for _ in range(layers)]
    layer_output, above, inner_other = [], None, None

    def took(got, reduces):
        for result, (reduce, what) in zip(got, reduces):
            (reduce.flipped if what == "flip" else reduce.arrived)(result)

    def moves_of(reduces):
        return [getattr(reduce, what)() for reduce, what in reduces]

    for l in reversed(range(layers)):
        w_qkv, w_out, w_up, w_down = weights[l]
        hidden, normed, query, pairs, extra, attended, middle, normed_feed, both, inner = saved[l]
        low = grad.astype(BF)
        last_layer = above is None

        reduces = [] if last_layer else [(above[1], "flip"), (above[2][0], "far")]
        total, got = product(grid, inner, inner_other, low, moves_of(reduces))
        took(got, reduces)
        down = Reduce(grid, total)

        reduces = [(down, "flip")]
        if not last_layer:
            reduces += [(above[0], "flip"), (above[1], "flip"), (above[2][0], "near")]
        moves = moves_of(reduces) + [swap_move(normed_feed), swap_move(normed), swap_move(attended)]
        if last_layer:
            moves += [swap_move(saved[l - 1][9]), regroup_back_move(grid, out_rows[0])]
        (grad, grad_low, grads, gain_feed), got = feed_back(
            grid, grad, middle, gain(l, 1), both, w_up, w_down, moves
        )
        took(got, reduces)
        normed_feed_other, normed_other, attended_other = got[len(reduces) : len(reduces) + 3]
        if last_layer:
            inner_other = got[-2]
            layer_output.append(got[-1])

        ups = []
        pieces_of_up = 1 if last_layer else 2
        for piece in range(pieces_of_up):
            if piece == 0:
                reduces = [(down, "flip")] if last_layer else [(down, "flip"), (above[1], "far")]
            else:
                reduces = [(ups[0], "flip"), (above[1], "near")]
            total, got = product(
                grid, normed_feed, normed_feed_other, grads, moves_of(reduces), (piece, pieces_of_up)
            )
            took(got, reduces)
            ups.append(Reduce(grid, total))

        reduces = [(ups[-1], "flip"), (down, "ring")]
        if not last_layer:
            reduces += [(ups[0], "flip"), (above[0], "ring")]
        memory_grad = None
        if extra is None:
            outs, got = attend_back(grid, valid, tables, query, grad_low, w_out, pairs, moves_of(reduces))
            took(got, reduces)
        else:
            grad_heads = mm(grad_low, w_out, (1, 1)).astype(BF)
            moves = moves_of(reduces)
            if last_layer:
                moves.append(regroup_back_move(grid, out_rows[1]))
            outs, got = memory_back(grid, grad_heads, attended, extra, moves)
            took(got, reduces)
            if last_layer:
                layer_output.append(got[-1])
            joined = half(outs[1], grid.c).astype(F32) + outs[2].astype(F32)
            joined = joined.astype(BF).reshape(2, n_dp, topk, -1)
            outs, got = attend_back(
                grid, valid, tables, query, grad_heads, w_out, pairs, [slots_move(grid, joined, True)],
                [attended, extra["logsum"], outs[0]],
            )
            total = joined[:, 0].astype(F32) + sum(got[0][t].astype(F32) for t in range(n_dp - 1))
            for t in range(1, grid.Q):
                total = total + grid.within(total.astype(BF), t).astype(F32)
            total = total.astype(BF)
            memory_grad = both_halves(total, grid.swap(total))
        grad_query, own, others = outs[:3]
        total, got = product(grid, attended, attended_other, grad_low)
        across = Reduce(grid, total)
        reduces = [(ups[-1], "flip")]
        if not last_layer:
            reduces += [(across, "flip"), (ups[0], "ring")]
        grad_projected, got = finish_gradient(
            grid, grad_query, own, others, picks, memory_grad, moves_of(reduces)
        )
        took(got, reduces)
        pulled, gain_attention = norm_back(
            hidden.astype(F32), gain(l, 0), mm(grad_projected, w_qkv, (1, 1))
        )
        grad = grad + pulled
        grad_gains[l] = [gain_attention[0], gain_feed[0]]
        reduces, moves = [(across, "flip")], []
        if l == 0:
            small = GainSum(grid, jnp.stack([jnp.stack(pair) for pair in grad_gains]).reshape(-1, HEAD_DIM))
            reduces = [(ups[-1], "ring"), (across, "flip")]
            moves = [small.move()]
        total, got = product(grid, normed, normed_other, grad_projected, moves_of(reduces) + moves)
        took(got, reduces)
        if l == 0:
            small.took(got[-1])
        last = Reduce(grid, total)
        found[l] = [[last], [across], ups, [down]]
        above = (across, last, ups)
    across, last, ups = above
    in_rows = row_halves(grad)
    input_grad = []
    for i, reduces in enumerate([[(last, "flip"), (across, "ring")], [(last, "flip")]]):
        got = send(grid, moves_of(reduces) + [regroup_back_move(grid, in_rows[i]), small.move()])
        took(got, reduces)
        small.took(got[-1])
        input_grad.append(got[-2])
    wanted = [[found[l][0] for l in range(1, layers)]]
    wanted += [[found[l][i] for l in range(layers)] for i in range(1, 4)]
    outs, got = settle(grid, wanted, input_grad, [last.ring(), small.move()])
    last.arrived(got[0])
    small.took(got[1])
    grad_in, grad_out, grad_up, grad_down, input_grad = outs
    grad_in = jnp.concatenate([last.done()[None], grad_in])
    layer_output = jnp.concatenate(layer_output, axis=1)
    total_gains = small.finish().reshape(layers, 2, n_dp * pieces, -1)
    device = (grid.j * 2 + grid.c) * grid.F + grid.f
    return (
        layer_output,
        input_grad,
        grad_in,
        grad_out,
        grad_up,
        grad_down,
        lax.dynamic_index_in_dim(total_gains, device, 2, keepdims=False),
    )


def solution(mesh):
    rows = P(None, ("dp", "fsdp"), None)
    in_specs = (rows, rows, P(), P(), P(None, "dp", None, None), rows, rows, rows, rows, P(None, None, ("dp", "fsdp")))
    out_specs = (rows, rows, rows, rows, rows, rows, P(None, None, ("dp", "fsdp")))
    body = functools.partial(local, mesh.shape["dp"], mesh.shape["fsdp"])
    return jax.shard_map(body, mesh=mesh, in_specs=in_specs, out_specs=out_specs, check_vma=False)
```
